32 devices in a mesh: section: 2 (over x), dp: 8 (over z, y), tensor: 2 (over core).
Axes of the slice: x: 2, y: 2, z: 4, core: 2. Of those that a mesh axis runs over, the one named last changes fastest.
Arguments:
- tokens: bfloat16 [2, 8, 128, 768], P(None, 'dp'), may hold values from -6 to 6
- cotangent: bfloat16 [2, 8, 128, 768], P(None, 'dp'), may hold values from -6 to 6
- segments: int32 [2, 8, 128], P(None, 'dp'), may hold values from 0 to 7, never falling along the last dimension, each value on 1 to 96 neighbouring positions
- pad_mask: int32 [2, 8, 128], P(None, 'dp'), may hold values 0 or 1
- routes: int32 [2, 8, 128, 2], P(None, 'dp'), may hold values from 0 to 7, all different within a row; in each aligned block of 128 rows (0 to 127, 128 to 255, ..., all dimensions but the last counted through in order) at most 48 rows name the same one
- dist_bucket: int32 [128], replicated, may hold values from 0 to 31, as said below
- norm_gains: bfloat16 [2, 2, 768], P('section'), may hold values from 0.5 to 1.5
- qkv_weight: bfloat16 [2, 768, 3, 768], P('section', None, None, 'tensor'), may hold values from -0.21875 to 0.21875
- out_weight: bfloat16 [2, 768, 768], P('section', 'tensor'), may hold values from -0.875 to 0.875
- rel_bias: bfloat16 [2, 32, 12], P('section', None, 'tensor'), may hold values from -4 to 4
- router_weight: bfloat16 [2, 768, 8], P('section'), may hold values from -0.15625 to 0.15625
- expert_up: bfloat16 [2, 8, 768, 3072], P('section', 'dp', None, 'tensor'), may hold values from -0.21875 to 0.21875
- expert_down: bfloat16 [2, 8, 3072, 768], P('section', 'dp', 'tensor'), may hold values from -0.21875 to 0.21875
Outputs:
- section_outputs: float32 [2, 2, 8, 128, 768], P('section', None, 'dp', None, 'tensor')
- input_grads: float32 [2, 2, 8, 128, 768], P('section', None, 'dp', None, 'tensor')
- grad_gains: float32 [2, 2, 768], P('section')
- grad_qkv: float32 [2, 768, 3, 768], P('section', None, None, 'tensor')
- grad_out: float32 [2, 768, 768], P('section', 'tensor')
- grad_bias: float32 [2, 32, 12], P('section', None, 'tensor')
- grad_router: float32 [2, 768, 8], P('section')
- grad_up: float32 [2, 8, 768, 3072], P('section', 'dp', None, 'tensor')
- grad_down: float32 [2, 8, 3072, 768], P('section', 'dp', 'tensor')
The draws below stay inside these ranges and needn't reach their ends.
Inputs may be any that keep to these rules, and one draw needn't show every extreme that they name: `routes`: in each aligned block of 128 rows (one sequence) no expert is named by more than 48 route entries, a bound that some block reaches; a token's two experts differ. `dist_bucket`: never falls as the distance grows; 0 at distance 0.
All inputs are finite; a program needn't handle non-finite values. No bound on the sum of `pad_mask` on one device may be relied on, other than what follows from the above.
Results may differ from the reference program's by a relative error of at most 0.02.
Values may be sent and summed in bfloat16 or wider, within the bound.
A program may use at most 192 MiB of HBM per device.

```python
import math
import jax
import jax.numpy as jnp
import numpy as np
from jax import lax

D = 768
H = 12
HD = 64
FF = 3072
BUCKETS = 32
MICRO = 2
LEN = 128
EXPERTS = 8
SEQS = 8
CAP = 48
SECTIONS = 2


def draw_dist_bucket(key, part):
    key = jax.random.fold_in(key, 11)
    raises = jax.random.randint(key, (LEN,), 0, 2)
    places = jnp.arange(LEN)
    raises = jnp.where(places == 0, 0, raises)
    levels = jnp.minimum(jnp.cumsum(raises), BUCKETS - 1)
    return jnp.where(places == LEN - 1, BUCKETS - 1, levels).astype(jnp.int32)


def plant(result, own_key, smallest, largest):
    extent = result.shape
    place = [jax.random.randint(jax.random.fold_in(own_key, axis), (), 0, extent[axis]) for axis in range(len(extent))]
    result = result.at[tuple(place)].set(smallest)
    longest = extent.index(max(extent))
    place[longest] = (place[longest] + 1) % extent[longest]
    return result.at[tuple(place)].set(largest)


def shard_levels(rng, extent, shards, least, high):
    gain, own = 1.0, jax.random.fold_in(rng, 6)
    for dim, parts in shards:
        steps = jnp.exp(jax.random.uniform(jax.random.fold_in(own, dim), (parts,), jnp.float32, least / len(shards), high / len(shards)))
        gain = gain * jnp.repeat(steps, extent[dim] // parts).reshape([-1 if axis == dim else 1 for axis in range(len(extent))])
    return gain


def split_up(amount, total, most, skew):
    weights = [(1 << 20) // math.isqrt(rank ** skew) + 1 for rank in range(2, amount + 1)]
    rest, counts = total - most - (amount - 1), [1] * (amount - 1)
    while rest > 0:
        movable = [i for i in range(amount - 1) if counts[i] < most]
        mass, budget = sum([weights[i] for i in movable]), rest
        for i in movable:
            extra = min(most - counts[i], max(1, budget * weights[i] // mass), rest)
            counts[i] = counts[i] + extra
            rest = rest - extra
    return np.array([most] + counts)


def uneven_parts(own_key, amount, total, limit, slope):
    if amount == 2:
        one = jax.random.randint(own_key, (), max(1, total - limit), min(limit, total - 1) + 1)
        return jnp.stack([one, total - one])
    lengths = jnp.asarray(split_up(amount, total, limit, slope), jnp.int32)
    couples = (amount - 1) // 2
    donor, taker = lengths[1:1 + 2 * couples:2], lengths[2:2 + 2 * couples:2]
    room = jnp.minimum(donor - 1, limit - taker)
    passed = jax.random.randint(jax.random.fold_in(own_key, 1), (couples,), 0, 1 << 20) % (room + 1)
    lengths = lengths.at[1:1 + 2 * couples:2].set(donor - passed).at[2:2 + 2 * couples:2].set(taker + passed)
    return lengths[jax.random.permutation(jax.random.fold_in(own_key, 2), amount)]


def shared_out(key, own, number, rows, number_of, top, bound, lean):
    ranking = jax.random.permutation(key, number_of)
    packed, common = shares(number_of, rows * top, bound, lean, True), shares(number_of, rows * top, bound, lean, False)
    places = jnp.arange(number_of)

    def named(lengths, offset_by):
        used = int((lengths > 0).sum())
        fixed = max(1, used // 4)
        shifted = fixed + (places - fixed + offset_by * (used - fixed)) % max(1, number_of - fixed)
        return jnp.zeros((number_of,), jnp.int32).at[ranking[jnp.where(places < fixed, places, shifted)]].set(jnp.asarray(lengths, jnp.int32))

    lengths = jnp.where(number % 4 == 0, named(packed, number // 4), named(common, number - number // 4 - 1))
    mixed = jax.random.permutation(jax.random.fold_in(own, 3), number_of)
    source_of, receiver = mixed[0:number_of // 2 * 2:2], mixed[1:number_of // 2 * 2:2]
    slack = jnp.minimum(lengths[source_of] - 1, bound - lengths[receiver]) // 2
    slack = jnp.where((source_of == ranking[0]) | (receiver == ranking[0]) | (lengths[receiver] == 0), 0, jnp.maximum(slack, 0))
    shifted = jax.random.randint(jax.random.fold_in(own, 4), (number_of // 2,), 0, 1 << 20) % (slack + 1)
    lengths = lengths.at[source_of].add(-shifted).at[receiver].add(shifted)
    items = jnp.searchsorted(jnp.cumsum(lengths), jnp.arange(rows * top), side="right").astype(jnp.int32)
    table = items.reshape(top, rows).T
    table = table[jax.random.permutation(jax.random.fold_in(own, 1), rows)]
    offset_by = jax.random.randint(jax.random.fold_in(own, 2), (rows, 1), 0, top)
    return jnp.take_along_axis(table, (jnp.arange(top)[None, :] + offset_by) % top, axis=1)


def shares(number_of, total, reach, lean, full):
    weights = [(1 << 20) // math.isqrt(standing ** lean) + 1 for standing in range(1, number_of + 1)]
    largest = reach if full else min(reach, max(-(-total // number_of), total * weights[0] // sum(weights)))
    least = 1 if total - largest >= number_of - 1 else 0
    counts, rest = [largest] + [least] * (number_of - 1), total - largest - least * (number_of - 1)
    while rest > 0:
        free = [i for i in range(1, number_of) if counts[i] < largest] or [i for i in range(1, number_of) if counts[i] < reach]
        whole, left = sum([weights[i] for i in free]), rest
        for i in free:
            addition = min(reach - counts[i], max(1, left * weights[i] // whole), rest)
            counts[i] = counts[i] + addition
            rest = rest - addition
    return np.array(counts)


def bell_draw(rng, extent, spread, most, split=(), held_as=jnp.bfloat16):
    gain = shard_levels(rng, extent, split, -0.22, 0.18) if split else 1.0
    result = jax.random.normal(rng, extent, jnp.float32) * spread * gain
    return jnp.minimum(jnp.maximum(result, -most), most).astype(held_as)


def setup_inputs(seed: int = 0) -> dict:
    seeds = jax.random.split(jax.random.key(seed), 14)
    tokens = bell_draw(seeds[0], (MICRO, SEQS, LEN, D), 1.0, 6.0, ((1, 8),))
    cotangent = bell_draw(seeds[1], (MICRO, SEQS, LEN, D), 1.0, 6.0, ((1, 8),))
    segments = jax.vmap(lambda own: jnp.searchsorted(jnp.cumsum(uneven_parts(own, max(2, LEN // 16), LEN, 3 * LEN // 4, 0)), jnp.arange(LEN), side="right"))(jax.random.split(seeds[2], MICRO * SEQS)).reshape((MICRO, SEQS, LEN)).astype(jnp.int32)
    pad_mask = plant((jax.random.randint(seeds[3], (MICRO, SEQS, LEN), 0, 8) < 7).astype(jnp.int32), jax.random.fold_in(seeds[3], 1), 0, 1)
    routes_keys = jax.random.split(jax.random.fold_in(seeds[4], 1), MICRO * SEQS * LEN // LEN)
    routes_turns = jax.random.permutation(jax.random.fold_in(seeds[4], 3), MICRO * SEQS * LEN // LEN)
    routes = jax.vmap(lambda own, number: shared_out(jax.random.fold_in(seeds[4], 2), own, number, LEN, EXPERTS, 2, CAP, 1))(routes_keys, routes_turns).reshape((MICRO, SEQS, LEN, 2))
    dist_bucket = draw_dist_bucket(jax.random.fold_in(seeds[13], 71), 0)
    norm_gains = jnp.clip(1.0 + 0.1 * jax.random.normal(seeds[6], (SECTIONS, 2, D), jnp.float32), 0.5, 1.5).astype(jnp.bfloat16)
    qkv_weight = bell_draw(seeds[7], (SECTIONS, D, 3, H * HD), D ** -0.5, 0.21875, ((0, 2), (3, 2)))
    out_weight = bell_draw(seeds[8], (SECTIONS, H * HD, D), (H * HD // 16) ** -0.5, 0.875, ((0, 2), (1, 2)))
    rel_bias = bell_draw(seeds[9], (SECTIONS, BUCKETS, H), 0.7, 4.0, ((0, 2), (2, 2)))
    router_weight = bell_draw(seeds[10], (SECTIONS, D, EXPERTS), (2 * D) ** -0.5, 0.15625, ((0, 2),))
    expert_up = bell_draw(seeds[11], (SECTIONS, EXPERTS, D, FF), D ** -0.5, 0.21875, ((0, 2), (1, 8), (3, 2)))
    expert_down = bell_draw(seeds[12], (SECTIONS, EXPERTS, FF, D), (FF // 4) ** -0.5, 0.21875, ((0, 2), (1, 8), (2, 2)))
    return {"tokens": tokens, "cotangent": cotangent, "segments": segments, "pad_mask": pad_mask, "routes": routes, "dist_bucket": dist_bucket, "norm_gains": norm_gains, "qkv_weight": qkv_weight, "out_weight": out_weight, "rel_bias": rel_bias, "router_weight": router_weight, "expert_up": expert_up, "expert_down": expert_down}


highest = lax.Precision.HIGHEST
masked_score = -1e+30

@jax.custom_vjp
def low(v):
    return lax.optimization_barrier(v.astype(jnp.bfloat16)).astype(jnp.float32)

@jax.custom_vjp
def low_back(v):
    return v

def low_keep(v):
    return (low(v), None)

def low_pass(kept, grad):
    return (grad,)

def back_keep(v):
    return (v, None)

def back_low(kept, grad):
    return (low(grad),)
low.defvjp(low_keep, low_pass)
low_back.defvjp(back_keep, back_low)

def rms_scale(values, gain_row):
    return values * lax.rsqrt(lax.optimization_barrier(jnp.mean(values * values, axis=-1, keepdims=True)) + 1e-06) * gain_row

def apply_layer(inputs, gain_set, qkv_set, out_set, bias_set, router_set, upper_set, lower_set, segment_rows, pad_rows, route_rows, dist_bucket):
    batch_rows, length, model_width = inputs.shape
    head_count = bias_set.shape[1]
    head_cols = qkv_set.shape[2]
    head_dim = head_cols // head_count
    experts = router_set.shape[1]
    normed_one = low(rms_scale(inputs, gain_set[0]))
    qkv_rows = low(low_back(jnp.einsum('bld,dch->blch', normed_one, qkv_set, precision=highest)))
    queries = qkv_rows[:, :, 0].reshape(batch_rows, length, head_count, head_dim)
    keys_in = qkv_rows[:, :, 1].reshape(batch_rows, length, head_count, head_dim)
    values_in = qkv_rows[:, :, 2].reshape(batch_rows, length, head_count, head_dim)
    places = jnp.arange(length, dtype=jnp.int32)
    offsets = jnp.clip(places[:, None] - places[None, :], 0, length - 1)
    bias_grid = jnp.transpose(jnp.take(bias_set, jnp.take(dist_bucket, offsets), axis=0), (2, 0, 1))
    causal = places[None, :] <= places[:, None]
    diagonal = places[None, :] == places[:, None]

    def attend(block_in):
        query_blk, key_blk, value_blk, segment_blk, pad_blk = block_in
        raw_scores = jnp.einsum('gqhd,gkhd->ghqk', query_blk, key_blk, precision=highest)
        logits = 0.125 * low_back(raw_scores) + bias_grid[None]
        allowed = causal[None] & (segment_blk[:, :, None] == segment_blk[:, None, :])
        allowed = allowed & ((pad_blk[:, None, :] == 1) | diagonal[None])
        logits = jnp.where(allowed[:, None], logits, masked_score)
        attn_probs = low(jax.nn.softmax(logits, axis=-1))
        return jnp.einsum('ghqk,gkhd->gqhd', attn_probs, value_blk, precision=highest)
    group_size = math.gcd(batch_rows, max(1, 4096 // length))

    def grouped(array_in):
        return array_in.reshape((batch_rows // group_size, group_size) + array_in.shape[1:])
    mixed_rows = lax.map(jax.checkpoint(attend), (grouped(queries), grouped(keys_in), grouped(values_in), grouped(segment_rows), grouped(pad_rows)))
    mixed_rows = low(low_back(mixed_rows.reshape(batch_rows, length, head_cols)))
    attn_out = low_back(jnp.einsum('blh,hd->bld', mixed_rows, out_set, precision=highest))
    middle = inputs + attn_out
    normed_two = low(rms_scale(middle, gain_set[1]))
    logits_all = low_back(jnp.einsum('bld,de->ble', normed_two, router_set, precision=highest))
    chosen = jnp.take_along_axis(logits_all, route_rows, axis=-1)
    gate_probs = jax.nn.softmax(chosen, axis=-1)
    copies = low_back(jnp.broadcast_to(normed_two[:, :, None, :], (batch_rows, length, 2, model_width)))
    copies = copies.reshape(batch_rows, 2 * length, model_width)
    flat_routes = route_rows.reshape(batch_rows, 2 * length)
    onehot = (flat_routes[:, :, None] == jnp.arange(experts, dtype=jnp.int32)[None, None, :]).astype(jnp.int32)
    earlier = jnp.cumsum(onehot, axis=1) - onehot
    position = lax.optimization_barrier(jnp.sum(earlier * onehot, axis=-1)).astype(jnp.int32)
    slot_index = jnp.arange(batch_rows, dtype=jnp.int32)[:, None] * CAP + position
    buffer = jnp.zeros((experts, batch_rows * CAP, model_width), jnp.float32).at[flat_routes, slot_index].set(copies)

    def expert_apply(operands):
        rows_in, up_weight, down_weight = operands
        hidden_pre = low_back(jnp.dot(rows_in, up_weight, precision=highest))
        hidden = low(jax.nn.gelu(hidden_pre, approximate=False))
        return low_back(low(jnp.dot(hidden, down_weight, precision=highest)))
    results = lax.map(jax.checkpoint(expert_apply), (buffer, upper_set, lower_set))
    back_rows = results[flat_routes, slot_index].reshape(batch_rows, length, 2, model_width)
    return middle + lax.optimization_barrier(jnp.sum(gate_probs[..., None] * back_rows, axis=2))

def reference(tokens, cotangent, segments, pad_mask, routes, dist_bucket, norm_gains, qkv_weight, out_weight, rel_bias, router_weight, expert_up, expert_down):
    batch_rows = MICRO * SEQS

    def flatten(array_in):
        return array_in.reshape((batch_rows,) + array_in.shape[2:])
    segment_rows = flatten(segments)
    pad_rows = flatten(pad_mask)
    route_rows = flatten(routes)

    def section_apply(inputs, gain_set, qkv_set, out_set, bias_set, router_set, upper_set, lower_set):
        return apply_layer(inputs, gain_set, qkv_set, out_set, bias_set, router_set, upper_set, lower_set, segment_rows, pad_rows, route_rows, dist_bucket)

    def section_params(section_id):
        return tuple((array_in[section_id].astype(jnp.float32) for array_in in (norm_gains, qkv_weight, out_weight, rel_bias, router_weight, expert_up, expert_down)))
    first_in = flatten(tokens).astype(jnp.float32)
    first_out, first_pull = jax.vjp(section_apply, first_in, *section_params(0))
    second_in = low(first_out)
    second_out, second_pull = jax.vjp(section_apply, second_in, *section_params(1))
    second_grads = second_pull(flatten(cotangent).astype(jnp.float32))
    first_grads = first_pull(low(second_grads[0]))
    out_shape = (2, MICRO, SEQS, LEN, D)
    section_outputs = jnp.stack([first_out, second_out]).reshape(out_shape)
    input_grads = jnp.stack([first_grads[0], second_grads[0]]).reshape(out_shape)
    stacked = [jnp.stack([first_grads[index_w], second_grads[index_w]]) for index_w in range(1, 8)]
    return (section_outputs, input_grads, stacked[0], stacked[1], stacked[2], stacked[3], stacked[4], stacked[5], stacked[6])
```

```python
from functools import partial

import jax
import jax.numpy as jnp
from jax import lax
from jax.experimental import pallas as pl
from jax.experimental.pallas import tpu as pltpu
from jax.sharding import PartitionSpec as P

norm_eps = 1e-06
masked_score = -1e30
highest = lax.Precision.HIGHEST


def shifted(block, axis, distance):
    devices = range(lax.axis_size(axis))
    route = [(i - distance, i) for i in devices if i - distance in devices]
    return lax.ppermute(block, axis, route)


def normalize(values, gain_row):
    scale_inv = lax.rsqrt(jnp.mean(values * values, axis=-1, keepdims=True) + norm_eps)
    return values * scale_inv * gain_row


def normalize_back(values, gain_row, upstream):
    scale_inv = lax.rsqrt(jnp.mean(values * values, axis=-1, keepdims=True) + norm_eps)
    normed = values * scale_inv
    gain_grad = jnp.sum(upstream * normed, axis=0)
    scaled = upstream * gain_row
    input_grad = scale_inv * (scaled - normed * jnp.mean(scaled * normed, axis=-1, keepdims=True))
    return (input_grad, gain_grad)


def send_rows(rows):
    return lax.all_to_all(rows, "dp", split_axis=0, concat_axis=0, tiled=True)


def sum_slots(partial_rows):
    return lax.psum(partial_rows, "tensor")


def score_context(segment_row, pad_row, dist_bucket, bucket_count):
    length = segment_row.shape[0]
    places = jnp.arange(length, dtype=jnp.int32)
    offsets = jnp.clip(places[:, None] - places[None, :], 0, length - 1)
    bucket_grid = jnp.take(dist_bucket, offsets)
    bucket_onehot = (
        bucket_grid[:, :, None] == jnp.arange(bucket_count, dtype=jnp.int32)[None, None, :]
    ).astype(jnp.float32)
    allowed = (places[None, :] <= places[:, None]) & (segment_row[:, None] == segment_row[None, :])
    allowed = allowed & ((pad_row[None, :] == 1) | (places[None, :] == places[:, None]))
    return (bucket_onehot, allowed)


def attention_front(inputs, context, weights):
    segment_row, pad_row, route_rows, dist_bucket = context
    gain_pair, qkv_weight, out_weight, bias_table, router_weight, upper_weight, lower_weight = (
        weights
    )
    length = inputs.shape[0]
    head_count = bias_table.shape[1]
    bucket_onehot, allowed = score_context(segment_row, pad_row, dist_bucket, bias_table.shape[0])
    normed_one = normalize(inputs, gain_pair[0]).astype(jnp.bfloat16)
    qkv_rows = jnp.einsum(
        "ld,dch->lch", normed_one, qkv_weight, preferred_element_type=jnp.float32
    ).astype(jnp.bfloat16)
    head_dim = qkv_rows.shape[2] // head_count
    queries = qkv_rows[:, 0].reshape(length, head_count, head_dim)
    keys_in = qkv_rows[:, 1].reshape(length, head_count, head_dim)
    values_in = qkv_rows[:, 2].reshape(length, head_count, head_dim)
    raw_scores = jnp.einsum("qhd,khd->hqk", queries, keys_in, preferred_element_type=jnp.float32)
    bias_grid = jnp.einsum(
        "qkb,bh->hqk", bucket_onehot, bias_table.astype(jnp.float32), precision=highest
    )
    logits = jnp.where(allowed[None], 0.125 * raw_scores + bias_grid, masked_score)
    exp_terms = jnp.exp(logits - jnp.max(logits, axis=-1, keepdims=True))
    attn_probs = exp_terms / jnp.sum(exp_terms, axis=-1, keepdims=True)
    mixed_rows = jnp.einsum(
        "hqk,khd->qhd",
        attn_probs.astype(jnp.bfloat16),
        values_in,
        preferred_element_type=jnp.float32,
    )
    mixed_rows = mixed_rows.reshape(length, -1).astype(jnp.bfloat16)
    return (normed_one, queries, keys_in, values_in, attn_probs, mixed_rows, bucket_onehot)


def slot_tables(route_rows, experts, capacity):
    flat_routes = route_rows.reshape(-1)
    route_hits = (flat_routes[:, None] == jnp.arange(experts, dtype=jnp.int32)[None, :]).astype(
        jnp.int32
    )
    earlier = jnp.cumsum(route_hits, axis=0) - route_hits
    position = jnp.sum(earlier * route_hits, axis=1)
    target = flat_routes * capacity + position
    slot_hits = (
        jnp.arange(experts * capacity, dtype=jnp.int32)[:, None] == target[None, :]
    ).astype(jnp.int32)
    source = jnp.sum(slot_hits * jnp.arange(target.shape[0], dtype=jnp.int32)[None, :], axis=1)
    filled = jnp.sum(slot_hits, axis=1) > 0
    return (target, source, filled, route_hits)


def route_gates(normed_two, router_weight, route_hits):
    length = normed_two.shape[0]
    logits = jnp.dot(normed_two, router_weight, preferred_element_type=jnp.float32)
    route_onehot = route_hits.reshape(length, 2, -1).astype(jnp.float32)
    chosen = jnp.einsum("le,lre->lr", logits, route_onehot, precision=highest)
    return (jax.nn.softmax(chosen, axis=-1), route_onehot)


def gather_back(back_slots, target, length):
    flat_slots = back_slots.reshape(-1, back_slots.shape[-1])
    return jnp.take(flat_slots, target, axis=0).reshape(length, 2, -1)


def forward_rest(inputs, front, context, weights):
    segment_row, pad_row, route_rows, dist_bucket = context
    gain_pair, qkv_weight, out_weight, bias_table, router_weight, upper_weight, lower_weight = (
        weights
    )
    mixed_rows = front[5]
    length, model_width = inputs.shape
    experts = router_weight.shape[1]
    capacity = max(2, 3 * length // experts)
    local_experts = upper_weight.shape[0]
    attn_out = lax.psum(
        jnp.dot(mixed_rows, out_weight, preferred_element_type=jnp.float32), "tensor"
    )
    middle = inputs + attn_out
    normed_two = normalize(middle, gain_pair[1]).astype(jnp.bfloat16)
    target, source, filled, route_hits = slot_tables(route_rows, experts, capacity)
    outgoing = jnp.where(
        filled[:, None], jnp.take(normed_two, source // 2, axis=0), jnp.zeros((), jnp.bfloat16)
    )
    outgoing = outgoing.reshape(experts, capacity, model_width)
    arrived = send_rows(outgoing)
    grouped = arrived.reshape(-1, local_experts, capacity, model_width)
    pre_act = jnp.einsum(
        "secd,edf->secf", grouped, upper_weight, preferred_element_type=jnp.float32
    )
    hidden = jax.nn.gelu(pre_act, approximate=False).astype(jnp.bfloat16)
    partial_out = jnp.einsum(
        "secf,efd->secd", hidden, lower_weight, preferred_element_type=jnp.float32
    )
    summed = sum_slots(partial_out)
    returned = summed.astype(jnp.bfloat16).reshape(arrived.shape[0], arrived.shape[1], -1)
    back_slots = send_rows(returned)
    gate_probs, route_onehot = route_gates(normed_two, router_weight, route_hits)
    back_rows = gather_back(back_slots, target, length)
    output = middle + jnp.sum(gate_probs[:, :, None] * back_rows.astype(jnp.float32), axis=1)
    return (output, (attn_out, arrived, back_slots, pre_act))


def backward_layer(inputs, upstream, context, weights, front, saved_state):
    segment_row, pad_row, route_rows, dist_bucket = context
    gain_pair, qkv_weight, out_weight, bias_table, router_weight, upper_weight, lower_weight = (
        weights
    )
    normed_one, queries, keys_in, values_in, attn_probs, mixed_rows, bucket_onehot = front
    attn_out, arrived_rows, back_slots, pre_rows = saved_state
    length, model_width = inputs.shape
    head_count = bias_table.shape[1]
    head_cols = qkv_weight.shape[2]
    experts = router_weight.shape[1]
    capacity = max(2, 3 * length // experts)
    local_experts = upper_weight.shape[0]
    middle = inputs + attn_out
    normed_two = normalize(middle, gain_pair[1]).astype(jnp.bfloat16)
    target, source, filled, route_hits = slot_tables(route_rows, experts, capacity)
    gate_probs, route_onehot = route_gates(normed_two, router_weight, route_hits)
    back_rows = gather_back(back_slots, target, length)
    gate_grad = jnp.sum(upstream[:, None, :] * back_rows.astype(jnp.float32), axis=-1)
    chosen_grad = gate_probs * (gate_grad - jnp.sum(gate_probs * gate_grad, axis=-1, keepdims=True))
    logit_grad = jnp.einsum("lr,lre->le", chosen_grad, route_onehot, precision=highest).astype(
        jnp.bfloat16
    )
    router_grad = jnp.dot(normed_two.T, logit_grad, preferred_element_type=jnp.float32)
    normed_two_grad = jnp.dot(logit_grad, router_weight.T, preferred_element_type=jnp.float32)
    route_grads = (
        (gate_probs[:, :, None] * upstream[:, None, :])
        .reshape(2 * length, model_width)
        .astype(jnp.bfloat16)
    )
    slot_grads = jnp.where(
        filled[:, None], jnp.take(route_grads, source, axis=0), jnp.zeros((), jnp.bfloat16)
    )
    arrived_grads = send_rows(slot_grads.reshape(experts, capacity, model_width))
    grouped = arrived_rows.reshape(-1, local_experts, capacity, model_width)
    grouped_grads = arrived_grads.reshape(-1, local_experts, capacity, model_width)
    hidden, gelu_pull = jax.vjp(partial(jax.nn.gelu, approximate=False), pre_rows)
    hidden_low = hidden.astype(jnp.bfloat16)
    down_grad = jnp.einsum(
        "secf,secd->efd", hidden_low, grouped_grads, preferred_element_type=jnp.float32
    )
    hidden_grad = jnp.einsum(
        "secd,efd->secf", grouped_grads, lower_weight, preferred_element_type=jnp.float32
    )
    pre_grad = gelu_pull(hidden_grad)[0].astype(jnp.bfloat16)
    up_grad = jnp.einsum("secd,secf->edf", grouped, pre_grad, preferred_element_type=jnp.float32)
    rows_grad = sum_slots(
        jnp.einsum("secf,edf->secd", pre_grad, upper_weight, preferred_element_type=jnp.float32)
    )
    sent_back = send_rows(
        rows_grad.astype(jnp.bfloat16).reshape(arrived_rows.shape[0], arrived_rows.shape[1], -1)
    )
    copy_grads = gather_back(sent_back, target, length).astype(jnp.float32)
    normed_two_grad = normed_two_grad + jnp.sum(copy_grads, axis=1)
    middle_part, gain_two = normalize_back(middle, gain_pair[1], normed_two_grad)
    middle_grad = upstream + middle_part
    attn_grad = middle_grad.astype(jnp.bfloat16)
    out_grad = jnp.dot(mixed_rows.T, attn_grad, preferred_element_type=jnp.float32)
    mixed_grad = jnp.dot(attn_grad, out_weight.T, preferred_element_type=jnp.float32).astype(
        jnp.bfloat16
    )
    mixed_grad = mixed_grad.reshape(length, head_count, -1)
    prob_grad = jnp.einsum(
        "qhd,khd->hqk", mixed_grad, values_in, preferred_element_type=jnp.float32
    )
    value_grad = jnp.einsum(
        "hqk,qhd->khd",
        attn_probs.astype(jnp.bfloat16),
        mixed_grad,
        preferred_element_type=jnp.float32,
    )
    score_grad = attn_probs * (prob_grad - jnp.sum(prob_grad * attn_probs, axis=-1, keepdims=True))
    table_grad = jnp.einsum("hqk,qkb->bh", score_grad, bucket_onehot, precision=highest)
    raw_grad = (0.125 * score_grad).astype(jnp.bfloat16)
    query_grad = jnp.einsum("hqk,khd->qhd", raw_grad, keys_in, preferred_element_type=jnp.float32)
    key_grad = jnp.einsum("hqk,qhd->khd", raw_grad, queries, preferred_element_type=jnp.float32)
    qkv_grad = (
        jnp.stack([query_grad, key_grad, value_grad], axis=1)
        .reshape(length, 3, head_cols)
        .astype(jnp.bfloat16)
    )
    qkv_weight_grad = jnp.einsum(
        "ld,lch->dch", normed_one, qkv_grad, preferred_element_type=jnp.float32
    )
    normed_one_grad = lax.psum(
        jnp.einsum("lch,dch->ld", qkv_grad, qkv_weight, preferred_element_type=jnp.float32),
        "tensor",
    )
    input_part, gain_one = normalize_back(inputs, gain_pair[0], normed_one_grad)
    input_grad = middle_grad + input_part
    gain_grads = jnp.stack([gain_one, gain_two])
    return (
        input_grad,
        (gain_grads, qkv_weight_grad, out_grad, table_grad, router_grad, up_grad, down_grad),
    )


def pick_context(segments, pad_mask, routes, dist_bucket, micro_slot):
    segment_row = lax.dynamic_index_in_dim(segments[:, 0], micro_slot, 0, False)
    pad_row = lax.dynamic_index_in_dim(pad_mask[:, 0], micro_slot, 0, False)
    route_rows = lax.dynamic_index_in_dim(routes[:, 0], micro_slot, 0, False)
    return (segment_row, pad_row, route_rows, dist_bucket)


def place_row(store_all, new_value, micro_slot, is_valid):
    current = lax.dynamic_index_in_dim(store_all, micro_slot, 0, False)
    return lax.dynamic_update_index_in_dim(
        store_all, jnp.where(is_valid, new_value, current), micro_slot, 0
    )


def pick_row(store_all, micro_slot):
    return lax.dynamic_index_in_dim(store_all, micro_slot, 0, False)


def mask_grad(grad_value, is_valid):
    return jnp.where(is_valid, grad_value, jnp.zeros((), grad_value.dtype))


def tensor_half(full_rows, tensor_id, half_width):
    return lax.dynamic_slice_in_dim(full_rows, tensor_id * half_width, half_width, 2)[None, :, None]


def local(
    tokens,
    cotangent,
    segments,
    pad_mask,
    routes,
    dist_bucket,
    norm_gains,
    qkv_weight,
    out_weight,
    rel_bias,
    router_weight,
    expert_up,
    expert_down,
):
    section_id = lax.axis_index("section")
    section_count = lax.axis_size("section")
    micro_count = tokens.shape[0]
    length = tokens.shape[2]
    model_width = tokens.shape[3]
    tick_count = micro_count + section_count - 1
    weights = (
        norm_gains[0].astype(jnp.float32),
        qkv_weight[0],
        out_weight[0],
        rel_bias[0],
        router_weight[0],
        expert_up[0],
        expert_down[0],
    )
    empty_rows = jnp.zeros((length, model_width), jnp.bfloat16)
    arriving = empty_rows
    kept_inputs = jnp.zeros((micro_count, length, model_width), jnp.bfloat16)
    section_out = jnp.zeros((micro_count, length, model_width), jnp.float32)
    for tick_index in range(tick_count):
        micro_index = tick_index - section_id
        is_valid = (micro_index >= 0) & (micro_index < micro_count)
        micro_slot = jnp.clip(micro_index, 0, micro_count - 1)
        own_rows = tokens[tick_index, 0] if tick_index < micro_count else empty_rows
        layer_in = jnp.where(section_id == 0, own_rows, arriving)
        context = pick_context(segments, pad_mask, routes, dist_bucket, micro_slot)
        inputs = layer_in.astype(jnp.float32)
        front = attention_front(inputs, context, weights)
        result, saved_state = forward_rest(inputs, front, context, weights)
        section_out = place_row(section_out, result, micro_slot, is_valid)
        kept_inputs = place_row(kept_inputs, layer_in, micro_slot, is_valid)
        arriving = shifted(result.astype(jnp.bfloat16), "section", 1)
    returning = empty_rows
    input_store = jnp.zeros((micro_count, length, model_width), jnp.float32)
    totals = None
    for tick_index in range(tick_count):
        micro_index = tick_index - (section_count - 1 - section_id)
        is_valid = (micro_index >= 0) & (micro_index < micro_count)
        micro_slot = jnp.clip(micro_index, 0, micro_count - 1)
        own_rows = cotangent[tick_index, 0] if tick_index < micro_count else empty_rows
        upstream = jnp.where(section_id == section_count - 1, own_rows, returning).astype(
            jnp.float32
        )
        inputs = pick_row(kept_inputs, micro_slot).astype(jnp.float32)
        context = pick_context(segments, pad_mask, routes, dist_bucket, micro_slot)
        front = attention_front(inputs, context, weights)
        saved_state = forward_rest(inputs, front, context, weights)[1]
        input_grad, grad_set = backward_layer(
            inputs, upstream, context, weights, front, saved_state
        )
        input_store = place_row(input_store, input_grad, micro_slot, is_valid)
        grad_set = jax.tree.map(partial(mask_grad, is_valid=is_valid), grad_set)
        totals = grad_set if totals is None else jax.tree.map(jnp.add, totals, grad_set)
        returning = shifted(input_grad.astype(jnp.bfloat16), "section", -1)
    shared = lax.psum((totals[0], totals[1], totals[2], totals[3], totals[4]), "dp")
    tensor_id = lax.axis_index("tensor")
    half_width = model_width // lax.axis_size("tensor")
    return (
        tensor_half(section_out, tensor_id, half_width),
        tensor_half(input_store, tensor_id, half_width),
        shared[0][None],
        shared[1][None],
        shared[2][None],
        shared[3][None],
        shared[4][None],
        totals[5][None],
        totals[6][None],
    )


def gelu_parts(values):
    size = jnp.abs(values)
    turn = 1.0 / (1.0 + 0.23164190 * size)
    bell = jnp.exp(-0.5 * values * values)
    poly = turn * (
        0.127414796
        + turn * (-0.142248368 + turn * (0.7107068705 + turn * (-0.7265760135 + turn * 0.5307027145)))
    )
    tail = poly * bell
    share = jnp.where(values >= 0.0, 1.0 - tail, tail)
    return (values * share, share + values * (0.3989422804 * bell))


def nn(left, right):
    return lax.dot_general(left, right, (((1,), (0,)), ((), ())), preferred_element_type=jnp.float32)


def nt(left, right):
    return lax.dot_general(left, right, (((1,), (1,)), ((), ())), preferred_element_type=jnp.float32)


def tn(left, right):
    return lax.dot_general(left, right, (((0,), (0,)), ((), ())), preferred_element_type=jnp.float32)


def tn_exact(left, right):
    return lax.dot_general(
        left, right, (((0,), (0,)), ((), ())), preferred_element_type=jnp.float32, precision=highest
    )


def split_low(values):
    high = values.astype(jnp.bfloat16)
    return (high, (values - high.astype(jnp.float32)).astype(jnp.bfloat16))


def inverse_rms(values):
    return lax.rsqrt(jnp.mean(values * values, axis=-1, keepdims=True) + norm_eps)


class Layout:
    pass


def layer_kernel(lay, *refs):
    (
        tok_ref, cot_ref, seg_ref, pad_ref, routes_ref, dist_ref, gains_ref, qkvw_ref, outw_ref, relb_ref, wr_ref,
        up_ref, down_ref,
        secout_ref, ingrad_ref, ggain_ref, gqkv_ref, gout_ref, gbias_ref, grouter_ref, gup_ref, gdown_ref,
        upv, downv, xb, dyb, rr, place, bias_buf, probs_buf, no1, qkvb, mixed, att_send, att_recv, mid, ntb,
        gate_t, hit_t, score_sum, disp_x, xrows, disp_y, dyrows, hidden, dgelu, eo_send, eo_recv, eob, eoret, out_own, x_send,
        other, og, gg_send, gg_recv, pg, cg_send, cg_recv, cgb, cgret, mgrad, ag, mg, qkvg,
        no_send, no_recv, ig_own, dy_send, guv, gdv, wsem, gsem, ss, rs,
    ) = refs
    bf = jnp.bfloat16
    f32 = jnp.float32
    micro, length, width = tok_ref.shape
    experts = lay.experts
    cap = lay.cap
    cols = outw_ref.shape[0]
    pairs = cols // 128
    ffn = up_ref.shape[1]
    slots = experts * cap
    half = width // 2
    s = lax.axis_index("section")
    d = lax.axis_index("dp")
    t = lax.axis_index("tensor")
    u = 1 - t
    sib = (s, d, u)
    across = (1 - s, d, t)
    steps = range(1, experts)
    ahead = [lax.rem(d + k, experts) for k in range(experts)]
    behind = [lax.rem(d + experts - k, experts) for k in range(experts)]

    def remote(src, dst, index, device):
        return pltpu.make_async_remote_copy(
            src_ref=src,
            dst_ref=dst,
            send_sem=ss.at[index],
            recv_sem=rs.at[index],
            device_id=device,
            device_id_type=pl.DeviceIdType.MESH,
        )

    counter = [0]

    def take(amount):
        counter[0] += amount
        return counter[0] - amount

    sent = []

    def fire(copy):
        copy.start()
        sent.append(copy)

    sem_routes = take(experts)
    sem_x = take(1)
    sem_xf = take(1)
    sem_dy = take(1)
    sem_att = take(1)
    sem_eo = take(1)
    sem_cg = take(1)
    sem_ag = take(1)
    sem_no = take(1)
    sem_so = take(1)
    sem_ig = take(1)
    sem_dx = take(experts)
    sem_dxf = take(experts)
    sem_ddy = take(experts)
    sem_ddyf = take(experts)
    sem_re = take(experts)
    sem_rc = take(experts)
    sem_gg = take(experts)
    assert counter[0] == lay.sems

    def block(index, rows):
        return pl.ds(pl.multiple_of(index * rows, rows), rows)

    load_up = pltpu.make_async_copy(up_ref, upv, wsem.at[0])
    load_down = pltpu.make_async_copy(down_ref, downv, wsem.at[1])
    load_up.start()
    load_down.start()

    barrier = pltpu.get_barrier_semaphore()
    for k in steps:
        pl.semaphore_signal(barrier, inc=1, device_id=(s, ahead[k], t), device_id_type=pl.DeviceIdType.MESH)
    pl.semaphore_signal(barrier, inc=1, device_id=sib, device_id_type=pl.DeviceIdType.MESH)
    pl.semaphore_signal(barrier, inc=1, device_id=across, device_id_type=pl.DeviceIdType.MESH)
    pl.semaphore_wait(barrier, experts + 1)

    for k in steps:
        fire(remote(routes_ref, rr.at[d], sem_routes + k, (s, ahead[k], t)))
    rr[d] = routes_ref[...]

    lanes8 = lax.broadcasted_iota(jnp.int32, (experts, length), 0)
    row_at = lax.broadcasted_iota(jnp.int32, (length, length), 0)
    col_at = lax.broadcasted_iota(jnp.int32, (length, length), 1)
    before = (row_at < col_at).astype(bf)
    slot_at = lax.broadcasted_iota(jnp.int32, (cap, length), 0).astype(f32)

    own_routes = routes_ref[t]
    hits = (lanes8 == own_routes[0:1, :]) | (lanes8 == own_routes[1:2, :])
    hit_f = hits.astype(f32)
    hit_t[...] = hit_f
    spot = jnp.where(hits, nn(hit_f.astype(bf), before), -1.0)
    for e in range(experts):
        place[e * cap : (e + 1) * cap, :] = (slot_at == spot[e : e + 1, :]).astype(f32).astype(bf)

    def dispatch(rows, send, landing, base, base_fwd):
        send[...] = nn(place[...], rows).astype(bf)
        mine = block(d, cap)
        out = [remote(send.at[block(ahead[k], cap)], landing.at[t, mine], base + k, (s, ahead[k], t)) for k in steps]
        for copy in out:
            copy.start()
        first = remote(send.at[mine], landing.at[t, mine], base_fwd, sib)
        first.start()
        landing[t, mine, :] = send[mine, :]
        passed = [first]
        for k in steps:
            out[k - 1].wait_recv()
            from_block = block(behind[k], cap)
            copy = remote(landing.at[t, from_block], landing.at[t, from_block], base_fwd + k, sib)
            copy.start()
            passed.append(copy)
        for copy in passed:
            copy.wait()
        for copy in out:
            copy.wait_send()

    @pl.when(s == 0)
    def _():
        xb[...] = tok_ref[...]

    @pl.when(s == 1)
    def _():
        dyb[...] = cot_ref[t]
        dispatch(dyb[...], disp_y, dyrows, sem_ddy, sem_ddyf)

    dist_rows = (
        lax.broadcasted_iota(jnp.int32, (lay.buckets, length), 0) == dist_ref[...]
    ).astype(f32).astype(bf)
    bias_rows = nn(relb_ref[...], dist_rows).astype(bf)
    mirror = ((row_at + col_at == length) | (row_at + col_at == 0)).astype(f32).astype(bf)
    bias_back = nn(bias_rows, mirror)
    for m in range(micro):
        seg_rows = jnp.broadcast_to(seg_ref[m : m + 1, :].astype(f32), (length, length))
        pads = jnp.broadcast_to(pad_ref[m : m + 1, :], (length, length))
        allowed = (col_at <= row_at) & (seg_rows == jnp.transpose(seg_rows))
        allowed = allowed & ((pads == 1) | (col_at == row_at))
        for p in range(pairs):
            for h in range(2):
                head = 2 * p + h
                grid = pltpu.roll(
                    jnp.broadcast_to(bias_back[head : head + 1, :], (length, length)), 0, 1, stride=1, stride_axis=0
                )
                bias_buf[m, p, :, h * length : (h + 1) * length] = jnp.where(allowed, grid, masked_score)

    @pl.when(s == 1)
    def _():
        remote(x_send, xb.at[t], sem_x, across).wait_recv()
        copy = remote(xb.at[t], xb.at[t], sem_xf, sib)
        copy.start()
        copy.wait()

    gain_one = gains_ref[0:1, :].astype(f32)
    gain_two = gains_ref[1:2, :].astype(f32)
    low_lanes = lax.broadcasted_iota(jnp.int32, (length, 128), 1) < 64

    def both_heads(pair_block):
        zero = jnp.zeros((), bf)
        return jnp.concatenate(
            [jnp.where(low_lanes, pair_block, zero), jnp.where(low_lanes, zero, pair_block)], axis=0
        )

    for m in range(micro):
        x_rows = xb[m].astype(f32)
        no1[m] = (x_rows * inverse_rms(x_rows) * gain_one).astype(bf)
    for c in range(3):
        w = qkvw_ref[c]
        for m in range(micro):
            qkvb[c, m] = nn(no1[m], w).astype(bf)
    for m in range(micro):
        for p in range(pairs):
            at = slice(p * 128, (p + 1) * 128)
            scores = 0.125 * nt(qkvb[0, m, :, at], both_heads(qkvb[1, m, :, at])) + bias_buf[m, p]
            for h in range(2):
                part = scores[:, h * length : (h + 1) * length]
                terms = jnp.exp(part - jnp.max(part, axis=-1, keepdims=True))
                probs_buf[m, p, :, h * length : (h + 1) * length] = terms * (
                    1.0 / jnp.sum(terms, axis=-1, keepdims=True)
                )
            mixed[m, :, at] = nn(probs_buf[m, p].astype(bf), both_heads(qkvb[2, m, :, at])).astype(bf)

    att_send[...] = nn(mixed[u], outw_ref[...])
    att_copy = remote(att_send, att_recv, sem_att, sib)
    att_copy.start()
    part_own = nn(mixed[t], outw_ref[...])
    att_copy.wait()
    middle = xb[t].astype(f32) + part_own + att_recv[...]
    mid[...] = middle
    ntb[...] = (middle * inverse_rms(middle) * gain_two).astype(bf)
    logits_t = jnp.where(hit_t[...] > 0.0, nt(wr_ref[...], ntb[...]), masked_score)
    terms = jnp.exp(logits_t - jnp.max(logits_t, axis=0, keepdims=True))
    gate_t[...] = terms / jnp.sum(terms, axis=0, keepdims=True)

    dispatch(ntb[...], disp_x, xrows, sem_dx, sem_dxf)

    load_up.wait()
    load_down.wait()
    flat = micro * slots
    row_tile = lay.row_tile
    col_tile = lay.col_tile
    per_micro = slots // row_tile

    def forward_tile(i, carry):
        at = pl.ds(pl.multiple_of((i % (ffn // col_tile)) * col_tile, col_tile), col_tile)
        j = i // (ffn // col_tile)
        m = j // per_micro
        rows = block(j % per_micro, row_tile)
        value, slope = gelu_parts(nn(xrows[m, rows, :], upv[:, at]))
        hidden[m, rows, at] = value.astype(bf)
        dgelu[m, rows, at] = slope.astype(bf)
        return carry

    lax.fori_loop(0, (flat // row_tile) * (ffn // col_tile), forward_tile, 0)

    eo_send[...] = nn(hidden[u], downv[...]).astype(bf)
    eo_copy = remote(eo_send, eo_recv, sem_eo, sib)
    eo_copy.start()
    part_own = nn(hidden[t], downv[...])
    eo_copy.wait()
    eob[...] = (part_own + eo_recv[...].astype(f32)).astype(bf)

    def send_back(source, landing, base):
        mine = block(d, cap)
        out = [remote(source.at[block(ahead[k], cap)], landing.at[mine], base + k, (s, ahead[k], t)) for k in steps]
        for copy in out:
            copy.start()
        landing[mine, :] = source[mine, :]
        return out

    def finish(copies):
        for copy in copies:
            copy.wait()

    def spread_gates():
        return jnp.concatenate(
            [
                jnp.broadcast_to(gate_t[e : e + 1, :], (cap, length)) * place[e * cap : (e + 1) * cap, :].astype(f32)
                for e in range(experts)
            ],
            axis=0,
        ).astype(bf)

    def layer_output():
        result = mid[...] + tn(spread_gates(), eoret[...])
        out_own[...] = result
        return result

    def own_half():
        return pl.ds(pl.multiple_of(t * half, half), half)

    def other_half():
        return pl.ds(pl.multiple_of(u * half, half), half)

    def hand_out(rows_ref, out_ref, index):
        copy = remote(rows_ref.at[:, other_half()], out_ref.at[t], index, sib)
        copy.start()
        out_ref[t] = rows_ref[:, own_half()]
        copy.wait()

    @pl.when(s == 0)
    def _():
        finish(send_back(eob, eoret, sem_re))
        x_send[...] = layer_output().astype(bf)
        copy = remote(x_send, xb.at[t], sem_x, across)
        copy.start()
        hand_out(out_own, secout_ref, sem_so)
        copy.wait_send()
        remote(dy_send, dyb, sem_dy, across).wait_recv()
        dispatch(dyb[...], disp_y, dyrows, sem_ddy, sem_ddyf)

    for k in steps:
        remote(routes_ref, rr.at[behind[k]], sem_routes + k, (s, ahead[k], t)).wait_recv()

    def other_experts(i, carry):
        q = i // micro
        m = i % micro
        pair = rr[q, m]
        first = pair[0:1, :] == d
        mine = first | (pair[1:2, :] == d)
        mine_f = jnp.broadcast_to(mine.astype(f32), (experts, length))
        spots = jnp.where(mine_f > 0.0, nn(mine_f.astype(bf), before), -1.0)
        where_slot = (slot_at == spots[0:1, :]).astype(f32).astype(bf)
        partner = jnp.where(first, pair[1:2, :], pair[0:1, :])
        partner_hot = (lanes8 == partner).astype(f32).astype(bf)
        other[m, block(q, cap), :] = nt(where_slot, partner_hot)
        return carry

    lax.fori_loop(0, experts * micro, other_experts, 0)
    mine_hot = (lax.broadcasted_iota(jnp.int32, (slots, experts), 1) == d).astype(f32)
    for m in range(micro):
        slot_logits = nt(xrows[m], wr_ref[...])
        own_logit = jnp.sum(slot_logits * mine_hot, axis=-1, keepdims=True)
        other_logit = jnp.sum(slot_logits * other[m], axis=-1, keepdims=True)
        gate = 1.0 / (1.0 + jnp.exp(other_logit - own_logit))
        og[m] = (dyrows[m].astype(f32) * gate).astype(bf)

    gg_send[...] = jnp.zeros_like(gg_send)
    ones = jnp.ones((8, width), bf)
    for q in range(experts):
        at = slice(q * cap, (q + 1) * cap)
        high, low = split_low(dyrows[t, at, :].astype(f32) * eob[at, :].astype(f32))
        gg_send[q, :, 0:cap] = nt(ones, high) + nt(ones, low)

    def backward_tile(i, carry):
        at = pl.ds(pl.multiple_of((i % (ffn // col_tile)) * col_tile, col_tile), col_tile)
        j = i // (ffn // col_tile)
        m = j // per_micro
        rows = block(j % per_micro, row_tile)
        grad = nt(og[m, rows, :], downv[at, :])
        pg[m, rows, at] = (grad * dgelu[m, rows, at].astype(f32)).astype(bf)
        return carry

    lax.fori_loop(0, (flat // row_tile) * (ffn // col_tile), backward_tile, 0)
    cg_send[...] = nt(pg[u], upv[...]).astype(bf)
    cg_copy = remote(cg_send, cg_recv, sem_cg, sib)
    cg_copy.start()
    gg_out = [remote(gg_send.at[ahead[k]], gg_recv.at[d], sem_gg + k, (s, ahead[k], t)) for k in steps]
    for copy in gg_out:
        copy.start()
    gg_recv[d] = gg_send[d]
    part_own = nt(pg[t], upv[...])
    cg_copy.wait()
    cgb[...] = (part_own + cg_recv[...].astype(f32)).astype(bf)
    cg_out = send_back(cgb, cgret, sem_rc)

    wide = lay.wide
    for n in range(ffn // wide):
        at = slice(n * wide, (n + 1) * wide)
        total = tn(xrows[0], pg[0, :, at])
        for m in range(1, micro):
            total = total + tn(xrows[m], pg[m, :, at])
        guv[:, at] = total
        pltpu.make_async_copy(guv.at[:, at], gup_ref.at[:, at], gsem.at[n]).start()
        total = tn(hidden[0, :, at], og[0])
        for m in range(1, micro):
            total = total + tn(hidden[m, :, at], og[m])
        gdv[at, :] = total
        pltpu.make_async_copy(gdv.at[at, :], gdown_ref.at[at, :], gsem.at[ffn // wide + n]).start()

    finish(gg_out)
    finish(cg_out)
    gg_rows = []
    for e in range(experts):
        high, low = split_low(gg_recv[e][:, 0:cap])
        spot_rows = place[e * cap : (e + 1) * cap, :]
        gg_rows.append((nn(high, spot_rows) + nn(low, spot_rows))[0:1, :])
    gate_grad = jnp.concatenate(gg_rows, axis=0)
    gates = gate_t[...]
    logit_grad = (gates * (gate_grad - jnp.sum(gates * gate_grad, axis=0, keepdims=True))).astype(bf)
    grouter_ref[...] = nn(logit_grad, ntb[...])
    two_grad = tn(logit_grad, wr_ref[...]) + tn(place[...], cgret[...])
    dy = dyb[...].astype(f32)
    middle = mid[...]
    scale = inverse_rms(middle)
    normed = middle * scale
    ggain_ref[1:2, :] = jnp.sum(two_grad * normed, axis=0, keepdims=True)
    scaled = two_grad * gain_two
    middle_grad = dy + scale * (scaled - normed * jnp.mean(scaled * normed, axis=-1, keepdims=True))
    mgrad[...] = middle_grad
    ag[t] = middle_grad.astype(bf)
    ag_copy = remote(ag.at[t], ag.at[t], sem_ag, sib)
    ag_copy.start()
    ag_copy.wait()

    for m in range(micro):
        mg[m] = nt(ag[m], outw_ref[...]).astype(bf)
    gout_ref[...] = tn(mixed[0], ag[0]) + tn(mixed[1], ag[1])
    for m in range(micro):
        for p in range(pairs):
            at = slice(p * 128, (p + 1) * 128)
            mg_pair = mg[m, :, at]
            probs = probs_buf[m, p]
            keys2 = both_heads(qkvb[1, m, :, at])
            queries2 = both_heads(qkvb[0, m, :, at])
            mg2 = both_heads(mg_pair)
            prob_grad = nt(mg_pair, both_heads(qkvb[2, m, :, at]))
            raws = []
            key_grad = jnp.zeros((length, 128), f32)
            value_grad = jnp.zeros((length, 128), f32)
            for h in range(2):
                lane = slice(h * length, (h + 1) * length)
                part = probs[:, lane]
                step = prob_grad[:, lane]
                score_grad = part * (step - jnp.sum(part * step, axis=-1, keepdims=True))
                score_sum[2 * p + h] = score_grad if m == 0 else score_sum[2 * p + h] + score_grad
                raw = (0.125 * score_grad).astype(bf)
                raws.append(raw)
                key_grad = key_grad + tn(raw, queries2[h * length : (h + 1) * length])
                value_grad = value_grad + tn(part.astype(bf), mg2[h * length : (h + 1) * length])
            qkvg[0, m, :, at] = nn(jnp.concatenate(raws, axis=1), keys2).astype(bf)
            qkvg[1, m, :, at] = key_grad.astype(bf)
            qkvg[2, m, :, at] = value_grad.astype(bf)
    def project_back(m):
        total = nt(qkvg[0, m], qkvw_ref[0])
        for c in range(1, 3):
            total = total + nt(qkvg[c, m], qkvw_ref[c])
        return total

    no_send[...] = project_back(u).astype(bf)
    no_copy = remote(no_send, no_recv, sem_no, sib)
    no_copy.start()
    one_grad = project_back(t)
    no_copy.wait()
    one_grad = one_grad + no_recv[...].astype(f32)
    x_rows = xb[t].astype(f32)
    scale = inverse_rms(x_rows)
    normed = x_rows * scale
    ggain_ref[0:1, :] = jnp.sum(one_grad * normed, axis=0, keepdims=True)
    scaled = one_grad * gain_one
    input_grad = mgrad[...] + scale * (scaled - normed * jnp.mean(scaled * normed, axis=-1, keepdims=True))
    ig_own[...] = input_grad

    @pl.when(s == 1)
    def _():
        dy_send[...] = input_grad.astype(bf)
        copy = remote(dy_send, dyb, sem_dy, across)
        copy.start()
        copy.wait_send()

    hand_out(ig_own, ingrad_ref, sem_ig)

    for c in range(3):
        gqkv_ref[c] = tn(no1[0], qkvg[c, 0]) + tn(no1[1], qkvg[c, 1])

    sums = []
    for head in range(2 * pairs):
        high, low = split_low(score_sum[head])
        turned = pltpu.roll(nn(high, mirror) + nn(low, mirror), 0, 1, stride=1, stride_axis=0)
        sums.append(jnp.sum(turned, axis=0, keepdims=True))
    high, low = split_low(jnp.concatenate(sums, axis=0))
    gbias_ref[...] = nt(high, dist_rows) + nt(low, dist_rows)

    @pl.when(s == 1)
    def _():
        finish(send_back(eob, eoret, sem_re))
        layer_output()
        hand_out(out_own, secout_ref, sem_so)

    for copy in sent:
        copy.wait_send()
    for n in range(ffn // wide):
        at = slice(n * wide, (n + 1) * wide)
        pltpu.make_async_copy(guv.at[:, at], gup_ref.at[:, at], gsem.at[n]).wait()
        pltpu.make_async_copy(gdv.at[at, :], gdown_ref.at[at, :], gsem.at[ffn // wide + n]).wait()


def fused_local(
    tokens,
    cotangent,
    segments,
    pad_mask,
    routes,
    dist_bucket,
    norm_gains,
    qkv_weight,
    out_weight,
    rel_bias,
    router_weight,
    expert_up,
    expert_down,
):
    micro, _, length, width = tokens.shape
    experts = router_weight.shape[2]
    cap = max(2, 3 * length // experts)
    cols = out_weight.shape[1]
    heads = rel_bias.shape[2]
    ffn = expert_up.shape[3]
    slots = experts * cap
    pairs = cols // 128
    lay = Layout()
    lay.experts = experts
    lay.cap = cap
    lay.buckets = rel_bias.shape[1]
    lay.row_tile = min(slots, 192)
    lay.col_tile = min(ffn, 256)
    lay.wide = min(ffn, 256)
    lay.sems = 8 * experts + 10
    bf = jnp.bfloat16
    f32 = jnp.float32
    vm = pltpu.VMEM
    shape = jax.ShapeDtypeStruct
    dma = pltpu.SemaphoreType.DMA
    scratch = [
        vm((width, ffn), bf),
        vm((ffn, width), bf),
        vm((micro, length, width), bf),
        vm((length, width), bf),
        vm((experts, micro, 2, length), jnp.int32),
        vm((slots, length), bf),
        vm((micro, pairs, length, 2 * length), f32),
        vm((micro, pairs, length, 2 * length), f32),
        vm((micro, length, width), bf),
        vm((3, micro, length, cols), bf),
        vm((micro, length, cols), bf),
        vm((length, width), f32),
        vm((length, width), f32),
        vm((length, width), f32),
        vm((length, width), bf),
        vm((experts, length), f32),
        vm((experts, length), f32),
        vm((2 * pairs, length, length), f32),
        vm((slots, width), bf),
        vm((micro, slots, width), bf),
        vm((slots, width), bf),
        vm((micro, slots, width), bf),
        vm((micro, slots, ffn), bf),
        vm((micro, slots, ffn), bf),
        vm((slots, width), bf),
        vm((slots, width), bf),
        vm((slots, width), bf),
        vm((slots, width), bf),
        vm((length, width), f32),
        vm((length, width), bf),
        vm((micro, slots, experts), f32),
        vm((micro, slots, width), bf),
        vm((experts, 8, 128), f32),
        vm((experts, 8, 128), f32),
        vm((micro, slots, ffn), bf),
        vm((slots, width), bf),
        vm((slots, width), bf),
        vm((slots, width), bf),
        vm((slots, width), bf),
        vm((length, width), f32),
        vm((micro, length, width), bf),
        vm((micro, length, cols), bf),
        vm((3, micro, length, cols), bf),
        vm((length, width), bf),
        vm((length, width), bf),
        vm((length, width), f32),
        vm((length, width), bf),
        vm((width, ffn), f32),
        vm((ffn, width), f32),
        dma((2,)),
        dma((2 * (ffn // lay.wide),)),
        dma((lay.sems,)),
        dma((lay.sems,)),
    ]
    whole = pl.BlockSpec(memory_space=pltpu.VMEM)
    anywhere = pl.BlockSpec(memory_space=pl.ANY)
    out_shape = (
        shape((micro, length, width // 2), f32),
        shape((micro, length, width // 2), f32),
        shape((2, width), f32),
        shape((3, width, cols), f32),
        shape((cols, width), f32),
        shape((heads, lay.buckets), f32),
        shape((experts, width), f32),
        shape((width, ffn), f32),
        shape((ffn, width), f32),
    )
    results = pl.pallas_call(
        partial(layer_kernel, lay),
        out_shape=out_shape,
        in_specs=[whole] * 11 + [anywhere] * 2,
        out_specs=[whole] * 7 + [anywhere] * 2,
        scratch_shapes=scratch,
        name="two_sections",
        compiler_params=pltpu.CompilerParams(
            collective_id=0, has_side_effects=True, vmem_limit_bytes=60 * 1024 * 1024
        ),
    )(
        tokens[:, 0],
        cotangent[:, 0],
        segments[:, 0],
        pad_mask[:, 0],
        routes[:, 0].transpose(0, 2, 1),
        dist_bucket[None],
        norm_gains[0],
        qkv_weight[0].transpose(1, 0, 2),
        out_weight[0],
        rel_bias[0].T,
        router_weight[0].T,
        expert_up[0, 0],
        expert_down[0, 0],
    )
    section_out, input_grads, gains, qkv, out, bias, router, up, down = results
    qkv, out, bias = lax.psum((qkv, out, bias), "dp")
    gains, router = lax.psum((gains, router), ("dp", "tensor"))
    return (
        section_out[None, :, None],
        input_grads[None, :, None],
        gains[None],
        qkv.transpose(1, 0, 2)[None],
        out[None],
        bias.T[None],
        router.T[None],
        up[None, None],
        down[None, None],
    )


def fits_kernel(mesh):
    return mesh.shape["section"] == 2 and mesh.shape["tensor"] == 2 and mesh.shape["dp"] == 8


def solution(mesh):
    in_specs = (
        P(None, "dp", None, None),
        P(None, "dp", None, None),
        P(None, "dp", None),
        P(None, "dp", None),
        P(None, "dp", None, None),
        P(),
        P("section", None, None),
        P("section", None, None, "tensor"),
        P("section", "tensor", None),
        P("section", None, "tensor"),
        P("section", None, None),
        P("section", "dp", None, "tensor"),
        P("section", "dp", "tensor", None),
    )
    out_specs = (
        P("section", None, "dp", None, "tensor"),
        P("section", None, "dp", None, "tensor"),
        P("section", None, None),
        P("section", None, None, "tensor"),
        P("section", "tensor", None),
        P("section", None, "tensor"),
        P("section", None, None),
        P("section", "dp", None, "tensor"),
        P("section", "dp", "tensor", None),
    )
    body = fused_local if fits_kernel(mesh) else local
    return jax.shard_map(body, mesh=mesh, in_specs=in_specs, out_specs=out_specs, check_vma=False)
```

```python
from functools import partial

import jax
import jax.numpy as jnp
from jax import lax
from jax.experimental import pallas as pl
from jax.experimental.pallas import tpu as pltpu
from jax.sharding import PartitionSpec as P

norm_eps = 1e-06
masked_score = -1e30
highest = lax.Precision.HIGHEST


def shifted(block, axis, distance):
    devices = range(lax.axis_size(axis))
    route = [(i - distance, i) for i in devices if i - distance in devices]
    return lax.ppermute(block, axis, route)


def normalize(values, gain_row):
    scale_inv = lax.rsqrt(jnp.mean(values * values, axis=-1, keepdims=True) + norm_eps)
    return values * scale_inv * gain_row


def normalize_back(values, gain_row, upstream):
    scale_inv = lax.rsqrt(jnp.mean(values * values, axis=-1, keepdims=True) + norm_eps)
    normed = values * scale_inv
    gain_grad = jnp.sum(upstream * normed, axis=0)
    scaled = upstream * gain_row
    input_grad = scale_inv * (scaled - normed * jnp.mean(scaled * normed, axis=-1, keepdims=True))
    return (input_grad, gain_grad)


def send_rows(rows):
    return lax.all_to_all(rows, "dp", split_axis=0, concat_axis=0, tiled=True)


def sum_slots(partial_rows):
    return lax.psum(partial_rows, "tensor")


def score_context(segment_row, pad_row, dist_bucket, bucket_count):
    length = segment_row.shape[0]
    places = jnp.arange(length, dtype=jnp.int32)
    offsets = jnp.clip(places[:, None] - places[None, :], 0, length - 1)
    bucket_grid = jnp.take(dist_bucket, offsets)
    bucket_onehot = (
        bucket_grid[:, :, None] == jnp.arange(bucket_count, dtype=jnp.int32)[None, None, :]
    ).astype(jnp.float32)
    allowed = (places[None, :] <= places[:, None]) & (segment_row[:, None] == segment_row[None, :])
    allowed = allowed & ((pad_row[None, :] == 1) | (places[None, :] == places[:, None]))
    return (bucket_onehot, allowed)


def attention_front(inputs, context, weights):
    segment_row, pad_row, route_rows, dist_bucket = context
    gain_pair, qkv_weight, out_weight, bias_table, router_weight, upper_weight, lower_weight = (
        weights
    )
    length = inputs.shape[0]
    head_count = bias_table.shape[1]
    bucket_onehot, allowed = score_context(segment_row, pad_row, dist_bucket, bias_table.shape[0])
    normed_one = normalize(inputs, gain_pair[0]).astype(jnp.bfloat16)
    qkv_rows = jnp.einsum(
        "ld,dch->lch", normed_one, qkv_weight, preferred_element_type=jnp.float32
    ).astype(jnp.bfloat16)
    head_dim = qkv_rows.shape[2] // head_count
    queries = qkv_rows[:, 0].reshape(length, head_count, head_dim)
    keys_in = qkv_rows[:, 1].reshape(length, head_count, head_dim)
    values_in = qkv_rows[:, 2].reshape(length, head_count, head_dim)
    raw_scores = jnp.einsum("qhd,khd->hqk", queries, keys_in, preferred_element_type=jnp.float32)
    bias_grid = jnp.einsum(
        "qkb,bh->hqk", bucket_onehot, bias_table.astype(jnp.float32), precision=highest
    )
    logits = jnp.where(allowed[None], 0.125 * raw_scores + bias_grid, masked_score)
    exp_terms = jnp.exp(logits - jnp.max(logits, axis=-1, keepdims=True))
    attn_probs = exp_terms / jnp.sum(exp_terms, axis=-1, keepdims=True)
    mixed_rows = jnp.einsum(
        "hqk,khd->qhd",
        attn_probs.astype(jnp.bfloat16),
        values_in,
        preferred_element_type=jnp.float32,
    )
    mixed_rows = mixed_rows.reshape(length, -1).astype(jnp.bfloat16)
    return (normed_one, queries, keys_in, values_in, attn_probs, mixed_rows, bucket_onehot)


def slot_tables(route_rows, experts, capacity):
    flat_routes = route_rows.reshape(-1)
    route_hits = (flat_routes[:, None] == jnp.arange(experts, dtype=jnp.int32)[None, :]).astype(
        jnp.int32
    )
    earlier = jnp.cumsum(route_hits, axis=0) - route_hits
    position = jnp.sum(earlier * route_hits, axis=1)
    target = flat_routes * capacity + position
    slot_hits = (
        jnp.arange(experts * capacity, dtype=jnp.int32)[:, None] == target[None, :]
    ).astype(jnp.int32)
    source = jnp.sum(slot_hits * jnp.arange(target.shape[0], dtype=jnp.int32)[None, :], axis=1)
    filled = jnp.sum(slot_hits, axis=1) > 0
    return (target, source, filled, route_hits)


def route_gates(normed_two, router_weight, route_hits):
    length = normed_two.shape[0]
    logits = jnp.dot(normed_two, router_weight, preferred_element_type=jnp.float32)
    route_onehot = route_hits.reshape(length, 2, -1).astype(jnp.float32)
    chosen = jnp.einsum("le,lre->lr", logits, route_onehot, precision=highest)
    return (jax.nn.softmax(chosen, axis=-1), route_onehot)


def gather_back(back_slots, target, length):
    flat_slots = back_slots.reshape(-1, back_slots.shape[-1])
    return jnp.take(flat_slots, target, axis=0).reshape(length, 2, -1)


def forward_rest(inputs, front, context, weights):
    segment_row, pad_row, route_rows, dist_bucket = context
    gain_pair, qkv_weight, out_weight, bias_table, router_weight, upper_weight, lower_weight = (
        weights
    )
    mixed_rows = front[5]
    length, model_width = inputs.shape
    experts = router_weight.shape[1]
    capacity = max(2, 3 * length // experts)
    local_experts = upper_weight.shape[0]
    attn_out = lax.psum(
        jnp.dot(mixed_rows, out_weight, preferred_element_type=jnp.float32), "tensor"
    )
    middle = inputs + attn_out
    normed_two = normalize(middle, gain_pair[1]).astype(jnp.bfloat16)
    target, source, filled, route_hits = slot_tables(route_rows, experts, capacity)
    outgoing = jnp.where(
        filled[:, None], jnp.take(normed_two, source // 2, axis=0), jnp.zeros((), jnp.bfloat16)
    )
    outgoing = outgoing.reshape(experts, capacity, model_width)
    arrived = send_rows(outgoing)
    grouped = arrived.reshape(-1, local_experts, capacity, model_width)
    pre_act = jnp.einsum(
        "secd,edf->secf", grouped, upper_weight, preferred_element_type=jnp.float32
    )
    hidden = jax.nn.gelu(pre_act, approximate=False).astype(jnp.bfloat16)
    partial_out = jnp.einsum(
        "secf,efd->secd", hidden, lower_weight, preferred_element_type=jnp.float32
    )
    summed = sum_slots(partial_out)
    returned = summed.astype(jnp.bfloat16).reshape(arrived.shape[0], arrived.shape[1], -1)
    back_slots = send_rows(returned)
    gate_probs, route_onehot = route_gates(normed_two, router_weight, route_hits)
    back_rows = gather_back(back_slots, target, length)
    output = middle + jnp.sum(gate_probs[:, :, None] * back_rows.astype(jnp.float32), axis=1)
    return (output, (attn_out, arrived, back_slots, pre_act))


def backward_layer(inputs, upstream, context, weights, front, saved_state):
    segment_row, pad_row, route_rows, dist_bucket = context
    gain_pair, qkv_weight, out_weight, bias_table, router_weight, upper_weight, lower_weight = (
        weights
    )
    normed_one, queries, keys_in, values_in, attn_probs, mixed_rows, bucket_onehot = front
    attn_out, arrived_rows, back_slots, pre_rows = saved_state
    length, model_width = inputs.shape
    head_count = bias_table.shape[1]
    head_cols = qkv_weight.shape[2]
    experts = router_weight.shape[1]
    capacity = max(2, 3 * length // experts)
    local_experts = upper_weight.shape[0]
    middle = inputs + attn_out
    normed_two = normalize(middle, gain_pair[1]).astype(jnp.bfloat16)
    target, source, filled, route_hits = slot_tables(route_rows, experts, capacity)
    gate_probs, route_onehot = route_gates(normed_two, router_weight, route_hits)
    back_rows = gather_back(back_slots, target, length)
    gate_grad = jnp.sum(upstream[:, None, :] * back_rows.astype(jnp.float32), axis=-1)
    chosen_grad = gate_probs * (gate_grad - jnp.sum(gate_probs * gate_grad, axis=-1, keepdims=True))
    logit_grad = jnp.einsum("lr,lre->le", chosen_grad, route_onehot, precision=highest).astype(
        jnp.bfloat16
    )
    router_grad = jnp.dot(normed_two.T, logit_grad, preferred_element_type=jnp.float32)
    normed_two_grad = jnp.dot(logit_grad, router_weight.T, preferred_element_type=jnp.float32)
    route_grads = (
        (gate_probs[:, :, None] * upstream[:, None, :])
        .reshape(2 * length, model_width)
        .astype(jnp.bfloat16)
    )
    slot_grads = jnp.where(
        filled[:, None], jnp.take(route_grads, source, axis=0), jnp.zeros((), jnp.bfloat16)
    )
    arrived_grads = send_rows(slot_grads.reshape(experts, capacity, model_width))
    grouped = arrived_rows.reshape(-1, local_experts, capacity, model_width)
    grouped_grads = arrived_grads.reshape(-1, local_experts, capacity, model_width)
    hidden, gelu_pull = jax.vjp(partial(jax.nn.gelu, approximate=False), pre_rows)
    hidden_low = hidden.astype(jnp.bfloat16)
    down_grad = jnp.einsum(
        "secf,secd->efd", hidden_low, grouped_grads, preferred_element_type=jnp.float32
    )
    hidden_grad = jnp.einsum(
        "secd,efd->secf", grouped_grads, lower_weight, preferred_element_type=jnp.float32
    )
    pre_grad = gelu_pull(hidden_grad)[0].astype(jnp.bfloat16)
    up_grad = jnp.einsum("secd,secf->edf", grouped, pre_grad, preferred_element_type=jnp.float32)
    rows_grad = sum_slots(
        jnp.einsum("secf,edf->secd", pre_grad, upper_weight, preferred_element_type=jnp.float32)
    )
    sent_back = send_rows(
        rows_grad.astype(jnp.bfloat16).reshape(arrived_rows.shape[0], arrived_rows.shape[1], -1)
    )
    copy_grads = gather_back(sent_back, target, length).astype(jnp.float32)
    normed_two_grad = normed_two_grad + jnp.sum(copy_grads, axis=1)
    middle_part, gain_two = normalize_back(middle, gain_pair[1], normed_two_grad)
    middle_grad = upstream + middle_part
    attn_grad = middle_grad.astype(jnp.bfloat16)
    out_grad = jnp.dot(mixed_rows.T, attn_grad, preferred_element_type=jnp.float32)
    mixed_grad = jnp.dot(attn_grad, out_weight.T, preferred_element_type=jnp.float32).astype(
        jnp.bfloat16
    )
    mixed_grad = mixed_grad.reshape(length, head_count, -1)
    prob_grad = jnp.einsum(
        "qhd,khd->hqk", mixed_grad, values_in, preferred_element_type=jnp.float32
    )
    value_grad = jnp.einsum(
        "hqk,qhd->khd",
        attn_probs.astype(jnp.bfloat16),
        mixed_grad,
        preferred_element_type=jnp.float32,
    )
    score_grad = attn_probs * (prob_grad - jnp.sum(prob_grad * attn_probs, axis=-1, keepdims=True))
    table_grad = jnp.einsum("hqk,qkb->bh", score_grad, bucket_onehot, precision=highest)
    raw_grad = (0.125 * score_grad).astype(jnp.bfloat16)
    query_grad = jnp.einsum("hqk,khd->qhd", raw_grad, keys_in, preferred_element_type=jnp.float32)
    key_grad = jnp.einsum("hqk,qhd->khd", raw_grad, queries, preferred_element_type=jnp.float32)
    qkv_grad = (
        jnp.stack([query_grad, key_grad, value_grad], axis=1)
        .reshape(length, 3, head_cols)
        .astype(jnp.bfloat16)
    )
    qkv_weight_grad = jnp.einsum(
        "ld,lch->dch", normed_one, qkv_grad, preferred_element_type=jnp.float32
    )
    normed_one_grad = lax.psum(
        jnp.einsum("lch,dch->ld", qkv_grad, qkv_weight, preferred_element_type=jnp.float32),
        "tensor",
    )
    input_part, gain_one = normalize_back(inputs, gain_pair[0], normed_one_grad)
    input_grad = middle_grad + input_part
    gain_grads = jnp.stack([gain_one, gain_two])
    return (
        input_grad,
        (gain_grads, qkv_weight_grad, out_grad, table_grad, router_grad, up_grad, down_grad),
    )


def pick_context(segments, pad_mask, routes, dist_bucket, micro_slot):
    segment_row = lax.dynamic_index_in_dim(segments[:, 0], micro_slot, 0, False)
    pad_row = lax.dynamic_index_in_dim(pad_mask[:, 0], micro_slot, 0, False)
    route_rows = lax.dynamic_index_in_dim(routes[:, 0], micro_slot, 0, False)
    return (segment_row, pad_row, route_rows, dist_bucket)


def place_row(store_all, new_value, micro_slot, is_valid):
    current = lax.dynamic_index_in_dim(store_all, micro_slot, 0, False)
    return lax.dynamic_update_index_in_dim(
        store_all, jnp.where(is_valid, new_value, current), micro_slot, 0
    )


def pick_row(store_all, micro_slot):
    return lax.dynamic_index_in_dim(store_all, micro_slot, 0, False)


def mask_grad(grad_value, is_valid):
    return jnp.where(is_valid, grad_value, jnp.zeros((), grad_value.dtype))


def tensor_half(full_rows, tensor_id, half_width):
    return lax.dynamic_slice_in_dim(full_rows, tensor_id * half_width, half_width, 2)[None, :, None]


def local(
    tokens,
    cotangent,
    segments,
    pad_mask,
    routes,
    dist_bucket,
    norm_gains,
    qkv_weight,
    out_weight,
    rel_bias,
    router_weight,
    expert_up,
    expert_down,
):
    section_id = lax.axis_index("section")
    section_count = lax.axis_size("section")
    micro_count = tokens.shape[0]
    length = tokens.shape[2]
    model_width = tokens.shape[3]
    tick_count = micro_count + section_count - 1
    weights = (
        norm_gains[0].astype(jnp.float32),
        qkv_weight[0],
        out_weight[0],
        rel_bias[0],
        router_weight[0],
        expert_up[0],
        expert_down[0],
    )
    empty_rows = jnp.zeros((length, model_width), jnp.bfloat16)
    arriving = empty_rows
    kept_inputs = jnp.zeros((micro_count, length, model_width), jnp.bfloat16)
    section_out = jnp.zeros((micro_count, length, model_width), jnp.float32)
    for tick_index in range(tick_count):
        micro_index = tick_index - section_id
        is_valid = (micro_index >= 0) & (micro_index < micro_count)
        micro_slot = jnp.clip(micro_index, 0, micro_count - 1)
        own_rows = tokens[tick_index, 0] if tick_index < micro_count else empty_rows
        layer_in = jnp.where(section_id == 0, own_rows, arriving)
        context = pick_context(segments, pad_mask, routes, dist_bucket, micro_slot)
        inputs = layer_in.astype(jnp.float32)
        front = attention_front(inputs, context, weights)
        result, saved_state = forward_rest(inputs, front, context, weights)
        section_out = place_row(section_out, result, micro_slot, is_valid)
        kept_inputs = place_row(kept_inputs, layer_in, micro_slot, is_valid)
        arriving = shifted(result.astype(jnp.bfloat16), "section", 1)
    returning = empty_rows
    input_store = jnp.zeros((micro_count, length, model_width), jnp.float32)
    totals = None
    for tick_index in range(tick_count):
        micro_index = tick_index - (section_count - 1 - section_id)
        is_valid = (micro_index >= 0) & (micro_index < micro_count)
        micro_slot = jnp.clip(micro_index, 0, micro_count - 1)
        own_rows = cotangent[tick_index, 0] if tick_index < micro_count else empty_rows
        upstream = jnp.where(section_id == section_count - 1, own_rows, returning).astype(
            jnp.float32
        )
        inputs = pick_row(kept_inputs, micro_slot).astype(jnp.float32)
        context = pick_context(segments, pad_mask, routes, dist_bucket, micro_slot)
        front = attention_front(inputs, context, weights)
        saved_state = forward_rest(inputs, front, context, weights)[1]
        input_grad, grad_set = backward_layer(
            inputs, upstream, context, weights, front, saved_state
        )
        input_store = place_row(input_store, input_grad, micro_slot, is_valid)
        grad_set = jax.tree.map(partial(mask_grad, is_valid=is_valid), grad_set)
        totals = grad_set if totals is None else jax.tree.map(jnp.add, totals, grad_set)
        returning = shifted(input_grad.astype(jnp.bfloat16), "section", -1)
    shared = lax.psum((totals[0], totals[1], totals[2], totals[3], totals[4]), "dp")
    tensor_id = lax.axis_index("tensor")
    half_width = model_width // lax.axis_size("tensor")
    return (
        tensor_half(section_out, tensor_id, half_width),
        tensor_half(input_store, tensor_id, half_width),
        shared[0][None],
        shared[1][None],
        shared[2][None],
        shared[3][None],
        shared[4][None],
        totals[5][None],
        totals[6][None],
    )


def gelu_parts(values):
    share = 0.5 + 0.5 * lax.erf(values * 0.7071067811865476)
    return (values * share, share + values * (0.3989422804014327 * jnp.exp(-0.5 * values * values)))


def nn(left, right):
    return lax.dot_general(left, right, (((1,), (0,)), ((), ())), preferred_element_type=jnp.float32)


def nt(left, right):
    return lax.dot_general(left, right, (((1,), (1,)), ((), ())), preferred_element_type=jnp.float32)


def tn(left, right):
    return lax.dot_general(left, right, (((0,), (0,)), ((), ())), preferred_element_type=jnp.float32)


def split_low(values):
    high = values.astype(jnp.bfloat16)
    return (high, (values - high.astype(jnp.float32)).astype(jnp.bfloat16))


def inverse_rms(values):
    return lax.rsqrt(jnp.mean(values * values, axis=-1, keepdims=True) + norm_eps)


class Layout:
    pass


def layer_kernel(lay, *refs):
    (
        tok_ref, cot_ref, seg_ref, pad_ref, routes_ref, dist_ref, gains_ref, qkvw_ref, outw_ref, relb_ref, wr_ref,
        up_ref, down_ref,
        secout_ref, ingrad_ref, ggain_ref, shared_ref, gbias_ref, grouter_ref, gup_ref, gdown_ref,
        upv, downv, xb, dyb, rr, place, bias_buf, probs_buf, no1, qkvb, mixed, att_send, att_recv, mid, ntb,
        gate_t, hit_t, score_sum, disp_x, xrows, disp_y, dyrows, hidden, dgelu, eo_send, eo_recv, eob, eoret, out_own, x_send,
        other, og, gg_send, gg_recv, pg, cg_send, cg_recv, cgb, cgret, mgrad, ag, mg, qkvg,
        no_send, no_recv, ig_own, dy_send, guv, gdv,
        no_all, mix_all, qgt, qt_all, agt, agt_all, early_send, early_all, late_send, late_all, sums_send, sums_recv,
        wsem, gsem, ss, rs,
    ) = refs
    bf = jnp.bfloat16
    f32 = jnp.float32
    micro, length, width = tok_ref.shape
    experts = lay.experts
    cap = lay.cap
    cols = outw_ref.shape[0]
    pairs = cols // 128
    ffn = up_ref.shape[1]
    slots = experts * cap
    half = width // 2
    s = lax.axis_index("section")
    d = lax.axis_index("dp")
    t = lax.axis_index("tensor")
    u = 1 - t
    sib = (s, d, u)
    across = (1 - s, d, t)
    steps = range(1, experts)
    ahead = [lax.rem(d + k, experts) for k in range(experts)]
    behind = [lax.rem(d + experts - k, experts) for k in range(experts)]

    def remote(src, dst, index, device):
        return pltpu.make_async_remote_copy(
            src_ref=src,
            dst_ref=dst,
            send_sem=ss.at[index],
            recv_sem=rs.at[index],
            device_id=device,
            device_id_type=pl.DeviceIdType.MESH,
        )

    counter = [0]

    def take(amount):
        counter[0] += amount
        return counter[0] - amount

    sent = []

    def fire(copy):
        copy.start()
        sent.append(copy)

    sem_routes = take(experts)
    sem_x = take(1)
    sem_xf = take(1)
    sem_dy = take(1)
    sem_att = take(1)
    sem_eo = take(1)
    sem_cg = take(1)
    sem_ag = take(1)
    sem_no = take(1)
    sem_so = take(1)
    sem_ig = take(1)
    sem_dx = take(experts)
    sem_dxf = take(experts)
    sem_ddy = take(experts)
    sem_ddyf = take(experts)
    sem_re = take(experts)
    sem_rc = take(experts)
    sem_gg = take(experts)
    sem_agt = take(experts)
    sem_qgt = take(experts)
    sem_early = take(experts)
    sem_late = take(experts)
    sem_sums = take(1)
    sem_noall = take(1)
    sem_ring_no = take(2 * experts)
    sem_ring_mix = take(2 * experts)
    sem_ring_out = take(4 * experts)
    assert counter[0] == lay.sems

    def block(index, rows):
        return pl.ds(pl.multiple_of(index * rows, rows), rows)

    place_y = lax.rem(d, 2)
    place_z = d // 2
    ring_at = place_z + place_y * (experts - 1 - 2 * place_z)

    def ring_device(position):
        p = lax.rem(position + 2 * experts, experts)
        return 2 * p + (p // (experts // 2)) * (2 * experts - 1 - 4 * p)

    def ring_gather(streams):
        moved = []
        for k in range(experts - 1):
            for number, (view, direction, base) in enumerate(streams):
                if k > 0:
                    moved[(k - 1) * len(streams) + number].wait_recv()
                held = view(ring_device(ring_at - direction * k))
                copy = remote(held, held, base + k, (s, ring_device(ring_at + direction), t))
                copy.start()
                moved.append(copy)
        for copy in moved[(experts - 2) * len(streams) :]:
            copy.wait_recv()
        for copy in moved:
            copy.wait_send()

    load_up = pltpu.make_async_copy(up_ref, upv, wsem.at[0])
    load_down = pltpu.make_async_copy(down_ref, downv, wsem.at[1])
    load_up.start()
    load_down.start()

    barrier = pltpu.get_barrier_semaphore()
    for k in steps:
        pl.semaphore_signal(barrier, inc=1, device_id=(s, ahead[k], t), device_id_type=pl.DeviceIdType.MESH)
    pl.semaphore_signal(barrier, inc=1, device_id=sib, device_id_type=pl.DeviceIdType.MESH)
    pl.semaphore_signal(barrier, inc=1, device_id=across, device_id_type=pl.DeviceIdType.MESH)
    pl.semaphore_wait(barrier, experts + 1)

    for k in steps:
        fire(remote(routes_ref, rr.at[d], sem_routes + k, (s, ahead[k], t)))
    rr[d] = routes_ref[...]

    lanes8 = lax.broadcasted_iota(jnp.int32, (experts, length), 0)
    row_at = lax.broadcasted_iota(jnp.int32, (length, length), 0)
    col_at = lax.broadcasted_iota(jnp.int32, (length, length), 1)
    before = (row_at < col_at).astype(bf)
    slot_at = lax.broadcasted_iota(jnp.int32, (cap, length), 0).astype(f32)

    own_routes = routes_ref[t]
    hits = (lanes8 == own_routes[0:1, :]) | (lanes8 == own_routes[1:2, :])
    hit_f = hits.astype(f32)
    hit_t[...] = hit_f
    spot = jnp.where(hits, nn(hit_f.astype(bf), before), -1.0)
    for e in range(experts):
        place[e * cap : (e + 1) * cap, :] = (slot_at == spot[e : e + 1, :]).astype(f32).astype(bf)

    def dispatch(rows, send, landing, base, base_fwd):
        send[...] = nn(place[...], rows).astype(bf)
        mine = block(d, cap)
        out = [remote(send.at[block(ahead[k], cap)], landing.at[t, mine], base + k, (s, ahead[k], t)) for k in steps]
        for copy in out:
            copy.start()
        first = remote(send.at[mine], landing.at[t, mine], base_fwd, sib)
        first.start()
        landing[t, mine, :] = send[mine, :]
        passed = [first]
        for k in steps:
            out[k - 1].wait_recv()
            from_block = block(behind[k], cap)
            copy = remote(landing.at[t, from_block], landing.at[t, from_block], base_fwd + k, sib)
            copy.start()
            passed.append(copy)
        for copy in passed:
            copy.wait()
        for copy in out:
            copy.wait_send()

    def other_experts():
        for k in steps:
            remote(routes_ref, rr.at[behind[k]], sem_routes + k, (s, ahead[k], t)).wait_recv()

        def one(i, carry):
            q = i // micro
            m = i % micro
            pair = rr[q, m]
            first = pair[0:1, :] == d
            mine = first | (pair[1:2, :] == d)
            mine_f = jnp.broadcast_to(mine.astype(f32), (experts, length))
            spots = jnp.where(mine_f > 0.0, nn(mine_f.astype(bf), before), -1.0)
            where_slot = (slot_at == spots[0:1, :]).astype(f32).astype(bf)
            partner = jnp.where(first, pair[1:2, :], pair[0:1, :])
            partner_hot = (lanes8 == partner).astype(f32).astype(bf)
            other[m, block(q, cap), :] = nt(where_slot, partner_hot)
            return carry

        lax.fori_loop(0, experts * micro, one, 0)

    @pl.when(s == 0)
    def _():
        xb[...] = tok_ref[...]

    @pl.when(s == 1)
    def _():
        dyb[...] = cot_ref[t]
        dispatch(dyb[...], disp_y, dyrows, sem_ddy, sem_ddyf)
        other_experts()

    dist_rows = (
        lax.broadcasted_iota(jnp.int32, (lay.buckets, length), 0) == dist_ref[...]
    ).astype(f32).astype(bf)
    bias_rows = nn(relb_ref[...], dist_rows).astype(bf)
    mirror = ((row_at + col_at == length) | (row_at + col_at == 0)).astype(f32).astype(bf)
    bias_back = nn(bias_rows, mirror)
    for m in range(micro):
        seg_rows = jnp.broadcast_to(seg_ref[m : m + 1, :].astype(f32), (length, length))
        pads = jnp.broadcast_to(pad_ref[m : m + 1, :], (length, length))
        allowed = (col_at <= row_at) & (seg_rows == jnp.transpose(seg_rows))
        allowed = allowed & ((pads == 1) | (col_at == row_at))
        for p in range(pairs):
            for h in range(2):
                head = 2 * p + h
                grid = pltpu.roll(
                    jnp.broadcast_to(bias_back[head : head + 1, :], (length, length)), 0, 1, stride=1, stride_axis=0
                )
                bias_buf[m, p, :, h * length : (h + 1) * length] = jnp.where(allowed, grid, masked_score)

    @pl.when(s == 1)
    def _():
        remote(x_send, xb.at[t], sem_x, across).wait_recv()
        copy = remote(xb.at[t], xb.at[t], sem_xf, sib)
        copy.start()
        copy.wait()

    gain_one = gains_ref[0:1, :].astype(f32)
    gain_two = gains_ref[1:2, :].astype(f32)
    low_lanes = lax.broadcasted_iota(jnp.int32, (length, 128), 1) < 64

    def both_heads(pair_block):
        zero = jnp.zeros((), bf)
        return jnp.concatenate(
            [jnp.where(low_lanes, pair_block, zero), jnp.where(low_lanes, zero, pair_block)], axis=0
        )

    for m in range(micro):
        x_rows = xb[m].astype(f32)
        no1[m] = (x_rows * inverse_rms(x_rows) * gain_one).astype(bf)
    for c in range(3):
        w = qkvw_ref[c]
        for m in range(micro):
            qkvb[c, m] = nn(no1[m], w).astype(bf)
    for m in range(micro):
        for p in range(pairs):
            at = slice(p * 128, (p + 1) * 128)
            scores = 0.125 * nt(qkvb[0, m, :, at], both_heads(qkvb[1, m, :, at])) + bias_buf[m, p]
            for h in range(2):
                part = scores[:, h * length : (h + 1) * length]
                terms = jnp.exp(part - jnp.max(part, axis=-1, keepdims=True))
                probs_buf[m, p, :, h * length : (h + 1) * length] = terms * (
                    1.0 / jnp.sum(terms, axis=-1, keepdims=True)
                )
            mixed[m, :, at] = nn(probs_buf[m, p].astype(bf), both_heads(qkvb[2, m, :, at])).astype(bf)

    att_send[...] = nn(mixed[u], outw_ref[...])
    att_copy = remote(att_send, att_recv, sem_att, sib)
    att_copy.start()
    part_own = nn(mixed[t], outw_ref[...])
    att_copy.wait()
    middle = xb[t].astype(f32) + part_own + att_recv[...]
    mid[...] = middle
    ntb[...] = (middle * inverse_rms(middle) * gain_two).astype(bf)
    logits_t = jnp.where(hit_t[...] > 0.0, nt(wr_ref[...], ntb[...]), masked_score)
    terms = jnp.exp(logits_t - jnp.max(logits_t, axis=0, keepdims=True))
    gate_t[...] = terms / jnp.sum(terms, axis=0, keepdims=True)

    dispatch(ntb[...], disp_x, xrows, sem_dx, sem_dxf)

    load_up.wait()
    load_down.wait()
    row_tile = lay.row_tile
    tiles = [(m, slice(r, r + row_tile)) for m in range(micro) for r in range(0, slots, row_tile)]
    for m, rows in tiles:
        value, slope = gelu_parts(nn(xrows[m, rows, :], upv[...]))
        hidden[m, rows, :] = value.astype(bf)
        dgelu[m, rows, :] = slope.astype(bf)

    def expert_rows():
        eo_send[...] = nn(hidden[u], downv[...]).astype(bf)
        eo_copy = remote(eo_send, eo_recv, sem_eo, sib)
        eo_copy.start()
        part = nn(hidden[t], downv[...])
        eo_copy.wait()
        eob[...] = (part + eo_recv[...].astype(f32)).astype(bf)

    def send_back(source, landing, base):
        mine = block(d, cap)
        out = [remote(source.at[block(ahead[k], cap)], landing.at[mine], base + k, (s, ahead[k], t)) for k in steps]
        for copy in out:
            copy.start()
        landing[mine, :] = source[mine, :]
        return out

    def finish(copies):
        for copy in copies:
            copy.wait()

    def spread_gates():
        return jnp.concatenate(
            [
                jnp.broadcast_to(gate_t[e : e + 1, :], (cap, length)) * place[e * cap : (e + 1) * cap, :].astype(f32)
                for e in range(experts)
            ],
            axis=0,
        ).astype(bf)

    def layer_output():
        result = mid[...] + tn(spread_gates(), eoret[...])
        out_own[...] = result
        return result

    def own_half():
        return pl.ds(pl.multiple_of(t * half, half), half)

    def other_half():
        return pl.ds(pl.multiple_of(u * half, half), half)

    def hand_out(rows_ref, out_ref, index):
        copy = remote(rows_ref.at[:, other_half()], out_ref.at[t], index, sib)
        copy.start()
        out_ref[t] = rows_ref[:, own_half()]
        copy.wait()

    def gather_factors():
        no_all[t, d] = no1[t]
        mix_all[d] = jnp.concatenate([mixed[m] for m in range(micro)], axis=0)
        ring_gather(
            [
                (lambda q: no_all.at[t, q, 0 : length // 2], 1, sem_ring_no),
                (lambda q: no_all.at[t, q, length // 2 : length], -1, sem_ring_no + experts),
                (lambda q: mix_all.at[q, 0:length], 1, sem_ring_mix),
                (lambda q: mix_all.at[q, length : 2 * length], -1, sem_ring_mix + experts),
            ]
        )
        copy = remote(no_all.at[t], no_all.at[t], sem_noall, sib)
        copy.start()
        copy.wait()

    @pl.when(s == 0)
    def _():
        expert_rows()
        finish(send_back(eob, eoret, sem_re))
        x_send[...] = layer_output().astype(bf)
        copy = remote(x_send, xb.at[t], sem_x, across)
        copy.start()
        hand_out(out_own, secout_ref, sem_so)
        copy.wait_send()
        other_experts()
        gather_factors()
        remote(dy_send, dyb, sem_dy, across).wait_recv()
        dispatch(dyb[...], disp_y, dyrows, sem_ddy, sem_ddyf)

    mine_hot = (lax.broadcasted_iota(jnp.int32, (slots, experts), 1) == d).astype(f32)
    for m in range(micro):
        slot_logits = nt(xrows[m], wr_ref[...])
        own_logit = jnp.sum(slot_logits * mine_hot, axis=-1, keepdims=True)
        other_logit = jnp.sum(slot_logits * other[m], axis=-1, keepdims=True)
        gate = 1.0 / (1.0 + jnp.exp(other_logit - own_logit))
        og[m] = (dyrows[m].astype(f32) * gate).astype(bf)

    for m, rows in tiles:
        pg[m, rows, :] = (nt(og[m, rows, :], downv[...]) * dgelu[m, rows, :].astype(f32)).astype(bf)
    cg_send[...] = nt(pg[u], upv[...]).astype(bf)
    cg_copy = remote(cg_send, cg_recv, sem_cg, sib)
    cg_copy.start()
    part_own = nt(pg[t], upv[...])
    cg_copy.wait()
    cgb[...] = (part_own + cg_recv[...].astype(f32)).astype(bf)
    cg_out = send_back(cgb, cgret, sem_rc)

    @pl.when(s == 1)
    def _():
        expert_rows()

    def send_gate_grads():
        gg_send[...] = jnp.zeros_like(gg_send)
        ones = jnp.ones((8, width), bf)
        for q in range(experts):
            at = slice(q * cap, (q + 1) * cap)
            high, low = split_low(dyrows[t, at, :].astype(f32) * eob[at, :].astype(f32))
            gg_send[q, :, 0:cap] = nt(ones, high) + nt(ones, low)
        out = [remote(gg_send.at[ahead[k]], gg_recv.at[d], sem_gg + k, (s, ahead[k], t)) for k in steps]
        for copy in out:
            copy.start()
        gg_recv[d] = gg_send[d]
        return out

    gg_out = send_gate_grads()

    wide = lay.wide
    for n in range(ffn // wide):
        at = slice(n * wide, (n + 1) * wide)
        total = tn(xrows[0], pg[0, :, at])
        for m in range(1, micro):
            total = total + tn(xrows[m], pg[m, :, at])
        guv[:, at] = total
        pltpu.make_async_copy(guv.at[:, at], gup_ref.at[:, at], gsem.at[n]).start()
        total = tn(hidden[0, :, at], og[0])
        for m in range(1, micro):
            total = total + tn(hidden[m, :, at], og[m])
        gdv[at, :] = total
        pltpu.make_async_copy(gdv.at[at, :], gdown_ref.at[at, :], gsem.at[ffn // wide + n]).start()

    finish(gg_out)
    finish(cg_out)
    gg_rows = []
    for e in range(experts):
        high, low = split_low(gg_recv[e][:, 0:cap])
        spot_rows = place[e * cap : (e + 1) * cap, :]
        gg_rows.append((nn(high, spot_rows) + nn(low, spot_rows))[0:1, :])
    gate_grad = jnp.concatenate(gg_rows, axis=0)
    gates = gate_t[...]
    logit_grad = (gates * (gate_grad - jnp.sum(gates * gate_grad, axis=0, keepdims=True))).astype(bf)
    early_send[0:experts, :] = nn(logit_grad, ntb[...]).astype(bf)
    two_grad = tn(logit_grad, wr_ref[...]) + tn(place[...], cgret[...])
    dy = dyb[...].astype(f32)
    middle = mid[...]
    scale = inverse_rms(middle)
    normed = middle * scale
    early_send[experts : 2 * experts, :] = jnp.broadcast_to(
        jnp.sum(two_grad * normed, axis=0, keepdims=True), (experts, width)
    ).astype(bf)
    scaled = two_grad * gain_two
    middle_grad = dy + scale * (scaled - normed * jnp.mean(scaled * normed, axis=-1, keepdims=True))
    mgrad[...] = middle_grad
    ag[t] = middle_grad.astype(bf)
    ag_copy = remote(ag.at[t], ag.at[t], sem_ag, sib)
    ag_copy.start()

    def to_all(source, landing, base):
        out = [remote(source, landing.at[d], base + k, (s, ahead[k], t)) for k in steps]
        for copy in out:
            copy.start()
        landing[d] = source[...]
        return out

    early_out = to_all(early_send, early_all, sem_early)
    ag_copy.wait()

    def spread(source, landing, rows, base):
        out = [remote(source.at[block(ahead[k], rows)], landing.at[d], base + k, (s, ahead[k], t)) for k in steps]
        for copy in out:
            copy.start()
        landing[d] = source[block(d, rows), :]
        return out

    for m in range(micro):
        agt[:, m * length : (m + 1) * length] = jnp.transpose(ag[m])
    agt_out = spread(agt, agt_all, width // experts, sem_agt)

    for m in range(micro):
        mg[m] = nt(ag[m], outw_ref[...]).astype(bf)
    for m in range(micro):
        for p in range(pairs):
            at = slice(p * 128, (p + 1) * 128)
            mg_pair = mg[m, :, at]
            probs = probs_buf[m, p]
            keys2 = both_heads(qkvb[1, m, :, at])
            queries2 = both_heads(qkvb[0, m, :, at])
            mg2 = both_heads(mg_pair)
            prob_grad = nt(mg_pair, both_heads(qkvb[2, m, :, at]))
            raws = []
            key_grad = jnp.zeros((length, 128), f32)
            value_grad = jnp.zeros((length, 128), f32)
            for h in range(2):
                lane = slice(h * length, (h + 1) * length)
                part = probs[:, lane]
                step = prob_grad[:, lane]
                score_grad = part * (step - jnp.sum(part * step, axis=-1, keepdims=True))
                score_sum[2 * p + h] = score_grad if m == 0 else score_sum[2 * p + h] + score_grad
                raw = (0.125 * score_grad).astype(bf)
                raws.append(raw)
                key_grad = key_grad + tn(raw, queries2[h * length : (h + 1) * length])
                value_grad = value_grad + tn(part.astype(bf), mg2[h * length : (h + 1) * length])
            query_grad = nn(jnp.concatenate(raws, axis=1), keys2)
            for c, grad in enumerate((query_grad, key_grad, value_grad)):
                qkvg[c, m, :, at] = grad.astype(bf)
                qgt[c * cols + p * 128 : c * cols + (p + 1) * 128, m * length : (m + 1) * length] = jnp.transpose(
                    grad
                ).astype(bf)
    qgt_out = spread(qgt, qt_all, 3 * cols // experts, sem_qgt)
    def project_back(m):
        total = nt(qkvg[0, m], qkvw_ref[0])
        for c in range(1, 3):
            total = total + nt(qkvg[c, m], qkvw_ref[c])
        return total

    no_send[...] = project_back(u).astype(bf)
    no_copy = remote(no_send, no_recv, sem_no, sib)
    no_copy.start()
    one_grad = project_back(t)
    no_copy.wait()
    one_grad = one_grad + no_recv[...].astype(f32)
    x_rows = xb[t].astype(f32)
    scale = inverse_rms(x_rows)
    normed = x_rows * scale
    gain_one_grad = jnp.sum(one_grad * normed, axis=0, keepdims=True)
    scaled = one_grad * gain_one
    input_grad = mgrad[...] + scale * (scaled - normed * jnp.mean(scaled * normed, axis=-1, keepdims=True))
    ig_own[...] = input_grad

    @pl.when(s == 1)
    def _():
        dy_send[...] = input_grad.astype(bf)
        copy = remote(dy_send, dyb, sem_dy, across)
        copy.start()
        copy.wait_send()

    hand_out(ig_own, ingrad_ref, sem_ig)

    sums = []
    for head in range(2 * pairs):
        high, low = split_low(score_sum[head])
        turned = pltpu.roll(nn(high, mirror) + nn(low, mirror), 0, 1, stride=1, stride_axis=0)
        sums.append(jnp.sum(turned, axis=0, keepdims=True))
    high, low = split_low(jnp.concatenate(sums, axis=0))
    late_send[...] = jnp.zeros_like(late_send)
    late_send[0 : 2 * pairs, 0 : lay.buckets] = nt(high, dist_rows) + nt(low, dist_rows)
    late_send[7:8, :] = gain_one_grad
    late_out = to_all(late_send, late_all, sem_late)

    @pl.when(s == 1)
    def _():
        gather_factors()

    finish(agt_out)
    total = nn(agt_all[0], mix_all[0])
    for q in range(1, experts):
        total = total + nn(agt_all[q], mix_all[q])
    qkv_rows = 3 * cols // experts
    out_rows = width // experts
    shared_ref[d, qkv_rows:, 0:cols] = total[0 : out_rows // 2].astype(bf)
    shared_ref[d, qkv_rows:, cols:] = total[out_rows // 2 :].astype(bf)
    finish(qgt_out)
    total = jnp.zeros((qkv_rows, width), f32)
    for q in range(experts):
        total = total + nn(qt_all[q], jnp.concatenate([no_all[0, q], no_all[1, q]], axis=0))
    shared_ref[d, 0:qkv_rows, :] = total.astype(bf)
    share = shared_ref.shape[1] // 4
    ring_gather(
        [
            (lambda q, c=c: shared_ref.at[q, c * share : (c + 1) * share], 1 if c < 2 else -1, sem_ring_out + c * experts)
            for c in range(4)
        ]
    )
    finish(early_out)
    finish(late_out)
    early_sum = early_all[0].astype(f32)
    late_sum = late_all[0]
    for q in range(1, experts):
        early_sum = early_sum + early_all[q].astype(f32)
        late_sum = late_sum + late_all[q]
    gbias_ref[...] = late_sum[0 : 2 * pairs, 0 : lay.buckets]
    sums_send[0 : 2 * experts, :] = early_sum
    sums_send[2 * experts :, :] = late_sum
    sums_copy = remote(sums_send, sums_recv, sem_sums, sib)
    sums_copy.start()
    sums_copy.wait()
    grouter_ref[...] = sums_send[0:experts, :] + sums_recv[0:experts, :]
    ggain_ref[0:1, :] = sums_send[2 * experts + 7 :, :] + sums_recv[2 * experts + 7 :, :]
    ggain_ref[1:2, :] = sums_send[experts : experts + 1, :] + sums_recv[experts : experts + 1, :]

    @pl.when(s == 1)
    def _():
        finish(send_back(eob, eoret, sem_re))
        layer_output()
        hand_out(out_own, secout_ref, sem_so)

    for copy in sent:
        copy.wait_send()
    for n in range(ffn // wide):
        at = slice(n * wide, (n + 1) * wide)
        pltpu.make_async_copy(guv.at[:, at], gup_ref.at[:, at], gsem.at[n]).wait()
        pltpu.make_async_copy(gdv.at[at, :], gdown_ref.at[at, :], gsem.at[ffn // wide + n]).wait()


def fused_local(
    tokens,
    cotangent,
    segments,
    pad_mask,
    routes,
    dist_bucket,
    norm_gains,
    qkv_weight,
    out_weight,
    rel_bias,
    router_weight,
    expert_up,
    expert_down,
):
    micro, _, length, width = tokens.shape
    experts = router_weight.shape[2]
    cap = max(2, 3 * length // experts)
    cols = out_weight.shape[1]
    heads = rel_bias.shape[2]
    ffn = expert_up.shape[3]
    slots = experts * cap
    pairs = cols // 128
    lay = Layout()
    lay.experts = experts
    lay.cap = cap
    lay.buckets = rel_bias.shape[1]
    lay.row_tile = min(slots, 192)
    lay.wide = min(ffn, 256)
    lay.sems = 20 * experts + 12
    bf = jnp.bfloat16
    f32 = jnp.float32
    vm = pltpu.VMEM
    shape = jax.ShapeDtypeStruct
    dma = pltpu.SemaphoreType.DMA
    scratch = [
        vm((width, ffn), bf),
        vm((ffn, width), bf),
        vm((micro, length, width), bf),
        vm((length, width), bf),
        vm((experts, micro, 2, length), jnp.int32),
        vm((slots, length), bf),
        vm((micro, pairs, length, 2 * length), f32),
        vm((micro, pairs, length, 2 * length), f32),
        vm((micro, length, width), bf),
        vm((3, micro, length, cols), bf),
        vm((micro, length, cols), bf),
        vm((length, width), f32),
        vm((length, width), f32),
        vm((length, width), f32),
        vm((length, width), bf),
        vm((experts, length), f32),
        vm((experts, length), f32),
        vm((2 * pairs, length, length), f32),
        vm((slots, width), bf),
        vm((micro, slots, width), bf),
        vm((slots, width), bf),
        vm((micro, slots, width), bf),
        vm((micro, slots, ffn), bf),
        vm((micro, slots, ffn), bf),
        vm((slots, width), bf),
        vm((slots, width), bf),
        vm((slots, width), bf),
        vm((slots, width), bf),
        vm((length, width), f32),
        vm((length, width), bf),
        vm((micro, slots, experts), f32),
        vm((micro, slots, width), bf),
        vm((experts, 8, 128), f32),
        vm((experts, 8, 128), f32),
        vm((micro, slots, ffn), bf),
        vm((slots, width), bf),
        vm((slots, width), bf),
        vm((slots, width), bf),
        vm((slots, width), bf),
        vm((length, width), f32),
        vm((micro, length, width), bf),
        vm((micro, length, cols), bf),
        vm((3, micro, length, cols), bf),
        vm((length, width), bf),
        vm((length, width), bf),
        vm((length, width), f32),
        vm((length, width), bf),
        vm((width, ffn), f32),
        vm((ffn, width), f32),
        vm((micro, experts, length, width), bf),
        vm((experts, micro * length, cols), bf),
        vm((3 * cols, micro * length), bf),
        vm((experts, 3 * cols // experts, micro * length), bf),
        vm((width, micro * length), bf),
        vm((experts, width // experts, micro * length), bf),
        vm((2 * experts, width), bf),
        vm((experts, 2 * experts, width), bf),
        vm((8, width), f32),
        vm((experts, 8, width), f32),
        vm((2 * experts + 8, width), f32),
        vm((2 * experts + 8, width), f32),
        dma((2,)),
        dma((2 * (ffn // lay.wide),)),
        dma((lay.sems,)),
        dma((lay.sems,)),
    ]
    whole = pl.BlockSpec(memory_space=pltpu.VMEM)
    anywhere = pl.BlockSpec(memory_space=pl.ANY)
    shared_rows = 3 * cols // experts + width // experts // 2
    out_shape = (
        shape((micro, length, width // 2), f32),
        shape((micro, length, width // 2), f32),
        shape((2, width), f32),
        shape((experts, shared_rows, width), bf),
        shape((heads, lay.buckets), f32),
        shape((experts, width), f32),
        shape((width, ffn), f32),
        shape((ffn, width), f32),
    )
    results = pl.pallas_call(
        partial(layer_kernel, lay),
        out_shape=out_shape,
        in_specs=[whole] * 11 + [anywhere] * 2,
        out_specs=[whole] * 6 + [anywhere] * 2,
        scratch_shapes=scratch,
        name="two_sections",
        compiler_params=pltpu.CompilerParams(
            collective_id=0, has_side_effects=True, vmem_limit_bytes=60 * 1024 * 1024
        ),
    )(
        tokens[:, 0],
        cotangent[:, 0],
        segments[:, 0],
        pad_mask[:, 0],
        routes[:, 0].transpose(0, 2, 1),
        dist_bucket[None],
        norm_gains[0],
        qkv_weight[0].transpose(1, 0, 2),
        out_weight[0],
        rel_bias[0].T,
        router_weight[0].T,
        expert_up[0, 0],
        expert_down[0, 0],
    )
    section_out, input_grads, gains, shared, bias, router, up, down = results
    qkv_rows = 3 * cols // experts
    qkv = shared[:, :qkv_rows].reshape(3, cols, width).astype(f32)
    out = shared[:, qkv_rows:].reshape(experts, -1, 2, cols).transpose(0, 2, 1, 3).reshape(width, cols).astype(f32)
    return (
        section_out[None, :, None],
        input_grads[None, :, None],
        gains[None],
        qkv.transpose(2, 0, 1)[None],
        out.T[None],
        bias.T[None],
        router.T[None],
        up[None, None],
        down[None, None],
    )


def fits_kernel(mesh):
    return mesh.shape["section"] == 2 and mesh.shape["tensor"] == 2 and mesh.shape["dp"] == 8


def solution(mesh):
    in_specs = (
        P(None, "dp", None, None),
        P(None, "dp", None, None),
        P(None, "dp", None),
        P(None, "dp", None),
        P(None, "dp", None, None),
        P(),
        P("section", None, None),
        P("section", None, None, "tensor"),
        P("section", "tensor", None),
        P("section", None, "tensor"),
        P("section", None, None),
        P("section", "dp", None, "tensor"),
        P("section", "dp", "tensor", None),
    )
    out_specs = (
        P("section", None, "dp", None, "tensor"),
        P("section", None, "dp", None, "tensor"),
        P("section", None, None),
        P("section", None, None, "tensor"),
        P("section", "tensor", None),
        P("section", None, "tensor"),
        P("section", None, None),
        P("section", "dp", None, "tensor"),
        P("section", "dp", "tensor", None),
    )
    body = fused_local if fits_kernel(mesh) else local
    return jax.shard_map(body, mesh=mesh, in_specs=in_specs, out_specs=out_specs, check_vma=False)
```

```python
from functools import partial

import jax
import jax.numpy as jnp
from jax import lax
from jax.experimental import pallas as pl
from jax.experimental.pallas import tpu as pltpu
from jax.sharding import PartitionSpec as P

norm_eps = 1e-06
masked_score = -1e30
highest = lax.Precision.HIGHEST


def shifted(block, axis, distance):
    devices = range(lax.axis_size(axis))
    route = [(i - distance, i) for i in devices if i - distance in devices]
    return lax.ppermute(block, axis, route)


def normalize(values, gain_row):
    scale_inv = lax.rsqrt(jnp.mean(values * values, axis=-1, keepdims=True) + norm_eps)
    return values * scale_inv * gain_row


def normalize_back(values, gain_row, upstream):
    scale_inv = lax.rsqrt(jnp.mean(values * values, axis=-1, keepdims=True) + norm_eps)
    normed = values * scale_inv
    gain_grad = jnp.sum(upstream * normed, axis=0)
    scaled = upstream * gain_row
    input_grad = scale_inv * (scaled - normed * jnp.mean(scaled * normed, axis=-1, keepdims=True))
    return (input_grad, gain_grad)


def send_rows(rows):
    return lax.all_to_all(rows, "dp", split_axis=0, concat_axis=0, tiled=True)


def sum_slots(partial_rows):
    return lax.psum(partial_rows, "tensor")


def score_context(segment_row, pad_row, dist_bucket, bucket_count):
    length = segment_row.shape[0]
    places = jnp.arange(length, dtype=jnp.int32)
    offsets = jnp.clip(places[:, None] - places[None, :], 0, length - 1)
    bucket_grid = jnp.take(dist_bucket, offsets)
    bucket_onehot = (
        bucket_grid[:, :, None] == jnp.arange(bucket_count, dtype=jnp.int32)[None, None, :]
    ).astype(jnp.float32)
    allowed = (places[None, :] <= places[:, None]) & (segment_row[:, None] == segment_row[None, :])
    allowed = allowed & ((pad_row[None, :] == 1) | (places[None, :] == places[:, None]))
    return (bucket_onehot, allowed)


def attention_front(inputs, context, weights):
    segment_row, pad_row, route_rows, dist_bucket = context
    gain_pair, qkv_weight, out_weight, bias_table, router_weight, upper_weight, lower_weight = (
        weights
    )
    length = inputs.shape[0]
    head_count = bias_table.shape[1]
    bucket_onehot, allowed = score_context(segment_row, pad_row, dist_bucket, bias_table.shape[0])
    normed_one = normalize(inputs, gain_pair[0]).astype(jnp.bfloat16)
    qkv_rows = jnp.einsum(
        "ld,dch->lch", normed_one, qkv_weight, preferred_element_type=jnp.float32
    ).astype(jnp.bfloat16)
    head_dim = qkv_rows.shape[2] // head_count
    queries = qkv_rows[:, 0].reshape(length, head_count, head_dim)
    keys_in = qkv_rows[:, 1].reshape(length, head_count, head_dim)
    values_in = qkv_rows[:, 2].reshape(length, head_count, head_dim)
    raw_scores = jnp.einsum("qhd,khd->hqk", queries, keys_in, preferred_element_type=jnp.float32)
    bias_grid = jnp.einsum(
        "qkb,bh->hqk", bucket_onehot, bias_table.astype(jnp.float32), precision=highest
    )
    logits = jnp.where(allowed[None], 0.125 * raw_scores + bias_grid, masked_score)
    exp_terms = jnp.exp(logits - jnp.max(logits, axis=-1, keepdims=True))
    attn_probs = exp_terms / jnp.sum(exp_terms, axis=-1, keepdims=True)
    mixed_rows = jnp.einsum(
        "hqk,khd->qhd",
        attn_probs.astype(jnp.bfloat16),
        values_in,
        preferred_element_type=jnp.float32,
    )
    mixed_rows = mixed_rows.reshape(length, -1).astype(jnp.bfloat16)
    return (normed_one, queries, keys_in, values_in, attn_probs, mixed_rows, bucket_onehot)


def slot_tables(route_rows, experts, capacity):
    flat_routes = route_rows.reshape(-1)
    route_hits = (flat_routes[:, None] == jnp.arange(experts, dtype=jnp.int32)[None, :]).astype(
        jnp.int32
    )
    earlier = jnp.cumsum(route_hits, axis=0) - route_hits
    position = jnp.sum(earlier * route_hits, axis=1)
    target = flat_routes * capacity + position
    slot_hits = (
        jnp.arange(experts * capacity, dtype=jnp.int32)[:, None] == target[None, :]
    ).astype(jnp.int32)
    source = jnp.sum(slot_hits * jnp.arange(target.shape[0], dtype=jnp.int32)[None, :], axis=1)
    filled = jnp.sum(slot_hits, axis=1) > 0
    return (target, source, filled, route_hits)


def route_gates(normed_two, router_weight, route_hits):
    length = normed_two.shape[0]
    logits = jnp.dot(normed_two, router_weight, preferred_element_type=jnp.float32)
    route_onehot = route_hits.reshape(length, 2, -1).astype(jnp.float32)
    chosen = jnp.einsum("le,lre->lr", logits, route_onehot, precision=highest)
    return (jax.nn.softmax(chosen, axis=-1), route_onehot)


def gather_back(back_slots, target, length):
    flat_slots = back_slots.reshape(-1, back_slots.shape[-1])
    return jnp.take(flat_slots, target, axis=0).reshape(length, 2, -1)


def forward_rest(inputs, front, context, weights):
    segment_row, pad_row, route_rows, dist_bucket = context
    gain_pair, qkv_weight, out_weight, bias_table, router_weight, upper_weight, lower_weight = (
        weights
    )
    mixed_rows = front[5]
    length, model_width = inputs.shape
    experts = router_weight.shape[1]
    capacity = max(2, 3 * length // experts)
    local_experts = upper_weight.shape[0]
    attn_out = lax.psum(
        jnp.dot(mixed_rows, out_weight, preferred_element_type=jnp.float32), "tensor"
    )
    middle = inputs + attn_out
    normed_two = normalize(middle, gain_pair[1]).astype(jnp.bfloat16)
    target, source, filled, route_hits = slot_tables(route_rows, experts, capacity)
    outgoing = jnp.where(
        filled[:, None], jnp.take(normed_two, source // 2, axis=0), jnp.zeros((), jnp.bfloat16)
    )
    outgoing = outgoing.reshape(experts, capacity, model_width)
    arrived = send_rows(outgoing)
    grouped = arrived.reshape(-1, local_experts, capacity, model_width)
    pre_act = jnp.einsum(
        "secd,edf->secf", grouped, upper_weight, preferred_element_type=jnp.float32
    )
    hidden = jax.nn.gelu(pre_act, approximate=False).astype(jnp.bfloat16)
    partial_out = jnp.einsum(
        "secf,efd->secd", hidden, lower_weight, preferred_element_type=jnp.float32
    )
    summed = sum_slots(partial_out)
    returned = summed.astype(jnp.bfloat16).reshape(arrived.shape[0], arrived.shape[1], -1)
    back_slots = send_rows(returned)
    gate_probs, route_onehot = route_gates(normed_two, router_weight, route_hits)
    back_rows = gather_back(back_slots, target, length)
    output = middle + jnp.sum(gate_probs[:, :, None] * back_rows.astype(jnp.float32), axis=1)
    return (output, (attn_out, arrived, back_slots, pre_act))


def backward_layer(inputs, upstream, context, weights, front, saved_state):
    segment_row, pad_row, route_rows, dist_bucket = context
    gain_pair, qkv_weight, out_weight, bias_table, router_weight, upper_weight, lower_weight = (
        weights
    )
    normed_one, queries, keys_in, values_in, attn_probs, mixed_rows, bucket_onehot = front
    attn_out, arrived_rows, back_slots, pre_rows = saved_state
    length, model_width = inputs.shape
    head_count = bias_table.shape[1]
    head_cols = qkv_weight.shape[2]
    experts = router_weight.shape[1]
    capacity = max(2, 3 * length // experts)
    local_experts = upper_weight.shape[0]
    middle = inputs + attn_out
    normed_two = normalize(middle, gain_pair[1]).astype(jnp.bfloat16)
    target, source, filled, route_hits = slot_tables(route_rows, experts, capacity)
    gate_probs, route_onehot = route_gates(normed_two, router_weight, route_hits)
    back_rows = gather_back(back_slots, target, length)
    gate_grad = jnp.sum(upstream[:, None, :] * back_rows.astype(jnp.float32), axis=-1)
    chosen_grad = gate_probs * (gate_grad - jnp.sum(gate_probs * gate_grad, axis=-1, keepdims=True))
    logit_grad = jnp.einsum("lr,lre->le", chosen_grad, route_onehot, precision=highest).astype(
        jnp.bfloat16
    )
    router_grad = jnp.dot(normed_two.T, logit_grad, preferred_element_type=jnp.float32)
    normed_two_grad = jnp.dot(logit_grad, router_weight.T, preferred_element_type=jnp.float32)
    route_grads = (
        (gate_probs[:, :, None] * upstream[:, None, :])
        .reshape(2 * length, model_width)
        .astype(jnp.bfloat16)
    )
    slot_grads = jnp.where(
        filled[:, None], jnp.take(route_grads, source, axis=0), jnp.zeros((), jnp.bfloat16)
    )
    arrived_grads = send_rows(slot_grads.reshape(experts, capacity, model_width))
    grouped = arrived_rows.reshape(-1, local_experts, capacity, model_width)
    grouped_grads = arrived_grads.reshape(-1, local_experts, capacity, model_width)
    hidden, gelu_pull = jax.vjp(partial(jax.nn.gelu, approximate=False), pre_rows)
    hidden_low = hidden.astype(jnp.bfloat16)
    down_grad = jnp.einsum(
        "secf,secd->efd", hidden_low, grouped_grads, preferred_element_type=jnp.float32
    )
    hidden_grad = jnp.einsum(
        "secd,efd->secf", grouped_grads, lower_weight, preferred_element_type=jnp.float32
    )
    pre_grad = gelu_pull(hidden_grad)[0].astype(jnp.bfloat16)
    up_grad = jnp.einsum("secd,secf->edf", grouped, pre_grad, preferred_element_type=jnp.float32)
    rows_grad = sum_slots(
        jnp.einsum("secf,edf->secd", pre_grad, upper_weight, preferred_element_type=jnp.float32)
    )
    sent_back = send_rows(
        rows_grad.astype(jnp.bfloat16).reshape(arrived_rows.shape[0], arrived_rows.shape[1], -1)
    )
    copy_grads = gather_back(sent_back, target, length).astype(jnp.float32)
    normed_two_grad = normed_two_grad + jnp.sum(copy_grads, axis=1)
    middle_part, gain_two = normalize_back(middle, gain_pair[1], normed_two_grad)
    middle_grad = upstream + middle_part
    attn_grad = middle_grad.astype(jnp.bfloat16)
    out_grad = jnp.dot(mixed_rows.T, attn_grad, preferred_element_type=jnp.float32)
    mixed_grad = jnp.dot(attn_grad, out_weight.T, preferred_element_type=jnp.float32).astype(
        jnp.bfloat16
    )
    mixed_grad = mixed_grad.reshape(length, head_count, -1)
    prob_grad = jnp.einsum(
        "qhd,khd->hqk", mixed_grad, values_in, preferred_element_type=jnp.float32
    )
    value_grad = jnp.einsum(
        "hqk,qhd->khd",
        attn_probs.astype(jnp.bfloat16),
        mixed_grad,
        preferred_element_type=jnp.float32,
    )
    score_grad = attn_probs * (prob_grad - jnp.sum(prob_grad * attn_probs, axis=-1, keepdims=True))
    table_grad = jnp.einsum("hqk,qkb->bh", score_grad, bucket_onehot, precision=highest)
    raw_grad = (0.125 * score_grad).astype(jnp.bfloat16)
    query_grad = jnp.einsum("hqk,khd->qhd", raw_grad, keys_in, preferred_element_type=jnp.float32)
    key_grad = jnp.einsum("hqk,qhd->khd", raw_grad, queries, preferred_element_type=jnp.float32)
    qkv_grad = (
        jnp.stack([query_grad, key_grad, value_grad], axis=1)
        .reshape(length, 3, head_cols)
        .astype(jnp.bfloat16)
    )
    qkv_weight_grad = jnp.einsum(
        "ld,lch->dch", normed_one, qkv_grad, preferred_element_type=jnp.float32
    )
    normed_one_grad = lax.psum(
        jnp.einsum("lch,dch->ld", qkv_grad, qkv_weight, preferred_element_type=jnp.float32),
        "tensor",
    )
    input_part, gain_one = normalize_back(inputs, gain_pair[0], normed_one_grad)
    input_grad = middle_grad + input_part
    gain_grads = jnp.stack([gain_one, gain_two])
    return (
        input_grad,
        (gain_grads, qkv_weight_grad, out_grad, table_grad, router_grad, up_grad, down_grad),
    )


def pick_context(segments, pad_mask, routes, dist_bucket, micro_slot):
    segment_row = lax.dynamic_index_in_dim(segments[:, 0], micro_slot, 0, False)
    pad_row = lax.dynamic_index_in_dim(pad_mask[:, 0], micro_slot, 0, False)
    route_rows = lax.dynamic_index_in_dim(routes[:, 0], micro_slot, 0, False)
    return (segment_row, pad_row, route_rows, dist_bucket)


def place_row(store_all, new_value, micro_slot, is_valid):
    current = lax.dynamic_index_in_dim(store_all, micro_slot, 0, False)
    return lax.dynamic_update_index_in_dim(
        store_all, jnp.where(is_valid, new_value, current), micro_slot, 0
    )


def pick_row(store_all, micro_slot):
    return lax.dynamic_index_in_dim(store_all, micro_slot, 0, False)


def mask_grad(grad_value, is_valid):
    return jnp.where(is_valid, grad_value, jnp.zeros((), grad_value.dtype))


def tensor_half(full_rows, tensor_id, half_width):
    return lax.dynamic_slice_in_dim(full_rows, tensor_id * half_width, half_width, 2)[None, :, None]


def local(
    tokens,
    cotangent,
    segments,
    pad_mask,
    routes,
    dist_bucket,
    norm_gains,
    qkv_weight,
    out_weight,
    rel_bias,
    router_weight,
    expert_up,
    expert_down,
):
    section_id = lax.axis_index("section")
    section_count = lax.axis_size("section")
    micro_count = tokens.shape[0]
    length = tokens.shape[2]
    model_width = tokens.shape[3]
    tick_count = micro_count + section_count - 1
    weights = (
        norm_gains[0].astype(jnp.float32),
        qkv_weight[0],
        out_weight[0],
        rel_bias[0],
        router_weight[0],
        expert_up[0],
        expert_down[0],
    )
    empty_rows = jnp.zeros((length, model_width), jnp.bfloat16)
    arriving = empty_rows
    kept_inputs = jnp.zeros((micro_count, length, model_width), jnp.bfloat16)
    section_out = jnp.zeros((micro_count, length, model_width), jnp.float32)
    for tick_index in range(tick_count):
        micro_index = tick_index - section_id
        is_valid = (micro_index >= 0) & (micro_index < micro_count)
        micro_slot = jnp.clip(micro_index, 0, micro_count - 1)
        own_rows = tokens[tick_index, 0] if tick_index < micro_count else empty_rows
        layer_in = jnp.where(section_id == 0, own_rows, arriving)
        context = pick_context(segments, pad_mask, routes, dist_bucket, micro_slot)
        inputs = layer_in.astype(jnp.float32)
        front = attention_front(inputs, context, weights)
        result, saved_state = forward_rest(inputs, front, context, weights)
        section_out = place_row(section_out, result, micro_slot, is_valid)
        kept_inputs = place_row(kept_inputs, layer_in, micro_slot, is_valid)
        arriving = shifted(result.astype(jnp.bfloat16), "section", 1)
    returning = empty_rows
    input_store = jnp.zeros((micro_count, length, model_width), jnp.float32)
    totals = None
    for tick_index in range(tick_count):
        micro_index = tick_index - (section_count - 1 - section_id)
        is_valid = (micro_index >= 0) & (micro_index < micro_count)
        micro_slot = jnp.clip(micro_index, 0, micro_count - 1)
        own_rows = cotangent[tick_index, 0] if tick_index < micro_count else empty_rows
        upstream = jnp.where(section_id == section_count - 1, own_rows, returning).astype(
            jnp.float32
        )
        inputs = pick_row(kept_inputs, micro_slot).astype(jnp.float32)
        context = pick_context(segments, pad_mask, routes, dist_bucket, micro_slot)
        front = attention_front(inputs, context, weights)
        saved_state = forward_rest(inputs, front, context, weights)[1]
        input_grad, grad_set = backward_layer(
            inputs, upstream, context, weights, front, saved_state
        )
        input_store = place_row(input_store, input_grad, micro_slot, is_valid)
        grad_set = jax.tree.map(partial(mask_grad, is_valid=is_valid), grad_set)
        totals = grad_set if totals is None else jax.tree.map(jnp.add, totals, grad_set)
        returning = shifted(input_grad.astype(jnp.bfloat16), "section", -1)
    shared = lax.psum((totals[0], totals[1], totals[2], totals[3], totals[4]), "dp")
    tensor_id = lax.axis_index("tensor")
    half_width = model_width // lax.axis_size("tensor")
    return (
        tensor_half(section_out, tensor_id, half_width),
        tensor_half(input_store, tensor_id, half_width),
        shared[0][None],
        shared[1][None],
        shared[2][None],
        shared[3][None],
        shared[4][None],
        totals[5][None],
        totals[6][None],
    )


def gelu_parts(values):
    share = 0.5 + 0.5 * lax.erf(values * 0.7071067811865476)
    return (values * share, share + values * (0.3989422804014327 * jnp.exp(-0.5 * values * values)))


def nn(left, right):
    return lax.dot_general(left, right, (((1,), (0,)), ((), ())), preferred_element_type=jnp.float32)


def nt(left, right):
    return lax.dot_general(left, right, (((1,), (1,)), ((), ())), preferred_element_type=jnp.float32)


def tn(left, right):
    return lax.dot_general(left, right, (((0,), (0,)), ((), ())), preferred_element_type=jnp.float32)


def split_low(values):
    high = values.astype(jnp.bfloat16)
    return (high, (values - high.astype(jnp.float32)).astype(jnp.bfloat16))


def inverse_rms(values):
    return lax.rsqrt(jnp.mean(values * values, axis=-1, keepdims=True) + norm_eps)


class Layout:
    pass


def layer_kernel(lay, *refs):
    (
        tok_ref, cot_ref, seg_ref, pad_ref, routes_ref, dist_ref, gains_ref, qkvw_hbm, outw_hbm, relb_ref, wr_ref,
        up_ref, down_ref,
        secout_ref, ingrad_ref, ggain_ref, shared_ref, gbias_ref, grouter_ref, gup_ref, gdown_ref,
        upv, downv, qkvw_ref, outw_ref, xb, dyb, rr, place, bias_buf, probs_buf, no1, qkvb, mixed, att_send, att_recv, mid, ntb,
        gate_t, hit_t, wrp, score_sum, disp_x, xrows, disp_y, dyrows, hidden, dgelu, halves, eo_send, eo_recv, eob, eoret, out_own,
        x_send,
        other, og, gg_send, gg_recv, pg, cg_send, cg_recv, cgb, cgret, mgrad, ag, mg, qkvg,
        no_send, no_recv, ig_own, dy_send, guv, gdv,
        no_all, mix_all, qgt, qt_all, agt, agt_all, small_send, small_in, small_all, small_sib,
        wsem, gsem, ss, rs,
    ) = refs
    bf = jnp.bfloat16
    f32 = jnp.float32
    micro, length, width = tok_ref.shape
    experts = lay.experts
    cap = lay.cap
    cols = outw_ref.shape[0]
    pairs = cols // 128
    ffn = up_ref.shape[1]
    slots = experts * cap
    half = width // 2
    s = lax.axis_index("section")
    d = lax.axis_index("dp")
    t = lax.axis_index("tensor")
    u = 1 - t
    sib = (s, d, u)
    across = (1 - s, d, t)
    bits = [lax.rem(d // bit, 2) for bit in (1, 2, 4)]

    def partner(flip):
        index = d
        for place, bit in enumerate((1, 2, 4)):
            if flip & bit:
                index = index + bit - 2 * bit * bits[place]
        return index

    peer = [partner(flip) for flip in (0, 4, 1, 6, 2, 5, 3, 7)]
    steps = range(1, experts)
    chunks = [slice(c, c + 2) for c in range(0, experts, 2)]

    def remote(src, dst, index, device):
        return pltpu.make_async_remote_copy(
            src_ref=src,
            dst_ref=dst,
            send_sem=ss.at[index],
            recv_sem=rs.at[index],
            device_id=device,
            device_id_type=pl.DeviceIdType.MESH,
        )

    counter = [0]

    def take(amount):
        counter[0] += amount
        return counter[0] - amount

    sent = []

    def fire(copy):
        copy.start()
        sent.append(copy)

    sem_routes = take(experts)
    sem_x = take(1)
    sem_xf = take(1)
    sem_dy = take(1)
    sem_att = take(1)
    sem_eo = take(experts)
    sem_cg = take(experts)
    sem_ag = take(1)
    sem_no = take(1)
    sem_so = take(1)
    sem_ig = take(1)
    sem_dx = take(experts)
    sem_dxf = take(experts)
    sem_ddy = take(experts)
    sem_ddyf = take(experts)
    sem_re = take(experts)
    sem_rc = take(experts)
    sem_gg = take(experts)
    sem_agt = take(experts)
    sem_agtf = take(experts)
    sem_qgt = take(experts)
    sem_small = take(experts)
    sem_back = take(experts)
    sem_sums = take(1)
    sem_noall = take(1)
    sem_ring_no = take(2 * experts)
    sem_ring_mix = take(2 * experts)
    sem_ring_out = take(6 * experts)
    assert counter[0] == lay.sems

    def block(index, rows):
        return pl.ds(pl.multiple_of(index * rows, rows), rows)

    place_y = lax.rem(d, 2)
    place_z = d // 2
    ring_at = place_z + place_y * (experts - 1 - 2 * place_z)

    def ring_device(position):
        p = lax.rem(position + 2 * experts, experts)
        return 2 * p + (p // (experts // 2)) * (2 * experts - 1 - 4 * p)

    def ring_gather(streams, at_half=None):
        moved = []
        for k in range(experts - 1):
            if k == experts // 2 and at_half is not None:
                at_half()
            for number, (view, direction, base) in enumerate(streams):
                if k > 0:
                    moved[(k - 1) * len(streams) + number].wait_recv()
                held = view(ring_device(ring_at - direction * k))
                copy = remote(held, held, base + k, (s, ring_device(ring_at + direction), t))
                copy.start()
                moved.append(copy)
        for copy in moved[(experts - 2) * len(streams) :]:
            copy.wait_recv()
        for copy in moved:
            copy.wait_send()

    load_up = pltpu.make_async_copy(up_ref, upv, wsem.at[0])
    load_down = pltpu.make_async_copy(down_ref, downv, wsem.at[1])
    load_qkvw = pltpu.make_async_copy(qkvw_hbm, qkvw_ref, wsem.at[2])
    load_outw = pltpu.make_async_copy(outw_hbm, outw_ref, wsem.at[3])
    load_tok = pltpu.make_async_copy(tok_ref, xb, wsem.at[4])
    load_cot = pltpu.make_async_copy(cot_ref.at[t], dyb, wsem.at[4])

    @pl.when(s == 0)
    def _():
        load_tok.start()

    @pl.when(s == 1)
    def _():
        load_cot.start()

    load_qkvw.start()
    load_outw.start()
    load_up.start()
    load_down.start()

    barrier = pltpu.get_barrier_semaphore()
    for k in steps:
        pl.semaphore_signal(barrier, inc=1, device_id=(s, peer[k], t), device_id_type=pl.DeviceIdType.MESH)
    pl.semaphore_signal(barrier, inc=1, device_id=sib, device_id_type=pl.DeviceIdType.MESH)
    pl.semaphore_signal(barrier, inc=1, device_id=across, device_id_type=pl.DeviceIdType.MESH)
    pl.semaphore_wait(barrier, experts + 1)

    for k in steps:
        fire(remote(routes_ref, rr.at[k], sem_routes + k, (s, peer[k], t)))
    rr[0] = routes_ref[...]

    lanes8 = lax.broadcasted_iota(jnp.int32, (experts, length), 0)
    row_at = lax.broadcasted_iota(jnp.int32, (length, length), 0)
    col_at = lax.broadcasted_iota(jnp.int32, (length, length), 1)
    before = (row_at < col_at).astype(bf)
    slot_at = lax.broadcasted_iota(jnp.int32, (cap, length), 0).astype(f32)

    expert_of = jnp.zeros((experts, length), jnp.int32)
    for k in range(experts):
        expert_of = jnp.where(lanes8 == k, peer[k], expert_of)
    turn = (lax.broadcasted_iota(jnp.int32, (experts, experts), 1) == expert_of[:, 0:experts]).astype(f32).astype(bf)
    wrp[...] = nn(turn, wr_ref[...]).astype(bf)
    own_routes = routes_ref[t]
    hits = (expert_of == own_routes[0:1, :]) | (expert_of == own_routes[1:2, :])
    hit_f = hits.astype(f32)
    hit_t[...] = hit_f
    spot = jnp.where(hits, nn(hit_f.astype(bf), before), -1.0)
    for e in range(experts):
        place[e * cap : (e + 1) * cap, :] = (slot_at == spot[e : e + 1, :]).astype(f32).astype(bf)

    def dispatch(rows, send, landing, base, base_fwd):
        send[...] = nn(place[...], rows).astype(bf).reshape(send.shape)
        out = [remote(send.at[k], landing.at[k, t], base + k, (s, peer[k], t)) for k in steps]
        for copy in out:
            copy.start()
        first = remote(send.at[0], landing.at[0, t], base_fwd, sib)
        first.start()
        landing[0, t] = send[0]

        def steps_of():
            passed = [first]

            def arrive(c):
                for k in (2 * c, 2 * c + 1):
                    if k > 0:
                        out[k - 1].wait_recv()
                        copy = remote(landing.at[k, t], landing.at[k, t], base_fwd + k, sib)
                        copy.start()
                        passed.append(copy)

            def joined(c):
                for k in (2 * c, 2 * c + 1):
                    passed[k].wait_recv()

            def drain():
                for copy in out + passed:
                    copy.wait_send()

            return arrive, joined, drain

        return steps_of

    def stream(dispatched, first, second, finish_chunk, eager):
        arrive, joined, drain = dispatched()
        last = len(chunks) - 1
        arrive(0)
        joined(0)
        for c in range(len(chunks)):
            first(c)
            if eager and c > 0:
                finish_chunk(c - 1)
            if eager and c < last:
                arrive(c + 1)
            second(c)
            if not eager and c < last:
                arrive(c + 1)
                finish_chunk(c)
            if c < last:
                joined(c + 1)
        finish_chunk(last)
        drain()

    def other_experts():
        for k in steps:
            remote(routes_ref, rr.at[k], sem_routes + k, (s, peer[k], t)).wait_recv()

        def one(i, carry):
            q = i // micro
            m = i % micro
            pair = rr[q, m]
            first = pair[0:1, :] == d
            mine = first | (pair[1:2, :] == d)
            mine_f = jnp.broadcast_to(mine.astype(f32), (experts, length))
            spots = jnp.where(mine_f > 0.0, nn(mine_f.astype(bf), before), -1.0)
            where_slot = (slot_at == spots[0:1, :]).astype(f32).astype(bf)
            partner = jnp.where(first, pair[1:2, :], pair[0:1, :])
            partner_hot = (lanes8 == partner).astype(f32).astype(bf)
            other[q, m] = nt(where_slot, partner_hot)
            return carry

        lax.fori_loop(0, experts * micro, one, 0)

    @pl.when(s == 0)
    def _():
        load_tok.wait()

    @pl.when(s == 1)
    def _():
        load_cot.wait()
        arrive, joined, drain = dispatch(dyb[...], disp_y, dyrows, sem_ddy, sem_ddyf)()
        for c in range(len(chunks)):
            arrive(c)
        for c in range(len(chunks)):
            joined(c)
        drain()
        other_experts()

    dist_rows = (
        lax.broadcasted_iota(jnp.int32, (lay.buckets, length), 0) == dist_ref[...]
    ).astype(f32).astype(bf)
    bias_rows = nn(relb_ref[...], dist_rows).astype(bf)
    mirror = ((row_at + col_at == length) | (row_at + col_at == 0)).astype(f32).astype(bf)
    bias_back = nn(bias_rows, mirror)
    for m in range(micro):
        seg_rows = jnp.broadcast_to(seg_ref[m : m + 1, :].astype(f32), (length, length))
        pads = jnp.broadcast_to(pad_ref[m : m + 1, :], (length, length))
        allowed = (col_at <= row_at) & (seg_rows == jnp.transpose(seg_rows))
        allowed = allowed & ((pads == 1) | (col_at == row_at))
        for p in range(pairs):
            for h in range(2):
                head = 2 * p + h
                grid = pltpu.roll(
                    jnp.broadcast_to(bias_back[head : head + 1, :], (length, length)), 0, 1, stride=1, stride_axis=0
                )
                bias_buf[m, p, :, h * length : (h + 1) * length] = jnp.where(allowed, grid, masked_score)

    x_copy = remote(x_send, xb.at[t], sem_x, across)
    dy_copy = remote(dy_send, dyb, sem_dy, across)
    x_forward = remote(xb.at[t], xb.at[t], sem_xf, sib)

    @pl.when(s == 1)
    def _():
        x_copy.wait_recv()
        x_forward.start()

    load_qkvw.wait()
    load_outw.wait()
    gain_one = gains_ref[0:1, :].astype(f32)
    gain_two = gains_ref[1:2, :].astype(f32)
    low_lanes = lax.broadcasted_iota(jnp.int32, (length, 128), 1) < 64

    def both_heads(pair_block):
        zero = jnp.zeros((), bf)
        return jnp.concatenate(
            [jnp.where(low_lanes, pair_block, zero), jnp.where(low_lanes, zero, pair_block)], axis=0
        )

    def attend(m):
        x_rows = xb[m].astype(f32)
        no1[m] = (x_rows * inverse_rms(x_rows) * gain_one).astype(bf)
        for c in range(3):
            qkvb[c, m] = nn(no1[m], qkvw_ref[c]).astype(bf)
        for p in range(pairs):
            at = slice(p * 128, (p + 1) * 128)
            scores = 0.125 * nt(qkvb[0, m, :, at], both_heads(qkvb[1, m, :, at])) + bias_buf[m, p]
            for h in range(2):
                part = scores[:, h * length : (h + 1) * length]
                terms = jnp.exp(part - jnp.max(part, axis=-1, keepdims=True))
                probs_buf[m, p, :, h * length : (h + 1) * length] = terms * (
                    1.0 / jnp.sum(terms, axis=-1, keepdims=True)
                )
            mixed[m, :, at] = nn(probs_buf[m, p].astype(bf), both_heads(qkvb[2, m, :, at])).astype(bf)

    att_copy = remote(att_send, att_recv, sem_att, sib)

    def project_other():
        att_send[...] = nn(mixed[u], outw_ref[...])
        att_copy.start()

    begin = u + s * (t - u)
    attend(begin)

    @pl.when(s == 0)
    def _():
        project_other()

    @pl.when(s == 1)
    def _():
        x_forward.wait()

    attend(1 - begin)

    @pl.when(s == 1)
    def _():
        project_other()

    part_own = nn(mixed[t], outw_ref[...])
    att_copy.wait()
    middle = xb[t].astype(f32) + part_own + att_recv[...]
    mid[...] = middle
    ntb[...] = (middle * inverse_rms(middle) * gain_two).astype(bf)
    logits_t = jnp.where(hit_t[...] > 0.0, nt(wrp[...], ntb[...]), masked_score)
    terms = jnp.exp(logits_t - jnp.max(logits_t, axis=0, keepdims=True))
    gate_t[...] = terms / jnp.sum(terms, axis=0, keepdims=True)

    arrivals = dispatch(ntb[...], disp_x, xrows, sem_dx, sem_dxf)
    load_up.wait()
    load_down.wait()
    rows_of = 2 * micro * cap

    def flat(ref, chunk):
        return ref[chunk].reshape(rows_of, ref.shape[-1])

    def front_chunk(c):
        value, slope = gelu_parts(nn(flat(xrows, chunks[c]), upv[...]))
        hidden[chunks[c]] = value.astype(bf).reshape(2, micro, cap, ffn)
        dgelu[chunks[c]] = slope.astype(bf).reshape(2, micro, cap, ffn)

    def split_sum(c, total, send, recv, base):
        for m in range(micro):
            halves[m] = total.reshape(2, micro, cap, width)[:, m]
        send[chunks[c]] = halves[u].astype(bf)
        remote(send.at[chunks[c]], recv.at[chunks[c]], base + c, sib).start()

    def hand_back(c, send, recv, base, total, landing, base_back):
        remote(send.at[chunks[c]], recv.at[chunks[c]], base + c, sib).wait()
        total[chunks[c]] = (halves[t] + recv[chunks[c]].astype(f32)).astype(bf)
        for k in (2 * c, 2 * c + 1):
            if k == 0:
                landing[0] = total[0]
            else:
                remote(total.at[k], landing.at[k], base_back + k, (s, peer[k], t)).start()

    def wait_back(total, landing, base_back):
        for k in steps:
            remote(total.at[k], landing.at[k], base_back + k, (s, peer[k], t)).wait()

    def rows_chunk(c):
        split_sum(c, nn(flat(hidden, chunks[c]), downv[...]), eo_send, eo_recv, sem_eo)

    def rows_finish(c):
        hand_back(c, eo_send, eo_recv, sem_eo, eob, eoret, sem_re)

    mine_hot = (lax.broadcasted_iota(jnp.int32, (rows_of, experts), 1) == d).astype(f32)

    def slope_chunk(c):
        slot_logits = nt(flat(xrows, chunks[c]), wr_ref[...])
        own_logit = jnp.sum(slot_logits * mine_hot, axis=-1, keepdims=True)
        other_logit = jnp.sum(slot_logits * flat(other, chunks[c]), axis=-1, keepdims=True)
        gate = 1.0 / (1.0 + jnp.exp(other_logit - own_logit))
        out_grad = (flat(dyrows, chunks[c]).astype(f32) * gate).astype(bf)
        og[chunks[c]] = out_grad.reshape(2, micro, cap, width)
        grad = (nt(out_grad, downv[...]) * flat(dgelu, chunks[c]).astype(f32)).astype(bf)
        pg[chunks[c]] = grad.reshape(2, micro, cap, ffn)

    def back_chunk(c):
        split_sum(c, nt(flat(pg, chunks[c]), upv[...]), cg_send, cg_recv, sem_cg)

    def both_chunk(c):
        front_chunk(c)
        slope_chunk(c)

    def back_finish(c):
        hand_back(c, cg_send, cg_recv, sem_cg, cgb, cgret, sem_rc)

    def hidden_of(m):
        return jnp.concatenate([hidden[k, m] for k in range(experts)], axis=0)

    def expert_rows():
        eo_send[...] = nn(hidden_of(u), downv[...]).astype(bf).reshape(eo_send.shape)
        eo_copy = remote(eo_send, eo_recv, sem_eo, sib)
        eo_copy.start()
        total = nn(hidden_of(t), downv[...])
        eo_copy.wait()
        eob[...] = (total + eo_recv[...].astype(f32).reshape(slots, width)).astype(bf).reshape(eob.shape)

    def send_back(source, landing, base):
        for k in steps:
            remote(source.at[k], landing.at[k], base + k, (s, peer[k], t)).start()
        landing[0] = source[0]

    def finish(copies):
        for copy in copies:
            copy.wait()

    def spread_gates():
        return jnp.concatenate(
            [
                jnp.broadcast_to(gate_t[e : e + 1, :], (cap, length)) * place[e * cap : (e + 1) * cap, :].astype(f32)
                for e in range(experts)
            ],
            axis=0,
        ).astype(bf)

    def layer_output():
        result = mid[...] + tn(spread_gates(), eoret[...].reshape(slots, width))
        out_own[...] = result
        return result

    def own_half():
        return pl.ds(pl.multiple_of(t * half, half), half)

    def other_half():
        return pl.ds(pl.multiple_of(u * half, half), half)

    def hand_out(rows_ref, out_ref, index):
        copy = remote(rows_ref.at[:, other_half()], out_ref.at[t], index, sib)
        copy.start()
        out_ref[t] = rows_ref[:, own_half()]
        copy.wait()

    def gather_factors():
        no_all[t, d] = no1[t]
        mix_all[d] = mixed[...]
        ring_gather(
            [
                (lambda q: no_all.at[t, q, 0 : length // 2], 1, sem_ring_no),
                (lambda q: no_all.at[t, q, length // 2 : length], -1, sem_ring_no + experts),
                (lambda q: mix_all.at[q, 0], 1, sem_ring_mix),
                (lambda q: mix_all.at[q, 1], -1, sem_ring_mix + experts),
            ]
        )
        copy = remote(no_all.at[t], no_all.at[t], sem_noall, sib)
        copy.start()
        copy.wait()

    @pl.when(s == 0)
    def _():
        stream(arrivals, front_chunk, rows_chunk, rows_finish, False)
        wait_back(eob, eoret, sem_re)
        x_send[...] = layer_output().astype(bf)
        x_copy.start()
        hand_out(out_own, secout_ref, sem_so)
        x_copy.wait_send()
        other_experts()
        gather_factors()
        dy_copy.wait_recv()
        arrivals_y = dispatch(dyb[...], disp_y, dyrows, sem_ddy, sem_ddyf)
        stream(arrivals_y, slope_chunk, back_chunk, back_finish, True)

    @pl.when(s == 1)
    def _():
        stream(arrivals, both_chunk, back_chunk, back_finish, True)
        expert_rows()

    def send_gate_grads():
        gg_send[...] = jnp.zeros_like(gg_send)
        ones = jnp.ones((8, width), bf)
        for k in range(experts):
            high, low = split_low(dyrows[k, t].astype(f32) * eob[k].astype(f32))
            gg_send[k, :, 0:cap] = nt(ones, high) + nt(ones, low)
        out = [remote(gg_send.at[k], gg_recv.at[k], sem_gg + k, (s, peer[k], t)) for k in steps]
        for copy in out:
            copy.start()
        gg_recv[0] = gg_send[0]
        return out

    gg_out = send_gate_grads()

    finish(gg_out)
    wait_back(cgb, cgret, sem_rc)

    @pl.when(s == 1)
    def _():
        send_back(eob, eoret, sem_re)

    gg_rows = []
    for e in range(experts):
        high, low = split_low(gg_recv[e][:, 0:cap])
        spot_rows = place[e * cap : (e + 1) * cap, :]
        gg_rows.append((nn(high, spot_rows) + nn(low, spot_rows))[0:1, :])
    gate_grad = jnp.concatenate(gg_rows, axis=0)
    gates = gate_t[...]
    logit_grad = (gates * (gate_grad - jnp.sum(gates * gate_grad, axis=0, keepdims=True))).astype(bf)
    router_grad = nn(tn(turn, logit_grad).astype(bf), ntb[...])
    two_grad = tn(logit_grad, wrp[...]) + tn(place[...], cgret[...].reshape(slots, width))
    dy = dyb[...].astype(f32)
    middle = mid[...]
    scale = inverse_rms(middle)
    normed = middle * scale
    gain_two_grad = jnp.sum(two_grad * normed, axis=0, keepdims=True)
    groups = width // 128
    small_send[...] = jnp.zeros_like(small_send)
    for g in range(groups):
        small_send[g, 0:experts, :] = router_grad[:, g * 128 : (g + 1) * 128]
        small_send[g, experts + 1 : experts + 2, :] = gain_two_grad[:, g * 128 : (g + 1) * 128]
    scaled = two_grad * gain_two
    middle_grad = dy + scale * (scaled - normed * jnp.mean(scaled * normed, axis=-1, keepdims=True))
    mgrad[...] = middle_grad
    ag[t] = middle_grad.astype(bf)
    ag_copy = remote(ag.at[t], ag.at[t], sem_ag, sib)
    ag_copy.start()

    agt[...] = jnp.transpose(ag[t])
    agt_rows = width // experts
    agt_out = []
    for k in reversed(steps):
        copy = remote(agt.at[block(peer[k], agt_rows)], agt_all.at[d, t], sem_agt + k, (s, peer[k], t))
        copy.start()
        agt_out.append((copy, k))
    agt_all[d, t] = agt[block(d, agt_rows), :]
    agt_own = remote(agt.at[block(d, agt_rows)], agt_all.at[d, t], sem_agtf, sib)
    agt_own.start()

    def attend_back(m, lane_of_m, fresh):
        mg[m] = nt(ag[m], outw_ref[...]).astype(bf)
        for p in range(pairs):
            at = slice(p * 128, (p + 1) * 128)
            mg_pair = mg[m, :, at]
            probs = probs_buf[m, p]
            keys2 = both_heads(qkvb[1, m, :, at])
            queries2 = both_heads(qkvb[0, m, :, at])
            mg2 = both_heads(mg_pair)
            prob_grad = nt(mg_pair, both_heads(qkvb[2, m, :, at]))
            raws = []
            key_grad = jnp.zeros((length, 128), f32)
            value_grad = jnp.zeros((length, 128), f32)
            for h in range(2):
                lane = slice(h * length, (h + 1) * length)
                part = probs[:, lane]
                step = prob_grad[:, lane]
                score_grad = part * (step - jnp.sum(part * step, axis=-1, keepdims=True))
                score_sum[2 * p + h] = score_grad if fresh else score_sum[2 * p + h] + score_grad
                raw = (0.125 * score_grad).astype(bf)
                raws.append(raw)
                key_grad = key_grad + tn(raw, queries2[h * length : (h + 1) * length])
                value_grad = value_grad + tn(part.astype(bf), mg2[h * length : (h + 1) * length])
            query_grad = nn(jnp.concatenate(raws, axis=1), keys2)
            for c, grad in enumerate((query_grad, key_grad, value_grad)):
                qkvg[c, m, :, at] = grad.astype(bf)
                qgt[c * cols + p * 128 : c * cols + (p + 1) * 128, lane_of_m] = jnp.transpose(grad).astype(bf)

    attend_back(t, slice(0, length), True)
    ag_copy.wait()
    attend_back(u, slice(length, 2 * length), False)
    qgt_rows = 3 * cols // experts
    qgt_out = []
    for k in reversed(steps):
        copy = remote(qgt.at[block(peer[k], qgt_rows)], qt_all.at[d], sem_qgt + k, (s, peer[k], t))
        copy.start()
        qgt_out.append(copy)
    qt_all[d] = qgt[block(d, qgt_rows), :]
    def project_back(m):
        total = nt(qkvg[0, m], qkvw_ref[0])
        for c in range(1, 3):
            total = total + nt(qkvg[c, m], qkvw_ref[c])
        return total

    no_send[...] = project_back(u).astype(bf)
    no_copy = remote(no_send, no_recv, sem_no, sib)
    no_copy.start()
    one_grad = project_back(t)
    no_copy.wait()
    one_grad = one_grad + no_recv[...].astype(f32)
    x_rows = xb[t].astype(f32)
    scale = inverse_rms(x_rows)
    normed = x_rows * scale
    gain_one_grad = jnp.sum(one_grad * normed, axis=0, keepdims=True)
    scaled = one_grad * gain_one
    input_grad = mgrad[...] + scale * (scaled - normed * jnp.mean(scaled * normed, axis=-1, keepdims=True))
    ig_own[...] = input_grad

    @pl.when(s == 1)
    def _():
        dy_send[...] = input_grad.astype(bf)
        dy_copy.start()

    hand_out(ig_own, ingrad_ref, sem_ig)

    sums = []
    for head in range(2 * pairs):
        high, low = split_low(score_sum[head])
        turned = pltpu.roll(nn(high, mirror) + nn(low, mirror), 0, 1, stride=1, stride_axis=0)
        sums.append(jnp.sum(turned, axis=0, keepdims=True))
    high, low = split_low(jnp.concatenate(sums, axis=0))
    small_send[groups, 0 : 2 * pairs, 0 : lay.buckets] = nt(high, dist_rows) + nt(low, dist_rows)
    for g in range(groups):
        small_send[g, experts : experts + 1, :] = gain_one_grad[:, g * 128 : (g + 1) * 128]
    small_out = [remote(small_send.at[peer[k]], small_in.at[k], sem_small + k, (s, peer[k], t)) for k in steps]
    for copy in small_out:
        copy.start()
    small_in[0] = small_send[d]

    wide = lay.wide
    every = micro * slots
    for n in range(ffn // wide):
        at = slice(n * wide, (n + 1) * wide)
        guv[:, at] = tn(xrows[...].reshape(every, width), pg[:, :, :, at].reshape(every, wide)).astype(bf)
        pltpu.make_async_copy(guv.at[:, at], gup_ref.at[:, at], gsem.at[n]).start()
        gdv[at, :] = tn(hidden[:, :, :, at].reshape(every, wide), og[...].reshape(every, width)).astype(bf)
        pltpu.make_async_copy(gdv.at[at, :], gdown_ref.at[at, :], gsem.at[ffn // wide + n]).start()

    @pl.when(s == 1)
    def _():
        gather_factors()

    passed = [agt_own]
    for copy, k in agt_out:
        copy.wait_recv()
        forward = remote(agt_all.at[peer[k], t], agt_all.at[peer[k], t], sem_agtf + k, sib)
        forward.start()
        passed.append(forward)
    for copy in passed:
        copy.wait()
    for copy, _ in agt_out:
        copy.wait_send()
    total = jnp.zeros((agt_rows, cols), f32)
    for q in range(experts):
        for m in range(micro):
            total = total + nn(agt_all[q, m], mix_all[q, m])
    qkv_rows = 3 * cols // experts
    shared_ref[d, qkv_rows:, 0:cols] = total[0 : agt_rows // 2].astype(bf)
    shared_ref[d, qkv_rows:, cols:] = total[agt_rows // 2 :].astype(bf)
    def qkv_slice(q):
        return nn(qt_all[q], jnp.concatenate([no_all[t, q], no_all[u, q]], axis=0))

    total = qkv_slice(d)
    for copy, k in zip(qgt_out, reversed(steps)):
        copy.wait_recv()
        total = total + qkv_slice(peer[k])
    for copy in qgt_out:
        copy.wait_send()
    shared_ref[d, 0:qkv_rows, :] = total.astype(bf)
    finish(small_out)
    small_total = small_in[0]
    for k in steps:
        small_total = small_total + small_in[k]
    small_all[d] = small_total
    small_back = [remote(small_all.at[d], small_all.at[d], sem_back + k, (s, peer[k], t)) for k in steps]
    for copy in small_back:
        copy.start()

    sums_copy = remote(small_all, small_sib, sem_sums, sib)

    def pass_sums():
        finish(small_back)
        sums_copy.start()

    share = shared_ref.shape[1] // 6
    ring_gather(
        [
            (
                lambda q, c=c: shared_ref.at[q, c * share : (c + 1) * share],
                1 if c % 2 == 0 else -1,
                sem_ring_out + c * experts,
            )
            for c in range(6)
        ],
        pass_sums,
    )
    sums_copy.wait()
    for g in range(groups):
        lanes = slice(g * 128, (g + 1) * 128)
        grouter_ref[:, lanes] = small_all[g, 0:experts, :] + small_sib[g, 0:experts, :]
        ggain_ref[:, lanes] = small_all[g, experts : experts + 2, :] + small_sib[g, experts : experts + 2, :]
    gbias_ref[...] = small_all[groups, 0 : 2 * pairs, :]
    @pl.when(s == 1)
    def _():
        dy_copy.wait_send()
        wait_back(eob, eoret, sem_re)
        layer_output()
        hand_out(out_own, secout_ref, sem_so)

    for copy in sent:
        copy.wait_send()
    for n in range(ffn // wide):
        at = slice(n * wide, (n + 1) * wide)
        pltpu.make_async_copy(guv.at[:, at], gup_ref.at[:, at], gsem.at[n]).wait()
        pltpu.make_async_copy(gdv.at[at, :], gdown_ref.at[at, :], gsem.at[ffn // wide + n]).wait()


def widen_kernel(
    sec_ref, ing_ref, gain_ref, shared_ref, bias_ref, router_ref, up_ref, down_ref,
    sec_out, ing_out, gain_out, bias_out, router_out, qkv_out, out_out, up_out, down_out,
    up_low, up_wide, down_low, down_wide, shared_low, qkv_wide, out_wide, bias_low, bias_wide,
    sec_low, ing_low, gain_low, router_low, in_sem, out_sem,
):
    f32 = jnp.float32
    parts = 3
    experts, shared_rows, width = shared_ref.shape
    cols = out_wide.shape[0]
    qkv_rows = 3 * cols // experts
    low = ((up_ref, up_low), (down_ref, down_low))
    wide = ((up_low, up_wide, up_out), (down_low, down_wide, down_out))
    stores = []

    def store(src, dst):
        copy = pltpu.make_async_copy(src, dst, out_sem.at[len(stores)])
        copy.start()
        stores.append(copy)

    def rows(ref, n):
        size = ref.shape[0] // parts
        return pl.ds(n * size, size)

    load_shared = pltpu.make_async_copy(shared_ref, shared_low, in_sem.at[2 * parts])
    load_bias = pltpu.make_async_copy(bias_ref, bias_low, in_sem.at[2 * parts + 1])
    loads = [
        pltpu.make_async_copy(src.at[rows(src, n)], dst.at[rows(dst, n)], in_sem.at[i * parts + n])
        for i, (src, dst) in enumerate(low)
        for n in range(parts)
    ]
    loads[0].start()
    load_shared.start()
    for copy in loads[1:]:
        copy.start()
    load_bias.start()
    through = ((sec_ref, sec_low, sec_out), (ing_ref, ing_low, ing_out), (gain_ref, gain_low, gain_out), (router_ref, router_low, router_out))
    passing = [
        pltpu.make_async_copy(src, mid, in_sem.at[2 * parts + 2 + i]) for i, (src, mid, _) in enumerate(through)
    ]
    for copy in passing:
        copy.start()

    def widen(i, n):
        loads[i * parts + n].wait()
        src, dst, out = wide[i]
        dst[rows(dst, n), :] = src[rows(src, n), :].astype(f32)
        store(dst.at[rows(dst, n)], out.at[rows(out, n)])

    def turn_qkv(c):
        block = shared_low[:, 0:qkv_rows, :].reshape(3 * cols, width)[c * cols : (c + 1) * cols]
        qkv_wide[c] = jnp.transpose(block.astype(f32))
        store(qkv_wide.at[c], qkv_out.at[c])

    widen(0, 0)
    load_shared.wait()
    turn_qkv(0)
    widen(0, 1)
    widen(0, 2)
    turn_qkv(1)
    widen(1, 0)
    widen(1, 1)
    turn_qkv(2)
    out_block = jnp.concatenate(
        [
            shared_low[e, qkv_rows:, h * cols : (h + 1) * cols].astype(f32)
            for e in range(experts)
            for h in range(2)
        ],
        axis=0,
    )
    out_wide[...] = jnp.transpose(out_block)
    store(out_wide, out_out)
    widen(1, 2)
    for copy, (_, mid, out) in zip(passing, through):
        copy.wait()
        store(mid, out)
    load_bias.wait()
    for h in range(bias_wide.shape[0]):
        bias_wide[h] = bias_low[h : h + 1, 0 : bias_wide.shape[2]]
    store(bias_wide, bias_out)
    for copy in stores:
        copy.wait()


def fused_local(
    tokens,
    cotangent,
    segments,
    pad_mask,
    routes,
    dist_bucket,
    norm_gains,
    qkv_weight,
    out_weight,
    rel_bias,
    router_weight,
    expert_up,
    expert_down,
):
    micro, _, length, width = tokens.shape
    experts = router_weight.shape[2]
    cap = max(2, 3 * length // experts)
    cols = out_weight.shape[1]
    heads = rel_bias.shape[2]
    ffn = expert_up.shape[3]
    slots = experts * cap
    pairs = cols // 128
    lay = Layout()
    lay.experts = experts
    lay.cap = cap
    lay.buckets = rel_bias.shape[1]
    lay.wide = min(ffn, 256)
    lay.sems = 25 * experts + 10
    bf = jnp.bfloat16
    f32 = jnp.float32
    vm = pltpu.VMEM
    shape = jax.ShapeDtypeStruct
    dma = pltpu.SemaphoreType.DMA
    scratch = [
        vm((width, ffn), bf),
        vm((ffn, width), bf),
        vm((3, width, cols), bf),
        vm((cols, width), bf),
        vm((micro, length, width), bf),
        vm((length, width), bf),
        vm((experts, micro, 2, length), jnp.int32),
        vm((slots, length), bf),
        vm((micro, pairs, length, 2 * length), f32),
        vm((micro, pairs, length, 2 * length), f32),
        vm((micro, length, width), bf),
        vm((3, micro, length, cols), bf),
        vm((micro, length, cols), bf),
        vm((length, width), f32),
        vm((length, width), f32),
        vm((length, width), f32),
        vm((length, width), bf),
        vm((experts, length), f32),
        vm((experts, length), f32),
        vm((experts, width), bf),
        vm((2 * pairs, length, length), f32),
        vm((experts, cap, width), bf),
        vm((experts, micro, cap, width), bf),
        vm((experts, cap, width), bf),
        vm((experts, micro, cap, width), bf),
        vm((experts, micro, cap, ffn), bf),
        vm((experts, micro, cap, ffn), bf),
        vm((micro, 2, cap, width), f32),
        vm((experts, cap, width), bf),
        vm((experts, cap, width), bf),
        vm((experts, cap, width), bf),
        vm((experts, cap, width), bf),
        vm((length, width), f32),
        vm((length, width), bf),
        vm((experts, micro, cap, experts), f32),
        vm((experts, micro, cap, width), bf),
        vm((experts, 8, 128), f32),
        vm((experts, 8, 128), f32),
        vm((experts, micro, cap, ffn), bf),
        vm((experts, cap, width), bf),
        vm((experts, cap, width), bf),
        vm((experts, cap, width), bf),
        vm((experts, cap, width), bf),
        vm((length, width), f32),
        vm((micro, length, width), bf),
        vm((micro, length, cols), bf),
        vm((3, micro, length, cols), bf),
        vm((length, width), bf),
        vm((length, width), bf),
        vm((length, width), f32),
        vm((length, width), bf),
        vm((width, ffn), bf),
        vm((ffn, width), bf),
        vm((micro, experts, length, width), bf),
        vm((experts, micro, length, cols), bf),
        vm((3 * cols, micro * length), bf),
        vm((experts, 3 * cols // experts, micro * length), bf),
        vm((width, length), bf),
        vm((experts, micro, width // experts, length), bf),
        vm((experts, 2 * experts, 128), f32),
        vm((experts, 2 * experts, 128), f32),
        vm((experts, 2 * experts, 128), f32),
        vm((experts, 2 * experts, 128), f32),
        dma((5,)),
        dma((2 * (ffn // lay.wide),)),
        dma((lay.sems,)),
        dma((lay.sems,)),
    ]
    whole = pl.BlockSpec(memory_space=pltpu.VMEM)
    anywhere = pl.BlockSpec(memory_space=pl.ANY)
    shared_rows = 3 * cols // experts + width // experts // 2
    out_shape = (
        shape((micro, length, width // 2), f32),
        shape((micro, length, width // 2), f32),
        shape((2, width), f32),
        shape((experts, shared_rows, width), bf),
        shape((heads, 128), f32),
        shape((experts, width), f32),
        shape((width, ffn), bf),
        shape((ffn, width), bf),
    )
    results = pl.pallas_call(
        partial(layer_kernel, lay),
        out_shape=out_shape,
        in_specs=[anywhere] * 2 + [whole] * 5 + [anywhere] * 2 + [whole] * 2 + [anywhere] * 2,
        out_specs=[whole] * 6 + [anywhere] * 2,
        scratch_shapes=scratch,
        name="two_sections",
        compiler_params=pltpu.CompilerParams(
            collective_id=0, has_side_effects=True, vmem_limit_bytes=60 * 1024 * 1024
        ),
    )(
        tokens[:, 0],
        cotangent[:, 0],
        segments[:, 0],
        pad_mask[:, 0],
        routes[:, 0].transpose(0, 2, 1),
        dist_bucket[None],
        norm_gains[0],
        qkv_weight[0].transpose(1, 0, 2),
        out_weight[0],
        rel_bias[0].T,
        router_weight[0].T,
        expert_up[0, 0],
        expert_down[0, 0],
    )
    section_out, input_grads, gains, bias, router, qkv, out, up, down = pl.pallas_call(
        widen_kernel,
        out_shape=(
            out_shape[0],
            out_shape[1],
            out_shape[2],
            shape((heads, 1, lay.buckets), f32),
            out_shape[5],
            shape((3, width, cols), f32),
            shape((cols, width), f32),
            shape((width, ffn), f32),
            shape((ffn, width), f32),
        ),
        in_specs=[anywhere] * 8,
        out_specs=[anywhere] * 9,
        scratch_shapes=[
            vm((width, ffn), bf),
            vm((width, ffn), f32),
            vm((ffn, width), bf),
            vm((ffn, width), f32),
            vm((experts, shared_rows, width), bf),
            vm((3, width, cols), f32),
            vm((cols, width), f32),
            vm((heads, 128), f32),
            vm((heads, 1, lay.buckets), f32),
            vm((micro, length, width // 2), f32),
            vm((micro, length, width // 2), f32),
            vm((2, width), f32),
            vm((experts, width), f32),
            dma((12,)),
            dma((15,)),
        ],
        name="widen",
        compiler_params=pltpu.CompilerParams(vmem_limit_bytes=60 * 1024 * 1024),
    )(*results)
    return (
        section_out[None, :, None],
        input_grads[None, :, None],
        gains[None],
        qkv.transpose(1, 0, 2)[None],
        out[None],
        bias.transpose(1, 2, 0),
        router.T[None],
        up[None, None],
        down[None, None],
    )


def fits_kernel(mesh):
    return mesh.shape["section"] == 2 and mesh.shape["tensor"] == 2 and mesh.shape["dp"] == 8


def solution(mesh):
    in_specs = (
        P(None, "dp", None, None),
        P(None, "dp", None, None),
        P(None, "dp", None),
        P(None, "dp", None),
        P(None, "dp", None, None),
        P(),
        P("section", None, None),
        P("section", None, None, "tensor"),
        P("section", "tensor", None),
        P("section", None, "tensor"),
        P("section", None, None),
        P("section", "dp", None, "tensor"),
        P("section", "dp", "tensor", None),
    )
    out_specs = (
        P("section", None, "dp", None, "tensor"),
        P("section", None, "dp", None, "tensor"),
        P("section", None, None),
        P("section", None, None, "tensor"),
        P("section", "tensor", None),
        P("section", None, "tensor"),
        P("section", None, None),
        P("section", "dp", None, "tensor"),
        P("section", "dp", "tensor", None),
    )
    body = fused_local if fits_kernel(mesh) else local
    return jax.shard_map(body, mesh=mesh, in_specs=in_specs, out_specs=out_specs, check_vma=False)
```

```python
from functools import partial

import jax
import jax.numpy as jnp
from jax import lax
from jax.experimental import pallas as pl
from jax.experimental.pallas import tpu as pltpu
from jax.sharding import PartitionSpec as P

norm_eps = 1e-06
masked_score = -1e30
highest = lax.Precision.HIGHEST


def shifted(block, axis, distance):
    devices = range(lax.axis_size(axis))
    route = [(i - distance, i) for i in devices if i - distance in devices]
    return lax.ppermute(block, axis, route)


def normalize(values, gain_row):
    scale_inv = lax.rsqrt(jnp.mean(values * values, axis=-1, keepdims=True) + norm_eps)
    return values * scale_inv * gain_row


def normalize_back(values, gain_row, upstream):
    scale_inv = lax.rsqrt(jnp.mean(values * values, axis=-1, keepdims=True) + norm_eps)
    normed = values * scale_inv
    gain_grad = jnp.sum(upstream * normed, axis=0)
    scaled = upstream * gain_row
    input_grad = scale_inv * (scaled - normed * jnp.mean(scaled * normed, axis=-1, keepdims=True))
    return (input_grad, gain_grad)


def send_rows(rows):
    return lax.all_to_all(rows, "dp", split_axis=0, concat_axis=0, tiled=True)


def sum_slots(partial_rows):
    return lax.psum(partial_rows, "tensor")


def score_context(segment_row, pad_row, dist_bucket, bucket_count):
    length = segment_row.shape[0]
    places = jnp.arange(length, dtype=jnp.int32)
    offsets = jnp.clip(places[:, None] - places[None, :], 0, length - 1)
    bucket_grid = jnp.take(dist_bucket, offsets)
    bucket_onehot = (
        bucket_grid[:, :, None] == jnp.arange(bucket_count, dtype=jnp.int32)[None, None, :]
    ).astype(jnp.float32)
    allowed = (places[None, :] <= places[:, None]) & (segment_row[:, None] == segment_row[None, :])
    allowed = allowed & ((pad_row[None, :] == 1) | (places[None, :] == places[:, None]))
    return (bucket_onehot, allowed)


def attention_front(inputs, context, weights):
    segment_row, pad_row, route_rows, dist_bucket = context
    gain_pair, qkv_weight, out_weight, bias_table, router_weight, upper_weight, lower_weight = (
        weights
    )
    length = inputs.shape[0]
    head_count = bias_table.shape[1]
    bucket_onehot, allowed = score_context(segment_row, pad_row, dist_bucket, bias_table.shape[0])
    normed_one = normalize(inputs, gain_pair[0]).astype(jnp.bfloat16)
    qkv_rows = jnp.einsum(
        "ld,dch->lch", normed_one, qkv_weight, preferred_element_type=jnp.float32
    ).astype(jnp.bfloat16)
    head_dim = qkv_rows.shape[2] // head_count
    queries = qkv_rows[:, 0].reshape(length, head_count, head_dim)
    keys_in = qkv_rows[:, 1].reshape(length, head_count, head_dim)
    values_in = qkv_rows[:, 2].reshape(length, head_count, head_dim)
    raw_scores = jnp.einsum("qhd,khd->hqk", queries, keys_in, preferred_element_type=jnp.float32)
    bias_grid = jnp.einsum(
        "qkb,bh->hqk", bucket_onehot, bias_table.astype(jnp.float32), precision=highest
    )
    logits = jnp.where(allowed[None], 0.125 * raw_scores + bias_grid, masked_score)
    exp_terms = jnp.exp(logits - jnp.max(logits, axis=-1, keepdims=True))
    attn_probs = exp_terms / jnp.sum(exp_terms, axis=-1, keepdims=True)
    mixed_rows = jnp.einsum(
        "hqk,khd->qhd",
        attn_probs.astype(jnp.bfloat16),
        values_in,
        preferred_element_type=jnp.float32,
    )
    mixed_rows = mixed_rows.reshape(length, -1).astype(jnp.bfloat16)
    return (normed_one, queries, keys_in, values_in, attn_probs, mixed_rows, bucket_onehot)


def slot_tables(route_rows, experts, capacity):
    flat_routes = route_rows.reshape(-1)
    route_hits = (flat_routes[:, None] == jnp.arange(experts, dtype=jnp.int32)[None, :]).astype(
        jnp.int32
    )
    earlier = jnp.cumsum(route_hits, axis=0) - route_hits
    position = jnp.sum(earlier * route_hits, axis=1)
    target = flat_routes * capacity + position
    slot_hits = (
        jnp.arange(experts * capacity, dtype=jnp.int32)[:, None] == target[None, :]
    ).astype(jnp.int32)
    source = jnp.sum(slot_hits * jnp.arange(target.shape[0], dtype=jnp.int32)[None, :], axis=1)
    filled = jnp.sum(slot_hits, axis=1) > 0
    return (target, source, filled, route_hits)


def route_gates(normed_two, router_weight, route_hits):
    length = normed_two.shape[0]
    logits = jnp.dot(normed_two, router_weight, preferred_element_type=jnp.float32)
    route_onehot = route_hits.reshape(length, 2, -1).astype(jnp.float32)
    chosen = jnp.einsum("le,lre->lr", logits, route_onehot, precision=highest)
    return (jax.nn.softmax(chosen, axis=-1), route_onehot)


def gather_back(back_slots, target, length):
    flat_slots = back_slots.reshape(-1, back_slots.shape[-1])
    return jnp.take(flat_slots, target, axis=0).reshape(length, 2, -1)


def forward_rest(inputs, front, context, weights):
    segment_row, pad_row, route_rows, dist_bucket = context
    gain_pair, qkv_weight, out_weight, bias_table, router_weight, upper_weight, lower_weight = (
        weights
    )
    mixed_rows = front[5]
    length, model_width = inputs.shape
    experts = router_weight.shape[1]
    capacity = max(2, 3 * length // experts)
    local_experts = upper_weight.shape[0]
    attn_out = lax.psum(
        jnp.dot(mixed_rows, out_weight, preferred_element_type=jnp.float32), "tensor"
    )
    middle = inputs + attn_out
    normed_two = normalize(middle, gain_pair[1]).astype(jnp.bfloat16)
    target, source, filled, route_hits = slot_tables(route_rows, experts, capacity)
    outgoing = jnp.where(
        filled[:, None], jnp.take(normed_two, source // 2, axis=0), jnp.zeros((), jnp.bfloat16)
    )
    outgoing = outgoing.reshape(experts, capacity, model_width)
    arrived = send_rows(outgoing)
    grouped = arrived.reshape(-1, local_experts, capacity, model_width)
    pre_act = jnp.einsum(
        "secd,edf->secf", grouped, upper_weight, preferred_element_type=jnp.float32
    )
    hidden = jax.nn.gelu(pre_act, approximate=False).astype(jnp.bfloat16)
    partial_out = jnp.einsum(
        "secf,efd->secd", hidden, lower_weight, preferred_element_type=jnp.float32
    )
    summed = sum_slots(partial_out)
    returned = summed.astype(jnp.bfloat16).reshape(arrived.shape[0], arrived.shape[1], -1)
    back_slots = send_rows(returned)
    gate_probs, route_onehot = route_gates(normed_two, router_weight, route_hits)
    back_rows = gather_back(back_slots, target, length)
    output = middle + jnp.sum(gate_probs[:, :, None] * back_rows.astype(jnp.float32), axis=1)
    return (output, (attn_out, arrived, back_slots, pre_act))


def backward_layer(inputs, upstream, context, weights, front, saved_state):
    segment_row, pad_row, route_rows, dist_bucket = context
    gain_pair, qkv_weight, out_weight, bias_table, router_weight, upper_weight, lower_weight = (
        weights
    )
    normed_one, queries, keys_in, values_in, attn_probs, mixed_rows, bucket_onehot = front
    attn_out, arrived_rows, back_slots, pre_rows = saved_state
    length, model_width = inputs.shape
    head_count = bias_table.shape[1]
    head_cols = qkv_weight.shape[2]
    experts = router_weight.shape[1]
    capacity = max(2, 3 * length // experts)
    local_experts = upper_weight.shape[0]
    middle = inputs + attn_out
    normed_two = normalize(middle, gain_pair[1]).astype(jnp.bfloat16)
    target, source, filled, route_hits = slot_tables(route_rows, experts, capacity)
    gate_probs, route_onehot = route_gates(normed_two, router_weight, route_hits)
    back_rows = gather_back(back_slots, target, length)
    gate_grad = jnp.sum(upstream[:, None, :] * back_rows.astype(jnp.float32), axis=-1)
    chosen_grad = gate_probs * (gate_grad - jnp.sum(gate_probs * gate_grad, axis=-1, keepdims=True))
    logit_grad = jnp.einsum("lr,lre->le", chosen_grad, route_onehot, precision=highest).astype(
        jnp.bfloat16
    )
    router_grad = jnp.dot(normed_two.T, logit_grad, preferred_element_type=jnp.float32)
    normed_two_grad = jnp.dot(logit_grad, router_weight.T, preferred_element_type=jnp.float32)
    route_grads = (
        (gate_probs[:, :, None] * upstream[:, None, :])
        .reshape(2 * length, model_width)
        .astype(jnp.bfloat16)
    )
    slot_grads = jnp.where(
        filled[:, None], jnp.take(route_grads, source, axis=0), jnp.zeros((), jnp.bfloat16)
    )
    arrived_grads = send_rows(slot_grads.reshape(experts, capacity, model_width))
    grouped = arrived_rows.reshape(-1, local_experts, capacity, model_width)
    grouped_grads = arrived_grads.reshape(-1, local_experts, capacity, model_width)
    hidden, gelu_pull = jax.vjp(partial(jax.nn.gelu, approximate=False), pre_rows)
    hidden_low = hidden.astype(jnp.bfloat16)
    down_grad = jnp.einsum(
        "secf,secd->efd", hidden_low, grouped_grads, preferred_element_type=jnp.float32
    )
    hidden_grad = jnp.einsum(
        "secd,efd->secf", grouped_grads, lower_weight, preferred_element_type=jnp.float32
    )
    pre_grad = gelu_pull(hidden_grad)[0].astype(jnp.bfloat16)
    up_grad = jnp.einsum("secd,secf->edf", grouped, pre_grad, preferred_element_type=jnp.float32)
    rows_grad = sum_slots(
        jnp.einsum("secf,edf->secd", pre_grad, upper_weight, preferred_element_type=jnp.float32)
    )
    sent_back = send_rows(
        rows_grad.astype(jnp.bfloat16).reshape(arrived_rows.shape[0], arrived_rows.shape[1], -1)
    )
    copy_grads = gather_back(sent_back, target, length).astype(jnp.float32)
    normed_two_grad = normed_two_grad + jnp.sum(copy_grads, axis=1)
    middle_part, gain_two = normalize_back(middle, gain_pair[1], normed_two_grad)
    middle_grad = upstream + middle_part
    attn_grad = middle_grad.astype(jnp.bfloat16)
    out_grad = jnp.dot(mixed_rows.T, attn_grad, preferred_element_type=jnp.float32)
    mixed_grad = jnp.dot(attn_grad, out_weight.T, preferred_element_type=jnp.float32).astype(
        jnp.bfloat16
    )
    mixed_grad = mixed_grad.reshape(length, head_count, -1)
    prob_grad = jnp.einsum(
        "qhd,khd->hqk", mixed_grad, values_in, preferred_element_type=jnp.float32
    )
    value_grad = jnp.einsum(
        "hqk,qhd->khd",
        attn_probs.astype(jnp.bfloat16),
        mixed_grad,
        preferred_element_type=jnp.float32,
    )
    score_grad = attn_probs * (prob_grad - jnp.sum(prob_grad * attn_probs, axis=-1, keepdims=True))
    table_grad = jnp.einsum("hqk,qkb->bh", score_grad, bucket_onehot, precision=highest)
    raw_grad = (0.125 * score_grad).astype(jnp.bfloat16)
    query_grad = jnp.einsum("hqk,khd->qhd", raw_grad, keys_in, preferred_element_type=jnp.float32)
    key_grad = jnp.einsum("hqk,qhd->khd", raw_grad, queries, preferred_element_type=jnp.float32)
    qkv_grad = (
        jnp.stack([query_grad, key_grad, value_grad], axis=1)
        .reshape(length, 3, head_cols)
        .astype(jnp.bfloat16)
    )
    qkv_weight_grad = jnp.einsum(
        "ld,lch->dch", normed_one, qkv_grad, preferred_element_type=jnp.float32
    )
    normed_one_grad = lax.psum(
        jnp.einsum("lch,dch->ld", qkv_grad, qkv_weight, preferred_element_type=jnp.float32),
        "tensor",
    )
    input_part, gain_one = normalize_back(inputs, gain_pair[0], normed_one_grad)
    input_grad = middle_grad + input_part
    gain_grads = jnp.stack([gain_one, gain_two])
    return (
        input_grad,
        (gain_grads, qkv_weight_grad, out_grad, table_grad, router_grad, up_grad, down_grad),
    )


def pick_context(segments, pad_mask, routes, dist_bucket, micro_slot):
    segment_row = lax.dynamic_index_in_dim(segments[:, 0], micro_slot, 0, False)
    pad_row = lax.dynamic_index_in_dim(pad_mask[:, 0], micro_slot, 0, False)
    route_rows = lax.dynamic_index_in_dim(routes[:, 0], micro_slot, 0, False)
    return (segment_row, pad_row, route_rows, dist_bucket)


def place_row(store_all, new_value, micro_slot, is_valid):
    current = lax.dynamic_index_in_dim(store_all, micro_slot, 0, False)
    return lax.dynamic_update_index_in_dim(
        store_all, jnp.where(is_valid, new_value, current), micro_slot, 0
    )


def pick_row(store_all, micro_slot):
    return lax.dynamic_index_in_dim(store_all, micro_slot, 0, False)


def mask_grad(grad_value, is_valid):
    return jnp.where(is_valid, grad_value, jnp.zeros((), grad_value.dtype))


def tensor_half(full_rows, tensor_id, half_width):
    return lax.dynamic_slice_in_dim(full_rows, tensor_id * half_width, half_width, 2)[None, :, None]


def local(
    tokens,
    cotangent,
    segments,
    pad_mask,
    routes,
    dist_bucket,
    norm_gains,
    qkv_weight,
    out_weight,
    rel_bias,
    router_weight,
    expert_up,
    expert_down,
):
    section_id = lax.axis_index("section")
    section_count = lax.axis_size("section")
    micro_count = tokens.shape[0]
    length = tokens.shape[2]
    model_width = tokens.shape[3]
    tick_count = micro_count + section_count - 1
    weights = (
        norm_gains[0].astype(jnp.float32),
        qkv_weight[0],
        out_weight[0],
        rel_bias[0],
        router_weight[0],
        expert_up[0],
        expert_down[0],
    )
    empty_rows = jnp.zeros((length, model_width), jnp.bfloat16)
    arriving = empty_rows
    kept_inputs = jnp.zeros((micro_count, length, model_width), jnp.bfloat16)
    section_out = jnp.zeros((micro_count, length, model_width), jnp.float32)
    for tick_index in range(tick_count):
        micro_index = tick_index - section_id
        is_valid = (micro_index >= 0) & (micro_index < micro_count)
        micro_slot = jnp.clip(micro_index, 0, micro_count - 1)
        own_rows = tokens[tick_index, 0] if tick_index < micro_count else empty_rows
        layer_in = jnp.where(section_id == 0, own_rows, arriving)
        context = pick_context(segments, pad_mask, routes, dist_bucket, micro_slot)
        inputs = layer_in.astype(jnp.float32)
        front = attention_front(inputs, context, weights)
        result, saved_state = forward_rest(inputs, front, context, weights)
        section_out = place_row(section_out, result, micro_slot, is_valid)
        kept_inputs = place_row(kept_inputs, layer_in, micro_slot, is_valid)
        arriving = shifted(result.astype(jnp.bfloat16), "section", 1)
    returning = empty_rows
    input_store = jnp.zeros((micro_count, length, model_width), jnp.float32)
    totals = None
    for tick_index in range(tick_count):
        micro_index = tick_index - (section_count - 1 - section_id)
        is_valid = (micro_index >= 0) & (micro_index < micro_count)
        micro_slot = jnp.clip(micro_index, 0, micro_count - 1)
        own_rows = cotangent[tick_index, 0] if tick_index < micro_count else empty_rows
        upstream = jnp.where(section_id == section_count - 1, own_rows, returning).astype(
            jnp.float32
        )
        inputs = pick_row(kept_inputs, micro_slot).astype(jnp.float32)
        context = pick_context(segments, pad_mask, routes, dist_bucket, micro_slot)
        front = attention_front(inputs, context, weights)
        saved_state = forward_rest(inputs, front, context, weights)[1]
        input_grad, grad_set = backward_layer(
            inputs, upstream, context, weights, front, saved_state
        )
        input_store = place_row(input_store, input_grad, micro_slot, is_valid)
        grad_set = jax.tree.map(partial(mask_grad, is_valid=is_valid), grad_set)
        totals = grad_set if totals is None else jax.tree.map(jnp.add, totals, grad_set)
        returning = shifted(input_grad.astype(jnp.bfloat16), "section", -1)
    shared = lax.psum((totals[0], totals[1], totals[2], totals[3], totals[4]), "dp")
    tensor_id = lax.axis_index("tensor")
    half_width = model_width // lax.axis_size("tensor")
    return (
        tensor_half(section_out, tensor_id, half_width),
        tensor_half(input_store, tensor_id, half_width),
        shared[0][None],
        shared[1][None],
        shared[2][None],
        shared[3][None],
        shared[4][None],
        totals[5][None],
        totals[6][None],
    )


def gelu_parts(values):
    share = 0.5 + 0.5 * lax.erf(values * 0.7071067811865476)
    return (values * share, share + values * (0.3989422804014327 * jnp.exp(-0.5 * values * values)))


def nn(left, right):
    return lax.dot_general(left, right, (((1,), (0,)), ((), ())), preferred_element_type=jnp.float32)


def nt(left, right):
    return lax.dot_general(left, right, (((1,), (1,)), ((), ())), preferred_element_type=jnp.float32)


def tn(left, right):
    return lax.dot_general(left, right, (((0,), (0,)), ((), ())), preferred_element_type=jnp.float32)


def split_low(values):
    high = values.astype(jnp.bfloat16)
    return (high, (values - high.astype(jnp.float32)).astype(jnp.bfloat16))


def inverse_rms(values):
    return lax.rsqrt(jnp.mean(values * values, axis=-1, keepdims=True) + norm_eps)


class Layout:
    pass


def layer_kernel(lay, *refs):
    (
        tok_ref, cot_ref, seg_ref, pad_ref, routes_ref, dist_ref, gains_ref, qkvw_hbm, outw_hbm, relb_ref, wr_ref,
        up_ref, down_ref,
        secout_hbm, ingrad_hbm, ggain_ref, shared_hbm, gbias_ref, grouter_ref, gup_ref, gdown_ref,
        upv, downv, qkvw_ref, outw_ref, xb, dyb, rr, place, bias_buf, probs_buf, no1, qkvb, mixed, att_send, att_recv, mid, ntb,
        gate_t, hit_t, wrp, score_sum, disp_x, xrows, disp_y, dyrows, hidden, dgelu, halves, eo_send, eo_recv, eob, eoret, out_own,
        other, og, gg_part, gg_other, gg_send, gg_recv, pg, cg_send, cg_recv, cgb, cgret, mgrad, ag, mg, qkvg,
        no_send, no_recv, ig_own, dy_send, guv, gdv,
        no_all, mix_all, qgt, qt_all, agt, agt_all, small_send, small_in, small_all, small_sib,
        secout_ref, ingrad_ref, shared_ref, x_send, rs_buf, rs_in, help_buf, relay_buf,
        wsem, gsem, osem, ss, rs,
    ) = refs
    bf = jnp.bfloat16
    f32 = jnp.float32
    micro, length, width = tok_ref.shape
    experts = lay.experts
    cap = lay.cap
    cols = outw_ref.shape[0]
    pairs = cols // 128
    ffn = up_ref.shape[1]
    slots = experts * cap
    half = width // 2
    s = lax.axis_index("section")
    d = lax.axis_index("dp")
    t = lax.axis_index("tensor")
    u = 1 - t
    sib = (s, d, u)
    across = (1 - s, d, t)
    bits = [lax.rem(d // bit, 2) for bit in (1, 2, 4)]

    def partner(flip):
        index = d
        for place, bit in enumerate((1, 2, 4)):
            index = index + (flip // bit) % 2 * (bit - 2 * bit * bits[place])
        return index

    peer = [partner(flip) for flip in (0, 4, 1, 6, 2, 5, 3, 7)]
    steps = range(1, experts)
    relayed = (5, 7)
    chunks = range(experts // 2)

    def pair(c):
        return pl.ds(2 * c, 2)

    def partner_at(k):
        c = k // 2
        return partner(c + (k % 2) * (4 + 2 * (c % 2) + c // 2 - c))


    def remote(src, dst, index, device):
        return pltpu.make_async_remote_copy(
            src_ref=src,
            dst_ref=dst,
            send_sem=ss.at[index],
            recv_sem=rs.at[index],
            device_id=device,
            device_id_type=pl.DeviceIdType.MESH,
        )

    counter = [0]

    def take(amount):
        counter[0] += amount
        return counter[0] - amount

    sent = []

    def fire(copy):
        copy.start()
        sent.append(copy)

    sem_routes = take(experts)
    sem_x = take(1)
    sem_relay = take(2 * len(relayed))
    sem_pass = take(2 * len(relayed))
    sem_xf = take(1)
    sem_dy = take(1)
    sem_att = take(1)
    sem_eo = take(experts)
    sem_cg = take(experts)
    sem_ag = take(1)
    sem_no = take(1)
    sem_so = take(1)
    sem_ig = take(1)
    sem_dx = take(experts)
    sem_dxf = take(experts)
    sem_ddy = take(experts)
    sem_ddyf = take(experts)
    sem_re = take(experts)
    sem_rc = take(experts)
    sem_gg = take(experts)
    sem_gg_core = take(len(chunks))
    sem_help = take(2)
    sem_spread = take(2 * experts)
    sem_qgt = take(experts)
    sem_small = take(experts)
    sem_back = take(experts)
    sem_sums = take(1)
    sem_noall = take(1)
    sem_section_zero = take(6 * experts)
    sem_ring_no = sem_section_zero
    sem_ring_mix = sem_section_zero + 2 * experts
    sem_agt = sem_section_zero + 4 * experts
    sem_agtf = sem_section_zero + 5 * experts
    sem_ring_out = take(6 * experts)
    sem_ring_sum = sem_section_zero
    assert counter[0] == lay.sems

    def block(index, rows):
        return pl.ds(pl.multiple_of(index * rows, rows), rows)

    place_y = lax.rem(d, 2)
    place_z = d // 2
    ring_at = place_z + place_y * (experts - 1 - 2 * place_z)

    def ring_device(position):
        p = lax.rem(position + 2 * experts, experts)
        return 2 * p + (p // (experts // 2)) * (2 * experts - 1 - 4 * p)

    ways = ((1, 0), (-1, 4))

    def hops(number, direction):
        return experts // 2 - (number % 2 == (direction > 0))

    def ring_gather(parts, at_half=None):
        def hop(number, direction, shift, k):
            view, base = parts[number]
            held = view(ring_device(ring_at - direction * k))
            return remote(held, held, base + shift + k, (s, ring_device(ring_at + direction), t))

        lines = [(number, direction, shift) for number in range(len(parts)) for direction, shift in ways]
        for line in lines:
            hop(*line, 0).start()

        def one(k, carry):
            for line in lines:
                hop(*line, k - 1).wait_recv()
                hop(*line, k).start()
            return carry

        short = experts // 2 - 1
        lax.fori_loop(1, short, one, 0)
        if at_half is not None:
            at_half()
        for line in lines:
            hop(*line, short - 1).wait_recv()
            if hops(*line[:2]) > short:
                hop(*line, short).start()
        for line in lines:
            if hops(*line[:2]) > short:
                hop(*line, short).wait_recv()

        def sent_one(k, carry):
            for line in lines:
                hop(*line, k).wait_send()
            return carry

        lax.fori_loop(0, short, sent_one, 0)
        for line in lines:
            if hops(*line[:2]) > short:
                hop(*line, short).wait_send()

    load_up = pltpu.make_async_copy(up_ref, upv, wsem.at[0])
    load_down = pltpu.make_async_copy(down_ref, downv, wsem.at[1])
    load_qkvw = pltpu.make_async_copy(qkvw_hbm, qkvw_ref, wsem.at[2])
    load_outw = pltpu.make_async_copy(outw_hbm, outw_ref, wsem.at[3])
    load_tok = pltpu.make_async_copy(tok_ref, xb, wsem.at[4])
    load_cot = pltpu.make_async_copy(cot_ref.at[t], dyb, wsem.at[4])

    @pl.when(s == 0)
    def _():
        load_tok.start()

    @pl.when(s == 1)
    def _():
        load_cot.start()

    load_qkvw.start()
    load_outw.start()
    load_up.start()
    load_down.start()

    barrier = pltpu.get_barrier_semaphore()
    for k in steps:
        pl.semaphore_signal(barrier, inc=1, device_id=(s, peer[k], t), device_id_type=pl.DeviceIdType.MESH)
    pl.semaphore_signal(barrier, inc=1, device_id=sib, device_id_type=pl.DeviceIdType.MESH)
    for k in range(experts):
        pl.semaphore_signal(barrier, inc=1, device_id=(1 - s, peer[k], t), device_id_type=pl.DeviceIdType.MESH)
    pl.semaphore_wait(barrier, 2 * experts)

    for k in steps:
        fire(remote(routes_ref, rr.at[k], sem_routes + k, (s, peer[k], t)))
    rr[0] = routes_ref[...]

    lanes8 = lax.broadcasted_iota(jnp.int32, (experts, length), 0)
    row_at = lax.broadcasted_iota(jnp.int32, (length, length), 0)
    col_at = lax.broadcasted_iota(jnp.int32, (length, length), 1)
    before = (row_at < col_at).astype(bf)
    slot_at = lax.broadcasted_iota(jnp.int32, (cap, length), 0).astype(f32)

    expert_of = jnp.zeros((experts, length), jnp.int32)
    for k in range(experts):
        expert_of = jnp.where(lanes8 == k, peer[k], expert_of)
    turn = (lax.broadcasted_iota(jnp.int32, (experts, experts), 1) == expert_of[:, 0:experts]).astype(f32).astype(bf)
    wrp[...] = nn(turn, wr_ref[...]).astype(bf)
    own_routes = routes_ref[t]
    hits = (expert_of == own_routes[0:1, :]) | (expert_of == own_routes[1:2, :])
    hit_f = hits.astype(f32)
    hit_t[...] = hit_f
    spot = jnp.where(hits, nn(hit_f.astype(bf), before), -1.0)
    for e in range(experts):
        place[e * cap : (e + 1) * cap, :] = (slot_at == spot[e : e + 1, :]).astype(f32).astype(bf)

    def to_relay(source, k, leg):
        slot = leg * len(relayed) + relayed.index(k)
        return remote(source, relay_buf.at[slot], sem_relay + slot, across)

    def passed_on(landing, base, leg, k):
        slot = leg * len(relayed) + relayed.index(k)
        return pltpu.make_async_remote_copy(
            src_ref=relay_buf.at[slot],
            dst_ref=landing.at[k, t],
            send_sem=ss.at[sem_pass + slot],
            recv_sem=rs.at[base + k],
            device_id=(0, peer[k], t),
            device_id_type=pl.DeviceIdType.MESH,
        )

    def relay(landing, base, leg):
        for k in relayed:
            slot = leg * len(relayed) + relayed.index(k)
            held = relay_buf.at[slot]
            remote(held, held, sem_relay + slot, across).wait_recv()
            passed_on(landing, base, leg, k).start()

    def dispatch(rows, send, landing, base, base_fwd, leg=None, both=False):
        send[...] = nn(place[...], rows).astype(bf).reshape(send.shape)

        def start_relayed():
            for k in relayed:
                to_relay(send.at[k], k, leg).start()

        def start_direct():
            for k in relayed:
                remote(send.at[k], landing.at[k, t], base + k, (s, peer[k], t)).start()

        if both:
            pl.when(s == 0)(start_relayed)
        elif leg is not None:
            start_relayed()
        for k in steps:
            if k not in relayed:
                remote(send.at[k], landing.at[k, t], base + k, (s, peer[k], t)).start()
        if both:
            pl.when(s == 1)(start_direct)
        elif leg is None:
            start_direct()
        remote(send.at[0], landing.at[0, t], base_fwd, sib).start()
        landing[0, t] = send[0]

        def arrived(k):
            own = landing.at[k, t]
            remote(own, own, base + k, sib).wait_recv()
            remote(own, own, base_fwd + k, sib).start()

        def joined(k):
            own = landing.at[k, t]
            remote(own, own, base_fwd + k, sib).wait_recv()

        def drain(zero):
            def one(k, carry):
                remote(send.at[k], landing.at[k, t], base_fwd + k, sib).wait_send()
                return carry

            lax.fori_loop(0, experts, one, 0)
            for k in steps:
                if zero and k in relayed:
                    to_relay(send.at[k], k, leg).wait_send()
                else:
                    remote(send.at[k], landing.at[k, t], base + k, sib).wait_send()

        return arrived, joined, drain

    def stream(dispatched, first, second, finish_chunk, eager, zero):
        arrived, joined, drain = dispatched
        last = len(chunks) - 1
        arrived(1)
        joined(0)
        joined(1)

        def arrive_next(c):
            arrived(2 * c + 2)
            arrived(2 * c + 3)

        def one(c, carry):
            first(c)
            if eager:
                pl.when(c > 0)(lambda: finish_chunk(c - 1))
                pl.when(c < last)(lambda: arrive_next(c))
                second(c)
            else:
                second(c)

                @pl.when(c < last)
                def _():
                    arrive_next(c)
                    finish_chunk(c)


            @pl.when(c < last)
            def _():
                joined(2 * c + 2)
                joined(2 * c + 3)

            return carry

        lax.fori_loop(0, len(chunks), one, 0)
        finish_chunk(last)
        drain(zero)

    def other_experts():
        for k in steps:
            remote(routes_ref, rr.at[k], sem_routes + k, (s, peer[k], t)).wait_recv()

        def one(i, carry):
            q = i // micro
            m = i % micro
            pair = rr[q, m]
            first = pair[0:1, :] == d
            mine = first | (pair[1:2, :] == d)
            mine_f = jnp.broadcast_to(mine.astype(f32), (experts, length))
            spots = jnp.where(mine_f > 0.0, nn(mine_f.astype(bf), before), -1.0)
            where_slot = (slot_at == spots[0:1, :]).astype(f32).astype(bf)
            partner = jnp.where(first, pair[1:2, :], pair[0:1, :])
            partner_hot = (lanes8 == partner).astype(f32).astype(bf)
            other[q, m] = nt(where_slot, partner_hot)
            return carry

        lax.fori_loop(0, experts * micro, one, 0)

    @pl.when(s == 0)
    def _():
        load_tok.wait()

    @pl.when(s == 1)
    def _():
        load_cot.wait()
        relay(xrows, sem_dx, 0)
        other_experts()
        arrived, joined, drain = dispatch(dyb[...], disp_y, dyrows, sem_ddy, sem_ddyf)

        def pass_one(k, carry):
            arrived(k)
            return carry

        def join_one(k, carry):
            joined(k)
            return carry

        lax.fori_loop(1, experts, pass_one, 0)
        lax.fori_loop(0, experts, join_one, 0)
        drain(False)

    dist_rows = (
        lax.broadcasted_iota(jnp.int32, (lay.buckets, length), 0) == dist_ref[...]
    ).astype(f32).astype(bf)
    bias_rows = nn(relb_ref[...], dist_rows).astype(bf)
    mirror = ((row_at + col_at == length) | (row_at + col_at == 0)).astype(f32).astype(bf)
    bias_back = nn(bias_rows, mirror)
    for m in range(micro):
        seg_rows = jnp.broadcast_to(seg_ref[m : m + 1, :].astype(f32), (length, length))
        pads = jnp.broadcast_to(pad_ref[m : m + 1, :], (length, length))
        allowed = (col_at <= row_at) & (seg_rows == jnp.transpose(seg_rows))
        allowed = allowed & ((pads == 1) | (col_at == row_at))
        for p in range(pairs):
            for h in range(2):
                head = 2 * p + h
                grid = pltpu.roll(
                    jnp.broadcast_to(bias_back[head : head + 1, :], (length, length)), 0, 1, stride=1, stride_axis=0
                )
                bias_buf[m, p, :, h * length : (h + 1) * length] = jnp.where(allowed, grid, masked_score)

    x_copy = remote(x_send, xb.at[t], sem_x, across)
    dy_copy = remote(dy_send, dyb, sem_dy, across)
    x_forward = remote(xb.at[t], xb.at[t], sem_xf, sib)

    def spread_gates(gates_ref):
        return jnp.concatenate(
            [
                jnp.broadcast_to(gates_ref[e : e + 1, :], (cap, length)) * place[e * cap : (e + 1) * cap, :].astype(f32)
                for e in range(experts)
            ],
            axis=0,
        ).astype(bf)

    @pl.when(s == 1)
    def _():
        x_copy.wait_recv()
        x_forward.start()

    load_qkvw.wait()
    load_outw.wait()
    gain_one = gains_ref[0:1, :].astype(f32)
    gain_two = gains_ref[1:2, :].astype(f32)
    low_lanes = lax.broadcasted_iota(jnp.int32, (length, 128), 1) < 64

    def both_heads(pair_block):
        zero = jnp.zeros((), bf)
        return jnp.concatenate(
            [jnp.where(low_lanes, pair_block, zero), jnp.where(low_lanes, zero, pair_block)], axis=0
        )

    def attend(m):
        x_rows = xb[m].astype(f32)
        no1[m] = (x_rows * inverse_rms(x_rows) * gain_one).astype(bf)
        for c in range(3):
            qkvb[c, m] = nn(no1[m], qkvw_ref[c]).astype(bf)
        for p in range(pairs):
            at = slice(p * 128, (p + 1) * 128)
            scores = 0.125 * nt(qkvb[0, m, :, at], both_heads(qkvb[1, m, :, at])) + bias_buf[m, p]
            for h in range(2):
                part = scores[:, h * length : (h + 1) * length]
                terms = jnp.exp(part - jnp.max(part, axis=-1, keepdims=True))
                probs_buf[m, p, :, h * length : (h + 1) * length] = terms * (
                    1.0 / jnp.sum(terms, axis=-1, keepdims=True)
                )
            mixed[m, :, at] = nn(probs_buf[m, p].astype(bf), both_heads(qkvb[2, m, :, at])).astype(bf)

    att_copy = remote(att_send, att_recv, sem_att, sib)

    def project_other():
        att_send[...] = nn(mixed[u], outw_ref[...])
        att_copy.start()

    begin = u + s * (t - u)

    def attend_one(i, carry):
        @pl.when((s == 1) & (i == 1))
        def _():
            x_forward.wait()

        attend(begin + i * (1 - 2 * begin))

        @pl.when((s == 0) & (i == 0))
        def _():
            project_other()

        return carry

    lax.fori_loop(0, micro, attend_one, 0)

    @pl.when(s == 1)
    def _():
        project_other()

    part_own = nn(mixed[t], outw_ref[...])
    att_copy.wait()
    middle = xb[t].astype(f32) + part_own + att_recv[...]
    mid[...] = middle
    ntb[...] = (middle * inverse_rms(middle) * gain_two).astype(bf)
    logits_t = jnp.where(hit_t[...] > 0.0, nt(wrp[...], ntb[...]), masked_score)
    terms = jnp.exp(logits_t - jnp.max(logits_t, axis=0, keepdims=True))
    gate_t[...] = terms / jnp.sum(terms, axis=0, keepdims=True)

    arrivals = dispatch(ntb[...], disp_x, xrows, sem_dx, sem_dxf, 0, True)
    load_up.wait()
    load_down.wait()
    rows_of = 2 * micro * cap

    def flat(ref, chunk):
        return ref[chunk].reshape(rows_of, ref.shape[-1])

    def front_chunk(c):
        value, slope = gelu_parts(nn(flat(xrows, pair(c)), upv[...]))
        hidden[pair(c)] = value.astype(bf).reshape(2, micro, cap, ffn)
        dgelu[pair(c)] = slope.astype(bf).reshape(2, micro, cap, ffn)

    def split_sum(c, total, send, recv, base):
        for m in range(micro):
            halves[m] = total.reshape(2, micro, cap, width)[:, m]
        send[pair(c)] = halves[u].astype(bf)
        remote(send.at[pair(c)], recv.at[pair(c)], base + c, sib).start()

    def hand_back(c, send, recv, base, total, landing, base_back):
        remote(send.at[pair(c)], recv.at[pair(c)], base + c, sib).wait()
        total[pair(c)] = (halves[t] + recv[pair(c)].astype(f32)).astype(bf)

        def give(k):
            remote(total.at[k], landing.at[k], base_back + k, (s, partner_at(k), t)).start()

        def keep():
            landing[0] = total[0]

        if isinstance(c, int):
            give(2 * c)
        else:
            pl.when(c == 0)(keep)
            pl.when(c > 0)(lambda: give(2 * c))
        give(2 * c + 1)

    def wait_back(total, landing, base_back):
        def one(k, carry):
            remote(total.at[k], landing.at[k], base_back + k, sib).wait()
            return carry

        lax.fori_loop(1, experts, one, 0)

    def rows_chunk(c):
        split_sum(c, nn(flat(hidden, pair(c)), downv[...]), eo_send, eo_recv, sem_eo)

    def rows_finish(c):
        hand_back(c, eo_send, eo_recv, sem_eo, eob, eoret, sem_re)

    mine_hot = (lax.broadcasted_iota(jnp.int32, (rows_of, experts), 1) == d).astype(f32)

    ones = jnp.ones((8, ffn), bf)
    gg_part[...] = jnp.zeros_like(gg_part)

    def slope_chunk(c):
        slot_logits = nt(flat(xrows, pair(c)), wr_ref[...])
        own_logit = jnp.sum(slot_logits * mine_hot, axis=-1, keepdims=True)
        other_logit = jnp.sum(slot_logits * flat(other, pair(c)), axis=-1, keepdims=True)
        gate = 1.0 / (1.0 + jnp.exp(other_logit - own_logit))
        dy_flat = flat(dyrows, pair(c))
        og[pair(c)] = (dy_flat.astype(f32) * gate).astype(bf).reshape(2, micro, cap, width)
        grad = nt(dy_flat, downv[...])
        pg[pair(c)] = (grad * gate * flat(dgelu, pair(c)).astype(f32)).astype(bf).reshape(2, micro, cap, ffn)
        product = (grad * flat(hidden, pair(c)).astype(f32)).astype(bf)
        for i in range(2):
            for m in range(micro):
                at = (i * micro + m) * cap
                gg_part[m, 2 * c + i, :, 0:cap] = nt(ones, product[at : at + cap])

    def back_chunk(c):
        remote(gg_part.at[u, pair(c)], gg_other.at[pair(c)], sem_gg_core + c, sib).start()
        split_sum(c, nt(flat(pg, pair(c)), upv[...]), cg_send, cg_recv, sem_cg)

    def both_chunk(c):
        front_chunk(c)
        slope_chunk(c)

    def back_finish(c):
        hand_back(c, cg_send, cg_recv, sem_cg, cgb, cgret, sem_rc)
        remote(gg_part.at[u, pair(c)], gg_other.at[pair(c)], sem_gg_core + c, sib).wait()
        gg_send[pair(c)] = gg_part[t, pair(c)] + gg_other[pair(c)]

        def give(k):
            remote(gg_send.at[k], gg_recv.at[k], sem_gg + k, (s, partner_at(k), t)).start()

        def keep():
            gg_recv[0] = gg_send[0]

        if isinstance(c, int):
            give(2 * c)
        else:
            pl.when(c == 0)(keep)
            pl.when(c > 0)(lambda: give(2 * c))
        give(2 * c + 1)

    def hidden_of(m):
        return jnp.concatenate([hidden[k, m] for k in range(experts)], axis=0)

    def expert_rows():
        eo_send[...] = nn(hidden_of(u), downv[...]).astype(bf).reshape(eo_send.shape)
        eo_copy = remote(eo_send, eo_recv, sem_eo, sib)
        eo_copy.start()
        total = nn(hidden_of(t), downv[...])
        eo_copy.wait()
        eob[...] = (total + eo_recv[...].astype(f32).reshape(slots, width)).astype(bf).reshape(eob.shape)

    def send_back(source, landing, base):
        for k in steps:
            remote(source.at[k], landing.at[k], base + k, (s, peer[k], t)).start()
        landing[0] = source[0]

    def finish(copies):
        for copy in copies:
            copy.wait()

    def layer_output():
        result = mid[...] + tn(spread_gates(gate_t), eoret[...].reshape(slots, width))
        out_own[...] = result
        return result

    def own_half():
        return pl.ds(pl.multiple_of(t * half, half), half)

    def other_half():
        return pl.ds(pl.multiple_of(u * half, half), half)

    def hand_out(rows_ref, out_ref, index, hbm_ref, index_out):
        copy = remote(rows_ref.at[:, other_half()], out_ref.at[t], index, sib)
        copy.start()
        out_ref[t] = rows_ref[:, own_half()]
        copy.wait()
        pltpu.make_async_copy(out_ref, hbm_ref, osem.at[index_out]).start()

    def gather_factors():
        no_all[t, d] = no1[t]
        mix_all[d] = mixed[...]
        ring_gather(
            [
                (lambda q: no_all.at[t, q, 0 : length // 2], sem_ring_no),
                (lambda q: no_all.at[t, q, length // 2 : length], sem_ring_no + experts),
                (lambda q: mix_all.at[q, 0], sem_ring_mix),
                (lambda q: mix_all.at[q, 1], sem_ring_mix + experts),
            ]
        )
        copy = remote(no_all.at[t], no_all.at[t], sem_noall, sib)
        copy.start()
        copy.wait()

    @pl.when(s == 0)
    def _():
        stream(arrivals, front_chunk, rows_chunk, rows_finish, True, True)
        wait_back(eob, eoret, sem_re)
        x_send[...] = layer_output().astype(bf)
        x_copy.start()
        hand_out(out_own, secout_ref, sem_so, secout_hbm, 0)
        other_experts()
        gather_factors()
        x_copy.wait_send()
        dy_copy.wait_recv()
        arrivals_y = dispatch(dyb[...], disp_y, dyrows, sem_ddy, sem_ddyf, 1)
        stream(arrivals_y, slope_chunk, back_chunk, back_finish, True, True)

    @pl.when(s == 1)
    def _():
        stream(arrivals, both_chunk, back_chunk, back_finish, True, False)
        expert_rows()

    wait_back(gg_send, gg_recv, sem_gg)
    wait_back(cgb, cgret, sem_rc)

    @pl.when(s == 1)
    def _():
        send_back(eob, eoret, sem_re)


    gg_rows = []
    for e in range(experts):
        high, low = split_low(gg_recv[e][:, 0:cap])
        spot_rows = place[e * cap : (e + 1) * cap, :]
        gg_rows.append((nn(high, spot_rows) + nn(low, spot_rows))[0:1, :])
    gate_grad = jnp.concatenate(gg_rows, axis=0)
    gates = gate_t[...]
    logit_grad = (gates * (gate_grad - jnp.sum(gates * gate_grad, axis=0, keepdims=True))).astype(bf)
    router_grad = nn(tn(turn, logit_grad).astype(bf), ntb[...])
    two_grad = tn(logit_grad, wrp[...]) + tn(place[...], cgret[...].reshape(slots, width))
    dy = dyb[...].astype(f32)
    middle = mid[...]
    scale = inverse_rms(middle)
    normed = middle * scale
    gain_two_grad = jnp.sum(two_grad * normed, axis=0, keepdims=True)
    groups = width // 128
    small_send[...] = jnp.zeros_like(small_send)
    for g in range(groups):
        small_send[g, 0:experts, :] = router_grad[:, g * 128 : (g + 1) * 128]
        small_send[g, experts + 1 : experts + 2, :] = gain_two_grad[:, g * 128 : (g + 1) * 128]
    scaled = two_grad * gain_two
    middle_grad = dy + scale * (scaled - normed * jnp.mean(scaled * normed, axis=-1, keepdims=True))
    mgrad[...] = middle_grad
    ag[t] = middle_grad.astype(bf)
    ag_copy = remote(ag.at[t], ag.at[t], sem_ag, sib)
    ag_copy.start()

    agt_rows = width // experts
    agt_out = [
        (remote(agt.at[block(peer[k], agt_rows)], agt_all.at[d, t], sem_agt + k, (s, peer[k], t)), k)
        for k in reversed(steps)
    ]
    agt_own = remote(agt.at[block(d, agt_rows)], agt_all.at[d, t], sem_agtf, sib)

    @pl.when(s == 0)
    def _():
        agt[...] = jnp.transpose(ag[t])
        for copy, _ in agt_out:
            copy.start()
        agt_all[d, t] = agt[block(d, agt_rows), :]
        agt_own.start()

    def attend_back(m, lane_of_m):
        mg[m] = nt(ag[m], outw_ref[...]).astype(bf)
        for p in range(pairs):
            at = slice(p * 128, (p + 1) * 128)
            mg_pair = mg[m, :, at]
            probs = probs_buf[m, p]
            keys2 = both_heads(qkvb[1, m, :, at])
            queries2 = both_heads(qkvb[0, m, :, at])
            mg2 = both_heads(mg_pair)
            prob_grad = nt(mg_pair, both_heads(qkvb[2, m, :, at]))
            raws = []
            key_grad = jnp.zeros((length, 128), f32)
            value_grad = jnp.zeros((length, 128), f32)
            for h in range(2):
                lane = slice(h * length, (h + 1) * length)
                part = probs[:, lane]
                step = prob_grad[:, lane]
                score_grad = part * (step - jnp.sum(part * step, axis=-1, keepdims=True))
                score_sum[2 * p + h] += score_grad
                raw = (0.125 * score_grad).astype(bf)
                raws.append(raw)
                key_grad = key_grad + tn(raw, queries2[h * length : (h + 1) * length])
                value_grad = value_grad + tn(part.astype(bf), mg2[h * length : (h + 1) * length])
            query_grad = nn(jnp.concatenate(raws, axis=1), keys2)
            for c, grad in enumerate((query_grad, key_grad, value_grad)):
                qkvg[c, m, :, at] = grad.astype(bf)
                qgt[c * cols + p * 128 : c * cols + (p + 1) * 128, lane_of_m] = jnp.transpose(grad).astype(bf)

    score_sum[...] = jnp.zeros_like(score_sum)

    def back_one(i, carry):
        @pl.when(i == 1)
        def _():
            ag_copy.wait()

        attend_back(t + i * (u - t), pl.ds(pl.multiple_of(i * length, length), length))
        return carry

    lax.fori_loop(0, micro, back_one, 0)
    qgt_rows = 3 * cols // experts
    qgt_out = [
        remote(qgt.at[block(peer[k], qgt_rows)], qt_all.at[d], sem_qgt + k, (s, peer[k], t)) for k in reversed(steps)
    ]

    @pl.when(s == 0)
    def _():
        for copy in qgt_out:
            copy.start()
        qt_all[d] = qgt[block(d, qgt_rows), :]

    def project_back(m):
        total = nt(qkvg[0, m], qkvw_ref[0])
        for c in range(1, 3):
            total = total + nt(qkvg[c, m], qkvw_ref[c])
        return total

    no_send[...] = project_back(u).astype(bf)
    no_copy = remote(no_send, no_recv, sem_no, sib)
    no_copy.start()
    one_grad = project_back(t)
    no_copy.wait()
    one_grad = one_grad + no_recv[...].astype(f32)
    x_rows = xb[t].astype(f32)
    scale = inverse_rms(x_rows)
    normed = x_rows * scale
    gain_one_grad = jnp.sum(one_grad * normed, axis=0, keepdims=True)
    scaled = one_grad * gain_one
    input_grad = mgrad[...] + scale * (scaled - normed * jnp.mean(scaled * normed, axis=-1, keepdims=True))
    ig_own[...] = input_grad
    dy_send[...] = input_grad.astype(bf)

    @pl.when(s == 1)
    def _():
        dy_copy.start()

    hand_out(ig_own, ingrad_ref, sem_ig, ingrad_hbm, 1)

    sums = []
    for head in range(2 * pairs):
        high, low = split_low(score_sum[head])
        turned = pltpu.roll(nn(high, mirror) + nn(low, mirror), 0, 1, stride=1, stride_axis=0)
        sums.append(jnp.sum(turned, axis=0, keepdims=True))
    high, low = split_low(jnp.concatenate(sums, axis=0))
    small_send[groups, 0 : 2 * pairs, 0 : lay.buckets] = nt(high, dist_rows) + nt(low, dist_rows)
    for g in range(groups):
        small_send[g, experts : experts + 1, :] = gain_one_grad[:, g * 128 : (g + 1) * 128]
    small_out = [remote(small_send.at[peer[k]], small_in.at[k], sem_small + k, (s, peer[k], t)) for k in steps]
    for copy in small_out:
        copy.start()
    small_in[0] = small_send[d]

    wide = lay.wide
    every = micro * slots

    def expert_grads(n, carry):
        at = pl.ds(pl.multiple_of(n * wide, wide), wide)
        guv[:, at] = tn(xrows[...].reshape(every, width), pg[:, :, :, at].reshape(every, wide)).astype(bf)
        pltpu.make_async_copy(guv.at[:, at], gup_ref.at[:, at], gsem.at[n]).start()
        gdv[at, :] = tn(hidden[:, :, :, at].reshape(every, wide), og[...].reshape(every, width)).astype(bf)
        pltpu.make_async_copy(gdv.at[at, :], gdown_ref.at[at, :], gsem.at[ffn // wide + n]).start()
        return carry

    lax.fori_loop(0, ffn // wide, expert_grads, 0)

    qkv_rows = 3 * cols // experts
    share = shared_ref.shape[1] // 6
    parts = [slice(c * share, (c + 1) * share) for c in range(6)]

    def pack_out(total):
        half_rows = agt_rows // 2
        return jnp.concatenate([total[..., 0:half_rows, :], total[..., half_rows:, :]], axis=-1).astype(bf)

    @pl.when(s == 0)
    def _():
        passed = [agt_own]
        for copy, k in agt_out:
            copy.wait_recv()
            forward = remote(agt_all.at[peer[k], t], agt_all.at[peer[k], t], sem_agtf + k, sib)
            forward.start()
            passed.append(forward)
        for copy in passed:
            copy.wait()
        for copy, _ in agt_out:
            copy.wait_send()
        total = jnp.zeros((agt_rows, cols), f32)
        for q in range(experts):
            for m in range(micro):
                total = total + nn(agt_all[q, m], mix_all[q, m])
        shared_ref[d, qkv_rows:, :] = pack_out(total)

        def qkv_slice(q):
            return nn(qt_all[q], jnp.concatenate([no_all[t, q], no_all[u, q]], axis=0))

        total = qkv_slice(d)
        for copy, k in zip(qgt_out, reversed(steps)):
            copy.wait_recv()
            total = total + qkv_slice(peer[k])
        for copy in qgt_out:
            copy.wait_send()
        shared_ref[d, 0:qkv_rows, :] = total.astype(bf)

    @pl.when(s == 1)
    def _():
        normed_rows = no1[...].reshape(micro * length, width)
        own = jnp.concatenate([tn(qkvg[c].reshape(micro * length, cols), normed_rows) for c in range(3)], axis=0)
        rs_buf[:, 0:qkv_rows, :] = own.astype(bf).reshape(experts, qkv_rows, width)
        own = tn(ag[...].reshape(micro * length, width), mixed[...].reshape(micro * length, cols))
        rs_buf[:, qkv_rows:, :] = pack_out(own.reshape(experts, agt_rows, cols))

        relay(dyrows, sem_ddy, 1)

        def hop(number, direction, shift, k):
            owner = ring_device(ring_at + direction * (hops(number, direction) - k))
            return remote(
                rs_buf.at[owner, parts[number]],
                rs_in.at[shift + k, parts[number]],
                sem_ring_sum + number * experts + shift + k,
                (s, ring_device(ring_at + direction), t),
            )

        lines = [(number, direction, shift) for number in range(len(parts)) for direction, shift in ways]
        longest = experts // 2
        for k in range(longest):
            for number, direction, shift in lines:
                if k < hops(number, direction):
                    if k > 0:
                        rows = parts[number]
                        owner = ring_device(ring_at + direction * (hops(number, direction) - k))
                        hop(number, direction, shift, k - 1).wait_recv()
                        total = rs_buf[owner, rows, :].astype(f32) + rs_in[shift + k - 1, rows, :].astype(f32)
                        rs_buf[owner, rows, :] = total.astype(bf)
                    hop(number, direction, shift, k).start()
        for number, rows in enumerate(parts):
            total = rs_buf[d, rows, :].astype(f32)
            for direction, shift in ways:
                last = hops(number, direction) - 1
                hop(number, direction, shift, last).wait_recv()
                total = total + rs_in[shift + last, rows, :].astype(f32)
            shared_ref[d, rows, :] = total.astype(bf)
        for number, direction, shift in lines:
            for k in range(hops(number, direction)):
                hop(number, direction, shift, k).wait_send()

    finish(small_out)
    small_total = small_in[0]
    for k in steps:
        small_total = small_total + small_in[k]
    small_all[d] = small_total
    small_back = [remote(small_all.at[d], small_all.at[d], sem_back + k, (s, peer[k], t)) for k in steps]
    for copy in small_back:
        copy.start()

    sums_copy = remote(small_all, small_sib, sem_sums, sib)

    def pass_sums():
        finish(small_back)
        sums_copy.start()


    streams = [
        (lambda q, rows=rows: shared_ref.at[q, rows], sem_ring_out + c * experts) for c, rows in enumerate(parts)
    ]

    ring_gather(streams, pass_sums)
    for q in range(experts):
        pltpu.make_async_copy(shared_ref.at[q], shared_hbm.at[q], osem.at[2 + q]).start()
    sums_copy.wait()
    for g in range(groups):
        lanes = slice(g * 128, (g + 1) * 128)
        grouter_ref[:, lanes] = small_all[g, 0:experts, :] + small_sib[g, 0:experts, :]
        ggain_ref[:, lanes] = small_all[g, experts : experts + 2, :] + small_sib[g, experts : experts + 2, :]
    gbias_ref[...] = small_all[groups, 0 : 2 * pairs, :]
    @pl.when(s == 1)
    def _():
        dy_copy.wait_send()
        for k in relayed:
            passed_on(xrows, sem_dx, 0, k).wait_send()
            passed_on(dyrows, sem_ddy, 1, k).wait_send()
        wait_back(eob, eoret, sem_re)
        layer_output()
        hand_out(out_own, secout_ref, sem_so, secout_hbm, 0)

    for copy in sent:
        copy.wait_send()
    pltpu.make_async_copy(secout_ref, secout_hbm, osem.at[0]).wait()
    pltpu.make_async_copy(ingrad_ref, ingrad_hbm, osem.at[1]).wait()
    for q in range(experts):
        pltpu.make_async_copy(shared_ref.at[q], shared_hbm.at[q], osem.at[2 + q]).wait()
    for n in range(ffn // wide):
        at = slice(n * wide, (n + 1) * wide)
        pltpu.make_async_copy(guv.at[:, at], gup_ref.at[:, at], gsem.at[n]).wait()
        pltpu.make_async_copy(gdv.at[at, :], gdown_ref.at[at, :], gsem.at[ffn // wide + n]).wait()


def widen_kernel(
    sec_ref, ing_ref, gain_ref, shared_ref, bias_ref, router_ref, up_ref, down_ref,
    sec_out, ing_out, gain_out, bias_out, router_out, qkv_out, out_out, up_out, down_out,
    up_low, up_wide, down_low, down_wide, shared_low, qkv_wide, out_wide, bias_low, bias_wide,
    sec_low, ing_low, gain_low, router_low, in_sem, out_sem,
):
    f32 = jnp.float32
    parts = 3
    experts, shared_rows, width = shared_ref.shape
    cols = out_wide.shape[0]
    qkv_rows = 3 * cols // experts
    low = ((up_ref, up_low), (down_ref, down_low))
    wide = ((up_low, up_wide, up_out), (down_low, down_wide, down_out))
    stores = []

    def store(src, dst):
        copy = pltpu.make_async_copy(src, dst, out_sem.at[len(stores)])
        copy.start()
        stores.append(copy)

    def rows(ref, n):
        size = ref.shape[0] // parts
        return pl.ds(n * size, size)

    load_shared = pltpu.make_async_copy(shared_ref, shared_low, in_sem.at[2 * parts])
    load_bias = pltpu.make_async_copy(bias_ref, bias_low, in_sem.at[2 * parts + 1])
    loads = [
        pltpu.make_async_copy(src.at[rows(src, n)], dst.at[rows(dst, n)], in_sem.at[i * parts + n])
        for i, (src, dst) in enumerate(low)
        for n in range(parts)
    ]
    loads[0].start()
    load_shared.start()
    for copy in loads[1:]:
        copy.start()
    load_bias.start()
    through = ((sec_ref, sec_low, sec_out), (ing_ref, ing_low, ing_out), (gain_ref, gain_low, gain_out), (router_ref, router_low, router_out))
    passing = [
        pltpu.make_async_copy(src, mid, in_sem.at[2 * parts + 2 + i]) for i, (src, mid, _) in enumerate(through)
    ]
    for copy in passing:
        copy.start()

    def widen(i, n):
        loads[i * parts + n].wait()
        src, dst, out = wide[i]
        dst[rows(dst, n), :] = src[rows(src, n), :].astype(f32)
        store(dst.at[rows(dst, n)], out.at[rows(out, n)])

    def turn_qkv(c):
        block = shared_low[:, 0:qkv_rows, :].reshape(3 * cols, width)[c * cols : (c + 1) * cols]
        qkv_wide[c] = jnp.transpose(block.astype(f32))
        store(qkv_wide.at[c], qkv_out.at[c])

    widen(0, 0)
    load_shared.wait()
    turn_qkv(0)
    widen(0, 1)
    widen(0, 2)
    turn_qkv(1)
    widen(1, 0)
    widen(1, 1)
    turn_qkv(2)
    out_block = jnp.concatenate(
        [
            shared_low[e, qkv_rows:, h * cols : (h + 1) * cols].astype(f32)
            for e in range(experts)
            for h in range(2)
        ],
        axis=0,
    )
    out_wide[...] = jnp.transpose(out_block)
    store(out_wide, out_out)
    widen(1, 2)
    for copy, (_, mid, out) in zip(passing, through):
        copy.wait()
        store(mid, out)
    load_bias.wait()
    for h in range(bias_wide.shape[0]):
        bias_wide[h] = bias_low[h : h + 1, 0 : bias_wide.shape[2]]
    store(bias_wide, bias_out)
    for copy in stores:
        copy.wait()


def fused_local(
    tokens,
    cotangent,
    segments,
    pad_mask,
    routes,
    dist_bucket,
    norm_gains,
    qkv_weight,
    out_weight,
    rel_bias,
    router_weight,
    expert_up,
    expert_down,
):
    micro, _, length, width = tokens.shape
    experts = router_weight.shape[2]
    cap = max(2, 3 * length // experts)
    cols = out_weight.shape[1]
    heads = rel_bias.shape[2]
    ffn = expert_up.shape[3]
    slots = experts * cap
    pairs = cols // 128
    shared_rows = 3 * cols // experts + width // experts // 2
    lay = Layout()
    lay.experts = experts
    lay.cap = cap
    lay.buckets = rel_bias.shape[1]
    lay.wide = min(ffn, 256)
    lay.sems = 28 * experts + 12 + experts // 2
    bf = jnp.bfloat16
    f32 = jnp.float32
    vm = pltpu.VMEM
    shape = jax.ShapeDtypeStruct
    dma = pltpu.SemaphoreType.DMA
    scratch = [
        vm((width, ffn), bf),
        vm((ffn, width), bf),
        vm((3, width, cols), bf),
        vm((cols, width), bf),
        vm((micro, length, width), bf),
        vm((length, width), bf),
        vm((experts, micro, 2, length), jnp.int32),
        vm((slots, length), bf),
        vm((micro, pairs, length, 2 * length), f32),
        vm((micro, pairs, length, 2 * length), f32),
        vm((micro, length, width), bf),
        vm((3, micro, length, cols), bf),
        vm((micro, length, cols), bf),
        vm((length, width), f32),
        vm((length, width), f32),
        vm((length, width), f32),
        vm((length, width), bf),
        vm((experts, length), f32),
        vm((experts, length), f32),
        vm((experts, width), bf),
        vm((2 * pairs, length, length), f32),
        vm((experts, cap, width), bf),
        vm((experts, micro, cap, width), bf),
        vm((experts, cap, width), bf),
        vm((experts, micro, cap, width), bf),
        vm((experts, micro, cap, ffn), bf),
        vm((experts, micro, cap, ffn), bf),
        vm((micro, 2, cap, width), f32),
        vm((experts, cap, width), bf),
        vm((experts, cap, width), bf),
        vm((experts, cap, width), bf),
        vm((experts, cap, width), bf),
        vm((length, width), f32),
        vm((experts, micro, cap, experts), f32),
        vm((experts, micro, cap, width), bf),
        vm((micro, experts, 8, 128), f32),
        vm((experts, 8, 128), f32),
        vm((experts, 8, 128), f32),
        vm((experts, 8, 128), f32),
        vm((experts, micro, cap, ffn), bf),
        vm((experts, cap, width), bf),
        vm((experts, cap, width), bf),
        vm((experts, cap, width), bf),
        vm((experts, cap, width), bf),
        vm((length, width), f32),
        vm((micro, length, width), bf),
        vm((micro, length, cols), bf),
        vm((3, micro, length, cols), bf),
        vm((length, width), bf),
        vm((length, width), bf),
        vm((length, width), f32),
        vm((length, width), bf),
        vm((width, ffn), bf),
        vm((ffn, width), bf),
        vm((micro, experts, length, width), bf),
        vm((experts, micro, length, cols), bf),
        vm((3 * cols, micro * length), bf),
        vm((experts, 3 * cols // experts, micro * length), bf),
        vm((width, length), bf),
        vm((experts, micro, width // experts, length), bf),
        vm((experts, 2 * experts, 128), f32),
        vm((experts, 2 * experts, 128), f32),
        vm((experts, 2 * experts, 128), f32),
        vm((experts, 2 * experts, 128), f32),
        vm((micro, length, width // 2), f32),
        vm((micro, length, width // 2), f32),
        vm((experts, shared_rows, width), bf),
        vm((length, width), bf),
        vm((experts, shared_rows, width), bf),
        vm((experts, shared_rows, width), bf),
        vm((shared_rows, width), bf),
        vm((4, cap, width), bf),
        dma((5,)),
        dma((2 * (ffn // lay.wide),)),
        dma((experts + 2,)),
        dma((lay.sems,)),
        dma((lay.sems,)),
    ]
    whole = pl.BlockSpec(memory_space=pltpu.VMEM)
    anywhere = pl.BlockSpec(memory_space=pl.ANY)
    out_shape = (
        shape((micro, length, width // 2), f32),
        shape((micro, length, width // 2), f32),
        shape((2, width), f32),
        shape((experts, shared_rows, width), bf),
        shape((heads, 128), f32),
        shape((experts, width), f32),
        shape((width, ffn), bf),
        shape((ffn, width), bf),
    )
    results = pl.pallas_call(
        partial(layer_kernel, lay),
        out_shape=out_shape,
        in_specs=[anywhere] * 2 + [whole] * 5 + [anywhere] * 2 + [whole] * 2 + [anywhere] * 2,
        out_specs=[anywhere] * 2 + [whole, anywhere, whole, whole] + [anywhere] * 2,
        scratch_shapes=scratch,
        name="two_sections",
        compiler_params=pltpu.CompilerParams(
            collective_id=0, has_side_effects=True, vmem_limit_bytes=60 * 1024 * 1024
        ),
    )(
        tokens[:, 0],
        cotangent[:, 0],
        segments[:, 0],
        pad_mask[:, 0],
        routes[:, 0].transpose(0, 2, 1),
        dist_bucket[None],
        norm_gains[0],
        qkv_weight[0].transpose(1, 0, 2),
        out_weight[0],
        rel_bias[0].T,
        router_weight[0].T,
        expert_up[0, 0],
        expert_down[0, 0],
    )
    section_out, input_grads, gains, bias, router, qkv, out, up, down = pl.pallas_call(
        widen_kernel,
        out_shape=(
            out_shape[0],
            out_shape[1],
            out_shape[2],
            shape((heads, 1, lay.buckets), f32),
            out_shape[5],
            shape((3, width, cols), f32),
            shape((cols, width), f32),
            shape((width, ffn), f32),
            shape((ffn, width), f32),
        ),
        in_specs=[anywhere] * 8,
        out_specs=[anywhere] * 9,
        scratch_shapes=[
            vm((width, ffn), bf),
            vm((width, ffn), f32),
            vm((ffn, width), bf),
            vm((ffn, width), f32),
            vm((experts, shared_rows, width), bf),
            vm((3, width, cols), f32),
            vm((cols, width), f32),
            vm((heads, 128), f32),
            vm((heads, 1, lay.buckets), f32),
            vm((micro, length, width // 2), f32),
            vm((micro, length, width // 2), f32),
            vm((2, width), f32),
            vm((experts, width), f32),
            dma((12,)),
            dma((15,)),
        ],
        name="widen",
        compiler_params=pltpu.CompilerParams(vmem_limit_bytes=60 * 1024 * 1024),
    )(*results)
    return (
        section_out[None, :, None],
        input_grads[None, :, None],
        gains[None],
        qkv.transpose(1, 0, 2)[None],
        out[None],
        bias.transpose(1, 2, 0),
        router.T[None],
        up[None, None],
        down[None, None],
    )


def fits_kernel(mesh):
    return mesh.shape["section"] == 2 and mesh.shape["tensor"] == 2 and mesh.shape["dp"] == 8


def solution(mesh):
    in_specs = (
        P(None, "dp", None, None),
        P(None, "dp", None, None),
        P(None, "dp", None),
        P(None, "dp", None),
        P(None, "dp", None, None),
        P(),
        P("section", None, None),
        P("section", None, None, "tensor"),
        P("section", "tensor", None),
        P("section", None, "tensor"),
        P("section", None, None),
        P("section", "dp", None, "tensor"),
        P("section", "dp", "tensor", None),
    )
    out_specs = (
        P("section", None, "dp", None, "tensor"),
        P("section", None, "dp", None, "tensor"),
        P("section", None, None),
        P("section", None, None, "tensor"),
        P("section", "tensor", None),
        P("section", None, "tensor"),
        P("section", None, None),
        P("section", "dp", None, "tensor"),
        P("section", "dp", "tensor", None),
    )
    body = fused_local if fits_kernel(mesh) else local
    return jax.shard_map(body, mesh=mesh, in_specs=in_specs, out_specs=out_specs, check_vma=False)
```

```python
from functools import partial

import jax
import jax.numpy as jnp
from jax import lax
from jax.experimental import pallas as pl
from jax.experimental.pallas import tpu as pltpu
from jax.sharding import PartitionSpec as P

norm_eps = 1e-06
masked_score = -1e30
highest = lax.Precision.HIGHEST


def shifted(block, axis, distance):
    devices = range(lax.axis_size(axis))
    route = [(i - distance, i) for i in devices if i - distance in devices]
    return lax.ppermute(block, axis, route)


def normalize(values, gain_row):
    scale_inv = lax.rsqrt(jnp.mean(values * values, axis=-1, keepdims=True) + norm_eps)
    return values * scale_inv * gain_row


def normalize_back(values, gain_row, upstream):
    scale_inv = lax.rsqrt(jnp.mean(values * values, axis=-1, keepdims=True) + norm_eps)
    normed = values * scale_inv
    gain_grad = jnp.sum(upstream * normed, axis=0)
    scaled = upstream * gain_row
    input_grad = scale_inv * (scaled - normed * jnp.mean(scaled * normed, axis=-1, keepdims=True))
    return (input_grad, gain_grad)


def send_rows(rows):
    return lax.all_to_all(rows, "dp", split_axis=0, concat_axis=0, tiled=True)


def sum_slots(partial_rows):
    return lax.psum(partial_rows, "tensor")


def score_context(segment_row, pad_row, dist_bucket, bucket_count):
    length = segment_row.shape[0]
    places = jnp.arange(length, dtype=jnp.int32)
    offsets = jnp.clip(places[:, None] - places[None, :], 0, length - 1)
    bucket_grid = jnp.take(dist_bucket, offsets)
    bucket_onehot = (
        bucket_grid[:, :, None] == jnp.arange(bucket_count, dtype=jnp.int32)[None, None, :]
    ).astype(jnp.float32)
    allowed = (places[None, :] <= places[:, None]) & (segment_row[:, None] == segment_row[None, :])
    allowed = allowed & ((pad_row[None, :] == 1) | (places[None, :] == places[:, None]))
    return (bucket_onehot, allowed)


def attention_front(inputs, context, weights):
    segment_row, pad_row, route_rows, dist_bucket = context
    gain_pair, qkv_weight, out_weight, bias_table, router_weight, upper_weight, lower_weight = (
        weights
    )
    length = inputs.shape[0]
    head_count = bias_table.shape[1]
    bucket_onehot, allowed = score_context(segment_row, pad_row, dist_bucket, bias_table.shape[0])
    normed_one = normalize(inputs, gain_pair[0]).astype(jnp.bfloat16)
    qkv_rows = jnp.einsum(
        "ld,dch->lch", normed_one, qkv_weight, preferred_element_type=jnp.float32
    ).astype(jnp.bfloat16)
    head_dim = qkv_rows.shape[2] // head_count
    queries = qkv_rows[:, 0].reshape(length, head_count, head_dim)
    keys_in = qkv_rows[:, 1].reshape(length, head_count, head_dim)
    values_in = qkv_rows[:, 2].reshape(length, head_count, head_dim)
    raw_scores = jnp.einsum("qhd,khd->hqk", queries, keys_in, preferred_element_type=jnp.float32)
    bias_grid = jnp.einsum(
        "qkb,bh->hqk", bucket_onehot, bias_table.astype(jnp.float32), precision=highest
    )
    logits = jnp.where(allowed[None], 0.125 * raw_scores + bias_grid, masked_score)
    exp_terms = jnp.exp(logits - jnp.max(logits, axis=-1, keepdims=True))
    attn_probs = exp_terms / jnp.sum(exp_terms, axis=-1, keepdims=True)
    mixed_rows = jnp.einsum(
        "hqk,khd->qhd",
        attn_probs.astype(jnp.bfloat16),
        values_in,
        preferred_element_type=jnp.float32,
    )
    mixed_rows = mixed_rows.reshape(length, -1).astype(jnp.bfloat16)
    return (normed_one, queries, keys_in, values_in, attn_probs, mixed_rows, bucket_onehot)


def slot_tables(route_rows, experts, capacity):
    flat_routes = route_rows.reshape(-1)
    route_hits = (flat_routes[:, None] == jnp.arange(experts, dtype=jnp.int32)[None, :]).astype(
        jnp.int32
    )
    earlier = jnp.cumsum(route_hits, axis=0) - route_hits
    position = jnp.sum(earlier * route_hits, axis=1)
    target = flat_routes * capacity + position
    slot_hits = (
        jnp.arange(experts * capacity, dtype=jnp.int32)[:, None] == target[None, :]
    ).astype(jnp.int32)
    source = jnp.sum(slot_hits * jnp.arange(target.shape[0], dtype=jnp.int32)[None, :], axis=1)
    filled = jnp.sum(slot_hits, axis=1) > 0
    return (target, source, filled, route_hits)


def route_gates(normed_two, router_weight, route_hits):
    length = normed_two.shape[0]
    logits = jnp.dot(normed_two, router_weight, preferred_element_type=jnp.float32)
    route_onehot = route_hits.reshape(length, 2, -1).astype(jnp.float32)
    chosen = jnp.einsum("le,lre->lr", logits, route_onehot, precision=highest)
    return (jax.nn.softmax(chosen, axis=-1), route_onehot)


def gather_back(back_slots, target, length):
    flat_slots = back_slots.reshape(-1, back_slots.shape[-1])
    return jnp.take(flat_slots, target, axis=0).reshape(length, 2, -1)


def forward_rest(inputs, front, context, weights):
    segment_row, pad_row, route_rows, dist_bucket = context
    gain_pair, qkv_weight, out_weight, bias_table, router_weight, upper_weight, lower_weight = (
        weights
    )
    mixed_rows = front[5]
    length, model_width = inputs.shape
    experts = router_weight.shape[1]
    capacity = max(2, 3 * length // experts)
    local_experts = upper_weight.shape[0]
    attn_out = lax.psum(
        jnp.dot(mixed_rows, out_weight, preferred_element_type=jnp.float32), "tensor"
    )
    middle = inputs + attn_out
    normed_two = normalize(middle, gain_pair[1]).astype(jnp.bfloat16)
    target, source, filled, route_hits = slot_tables(route_rows, experts, capacity)
    outgoing = jnp.where(
        filled[:, None], jnp.take(normed_two, source // 2, axis=0), jnp.zeros((), jnp.bfloat16)
    )
    outgoing = outgoing.reshape(experts, capacity, model_width)
    arrived = send_rows(outgoing)
    grouped = arrived.reshape(-1, local_experts, capacity, model_width)
    pre_act = jnp.einsum(
        "secd,edf->secf", grouped, upper_weight, preferred_element_type=jnp.float32
    )
    hidden = jax.nn.gelu(pre_act, approximate=False).astype(jnp.bfloat16)
    partial_out = jnp.einsum(
        "secf,efd->secd", hidden, lower_weight, preferred_element_type=jnp.float32
    )
    summed = sum_slots(partial_out)
    returned = summed.astype(jnp.bfloat16).reshape(arrived.shape[0], arrived.shape[1], -1)
    back_slots = send_rows(returned)
    gate_probs, route_onehot = route_gates(normed_two, router_weight, route_hits)
    back_rows = gather_back(back_slots, target, length)
    output = middle + jnp.sum(gate_probs[:, :, None] * back_rows.astype(jnp.float32), axis=1)
    return (output, (attn_out, arrived, back_slots, pre_act))


def backward_layer(inputs, upstream, context, weights, front, saved_state):
    segment_row, pad_row, route_rows, dist_bucket = context
    gain_pair, qkv_weight, out_weight, bias_table, router_weight, upper_weight, lower_weight = (
        weights
    )
    normed_one, queries, keys_in, values_in, attn_probs, mixed_rows, bucket_onehot = front
    attn_out, arrived_rows, back_slots, pre_rows = saved_state
    length, model_width = inputs.shape
    head_count = bias_table.shape[1]
    head_cols = qkv_weight.shape[2]
    experts = router_weight.shape[1]
    capacity = max(2, 3 * length // experts)
    local_experts = upper_weight.shape[0]
    middle = inputs + attn_out
    normed_two = normalize(middle, gain_pair[1]).astype(jnp.bfloat16)
    target, source, filled, route_hits = slot_tables(route_rows, experts, capacity)
    gate_probs, route_onehot = route_gates(normed_two, router_weight, route_hits)
    back_rows = gather_back(back_slots, target, length)
    gate_grad = jnp.sum(upstream[:, None, :] * back_rows.astype(jnp.float32), axis=-1)
    chosen_grad = gate_probs * (gate_grad - jnp.sum(gate_probs * gate_grad, axis=-1, keepdims=True))
    logit_grad = jnp.einsum("lr,lre->le", chosen_grad, route_onehot, precision=highest).astype(
        jnp.bfloat16
    )
    router_grad = jnp.dot(normed_two.T, logit_grad, preferred_element_type=jnp.float32)
    normed_two_grad = jnp.dot(logit_grad, router_weight.T, preferred_element_type=jnp.float32)
    route_grads = (
        (gate_probs[:, :, None] * upstream[:, None, :])
        .reshape(2 * length, model_width)
        .astype(jnp.bfloat16)
    )
    slot_grads = jnp.where(
        filled[:, None], jnp.take(route_grads, source, axis=0), jnp.zeros((), jnp.bfloat16)
    )
    arrived_grads = send_rows(slot_grads.reshape(experts, capacity, model_width))
    grouped = arrived_rows.reshape(-1, local_experts, capacity, model_width)
    grouped_grads = arrived_grads.reshape(-1, local_experts, capacity, model_width)
    hidden, gelu_pull = jax.vjp(partial(jax.nn.gelu, approximate=False), pre_rows)
    hidden_low = hidden.astype(jnp.bfloat16)
    down_grad = jnp.einsum(
        "secf,secd->efd", hidden_low, grouped_grads, preferred_element_type=jnp.float32
    )
    hidden_grad = jnp.einsum(
        "secd,efd->secf", grouped_grads, lower_weight, preferred_element_type=jnp.float32
    )
    pre_grad = gelu_pull(hidden_grad)[0].astype(jnp.bfloat16)
    up_grad = jnp.einsum("secd,secf->edf", grouped, pre_grad, preferred_element_type=jnp.float32)
    rows_grad = sum_slots(
        jnp.einsum("secf,edf->secd", pre_grad, upper_weight, preferred_element_type=jnp.float32)
    )
    sent_back = send_rows(
        rows_grad.astype(jnp.bfloat16).reshape(arrived_rows.shape[0], arrived_rows.shape[1], -1)
    )
    copy_grads = gather_back(sent_back, target, length).astype(jnp.float32)
    normed_two_grad = normed_two_grad + jnp.sum(copy_grads, axis=1)
    middle_part, gain_two = normalize_back(middle, gain_pair[1], normed_two_grad)
    middle_grad = upstream + middle_part
    attn_grad = middle_grad.astype(jnp.bfloat16)
    out_grad = jnp.dot(mixed_rows.T, attn_grad, preferred_element_type=jnp.float32)
    mixed_grad = jnp.dot(attn_grad, out_weight.T, preferred_element_type=jnp.float32).astype(
        jnp.bfloat16
    )
    mixed_grad = mixed_grad.reshape(length, head_count, -1)
    prob_grad = jnp.einsum(
        "qhd,khd->hqk", mixed_grad, values_in, preferred_element_type=jnp.float32
    )
    value_grad = jnp.einsum(
        "hqk,qhd->khd",
        attn_probs.astype(jnp.bfloat16),
        mixed_grad,
        preferred_element_type=jnp.float32,
    )
    score_grad = attn_probs * (prob_grad - jnp.sum(prob_grad * attn_probs, axis=-1, keepdims=True))
    table_grad = jnp.einsum("hqk,qkb->bh", score_grad, bucket_onehot, precision=highest)
    raw_grad = (0.125 * score_grad).astype(jnp.bfloat16)
    query_grad = jnp.einsum("hqk,khd->qhd", raw_grad, keys_in, preferred_element_type=jnp.float32)
    key_grad = jnp.einsum("hqk,qhd->khd", raw_grad, queries, preferred_element_type=jnp.float32)
    qkv_grad = (
        jnp.stack([query_grad, key_grad, value_grad], axis=1)
        .reshape(length, 3, head_cols)
        .astype(jnp.bfloat16)
    )
    qkv_weight_grad = jnp.einsum(
        "ld,lch->dch", normed_one, qkv_grad, preferred_element_type=jnp.float32
    )
    normed_one_grad = lax.psum(
        jnp.einsum("lch,dch->ld", qkv_grad, qkv_weight, preferred_element_type=jnp.float32),
        "tensor",
    )
    input_part, gain_one = normalize_back(inputs, gain_pair[0], normed_one_grad)
    input_grad = middle_grad + input_part
    gain_grads = jnp.stack([gain_one, gain_two])
    return (
        input_grad,
        (gain_grads, qkv_weight_grad, out_grad, table_grad, router_grad, up_grad, down_grad),
    )


def pick_context(segments, pad_mask, routes, dist_bucket, micro_slot):
    segment_row = lax.dynamic_index_in_dim(segments[:, 0], micro_slot, 0, False)
    pad_row = lax.dynamic_index_in_dim(pad_mask[:, 0], micro_slot, 0, False)
    route_rows = lax.dynamic_index_in_dim(routes[:, 0], micro_slot, 0, False)
    return (segment_row, pad_row, route_rows, dist_bucket)


def place_row(store_all, new_value, micro_slot, is_valid):
    current = lax.dynamic_index_in_dim(store_all, micro_slot, 0, False)
    return lax.dynamic_update_index_in_dim(
        store_all, jnp.where(is_valid, new_value, current), micro_slot, 0
    )


def pick_row(store_all, micro_slot):
    return lax.dynamic_index_in_dim(store_all, micro_slot, 0, False)


def mask_grad(grad_value, is_valid):
    return jnp.where(is_valid, grad_value, jnp.zeros((), grad_value.dtype))


def tensor_half(full_rows, tensor_id, half_width):
    return lax.dynamic_slice_in_dim(full_rows, tensor_id * half_width, half_width, 2)[None, :, None]


def local(
    tokens,
    cotangent,
    segments,
    pad_mask,
    routes,
    dist_bucket,
    norm_gains,
    qkv_weight,
    out_weight,
    rel_bias,
    router_weight,
    expert_up,
    expert_down,
):
    section_id = lax.axis_index("section")
    section_count = lax.axis_size("section")
    micro_count = tokens.shape[0]
    length = tokens.shape[2]
    model_width = tokens.shape[3]
    tick_count = micro_count + section_count - 1
    weights = (
        norm_gains[0].astype(jnp.float32),
        qkv_weight[0],
        out_weight[0],
        rel_bias[0],
        router_weight[0],
        expert_up[0],
        expert_down[0],
    )
    empty_rows = jnp.zeros((length, model_width), jnp.bfloat16)
    arriving = empty_rows
    kept_inputs = jnp.zeros((micro_count, length, model_width), jnp.bfloat16)
    section_out = jnp.zeros((micro_count, length, model_width), jnp.float32)
    for tick_index in range(tick_count):
        micro_index = tick_index - section_id
        is_valid = (micro_index >= 0) & (micro_index < micro_count)
        micro_slot = jnp.clip(micro_index, 0, micro_count - 1)
        own_rows = tokens[tick_index, 0] if tick_index < micro_count else empty_rows
        layer_in = jnp.where(section_id == 0, own_rows, arriving)
        context = pick_context(segments, pad_mask, routes, dist_bucket, micro_slot)
        inputs = layer_in.astype(jnp.float32)
        front = attention_front(inputs, context, weights)
        result, saved_state = forward_rest(inputs, front, context, weights)
        section_out = place_row(section_out, result, micro_slot, is_valid)
        kept_inputs = place_row(kept_inputs, layer_in, micro_slot, is_valid)
        arriving = shifted(result.astype(jnp.bfloat16), "section", 1)
    returning = empty_rows
    input_store = jnp.zeros((micro_count, length, model_width), jnp.float32)
    totals = None
    for tick_index in range(tick_count):
        micro_index = tick_index - (section_count - 1 - section_id)
        is_valid = (micro_index >= 0) & (micro_index < micro_count)
        micro_slot = jnp.clip(micro_index, 0, micro_count - 1)
        own_rows = cotangent[tick_index, 0] if tick_index < micro_count else empty_rows
        upstream = jnp.where(section_id == section_count - 1, own_rows, returning).astype(
            jnp.float32
        )
        inputs = pick_row(kept_inputs, micro_slot).astype(jnp.float32)
        context = pick_context(segments, pad_mask, routes, dist_bucket, micro_slot)
        front = attention_front(inputs, context, weights)
        saved_state = forward_rest(inputs, front, context, weights)[1]
        input_grad, grad_set = backward_layer(
            inputs, upstream, context, weights, front, saved_state
        )
        input_store = place_row(input_store, input_grad, micro_slot, is_valid)
        grad_set = jax.tree.map(partial(mask_grad, is_valid=is_valid), grad_set)
        totals = grad_set if totals is None else jax.tree.map(jnp.add, totals, grad_set)
        returning = shifted(input_grad.astype(jnp.bfloat16), "section", -1)
    shared = lax.psum((totals[0], totals[1], totals[2], totals[3], totals[4]), "dp")
    tensor_id = lax.axis_index("tensor")
    half_width = model_width // lax.axis_size("tensor")
    return (
        tensor_half(section_out, tensor_id, half_width),
        tensor_half(input_store, tensor_id, half_width),
        shared[0][None],
        shared[1][None],
        shared[2][None],
        shared[3][None],
        shared[4][None],
        totals[5][None],
        totals[6][None],
    )


def gelu_parts(values):
    share = 0.5 + 0.5 * lax.erf(values * 0.7071067811865476)
    return (values * share, share + values * (0.3989422804014327 * jnp.exp(-0.5 * values * values)))


def nn(left, right):
    return lax.dot_general(left, right, (((1,), (0,)), ((), ())), preferred_element_type=jnp.float32)


def nt(left, right):
    return lax.dot_general(left, right, (((1,), (1,)), ((), ())), preferred_element_type=jnp.float32)


def tn(left, right):
    return lax.dot_general(left, right, (((0,), (0,)), ((), ())), preferred_element_type=jnp.float32)


def split_low(values):
    high = values.astype(jnp.bfloat16)
    return (high, (values - high.astype(jnp.float32)).astype(jnp.bfloat16))


def inverse_rms(values):
    return lax.rsqrt(jnp.mean(values * values, axis=-1, keepdims=True) + norm_eps)


class Layout:
    pass


def layer_kernel(lay, *refs):
    (
        tok_ref, cot_ref, seg_ref, pad_ref, routes_ref, dist_ref, gains_ref, qkvw_hbm, outw_hbm, relb_ref, wr_ref,
        up_ref, down_ref,
        secout_ref, ingrad_ref, ggain_ref, shared_ref, gbias_ref, grouter_ref, guv, gdv,
        upv, downv, qkvw_ref, outw_ref, xb, dyb, rr, place, bias_buf, probs_buf, no1, qkvb, mixed, att_send, att_recv, mid, ntb,
        gate_t, hit_t, wrp, score_sum, disp_x, xrows, disp_y, dyrows, hidden, dgelu, halves, eo_send, eo_recv, eob, eoret, out_own,
        other, og, gg_part, gg_other, gg_send, gg_recv, pg, cg_send, cg_recv, cgb, cgret, mgrad, ag, mg, qkvg,
        no_send, no_recv, ig_own, dy_send,
        no_all, mix_all, qgt, qt_all, agt, agt_all, small_send, small_in, small_all, small_sib,
        x_send, rs_buf, rs_in, relay_buf,
        wsem, ss, rs,
    ) = refs
    bf = jnp.bfloat16
    f32 = jnp.float32
    micro, length, width = tok_ref.shape
    experts = lay.experts
    cap = lay.cap
    cols = outw_ref.shape[0]
    pairs = cols // 128
    ffn = up_ref.shape[1]
    slots = experts * cap
    half = width // 2
    s = lax.axis_index("section")
    d = lax.axis_index("dp")
    t = lax.axis_index("tensor")
    u = 1 - t
    sib = (s, d, u)
    across = (1 - s, d, t)
    bits = [lax.rem(d // bit, 2) for bit in (1, 2, 4)]

    def partner(flip):
        index = d
        for place, bit in enumerate((1, 2, 4)):
            index = index + (flip // bit) % 2 * (bit - 2 * bit * bits[place])
        return index

    peer = [partner(flip) for flip in (0, 4, 1, 6, 2, 5, 3, 7)]
    steps = range(1, experts)
    relayed = (5, 7)
    chunks = range(experts // 2)

    def pair(c):
        return pl.ds(2 * c, 2)

    def partner_at(k):
        c = k // 2
        return partner(c + (k % 2) * (4 + 2 * (c % 2) + c // 2 - c))


    def remote(src, dst, sem, device, k=0):
        return pltpu.make_async_remote_copy(
            src_ref=src,
            dst_ref=dst,
            send_sem=ss.at[sem[0]],
            recv_sem=rs.at[sem[1] + k],
            device_id=device,
            device_id_type=pl.DeviceIdType.MESH,
        )

    counter = [0, 0]

    def take(arrivals=1):
        pair_of = (counter[0], counter[1])
        counter[0] += 1
        counter[1] += arrivals
        return pair_of

    def all_sent(like, sem):
        remote(like, like, sem, sib).wait_send()

    def all_here(like, sem, k=0):
        remote(like, like, sem, sib, k).wait_recv()

    ring_hops = experts - 1
    sem_routes = take()
    sem_x = take()
    sem_relay = [take(len(relayed)) for _ in range(2)]
    sem_pass = [take(0) for _ in range(2)]
    sem_xf = take()
    sem_dy = take()
    sem_att = take()
    sem_eo = take(len(chunks))
    sem_cg = take(len(chunks))
    sem_ag = take()
    sem_no = take()
    sem_so = take()
    sem_ig = take()
    sem_dx = take(len(chunks))
    sem_dxf = take(len(chunks))
    sem_ddy = take(len(chunks))
    sem_ddyf = take(len(chunks))
    sem_re = take()
    sem_rc = take()
    sem_gg = take()
    sem_gg_core = take(len(chunks))
    sem_qgt = take(experts)
    sem_agt = take()
    sem_agtf = take()
    sem_small = take()
    sem_back = take()
    sem_sums = take()
    sem_noall = take()
    sem_ring_no = take(2 * ring_hops)
    sem_ring_mix = take(2 * ring_hops)
    sem_ring_sum = (take(0)[0], sem_ring_no[1])
    sem_ring_out = take(4 * ring_hops)
    assert tuple(counter) == lay.sems

    def block(index, rows):
        return pl.ds(pl.multiple_of(index * rows, rows), rows)

    place_y = lax.rem(d, 2)
    place_z = d // 2
    ring_at = place_z + place_y * (experts - 1 - 2 * place_z)

    def ring_device(position):
        p = lax.rem(position + 2 * experts, experts)
        return 2 * p + (p // (experts // 2)) * (2 * experts - 1 - 4 * p)

    def hops(number, direction):
        return experts // 2 - (number % 2 == (direction > 0))

    def hop_index(number, direction, k):
        return number * ring_hops + k + (0 if direction > 0 else hops(number, 1))

    def lines_of(amount):
        return [(number, direction) for number in range(amount) for direction in (1, -1)]

    def ring_gather(parts, at_half=None):
        def hop(number, direction, k):
            view, sem, first = parts[number]
            held = view(ring_device(ring_at - direction * k))
            index = hop_index(number, direction, k) - first * ring_hops
            return remote(held, held, sem, (s, ring_device(ring_at + direction), t), index)

        lines = lines_of(len(parts))
        for line in lines:
            hop(*line, 0).start()

        def one(k, carry):
            for line in lines:
                hop(*line, k - 1).wait_recv()
                hop(*line, k).start()
            return carry

        short = experts // 2 - 1
        lax.fori_loop(1, short, one, 0)
        if at_half is not None:
            at_half()
        for line in lines:
            hop(*line, short - 1).wait_recv()
            if hops(*line) > short:
                hop(*line, short).start()
        for line in lines:
            if hops(*line) > short:
                hop(*line, short).wait_recv()

    load_up = pltpu.make_async_copy(up_ref, upv, wsem.at[0])
    load_down = pltpu.make_async_copy(down_ref, downv, wsem.at[1])
    load_qkvw = pltpu.make_async_copy(qkvw_hbm, qkvw_ref, wsem.at[2])
    load_outw = pltpu.make_async_copy(outw_hbm, outw_ref, wsem.at[3])
    load_tok = pltpu.make_async_copy(tok_ref, xb, wsem.at[4])
    load_cot = pltpu.make_async_copy(cot_ref.at[t], dyb, wsem.at[4])

    @pl.when(s == 0)
    def _():
        load_tok.start()

    @pl.when(s == 1)
    def _():
        load_cot.start()

    load_qkvw.start()
    load_outw.start()
    load_up.start()
    load_down.start()

    barrier = pltpu.get_barrier_semaphore()
    for k in steps:
        pl.semaphore_signal(barrier, inc=1, device_id=(s, peer[k], t), device_id_type=pl.DeviceIdType.MESH)
    pl.semaphore_signal(barrier, inc=1, device_id=sib, device_id_type=pl.DeviceIdType.MESH)
    for k in range(experts):
        pl.semaphore_signal(barrier, inc=1, device_id=(1 - s, peer[k], t), device_id_type=pl.DeviceIdType.MESH)
    pl.semaphore_wait(barrier, 2 * experts)

    for k in steps:
        remote(routes_ref, rr.at[k], sem_routes, (s, peer[k], t)).start()
    rr[0] = routes_ref[...]

    lanes8 = lax.broadcasted_iota(jnp.int32, (experts, length), 0)
    row_at = lax.broadcasted_iota(jnp.int32, (length, length), 0)
    col_at = lax.broadcasted_iota(jnp.int32, (length, length), 1)
    before = (row_at < col_at).astype(bf)
    slot_at = lax.broadcasted_iota(jnp.int32, (cap, length), 0).astype(f32)

    expert_of = jnp.zeros((experts, length), jnp.int32)
    for k in range(experts):
        expert_of = jnp.where(lanes8 == k, peer[k], expert_of)
    turn = (lax.broadcasted_iota(jnp.int32, (experts, experts), 1) == expert_of[:, 0:experts]).astype(f32).astype(bf)
    wrp[...] = nn(turn, wr_ref[...]).astype(bf)
    own_routes = routes_ref[t]
    hits = (expert_of == own_routes[0:1, :]) | (expert_of == own_routes[1:2, :])
    hit_f = hits.astype(f32)
    hit_t[...] = hit_f
    spot = jnp.where(hits, nn(hit_f.astype(bf), before), -1.0)
    for e in range(experts):
        place[e * cap : (e + 1) * cap, :] = (slot_at == spot[e : e + 1, :]).astype(f32).astype(bf)

    def to_relay(source, k, leg):
        i = relayed.index(k)
        return remote(source, relay_buf.at[leg * len(relayed) + i], sem_relay[leg], across, i)

    def relay(landing, sem, leg):
        for i, k in enumerate(relayed):
            held = relay_buf.at[leg * len(relayed) + i]
            all_here(held, sem_relay[leg], i)
            through = (sem_pass[leg][0], sem[1] + k // 2)
            remote(held, landing.at[k, t], through, (0, peer[k], t)).start()

    def dispatch(rows, send, landing, sem, sem_fwd, leg=None, both=False):
        send[...] = nn(place[...], rows).astype(bf).reshape(send.shape)

        def direct(k):
            remote(send.at[k], landing.at[k, t], sem, (s, peer[k], t), k // 2).start()

        def start_relayed():
            for k in relayed:
                to_relay(send.at[k], k, leg).start()

        def start_direct():
            for k in relayed:
                direct(k)

        direct(1)
        if both:
            pl.when(s == 0)(start_relayed)
        elif leg is not None:
            start_relayed()
        for k in steps[1:]:
            if k not in relayed:
                direct(k)
        if both:
            pl.when(s == 1)(start_direct)
        elif leg is None:
            start_direct()
        landing[0, t] = send[0]

        def arrive(c):
            held = landing.at[pair(c), t]
            all_here(landing.at[1, t] if isinstance(c, int) and c == 0 else held, sem, c)
            remote(held, held, sem_fwd, sib, c).start()

        def joined(c):
            all_here(landing.at[pair(c), t], sem_fwd, c)

        def drain(zero):
            all_sent(send, sem_fwd)
            if zero:
                all_sent(send.at[0 : experts - 1 - len(relayed)], sem)
                all_sent(send.at[0 : len(relayed)], sem_relay[leg])
            else:
                all_sent(send.at[1:experts], sem)

        return arrive, joined, drain

    def stream(dispatched, first, second, finish_chunk, eager, zero):
        arrive, joined, drain = dispatched
        last = len(chunks) - 1
        arrive(0)
        joined(0)

        def one(c, carry):
            first(c)
            if eager:
                pl.when(c > 0)(lambda: finish_chunk(c - 1))
                pl.when(c < last)(lambda: arrive(c + 1))
                second(c)
            else:
                second(c)

                @pl.when(c < last)
                def _():
                    arrive(c + 1)
                    finish_chunk(c)


            @pl.when(c < last)
            def _():
                joined(c + 1)

            return carry

        lax.fori_loop(0, len(chunks), one, 0)
        finish_chunk(last)
        drain(zero)

    def other_experts():
        all_here(rr.at[1:experts], sem_routes)

        def one(i, carry):
            q = i // micro
            m = i % micro
            pair = rr[q, m]
            first = pair[0:1, :] == d
            mine = first | (pair[1:2, :] == d)
            mine_f = jnp.broadcast_to(mine.astype(f32), (experts, length))
            spots = jnp.where(mine_f > 0.0, nn(mine_f.astype(bf), before), -1.0)
            where_slot = (slot_at == spots[0:1, :]).astype(f32).astype(bf)
            partner = jnp.where(first, pair[1:2, :], pair[0:1, :])
            partner_hot = (lanes8 == partner).astype(f32).astype(bf)
            other[q, m] = nt(where_slot, partner_hot)
            return carry

        lax.fori_loop(0, experts * micro, one, 0)

    @pl.when(s == 0)
    def _():
        load_tok.wait()

    @pl.when(s == 1)
    def _():
        load_cot.wait()
        relay(xrows, sem_dx, 0)
        other_experts()
        arrive, joined, drain = dispatch(dyb[...], disp_y, dyrows, sem_ddy, sem_ddyf)

        def pass_one(c, carry):
            arrive(c)
            return carry

        def join_one(c, carry):
            joined(c)
            return carry

        arrive(0)
        lax.fori_loop(1, len(chunks), pass_one, 0)
        lax.fori_loop(0, len(chunks), join_one, 0)
        drain(False)

    dist_rows = (
        lax.broadcasted_iota(jnp.int32, (lay.buckets, length), 0) == dist_ref[...]
    ).astype(f32).astype(bf)
    bias_rows = nn(relb_ref[...], dist_rows).astype(bf)
    mirror = ((row_at + col_at == length) | (row_at + col_at == 0)).astype(f32).astype(bf)
    bias_back = nn(bias_rows, mirror)
    for m in range(micro):
        seg_rows = jnp.broadcast_to(seg_ref[m : m + 1, :].astype(f32), (length, length))
        pads = jnp.broadcast_to(pad_ref[m : m + 1, :], (length, length))
        allowed = (col_at <= row_at) & (seg_rows == jnp.transpose(seg_rows))
        allowed = allowed & ((pads == 1) | (col_at == row_at))
        for p in range(pairs):
            for h in range(2):
                head = 2 * p + h
                grid = pltpu.roll(
                    jnp.broadcast_to(bias_back[head : head + 1, :], (length, length)), 0, 1, stride=1, stride_axis=0
                )
                bias_buf[m, p, :, h * length : (h + 1) * length] = jnp.where(allowed, grid, masked_score)

    x_copy = remote(x_send, xb.at[t], sem_x, across)
    dy_copy = remote(dy_send, dyb, sem_dy, across)
    x_forward = remote(xb.at[t], xb.at[t], sem_xf, sib)

    def spread_gates(gates_ref):
        return jnp.concatenate(
            [
                jnp.broadcast_to(gates_ref[e : e + 1, :], (cap, length)) * place[e * cap : (e + 1) * cap, :].astype(f32)
                for e in range(experts)
            ],
            axis=0,
        ).astype(bf)

    @pl.when(s == 1)
    def _():
        x_copy.wait_recv()
        x_forward.start()

    load_qkvw.wait()
    load_outw.wait()
    gain_one = gains_ref[0:1, :].astype(f32)
    gain_two = gains_ref[1:2, :].astype(f32)
    low_lanes = lax.broadcasted_iota(jnp.int32, (length, 128), 1) < 64

    def both_heads(pair_block):
        zero = jnp.zeros((), bf)
        return jnp.concatenate(
            [jnp.where(low_lanes, pair_block, zero), jnp.where(low_lanes, zero, pair_block)], axis=0
        )

    def attend(m):
        x_rows = xb[m].astype(f32)
        no1[m] = (x_rows * inverse_rms(x_rows) * gain_one).astype(bf)
        for c in range(3):
            qkvb[c, m] = nn(no1[m], qkvw_ref[c]).astype(bf)
        for p in range(pairs):
            at = slice(p * 128, (p + 1) * 128)
            scores = 0.125 * nt(qkvb[0, m, :, at], both_heads(qkvb[1, m, :, at])) + bias_buf[m, p]
            for h in range(2):
                part = scores[:, h * length : (h + 1) * length]
                terms = jnp.exp(part - jnp.max(part, axis=-1, keepdims=True))
                probs_buf[m, p, :, h * length : (h + 1) * length] = terms * (
                    1.0 / jnp.sum(terms, axis=-1, keepdims=True)
                )
            mixed[m, :, at] = nn(probs_buf[m, p].astype(bf), both_heads(qkvb[2, m, :, at])).astype(bf)

    att_copy = remote(att_send, att_recv, sem_att, sib)

    def project_other():
        att_send[...] = nn(mixed[u], outw_ref[...])
        att_copy.start()

    begin = u + s * (t - u)

    def attend_one(i, carry):
        @pl.when((s == 1) & (i == 1))
        def _():
            x_forward.wait()

        attend(begin + i * (1 - 2 * begin))

        @pl.when((s == 0) & (i == 0))
        def _():
            project_other()

        return carry

    lax.fori_loop(0, micro, attend_one, 0)

    @pl.when(s == 1)
    def _():
        project_other()

    part_own = nn(mixed[t], outw_ref[...])
    att_copy.wait()
    middle = xb[t].astype(f32) + part_own + att_recv[...]
    mid[...] = middle
    ntb[...] = (middle * inverse_rms(middle) * gain_two).astype(bf)
    logits_t = jnp.where(hit_t[...] > 0.0, nt(wrp[...], ntb[...]), masked_score)
    terms = jnp.exp(logits_t - jnp.max(logits_t, axis=0, keepdims=True))
    gate_t[...] = terms / jnp.sum(terms, axis=0, keepdims=True)

    arrivals = dispatch(ntb[...], disp_x, xrows, sem_dx, sem_dxf, 0, True)
    load_up.wait()
    load_down.wait()
    rows_of = 2 * micro * cap

    def flat(ref, chunk):
        return ref[chunk].reshape(rows_of, ref.shape[-1])

    def front_chunk(c):
        value, slope = gelu_parts(nn(flat(xrows, pair(c)), upv[...]))
        hidden[pair(c)] = value.astype(bf).reshape(2, micro, cap, ffn)
        dgelu[pair(c)] = slope.astype(bf).reshape(2, micro, cap, ffn)

    def split_sum(c, total, send, recv, base):
        for m in range(micro):
            halves[m] = total.reshape(2, micro, cap, width)[:, m]
        send[pair(c)] = halves[u].astype(bf)
        remote(send.at[pair(c)], recv.at[pair(c)], base, sib, c).start()

    def hand_back(c, send, recv, base, total, landing, base_back):
        all_here(recv.at[pair(c)], base, c)
        total[pair(c)] = (halves[t] + recv[pair(c)].astype(f32)).astype(bf)

        def give(k):
            remote(total.at[k], landing.at[k], base_back, (s, partner_at(k), t)).start()

        def keep():
            landing[0] = total[0]

        if isinstance(c, int):
            give(2 * c)
        else:
            pl.when(c == 0)(keep)
            pl.when(c > 0)(lambda: give(2 * c))
        give(2 * c + 1)

    def wait_back(total, landing, sem):
        all_here(landing.at[1:experts], sem)
        all_sent(total.at[1:experts], sem)

    def rows_chunk(c):
        split_sum(c, nn(flat(hidden, pair(c)), downv[...]), eo_send, eo_recv, sem_eo)

    def rows_finish(c):
        hand_back(c, eo_send, eo_recv, sem_eo, eob, eoret, sem_re)

    mine_hot = (lax.broadcasted_iota(jnp.int32, (rows_of, experts), 1) == d).astype(f32)

    ones = jnp.ones((8, ffn), bf)
    gg_part[...] = jnp.zeros_like(gg_part)

    def slope_chunk(c):
        slot_logits = nt(flat(xrows, pair(c)), wr_ref[...])
        own_logit = jnp.sum(slot_logits * mine_hot, axis=-1, keepdims=True)
        other_logit = jnp.sum(slot_logits * flat(other, pair(c)), axis=-1, keepdims=True)
        gate = 1.0 / (1.0 + jnp.exp(other_logit - own_logit))
        dy_flat = flat(dyrows, pair(c))
        og[pair(c)] = (dy_flat.astype(f32) * gate).astype(bf).reshape(2, micro, cap, width)
        grad = nt(dy_flat, downv[...])
        pg[pair(c)] = (grad * gate * flat(dgelu, pair(c)).astype(f32)).astype(bf).reshape(2, micro, cap, ffn)
        product = (grad * flat(hidden, pair(c)).astype(f32)).astype(bf)
        for i in range(2):
            for m in range(micro):
                at = (i * micro + m) * cap
                gg_part[m, 2 * c + i, :, 0:cap] = nt(ones, product[at : at + cap])

    def back_chunk(c):
        remote(gg_part.at[u, pair(c)], gg_other.at[pair(c)], sem_gg_core, sib, c).start()
        split_sum(c, nt(flat(pg, pair(c)), upv[...]), cg_send, cg_recv, sem_cg)

    def both_chunk(c):
        front_chunk(c)
        slope_chunk(c)

    def back_finish(c):
        hand_back(c, cg_send, cg_recv, sem_cg, cgb, cgret, sem_rc)
        all_here(gg_other.at[pair(c)], sem_gg_core, c)
        gg_send[pair(c)] = gg_part[t, pair(c)] + gg_other[pair(c)]

        def give(k):
            remote(gg_send.at[k], gg_recv.at[k], sem_gg, (s, partner_at(k), t)).start()

        def keep():
            gg_recv[0] = gg_send[0]

        if isinstance(c, int):
            give(2 * c)
        else:
            pl.when(c == 0)(keep)
            pl.when(c > 0)(lambda: give(2 * c))
        give(2 * c + 1)

    def hidden_of(m):
        return jnp.concatenate([hidden[k, m] for k in range(experts)], axis=0)

    def expert_rows():
        eo_send[...] = nn(hidden_of(u), downv[...]).astype(bf).reshape(eo_send.shape)
        eo_copy = remote(eo_send, eo_recv, sem_eo, sib)
        eo_copy.start()
        total = nn(hidden_of(t), downv[...])
        eo_copy.wait_recv()
        eob[...] = (total + eo_recv[...].astype(f32).reshape(slots, width)).astype(bf).reshape(eob.shape)

    def send_back(source, landing, base):
        for k in steps:
            remote(source.at[k], landing.at[k], base, (s, peer[k], t)).start()
        landing[0] = source[0]

    def layer_output():
        result = mid[...] + tn(spread_gates(gate_t), eoret[...].reshape(slots, width))
        out_own[...] = result
        return result

    def own_half():
        return pl.ds(pl.multiple_of(t * half, half), half)

    def other_half():
        return pl.ds(pl.multiple_of(u * half, half), half)

    def hand_out(rows_ref, out_ref, index):
        copy = remote(rows_ref.at[:, other_half()], out_ref.at[t], index, sib)
        copy.start()
        out_ref[t] = rows_ref[:, own_half()]
        copy.wait()

    def gather_factors():
        no_all[t, d] = no1[t]
        mix_all[d] = mixed[...]
        ring_gather(
            [
                (lambda q: no_all.at[t, q, 0 : length // 2], sem_ring_no, 0),
                (lambda q: no_all.at[t, q, length // 2 : length], sem_ring_no, 0),
                (lambda q: mix_all.at[q, 0], sem_ring_mix, 2),
                (lambda q: mix_all.at[q, 1], sem_ring_mix, 2),
            ]
        )
        all_sent(no_all.at[t, 1:experts], sem_ring_no)
        all_sent(mix_all.at[1:experts], sem_ring_mix)
        copy = remote(no_all.at[t], no_all.at[t], sem_noall, sib)
        copy.start()
        copy.wait()

    @pl.when(s == 0)
    def _():
        stream(arrivals, front_chunk, rows_chunk, rows_finish, True, True)
        wait_back(eob, eoret, sem_re)
        x_send[...] = layer_output().astype(bf)
        x_copy.start()
        hand_out(out_own, secout_ref, sem_so)
        other_experts()
        gather_factors()
        x_copy.wait_send()
        dy_copy.wait_recv()
        arrivals_y = dispatch(dyb[...], disp_y, dyrows, sem_ddy, sem_ddyf, 1)
        stream(arrivals_y, slope_chunk, back_chunk, back_finish, True, True)

    @pl.when(s == 1)
    def _():
        stream(arrivals, both_chunk, back_chunk, back_finish, True, False)
        expert_rows()

    wait_back(gg_send, gg_recv, sem_gg)
    wait_back(cgb, cgret, sem_rc)

    @pl.when(s == 1)
    def _():
        send_back(eob, eoret, sem_re)


    gg_rows = []
    for e in range(experts):
        high, low = split_low(gg_recv[e][:, 0:cap])
        spot_rows = place[e * cap : (e + 1) * cap, :]
        gg_rows.append((nn(high, spot_rows) + nn(low, spot_rows))[0:1, :])
    gate_grad = jnp.concatenate(gg_rows, axis=0)
    gates = gate_t[...]
    logit_grad = (gates * (gate_grad - jnp.sum(gates * gate_grad, axis=0, keepdims=True))).astype(bf)
    router_grad = nn(tn(turn, logit_grad).astype(bf), ntb[...])
    two_grad = tn(logit_grad, wrp[...]) + tn(place[...], cgret[...].reshape(slots, width))
    dy = dyb[...].astype(f32)
    middle = mid[...]
    scale = inverse_rms(middle)
    normed = middle * scale
    gain_two_grad = jnp.sum(two_grad * normed, axis=0, keepdims=True)
    groups = width // 128
    small_send[...] = jnp.zeros_like(small_send)
    for g in range(groups):
        small_send[g, 0:experts, :] = router_grad[:, g * 128 : (g + 1) * 128]
        small_send[g, experts + 1 : experts + 2, :] = gain_two_grad[:, g * 128 : (g + 1) * 128]
    scaled = two_grad * gain_two
    middle_grad = dy + scale * (scaled - normed * jnp.mean(scaled * normed, axis=-1, keepdims=True))
    mgrad[...] = middle_grad
    ag[t] = middle_grad.astype(bf)
    ag_copy = remote(ag.at[t], ag.at[t], sem_ag, sib)
    ag_copy.start()

    agt_rows = width // experts
    agt_own = remote(agt.at[block(d, agt_rows)], agt_all.at[d, t], sem_agtf, sib)

    @pl.when(s == 0)
    def _():
        agt[...] = jnp.transpose(ag[t])
        for k in reversed(steps):
            remote(agt.at[block(peer[k], agt_rows)], agt_all.at[d, t], sem_agt, (s, peer[k], t)).start()
        agt_all[d, t] = agt[block(d, agt_rows), :]
        agt_own.start()

    def attend_back(m, lane_of_m):
        mg[m] = nt(ag[m], outw_ref[...]).astype(bf)
        for p in range(pairs):
            at = slice(p * 128, (p + 1) * 128)
            mg_pair = mg[m, :, at]
            probs = probs_buf[m, p]
            keys2 = both_heads(qkvb[1, m, :, at])
            queries2 = both_heads(qkvb[0, m, :, at])
            mg2 = both_heads(mg_pair)
            prob_grad = nt(mg_pair, both_heads(qkvb[2, m, :, at]))
            raws = []
            key_grad = jnp.zeros((length, 128), f32)
            value_grad = jnp.zeros((length, 128), f32)
            for h in range(2):
                lane = slice(h * length, (h + 1) * length)
                part = probs[:, lane]
                step = prob_grad[:, lane]
                score_grad = part * (step - jnp.sum(part * step, axis=-1, keepdims=True))
                score_sum[2 * p + h] += score_grad
                raw = (0.125 * score_grad).astype(bf)
                raws.append(raw)
                key_grad = key_grad + tn(raw, queries2[h * length : (h + 1) * length])
                value_grad = value_grad + tn(part.astype(bf), mg2[h * length : (h + 1) * length])
            query_grad = nn(jnp.concatenate(raws, axis=1), keys2)
            for c, grad in enumerate((query_grad, key_grad, value_grad)):
                qkvg[c, m, :, at] = grad.astype(bf)

        @pl.when(s == 0)
        def _():
            for c in range(3):
                qgt[c * cols : (c + 1) * cols, lane_of_m] = jnp.transpose(qkvg[c, m])

    score_sum[...] = jnp.zeros_like(score_sum)

    def back_one(i, carry):
        @pl.when(i == 1)
        def _():
            ag_copy.wait()

        attend_back(t + i * (u - t), pl.ds(pl.multiple_of(i * length, length), length))
        return carry

    lax.fori_loop(0, micro, back_one, 0)
    qgt_rows = 3 * cols // experts
    @pl.when(s == 0)
    def _():
        for k in reversed(steps):
            remote(qgt.at[block(peer[k], qgt_rows)], qt_all.at[d], sem_qgt, (s, peer[k], t), k).start()
        qt_all[d] = qgt[block(d, qgt_rows), :]

    def project_back(m):
        total = nt(qkvg[0, m], qkvw_ref[0])
        for c in range(1, 3):
            total = total + nt(qkvg[c, m], qkvw_ref[c])
        return total

    no_send[...] = project_back(u).astype(bf)
    no_copy = remote(no_send, no_recv, sem_no, sib)
    no_copy.start()
    one_grad = project_back(t)
    no_copy.wait()
    one_grad = one_grad + no_recv[...].astype(f32)
    x_rows = xb[t].astype(f32)
    scale = inverse_rms(x_rows)
    normed = x_rows * scale
    gain_one_grad = jnp.sum(one_grad * normed, axis=0, keepdims=True)
    scaled = one_grad * gain_one
    input_grad = mgrad[...] + scale * (scaled - normed * jnp.mean(scaled * normed, axis=-1, keepdims=True))
    ig_own[...] = input_grad
    dy_send[...] = input_grad.astype(bf)

    @pl.when(s == 1)
    def _():
        dy_copy.start()

    hand_out(ig_own, ingrad_ref, sem_ig)

    sums = []
    for head in range(2 * pairs):
        high, low = split_low(score_sum[head])
        turned = pltpu.roll(nn(high, mirror) + nn(low, mirror), 0, 1, stride=1, stride_axis=0)
        sums.append(jnp.sum(turned, axis=0, keepdims=True))
    high, low = split_low(jnp.concatenate(sums, axis=0))
    small_send[groups, 0 : 2 * pairs, 0 : lay.buckets] = nt(high, dist_rows) + nt(low, dist_rows)
    for g in range(groups):
        small_send[g, experts : experts + 1, :] = gain_one_grad[:, g * 128 : (g + 1) * 128]
    for k in steps:
        remote(small_send.at[peer[k]], small_in.at[k], sem_small, (s, peer[k], t)).start()
    small_in[0] = small_send[d]

    wide = lay.wide
    every = micro * slots

    def expert_grads(n, carry):
        at = pl.ds(pl.multiple_of(n * wide, wide), wide)
        guv[:, at] = tn(xrows[...].reshape(every, width), pg[:, :, :, at].reshape(every, wide)).astype(bf)
        gdv[at, :] = tn(hidden[:, :, :, at].reshape(every, wide), og[...].reshape(every, width)).astype(bf)
        return carry

    lax.fori_loop(0, ffn // wide, expert_grads, 0)

    qkv_rows = 3 * cols // experts
    share = shared_ref.shape[1] // 4
    parts = [slice(c * share, (c + 1) * share) for c in range(4)]

    def pack_out(total):
        half_rows = agt_rows // 2
        return jnp.concatenate([total[..., 0:half_rows, :], total[..., half_rows:, :]], axis=-1).astype(bf)

    @pl.when(s == 0)
    def _():
        all_here(agt_all.at[1:experts, 0], sem_agt)
        for k in steps:
            held = agt_all.at[peer[k], t]
            remote(held, held, sem_agtf, sib).start()
        all_here(agt_all.at[:, 0], sem_agtf)
        all_sent(agt_all.at[1:experts, 0], sem_agt)
        all_sent(agt_all.at[:, 0], sem_agtf)
        total = jnp.zeros((agt_rows, cols), f32)
        for q in range(experts):
            for m in range(micro):
                total = total + nn(agt_all[q, m], mix_all[q, m])
        shared_ref[d, qkv_rows:, :] = pack_out(total)

        def qkv_slice(q):
            return nn(qt_all[q], jnp.concatenate([no_all[t, q], no_all[u, q]], axis=0))

        total = qkv_slice(d)
        for k in reversed(steps):
            all_here(qt_all.at[0], sem_qgt, k)
            total = total + qkv_slice(peer[k])
        all_sent(qt_all.at[1:experts], sem_qgt)
        shared_ref[d, 0:qkv_rows, :] = total.astype(bf)

    @pl.when(s == 1)
    def _():
        normed_rows = no1[...].reshape(micro * length, width)
        own = jnp.concatenate([tn(qkvg[c].reshape(micro * length, cols), normed_rows) for c in range(3)], axis=0)
        rs_buf[:, 0:qkv_rows, :] = own.astype(bf).reshape(experts, qkv_rows, width)
        own = tn(ag[...].reshape(micro * length, width), mixed[...].reshape(micro * length, cols))
        rs_buf[:, qkv_rows:, :] = pack_out(own.reshape(experts, agt_rows, cols))

        relay(dyrows, sem_ddy, 1)

        def owner_at(number, direction, k):
            return ring_device(ring_at + direction * (hops(number, direction) - k))

        def hop(number, direction, k):
            index = hop_index(number, direction, k)
            return remote(
                rs_buf.at[owner_at(number, direction, k), parts[number]],
                rs_in.at[index % ring_hops, parts[number]],
                sem_ring_sum,
                (s, ring_device(ring_at + direction), t),
                index,
            )

        lines = lines_of(len(parts))
        for k in range(experts // 2):
            for line in lines:
                if k < hops(*line):
                    if k > 0:
                        rows = parts[line[0]]
                        owner = owner_at(*line, k)
                        hop(*line, k - 1).wait_recv()
                        came = rs_in[hop_index(*line, k - 1) % ring_hops, rows, :].astype(f32)
                        rs_buf[owner, rows, :] = (rs_buf[owner, rows, :].astype(f32) + came).astype(bf)
                    hop(*line, k).start()
        for number, rows in enumerate(parts):
            total = rs_buf[d, rows, :].astype(f32)
            for direction in (1, -1):
                last = hops(number, direction) - 1
                hop(number, direction, last).wait_recv()
                total = total + rs_in[hop_index(number, direction, last) % ring_hops, rows, :].astype(f32)
            shared_ref[d, rows, :] = total.astype(bf)

    all_here(small_in.at[1:experts], sem_small)
    small_total = small_in[0]
    for k in steps:
        small_total = small_total + small_in[k]
    small_all[d] = small_total
    for k in steps:
        remote(small_all.at[d], small_all.at[d], sem_back, (s, peer[k], t)).start()

    sums_copy = remote(small_all, small_sib, sem_sums, sib)

    def pass_sums():
        all_here(small_all.at[1:experts], sem_back)
        sums_copy.start()


    streams = [
        (lambda q, rows=rows: shared_ref.at[q, rows], sem_ring_out, 0) for rows in parts
    ]

    ring_gather(streams, pass_sums)
    sums_copy.wait_recv()
    for g in range(groups):
        lanes = slice(g * 128, (g + 1) * 128)
        grouter_ref[:, lanes] = small_all[g, 0:experts, :] + small_sib[g, 0:experts, :]
        ggain_ref[:, lanes] = small_all[g, experts : experts + 2, :] + small_sib[g, experts : experts + 2, :]
    gbias_ref[...] = small_all[groups, 0 : 2 * pairs, :]
    @pl.when(s == 1)
    def _():
        dy_copy.wait_send()
        for sem in sem_pass:
            all_sent(relay_buf.at[0 : len(relayed)], sem)
        all_sent(rs_in, sem_ring_sum)
        wait_back(eob, eoret, sem_re)
        layer_output()
        hand_out(out_own, secout_ref, sem_so)

    all_sent(rr.at[1:experts], sem_routes)
    all_sent(eo_send, sem_eo)
    all_sent(cg_send, sem_cg)
    all_sent(gg_part.at[0], sem_gg_core)
    all_sent(small_in.at[1:experts], sem_small)
    all_sent(small_all.at[1:experts], sem_back)
    all_sent(small_all, sem_sums)
    all_sent(shared_ref.at[1:experts], sem_ring_out)


def widen_kernel(
    sec_ref, ing_ref, gain_ref, shared_ref, bias_ref, router_ref, up_ref, down_ref,
    sec_out, ing_out, gain_out, bias_out, router_out, qkv_out, out_out, up_out, down_out,
    up_wide, down_wide, qkv_wide, out_wide, bias_wide, out_sem,
):
    f32 = jnp.float32
    parts = 3
    experts, shared_rows, width = shared_ref.shape
    cols = out_wide.shape[0]
    qkv_rows = 3 * cols // experts
    wide = ((up_ref, up_wide, up_out), (down_ref, down_wide, down_out))
    stores = []

    def store(src, dst):
        copy = pltpu.make_async_copy(src, dst, out_sem.at[len(stores)])
        copy.start()
        stores.append(copy)

    def widen(i, n):
        src, dst, out = wide[i]
        size = src.shape[0] // parts
        rows = pl.ds(n * size, size)
        dst[rows, :] = src[rows, :].astype(f32)
        store(dst.at[rows], out.at[rows])

    def turn_qkv(c):
        block = shared_ref[:, 0:qkv_rows, :].reshape(3 * cols, width)[c * cols : (c + 1) * cols]
        qkv_wide[c] = jnp.transpose(block.astype(f32))
        store(qkv_wide.at[c], qkv_out.at[c])

    widen(0, 0)
    store(sec_ref, sec_out)
    store(ing_ref, ing_out)
    store(gain_ref, gain_out)
    store(router_ref, router_out)
    for h in range(bias_wide.shape[0]):
        bias_wide[h] = bias_ref[h : h + 1, 0 : bias_wide.shape[2]]
    store(bias_wide, bias_out)
    widen(0, 1)
    turn_qkv(0)
    widen(0, 2)
    turn_qkv(1)
    widen(1, 0)
    turn_qkv(2)
    widen(1, 1)
    out_block = jnp.concatenate(
        [
            shared_ref[e, qkv_rows:, h * cols : (h + 1) * cols].astype(f32)
            for e in range(experts)
            for h in range(2)
        ],
        axis=0,
    )
    out_wide[...] = jnp.transpose(out_block)
    store(out_wide, out_out)
    widen(1, 2)
    for copy in stores:
        copy.wait()


def fused_local(
    tokens,
    cotangent,
    segments,
    pad_mask,
    routes,
    dist_bucket,
    norm_gains,
    qkv_weight,
    out_weight,
    rel_bias,
    router_weight,
    expert_up,
    expert_down,
):
    micro, _, length, width = tokens.shape
    experts = router_weight.shape[2]
    cap = max(2, 3 * length // experts)
    cols = out_weight.shape[1]
    heads = rel_bias.shape[2]
    ffn = expert_up.shape[3]
    slots = experts * cap
    pairs = cols // 128
    shared_rows = 3 * cols // experts + width // experts // 2
    lay = Layout()
    lay.experts = experts
    lay.cap = cap
    lay.buckets = rel_bias.shape[1]
    lay.wide = min(ffn, 256)
    chunks = experts // 2
    lay.sems = (34, 7 * chunks + experts + 8 * (experts - 1) + 22)
    bf = jnp.bfloat16
    f32 = jnp.float32
    vm = pltpu.VMEM
    shape = jax.ShapeDtypeStruct
    dma = pltpu.SemaphoreType.DMA
    scratch = [
        vm((width, ffn), bf),
        vm((ffn, width), bf),
        vm((3, width, cols), bf),
        vm((cols, width), bf),
        vm((micro, length, width), bf),
        vm((length, width), bf),
        vm((experts, micro, 2, length), jnp.int32),
        vm((slots, length), bf),
        vm((micro, pairs, length, 2 * length), f32),
        vm((micro, pairs, length, 2 * length), f32),
        vm((micro, length, width), bf),
        vm((3, micro, length, cols), bf),
        vm((micro, length, cols), bf),
        vm((length, width), f32),
        vm((length, width), f32),
        vm((length, width), f32),
        vm((length, width), bf),
        vm((experts, length), f32),
        vm((experts, length), f32),
        vm((experts, width), bf),
        vm((2 * pairs, length, length), f32),
        vm((experts, cap, width), bf),
        vm((experts, micro, cap, width), bf),
        vm((experts, cap, width), bf),
        vm((experts, micro, cap, width), bf),
        vm((experts, micro, cap, ffn), bf),
        vm((experts, micro, cap, ffn), bf),
        vm((micro, 2, cap, width), f32),
        vm((experts, cap, width), bf),
        vm((experts, cap, width), bf),
        vm((experts, cap, width), bf),
        vm((experts, cap, width), bf),
        vm((length, width), f32),
        vm((experts, micro, cap, experts), f32),
        vm((experts, micro, cap, width), bf),
        vm((micro, experts, 8, 128), f32),
        vm((experts, 8, 128), f32),
        vm((experts, 8, 128), f32),
        vm((experts, 8, 128), f32),
        vm((experts, micro, cap, ffn), bf),
        vm((experts, cap, width), bf),
        vm((experts, cap, width), bf),
        vm((experts, cap, width), bf),
        vm((experts, cap, width), bf),
        vm((length, width), f32),
        vm((micro, length, width), bf),
        vm((micro, length, cols), bf),
        vm((3, micro, length, cols), bf),
        vm((length, width), bf),
        vm((length, width), bf),
        vm((length, width), f32),
        vm((length, width), bf),
        vm((micro, experts, length, width), bf),
        vm((experts, micro, length, cols), bf),
        vm((3 * cols, micro * length), bf),
        vm((experts, 3 * cols // experts, micro * length), bf),
        vm((width, length), bf),
        vm((experts, micro, width // experts, length), bf),
        vm((experts, 2 * experts, 128), f32),
        vm((experts, 2 * experts, 128), f32),
        vm((experts, 2 * experts, 128), f32),
        vm((experts, 2 * experts, 128), f32),
        vm((length, width), bf),
        vm((experts, shared_rows, width), bf),
        vm((experts - 1, shared_rows, width), bf),
        vm((4, cap, width), bf),
        dma((5,)),
        dma((lay.sems[0],)),
        dma((lay.sems[1],)),
    ]
    whole = pl.BlockSpec(memory_space=pltpu.VMEM)
    anywhere = pl.BlockSpec(memory_space=pl.ANY)
    out_shape = (
        vm((micro, length, width // 2), f32),
        vm((micro, length, width // 2), f32),
        vm((2, width), f32),
        vm((experts, shared_rows, width), bf),
        vm((heads, 128), f32),
        vm((experts, width), f32),
        vm((width, ffn), bf),
        vm((ffn, width), bf),
    )
    results = pl.pallas_call(
        partial(layer_kernel, lay),
        out_shape=out_shape,
        in_specs=[anywhere] * 2 + [whole] * 5 + [anywhere] * 2 + [whole] * 2 + [anywhere] * 2,
        out_specs=[whole] * 8,
        scratch_shapes=scratch,
        name="two_sections",
        compiler_params=pltpu.CompilerParams(
            collective_id=0, has_side_effects=True, vmem_limit_bytes=54 * 1024 * 1024
        ),
    )(
        tokens[:, 0],
        cotangent[:, 0],
        segments[:, 0],
        pad_mask[:, 0],
        routes[:, 0].transpose(0, 2, 1),
        dist_bucket[None],
        norm_gains[0],
        qkv_weight[0].transpose(1, 0, 2),
        out_weight[0],
        rel_bias[0].T,
        router_weight[0].T,
        expert_up[0, 0],
        expert_down[0, 0],
    )
    section_out, input_grads, gains, bias, router, qkv, out, up, down = pl.pallas_call(
        widen_kernel,
        out_shape=(
            shape((micro, length, width // 2), f32),
            shape((micro, length, width // 2), f32),
            shape((2, width), f32),
            shape((heads, 1, lay.buckets), f32),
            shape((experts, width), f32),
            shape((3, width, cols), f32),
            shape((cols, width), f32),
            shape((width, ffn), f32),
            shape((ffn, width), f32),
        ),
        in_specs=[whole] * 8,
        out_specs=[anywhere] * 9,
        scratch_shapes=[
            vm((width, ffn), f32),
            vm((ffn, width), f32),
            vm((3, width, cols), f32),
            vm((cols, width), f32),
            vm((heads, 1, lay.buckets), f32),
            dma((15,)),
        ],
        name="widen",
        compiler_params=pltpu.CompilerParams(vmem_limit_bytes=40 * 1024 * 1024),
    )(*[pltpu.with_memory_space_constraint(result, pltpu.VMEM) for result in results])
    return (
        section_out[None, :, None],
        input_grads[None, :, None],
        gains[None],
        qkv.transpose(1, 0, 2)[None],
        out[None],
        bias.transpose(1, 2, 0),
        router.T[None],
        up[None, None],
        down[None, None],
    )


def fits_kernel(mesh):
    return mesh.shape["section"] == 2 and mesh.shape["tensor"] == 2 and mesh.shape["dp"] == 8


def solution(mesh):
    in_specs = (
        P(None, "dp", None, None),
        P(None, "dp", None, None),
        P(None, "dp", None),
        P(None, "dp", None),
        P(None, "dp", None, None),
        P(),
        P("section", None, None),
        P("section", None, None, "tensor"),
        P("section", "tensor", None),
        P("section", None, "tensor"),
        P("section", None, None),
        P("section", "dp", None, "tensor"),
        P("section", "dp", "tensor", None),
    )
    out_specs = (
        P("section", None, "dp", None, "tensor"),
        P("section", None, "dp", None, "tensor"),
        P("section", None, None),
        P("section", None, None, "tensor"),
        P("section", "tensor", None),
        P("section", None, "tensor"),
        P("section", None, None),
        P("section", "dp", None, "tensor"),
        P("section", "dp", "tensor", None),
    )
    body = fused_local if fits_kernel(mesh) else local
    return jax.shard_map(body, mesh=mesh, in_specs=in_specs, out_specs=out_specs, check_vma=False)
```

```python
from functools import partial

import jax
import jax.numpy as jnp
from jax import lax
from jax.experimental import pallas as pl
from jax.experimental.pallas import tpu as pltpu
from jax.sharding import PartitionSpec as P

norm_eps = 1e-06
masked_score = -1e30
highest = lax.Precision.HIGHEST


def shifted(block, axis, distance):
    devices = range(lax.axis_size(axis))
    route = [(i - distance, i) for i in devices if i - distance in devices]
    return lax.ppermute(block, axis, route)


def normalize(values, gain_row):
    scale_inv = lax.rsqrt(jnp.mean(values * values, axis=-1, keepdims=True) + norm_eps)
    return values * scale_inv * gain_row


def normalize_back(values, gain_row, upstream):
    scale_inv = lax.rsqrt(jnp.mean(values * values, axis=-1, keepdims=True) + norm_eps)
    normed = values * scale_inv
    gain_grad = jnp.sum(upstream * normed, axis=0)
    scaled = upstream * gain_row
    input_grad = scale_inv * (scaled - normed * jnp.mean(scaled * normed, axis=-1, keepdims=True))
    return (input_grad, gain_grad)


def send_rows(rows):
    return lax.all_to_all(rows, "dp", split_axis=0, concat_axis=0, tiled=True)


def sum_slots(partial_rows):
    return lax.psum(partial_rows, "tensor")


def score_context(segment_row, pad_row, dist_bucket, bucket_count):
    length = segment_row.shape[0]
    places = jnp.arange(length, dtype=jnp.int32)
    offsets = jnp.clip(places[:, None] - places[None, :], 0, length - 1)
    bucket_grid = jnp.take(dist_bucket, offsets)
    bucket_onehot = (
        bucket_grid[:, :, None] == jnp.arange(bucket_count, dtype=jnp.int32)[None, None, :]
    ).astype(jnp.float32)
    allowed = (places[None, :] <= places[:, None]) & (segment_row[:, None] == segment_row[None, :])
    allowed = allowed & ((pad_row[None, :] == 1) | (places[None, :] == places[:, None]))
    return (bucket_onehot, allowed)


def attention_front(inputs, context, weights):
    segment_row, pad_row, route_rows, dist_bucket = context
    gain_pair, qkv_weight, out_weight, bias_table, router_weight, upper_weight, lower_weight = (
        weights
    )
    length = inputs.shape[0]
    head_count = bias_table.shape[1]
    bucket_onehot, allowed = score_context(segment_row, pad_row, dist_bucket, bias_table.shape[0])
    normed_one = normalize(inputs, gain_pair[0]).astype(jnp.bfloat16)
    qkv_rows = jnp.einsum(
        "ld,dch->lch", normed_one, qkv_weight, preferred_element_type=jnp.float32
    ).astype(jnp.bfloat16)
    head_dim = qkv_rows.shape[2] // head_count
    queries = qkv_rows[:, 0].reshape(length, head_count, head_dim)
    keys_in = qkv_rows[:, 1].reshape(length, head_count, head_dim)
    values_in = qkv_rows[:, 2].reshape(length, head_count, head_dim)
    raw_scores = jnp.einsum("qhd,khd->hqk", queries, keys_in, preferred_element_type=jnp.float32)
    bias_grid = jnp.einsum(
        "qkb,bh->hqk", bucket_onehot, bias_table.astype(jnp.float32), precision=highest
    )
    logits = jnp.where(allowed[None], 0.125 * raw_scores + bias_grid, masked_score)
    exp_terms = jnp.exp(logits - jnp.max(logits, axis=-1, keepdims=True))
    attn_probs = exp_terms / jnp.sum(exp_terms, axis=-1, keepdims=True)
    mixed_rows = jnp.einsum(
        "hqk,khd->qhd",
        attn_probs.astype(jnp.bfloat16),
        values_in,
        preferred_element_type=jnp.float32,
    )
    mixed_rows = mixed_rows.reshape(length, -1).astype(jnp.bfloat16)
    return (normed_one, queries, keys_in, values_in, attn_probs, mixed_rows, bucket_onehot)


def slot_tables(route_rows, experts, capacity):
    flat_routes = route_rows.reshape(-1)
    route_hits = (flat_routes[:, None] == jnp.arange(experts, dtype=jnp.int32)[None, :]).astype(
        jnp.int32
    )
    earlier = jnp.cumsum(route_hits, axis=0) - route_hits
    position = jnp.sum(earlier * route_hits, axis=1)
    target = flat_routes * capacity + position
    slot_hits = (
        jnp.arange(experts * capacity, dtype=jnp.int32)[:, None] == target[None, :]
    ).astype(jnp.int32)
    source = jnp.sum(slot_hits * jnp.arange(target.shape[0], dtype=jnp.int32)[None, :], axis=1)
    filled = jnp.sum(slot_hits, axis=1) > 0
    return (target, source, filled, route_hits)


def route_gates(normed_two, router_weight, route_hits):
    length = normed_two.shape[0]
    logits = jnp.dot(normed_two, router_weight, preferred_element_type=jnp.float32)
    route_onehot = route_hits.reshape(length, 2, -1).astype(jnp.float32)
    chosen = jnp.einsum("le,lre->lr", logits, route_onehot, precision=highest)
    return (jax.nn.softmax(chosen, axis=-1), route_onehot)


def gather_back(back_slots, target, length):
    flat_slots = back_slots.reshape(-1, back_slots.shape[-1])
    return jnp.take(flat_slots, target, axis=0).reshape(length, 2, -1)


def forward_rest(inputs, front, context, weights):
    segment_row, pad_row, route_rows, dist_bucket = context
    gain_pair, qkv_weight, out_weight, bias_table, router_weight, upper_weight, lower_weight = (
        weights
    )
    mixed_rows = front[5]
    length, model_width = inputs.shape
    experts = router_weight.shape[1]
    capacity = max(2, 3 * length // experts)
    local_experts = upper_weight.shape[0]
    attn_out = lax.psum(
        jnp.dot(mixed_rows, out_weight, preferred_element_type=jnp.float32), "tensor"
    )
    middle = inputs + attn_out
    normed_two = normalize(middle, gain_pair[1]).astype(jnp.bfloat16)
    target, source, filled, route_hits = slot_tables(route_rows, experts, capacity)
    outgoing = jnp.where(
        filled[:, None], jnp.take(normed_two, source // 2, axis=0), jnp.zeros((), jnp.bfloat16)
    )
    outgoing = outgoing.reshape(experts, capacity, model_width)
    arrived = send_rows(outgoing)
    grouped = arrived.reshape(-1, local_experts, capacity, model_width)
    pre_act = jnp.einsum(
        "secd,edf->secf", grouped, upper_weight, preferred_element_type=jnp.float32
    )
    hidden = jax.nn.gelu(pre_act, approximate=False).astype(jnp.bfloat16)
    partial_out = jnp.einsum(
        "secf,efd->secd", hidden, lower_weight, preferred_element_type=jnp.float32
    )
    summed = sum_slots(partial_out)
    returned = summed.astype(jnp.bfloat16).reshape(arrived.shape[0], arrived.shape[1], -1)
    back_slots = send_rows(returned)
    gate_probs, route_onehot = route_gates(normed_two, router_weight, route_hits)
    back_rows = gather_back(back_slots, target, length)
    output = middle + jnp.sum(gate_probs[:, :, None] * back_rows.astype(jnp.float32), axis=1)
    return (output, (attn_out, arrived, back_slots, pre_act))


def backward_layer(inputs, upstream, context, weights, front, saved_state):
    segment_row, pad_row, route_rows, dist_bucket = context
    gain_pair, qkv_weight, out_weight, bias_table, router_weight, upper_weight, lower_weight = (
        weights
    )
    normed_one, queries, keys_in, values_in, attn_probs, mixed_rows, bucket_onehot = front
    attn_out, arrived_rows, back_slots, pre_rows = saved_state
    length, model_width = inputs.shape
    head_count = bias_table.shape[1]
    head_cols = qkv_weight.shape[2]
    experts = router_weight.shape[1]
    capacity = max(2, 3 * length // experts)
    local_experts = upper_weight.shape[0]
    middle = inputs + attn_out
    normed_two = normalize(middle, gain_pair[1]).astype(jnp.bfloat16)
    target, source, filled, route_hits = slot_tables(route_rows, experts, capacity)
    gate_probs, route_onehot = route_gates(normed_two, router_weight, route_hits)
    back_rows = gather_back(back_slots, target, length)
    gate_grad = jnp.sum(upstream[:, None, :] * back_rows.astype(jnp.float32), axis=-1)
    chosen_grad = gate_probs * (gate_grad - jnp.sum(gate_probs * gate_grad, axis=-1, keepdims=True))
    logit_grad = jnp.einsum("lr,lre->le", chosen_grad, route_onehot, precision=highest).astype(
        jnp.bfloat16
    )
    router_grad = jnp.dot(normed_two.T, logit_grad, preferred_element_type=jnp.float32)
    normed_two_grad = jnp.dot(logit_grad, router_weight.T, preferred_element_type=jnp.float32)
    route_grads = (
        (gate_probs[:, :, None] * upstream[:, None, :])
        .reshape(2 * length, model_width)
        .astype(jnp.bfloat16)
    )
    slot_grads = jnp.where(
        filled[:, None], jnp.take(route_grads, source, axis=0), jnp.zeros((), jnp.bfloat16)
    )
    arrived_grads = send_rows(slot_grads.reshape(experts, capacity, model_width))
    grouped = arrived_rows.reshape(-1, local_experts, capacity, model_width)
    grouped_grads = arrived_grads.reshape(-1, local_experts, capacity, model_width)
    hidden, gelu_pull = jax.vjp(partial(jax.nn.gelu, approximate=False), pre_rows)
    hidden_low = hidden.astype(jnp.bfloat16)
    down_grad = jnp.einsum(
        "secf,secd->efd", hidden_low, grouped_grads, preferred_element_type=jnp.float32
    )
    hidden_grad = jnp.einsum(
        "secd,efd->secf", grouped_grads, lower_weight, preferred_element_type=jnp.float32
    )
    pre_grad = gelu_pull(hidden_grad)[0].astype(jnp.bfloat16)
    up_grad = jnp.einsum("secd,secf->edf", grouped, pre_grad, preferred_element_type=jnp.float32)
    rows_grad = sum_slots(
        jnp.einsum("secf,edf->secd", pre_grad, upper_weight, preferred_element_type=jnp.float32)
    )
    sent_back = send_rows(
        rows_grad.astype(jnp.bfloat16).reshape(arrived_rows.shape[0], arrived_rows.shape[1], -1)
    )
    copy_grads = gather_back(sent_back, target, length).astype(jnp.float32)
    normed_two_grad = normed_two_grad + jnp.sum(copy_grads, axis=1)
    middle_part, gain_two = normalize_back(middle, gain_pair[1], normed_two_grad)
    middle_grad = upstream + middle_part
    attn_grad = middle_grad.astype(jnp.bfloat16)
    out_grad = jnp.dot(mixed_rows.T, attn_grad, preferred_element_type=jnp.float32)
    mixed_grad = jnp.dot(attn_grad, out_weight.T, preferred_element_type=jnp.float32).astype(
        jnp.bfloat16
    )
    mixed_grad = mixed_grad.reshape(length, head_count, -1)
    prob_grad = jnp.einsum(
        "qhd,khd->hqk", mixed_grad, values_in, preferred_element_type=jnp.float32
    )
    value_grad = jnp.einsum(
        "hqk,qhd->khd",
        attn_probs.astype(jnp.bfloat16),
        mixed_grad,
        preferred_element_type=jnp.float32,
    )
    score_grad = attn_probs * (prob_grad - jnp.sum(prob_grad * attn_probs, axis=-1, keepdims=True))
    table_grad = jnp.einsum("hqk,qkb->bh", score_grad, bucket_onehot, precision=highest)
    raw_grad = (0.125 * score_grad).astype(jnp.bfloat16)
    query_grad = jnp.einsum("hqk,khd->qhd", raw_grad, keys_in, preferred_element_type=jnp.float32)
    key_grad = jnp.einsum("hqk,qhd->khd", raw_grad, queries, preferred_element_type=jnp.float32)
    qkv_grad = (
        jnp.stack([query_grad, key_grad, value_grad], axis=1)
        .reshape(length, 3, head_cols)
        .astype(jnp.bfloat16)
    )
    qkv_weight_grad = jnp.einsum(
        "ld,lch->dch", normed_one, qkv_grad, preferred_element_type=jnp.float32
    )
    normed_one_grad = lax.psum(
        jnp.einsum("lch,dch->ld", qkv_grad, qkv_weight, preferred_element_type=jnp.float32),
        "tensor",
    )
    input_part, gain_one = normalize_back(inputs, gain_pair[0], normed_one_grad)
    input_grad = middle_grad + input_part
    gain_grads = jnp.stack([gain_one, gain_two])
    return (
        input_grad,
        (gain_grads, qkv_weight_grad, out_grad, table_grad, router_grad, up_grad, down_grad),
    )


def pick_context(segments, pad_mask, routes, dist_bucket, micro_slot):
    segment_row = lax.dynamic_index_in_dim(segments[:, 0], micro_slot, 0, False)
    pad_row = lax.dynamic_index_in_dim(pad_mask[:, 0], micro_slot, 0, False)
    route_rows = lax.dynamic_index_in_dim(routes[:, 0], micro_slot, 0, False)
    return (segment_row, pad_row, route_rows, dist_bucket)


def place_row(store_all, new_value, micro_slot, is_valid):
    current = lax.dynamic_index_in_dim(store_all, micro_slot, 0, False)
    return lax.dynamic_update_index_in_dim(
        store_all, jnp.where(is_valid, new_value, current), micro_slot, 0
    )


def pick_row(store_all, micro_slot):
    return lax.dynamic_index_in_dim(store_all, micro_slot, 0, False)


def mask_grad(grad_value, is_valid):
    return jnp.where(is_valid, grad_value, jnp.zeros((), grad_value.dtype))


def tensor_half(full_rows, tensor_id, half_width):
    return lax.dynamic_slice_in_dim(full_rows, tensor_id * half_width, half_width, 2)[None, :, None]


def local(
    tokens,
    cotangent,
    segments,
    pad_mask,
    routes,
    dist_bucket,
    norm_gains,
    qkv_weight,
    out_weight,
    rel_bias,
    router_weight,
    expert_up,
    expert_down,
):
    section_id = lax.axis_index("section")
    section_count = lax.axis_size("section")
    micro_count = tokens.shape[0]
    length = tokens.shape[2]
    model_width = tokens.shape[3]
    tick_count = micro_count + section_count - 1
    weights = (
        norm_gains[0].astype(jnp.float32),
        qkv_weight[0],
        out_weight[0],
        rel_bias[0],
        router_weight[0],
        expert_up[0],
        expert_down[0],
    )
    empty_rows = jnp.zeros((length, model_width), jnp.bfloat16)
    arriving = empty_rows
    kept_inputs = jnp.zeros((micro_count, length, model_width), jnp.bfloat16)
    section_out = jnp.zeros((micro_count, length, model_width), jnp.float32)
    for tick_index in range(tick_count):
        micro_index = tick_index - section_id
        is_valid = (micro_index >= 0) & (micro_index < micro_count)
        micro_slot = jnp.clip(micro_index, 0, micro_count - 1)
        own_rows = tokens[tick_index, 0] if tick_index < micro_count else empty_rows
        layer_in = jnp.where(section_id == 0, own_rows, arriving)
        context = pick_context(segments, pad_mask, routes, dist_bucket, micro_slot)
        inputs = layer_in.astype(jnp.float32)
        front = attention_front(inputs, context, weights)
        result, saved_state = forward_rest(inputs, front, context, weights)
        section_out = place_row(section_out, result, micro_slot, is_valid)
        kept_inputs = place_row(kept_inputs, layer_in, micro_slot, is_valid)
        arriving = shifted(result.astype(jnp.bfloat16), "section", 1)
    returning = empty_rows
    input_store = jnp.zeros((micro_count, length, model_width), jnp.float32)
    totals = None
    for tick_index in range(tick_count):
        micro_index = tick_index - (section_count - 1 - section_id)
        is_valid = (micro_index >= 0) & (micro_index < micro_count)
        micro_slot = jnp.clip(micro_index, 0, micro_count - 1)
        own_rows = cotangent[tick_index, 0] if tick_index < micro_count else empty_rows
        upstream = jnp.where(section_id == section_count - 1, own_rows, returning).astype(
            jnp.float32
        )
        inputs = pick_row(kept_inputs, micro_slot).astype(jnp.float32)
        context = pick_context(segments, pad_mask, routes, dist_bucket, micro_slot)
        front = attention_front(inputs, context, weights)
        saved_state = forward_rest(inputs, front, context, weights)[1]
        input_grad, grad_set = backward_layer(
            inputs, upstream, context, weights, front, saved_state
        )
        input_store = place_row(input_store, input_grad, micro_slot, is_valid)
        grad_set = jax.tree.map(partial(mask_grad, is_valid=is_valid), grad_set)
        totals = grad_set if totals is None else jax.tree.map(jnp.add, totals, grad_set)
        returning = shifted(input_grad.astype(jnp.bfloat16), "section", -1)
    shared = lax.psum((totals[0], totals[1], totals[2], totals[3], totals[4]), "dp")
    tensor_id = lax.axis_index("tensor")
    half_width = model_width // lax.axis_size("tensor")
    return (
        tensor_half(section_out, tensor_id, half_width),
        tensor_half(input_store, tensor_id, half_width),
        shared[0][None],
        shared[1][None],
        shared[2][None],
        shared[3][None],
        shared[4][None],
        totals[5][None],
        totals[6][None],
    )


def gelu_parts(values):
    share = 0.5 + 0.5 * lax.erf(values * 0.7071067811865476)
    return (values * share, share + values * (0.3989422804014327 * jnp.exp(-0.5 * values * values)))


def nn(left, right):
    return lax.dot_general(left, right, (((1,), (0,)), ((), ())), preferred_element_type=jnp.float32)


def nt(left, right):
    return lax.dot_general(left, right, (((1,), (1,)), ((), ())), preferred_element_type=jnp.float32)


def tn(left, right):
    return lax.dot_general(left, right, (((0,), (0,)), ((), ())), preferred_element_type=jnp.float32)


def split_low(values):
    high = values.astype(jnp.bfloat16)
    return (high, (values - high.astype(jnp.float32)).astype(jnp.bfloat16))


def inverse_rms(values):
    return lax.rsqrt(jnp.mean(values * values, axis=-1, keepdims=True) + norm_eps)


class Layout:
    pass


def layer_kernel(lay, *refs):
    (
        tok_ref, cot_ref, seg_hbm, pad_hbm, routes_hbm, dist_hbm, gains_hbm, qkvw_hbm, outw_hbm, relb_hbm, wr_hbm,
        up_ref, down_ref,
        secout_ref, ingrad_ref, ggain_ref, shared_ref, gbias_ref, grouter_ref, guv, gdv,
        seg_ref, pad_ref, routes_ref, dist_ref, gains_ref, relb_ref, wr_ref, upv, downv, upt, downt, qkvwt, outwt, qkvw_ref, outw_ref, xb, dyb, rr, place, bias_buf, probs_buf, no1, qkvb, mixed, att_send, att_recv, mid, ntb,
        gate_t, hit_t, wrp, score_sum, disp_x, xrows, disp_y, dyrows, hidden, dgelu, halves, eo_send, eo_recv, eob, eoret, out_own,
        other, og, gg_part, gg_other, gg_send, gg_recv, pg, cg_send, cg_recv, cgb, cgret, mgrad, ag, mg, qkvg,
        no_send, no_recv, ig_own, dy_send,
        no_all, mix_all, qgt, qt_all, agt, agt_all, small_send, small_in, small_all, small_sib,
        x_send, rs_buf, rs_in, relay_buf, relay_q,
        wsem, ss, rs,
    ) = refs
    bf = jnp.bfloat16
    f32 = jnp.float32
    micro, length, width = tok_ref.shape
    experts = lay.experts
    cap = lay.cap
    cols = outw_ref.shape[0]
    pairs = cols // 128
    ffn = up_ref.shape[1]
    slots = experts * cap
    half = width // 2
    s = lax.axis_index("section")
    d = lax.axis_index("dp")
    t = lax.axis_index("tensor")
    u = 1 - t
    sib = (s, d, u)
    across = (1 - s, d, t)
    bits = [lax.rem(d // bit, 2) for bit in (1, 2, 4)]

    def partner(flip):
        index = d
        for place, bit in enumerate((1, 2, 4)):
            index = index + (flip // bit) % 2 * (bit - 2 * bit * bits[place])
        return index

    peer = [partner(flip) for flip in (0, 4, 1, 6, 2, 5, 3, 7)]
    steps = range(1, experts)
    relayed = (5, 7)
    chunks = range(experts // 2)

    def pair(c):
        return pl.ds(2 * c, 2)

    def partner_at(k):
        c = k // 2
        return partner(c + (k % 2) * (4 + 2 * (c % 2) + c // 2 - c))


    def remote(src, dst, sem, device, k=0):
        return pltpu.make_async_remote_copy(
            src_ref=src,
            dst_ref=dst,
            send_sem=ss.at[sem[0]],
            recv_sem=rs.at[sem[1] + k],
            device_id=device,
            device_id_type=pl.DeviceIdType.MESH,
        )

    counter = [0, 0]

    def take(arrivals=1):
        pair_of = (counter[0], counter[1])
        counter[0] += 1
        counter[1] += arrivals
        return pair_of

    def all_sent(like, sem):
        remote(like, like, sem, sib).wait_send()

    def all_here(like, sem, k=0):
        remote(like, like, sem, sib, k).wait_recv()

    ring_hops = experts - 1
    sem_routes = take()
    sem_x = take()
    sem_relay = [take(len(relayed)) for _ in range(2)]
    sem_pass = [take(0) for _ in range(2)]
    sem_relay_q = take(len(relayed))
    sem_pass_q = take(0)
    sem_xf = take()
    sem_dy = take()
    sem_att = take()
    sem_eo = take(len(chunks))
    sem_cg = take(len(chunks))
    sem_ag = take()
    sem_no = take()
    sem_so = take()
    sem_ig = take()
    sem_dx = take(len(chunks))
    sem_dxf = take(len(chunks))
    sem_ddy = take(len(chunks))
    sem_ddyf = take(len(chunks))
    sem_re = take()
    sem_rc = take()
    sem_gg = take()
    sem_gg_core = take(len(chunks))
    sem_qgt = take(experts)
    sem_agt = take()
    sem_agtf = take()
    sem_small = take()
    sem_back = take()
    sem_sums = take()
    sem_noall = take()
    sem_ring_no = take(2 * ring_hops)
    sem_ring_mix = take(2 * ring_hops)
    sem_ring_sum = (take(0)[0], sem_ring_no[1])
    sem_ring_out = take(4 * ring_hops)
    assert tuple(counter) == lay.sems

    def block(index, rows):
        return pl.ds(pl.multiple_of(index * rows, rows), rows)

    place_y = lax.rem(d, 2)
    place_z = d // 2
    ring_at = place_z + place_y * (experts - 1 - 2 * place_z)

    def ring_device(position):
        p = lax.rem(position + 2 * experts, experts)
        return 2 * p + (p // (experts // 2)) * (2 * experts - 1 - 4 * p)

    def hops(number, direction):
        return experts // 2 - (number % 2 == (direction > 0))

    def hop_index(number, direction, k):
        return number * ring_hops + k + (0 if direction > 0 else hops(number, 1))

    def lines_of(amount):
        return [(number, direction) for number in range(amount) for direction in (1, -1)]

    def ring_gather(parts, at_half=None):
        def hop(number, direction, k):
            view, sem, first = parts[number]
            held = view(ring_device(ring_at - direction * k))
            index = hop_index(number, direction, k) - first * ring_hops
            return remote(held, held, sem, (s, ring_device(ring_at + direction), t), index)

        lines = lines_of(len(parts))
        for line in lines:
            hop(*line, 0).start()

        def one(k, carry):
            for line in lines:
                hop(*line, k - 1).wait_recv()
                hop(*line, k).start()
            return carry

        short = experts // 2 - 1
        lax.fori_loop(1, short, one, 0)
        if at_half is not None:
            at_half()
        for line in lines:
            hop(*line, short - 1).wait_recv()
            if hops(*line) > short:
                hop(*line, short).start()
        for line in lines:
            if hops(*line) > short:
                hop(*line, short).wait_recv()

    small_loads = [
        pltpu.make_async_copy(src, dst, wsem.at[5 + i])
        for i, (src, dst) in enumerate(
            (
                (routes_hbm, routes_ref),
                (wr_hbm, wr_ref),
                (seg_hbm, seg_ref),
                (pad_hbm, pad_ref),
                (dist_hbm, dist_ref),
                (gains_hbm, gains_ref),
                (relb_hbm, relb_ref),
            )
        )
    ]
    for copy in small_loads:
        copy.start()
    load_up = pltpu.make_async_copy(up_ref, upv, wsem.at[0])
    load_down = pltpu.make_async_copy(down_ref, downv, wsem.at[1])
    load_qkvw = pltpu.make_async_copy(qkvw_hbm, qkvw_ref, wsem.at[2])
    load_outw = pltpu.make_async_copy(outw_hbm, outw_ref, wsem.at[3])
    load_tok = pltpu.make_async_copy(tok_ref, xb, wsem.at[4])
    load_cot = pltpu.make_async_copy(cot_ref.at[t], dyb, wsem.at[4])

    @pl.when(s == 0)
    def _():
        load_tok.start()

    @pl.when(s == 1)
    def _():
        load_cot.start()

    load_qkvw.start()
    load_outw.start()
    load_up.start()
    load_down.start()

    barrier = pltpu.get_barrier_semaphore()
    for k in steps:
        pl.semaphore_signal(barrier, inc=1, device_id=(s, peer[k], t), device_id_type=pl.DeviceIdType.MESH)
    pl.semaphore_signal(barrier, inc=1, device_id=sib, device_id_type=pl.DeviceIdType.MESH)
    for k in (0,) + relayed:
        pl.semaphore_signal(barrier, inc=1, device_id=(1 - s, peer[k], t), device_id_type=pl.DeviceIdType.MESH)
    pl.semaphore_wait(barrier, experts + 1 + len(relayed))

    for copy in small_loads:
        copy.wait()

    for k in steps:
        remote(routes_ref, rr.at[k], sem_routes, (s, peer[k], t)).start()
    rr[0] = routes_ref[...]

    lanes8 = lax.broadcasted_iota(jnp.int32, (experts, length), 0)
    row_at = lax.broadcasted_iota(jnp.int32, (length, length), 0)
    col_at = lax.broadcasted_iota(jnp.int32, (length, length), 1)
    before = (row_at < col_at).astype(bf)
    slot_at = lax.broadcasted_iota(jnp.int32, (cap, length), 0).astype(f32)

    expert_of = jnp.zeros((experts, length), jnp.int32)
    for k in range(experts):
        expert_of = jnp.where(lanes8 == k, peer[k], expert_of)
    turn = (lax.broadcasted_iota(jnp.int32, (experts, experts), 1) == expert_of[:, 0:experts]).astype(f32).astype(bf)
    wrp[...] = nn(turn, wr_ref[...]).astype(bf)
    own_routes = routes_ref[t]
    hits = (expert_of == own_routes[0:1, :]) | (expert_of == own_routes[1:2, :])
    hit_f = hits.astype(f32)
    hit_t[...] = hit_f
    spot = jnp.where(hits, nn(hit_f.astype(bf), before), -1.0)
    for e in range(experts):
        place[e * cap : (e + 1) * cap, :] = (slot_at == spot[e : e + 1, :]).astype(f32).astype(bf)

    def to_relay(source, k, leg):
        i = relayed.index(k)
        return remote(source, relay_buf.at[leg * len(relayed) + i], sem_relay[leg], across, i)

    def relay(landing, sem, leg):
        for i, k in enumerate(relayed):
            held = relay_buf.at[leg * len(relayed) + i]
            all_here(held, sem_relay[leg], i)
            through = (sem_pass[leg][0], sem[1] + k // 2)
            remote(held, landing.at[k, t], through, (0, peer[k], t)).start()

    def dispatch(rows, send, landing, sem, sem_fwd, leg=None, both=False):
        send[...] = nn(place[...], rows).astype(bf).reshape(send.shape)

        def direct(k):
            remote(send.at[k], landing.at[k, t], sem, (s, peer[k], t), k // 2).start()

        def start_relayed():
            for k in relayed:
                to_relay(send.at[k], k, leg).start()

        def start_direct():
            for k in relayed:
                direct(k)

        direct(1)
        if both:
            pl.when(s == 0)(start_relayed)
        elif leg is not None:
            start_relayed()
        for k in steps[1:]:
            if k not in relayed:
                direct(k)
        if both:
            pl.when(s == 1)(start_direct)
        elif leg is None:
            start_direct()
        landing[0, t] = send[0]

        def arrive(c):
            held = landing.at[pair(c), t]
            all_here(landing.at[1, t] if isinstance(c, int) and c == 0 else held, sem, c)
            remote(held, held, sem_fwd, sib, c).start()

        def joined(c):
            all_here(landing.at[pair(c), t], sem_fwd, c)

        def drain(zero):
            all_sent(send, sem_fwd)
            if zero:
                all_sent(send.at[0 : experts - 1 - len(relayed)], sem)
                all_sent(send.at[0 : len(relayed)], sem_relay[leg])
            else:
                all_sent(send.at[1:experts], sem)

        return arrive, joined, drain

    def stream(dispatched, first, second, finish_chunk, eager, zero):
        arrive, joined, drain = dispatched
        last = len(chunks) - 1
        arrive(0)
        joined(0)

        def one(c, carry):
            first(c)
            if eager:
                pl.when(c > 0)(lambda: finish_chunk(c - 1))
                pl.when(c < last)(lambda: arrive(c + 1))
                second(c)
            else:
                second(c)

                @pl.when(c < last)
                def _():
                    arrive(c + 1)
                    finish_chunk(c)


            @pl.when(c < last)
            def _():
                joined(c + 1)

            return carry

        lax.fori_loop(0, len(chunks), one, 0)
        finish_chunk(last)
        drain(zero)

    def turn_weights():
        upt[...] = jnp.transpose(upv[...])
        downt[...] = jnp.transpose(downv[...])
        for c in range(3):
            qkvwt[c] = jnp.transpose(qkvw_ref[c])
        outwt[...] = jnp.transpose(outw_ref[...])

    def other_experts():
        all_here(rr.at[1:experts], sem_routes)

        def one(i, carry):
            q = i // micro
            m = i % micro
            pair = rr[q, m]
            first = pair[0:1, :] == d
            mine = first | (pair[1:2, :] == d)
            mine_f = jnp.broadcast_to(mine.astype(f32), (experts, length))
            spots = jnp.where(mine_f > 0.0, nn(mine_f.astype(bf), before), -1.0)
            where_slot = (slot_at == spots[0:1, :]).astype(f32).astype(bf)
            partner = jnp.where(first, pair[1:2, :], pair[0:1, :])
            partner_hot = (lanes8 == partner).astype(f32).astype(bf)
            other[q, m] = nt(where_slot, partner_hot)
            return carry

        lax.fori_loop(0, experts * micro, one, 0)

    @pl.when(s == 0)
    def _():
        load_tok.wait()
        load_qkvw.wait()
        load_outw.wait()

    @pl.when(s == 1)
    def _():
        load_cot.wait()
        relay(xrows, sem_dx, 0)
        load_up.wait()
        load_down.wait()
        load_qkvw.wait()
        load_outw.wait()
        turn_weights()
        other_experts()
        arrive, joined, drain = dispatch(dyb[...], disp_y, dyrows, sem_ddy, sem_ddyf)

        def pass_one(c, carry):
            arrive(c)
            return carry

        def join_one(c, carry):
            joined(c)
            return carry

        arrive(0)
        lax.fori_loop(1, len(chunks), pass_one, 0)
        lax.fori_loop(0, len(chunks), join_one, 0)
        drain(False)

    dist_rows = (
        lax.broadcasted_iota(jnp.int32, (lay.buckets, length), 0) == dist_ref[...]
    ).astype(f32).astype(bf)
    bias_rows = nn(relb_ref[...], dist_rows).astype(bf)
    mirror = ((row_at + col_at == length) | (row_at + col_at == 0)).astype(f32).astype(bf)
    bias_back = nn(bias_rows, mirror)
    for m in range(micro):
        seg_rows = jnp.broadcast_to(seg_ref[m : m + 1, :].astype(f32), (length, length))
        pads = jnp.broadcast_to(pad_ref[m : m + 1, :], (length, length))
        allowed = (col_at <= row_at) & (seg_rows == jnp.transpose(seg_rows))
        allowed = allowed & ((pads == 1) | (col_at == row_at))
        for p in range(pairs):
            for h in range(2):
                head = 2 * p + h
                grid = pltpu.roll(
                    jnp.broadcast_to(bias_back[head : head + 1, :], (length, length)), 0, 1, stride=1, stride_axis=0
                )
                bias_buf[m, p, :, h * length : (h + 1) * length] = jnp.where(allowed, grid, masked_score)

    x_copy = remote(x_send, xb.at[t], sem_x, across)
    dy_copy = remote(dy_send, dyb, sem_dy, across)
    x_forward = remote(xb.at[t], xb.at[t], sem_xf, sib)

    def spread_gates(gates_ref):
        return jnp.concatenate(
            [
                jnp.broadcast_to(gates_ref[e : e + 1, :], (cap, length)) * place[e * cap : (e + 1) * cap, :].astype(f32)
                for e in range(experts)
            ],
            axis=0,
        ).astype(bf)

    @pl.when(s == 1)
    def _():
        x_copy.wait_recv()
        x_forward.start()

    gain_one = gains_ref[0:1, :].astype(f32)
    gain_two = gains_ref[1:2, :].astype(f32)
    low_lanes = lax.broadcasted_iota(jnp.int32, (length, 128), 1) < 64

    def both_heads(pair_block):
        zero = jnp.zeros((), bf)
        return jnp.concatenate(
            [jnp.where(low_lanes, pair_block, zero), jnp.where(low_lanes, zero, pair_block)], axis=0
        )

    def attend(m):
        x_rows = xb[m].astype(f32)
        no1[m] = (x_rows * inverse_rms(x_rows) * gain_one).astype(bf)
        for c in range(3):
            qkvb[c, m] = nn(no1[m], qkvw_ref[c]).astype(bf)
        for p in range(pairs):
            at = slice(p * 128, (p + 1) * 128)
            scores = 0.125 * nt(qkvb[0, m, :, at], both_heads(qkvb[1, m, :, at])) + bias_buf[m, p]
            for h in range(2):
                part = scores[:, h * length : (h + 1) * length]
                terms = jnp.exp(part - jnp.max(part, axis=-1, keepdims=True))
                probs_buf[m, p, :, h * length : (h + 1) * length] = terms * (
                    1.0 / jnp.sum(terms, axis=-1, keepdims=True)
                )
            mixed[m, :, at] = nn(probs_buf[m, p].astype(bf), both_heads(qkvb[2, m, :, at])).astype(bf)

    att_copy = remote(att_send, att_recv, sem_att, sib)

    def project_other():
        att_send[...] = nn(mixed[u], outw_ref[...])
        att_copy.start()

    begin = u + s * (t - u)

    def attend_one(i, carry):
        @pl.when((s == 1) & (i == 1))
        def _():
            x_forward.wait()

        attend(begin + i * (1 - 2 * begin))

        @pl.when((s == 0) & (i == 0))
        def _():
            project_other()

        return carry

    lax.fori_loop(0, micro, attend_one, 0)

    @pl.when(s == 1)
    def _():
        project_other()

    part_own = nn(mixed[t], outw_ref[...])
    att_copy.wait()
    middle = xb[t].astype(f32) + part_own + att_recv[...]
    mid[...] = middle
    ntb[...] = (middle * inverse_rms(middle) * gain_two).astype(bf)
    logits_t = jnp.where(hit_t[...] > 0.0, nt(wrp[...], ntb[...]), masked_score)
    terms = jnp.exp(logits_t - jnp.max(logits_t, axis=0, keepdims=True))
    gate_t[...] = terms / jnp.sum(terms, axis=0, keepdims=True)

    arrivals = dispatch(ntb[...], disp_x, xrows, sem_dx, sem_dxf, 0, True)
    rows_of = 2 * micro * cap

    def flat(ref, chunk):
        return ref[chunk].reshape(rows_of, ref.shape[-1])

    def front_chunk(c):
        value, slope = gelu_parts(nn(flat(xrows, pair(c)), upv[...]))
        hidden[pair(c)] = value.astype(bf).reshape(2, micro, cap, ffn)
        dgelu[pair(c)] = slope.astype(bf).reshape(2, micro, cap, ffn)

    def split_sum(c, total, send, recv, base):
        for m in range(micro):
            halves[m] = total.reshape(2, micro, cap, width)[:, m]
        send[pair(c)] = halves[u].astype(bf)
        remote(send.at[pair(c)], recv.at[pair(c)], base, sib, c).start()

    def hand_back(c, send, recv, base, total, landing, base_back):
        all_here(recv.at[pair(c)], base, c)
        total[pair(c)] = (halves[t] + recv[pair(c)].astype(f32)).astype(bf)

        def give(k):
            remote(total.at[k], landing.at[k], base_back, (s, partner_at(k), t)).start()

        def keep():
            landing[0] = total[0]

        if isinstance(c, int):
            give(2 * c)
        else:
            pl.when(c == 0)(keep)
            pl.when(c > 0)(lambda: give(2 * c))
        give(2 * c + 1)

    def wait_back(total, landing, sem):
        all_here(landing.at[1:experts], sem)
        all_sent(total.at[1:experts], sem)

    def rows_chunk(c):
        split_sum(c, nn(flat(hidden, pair(c)), downv[...]), eo_send, eo_recv, sem_eo)

    def rows_finish(c):
        hand_back(c, eo_send, eo_recv, sem_eo, eob, eoret, sem_re)

    mine_hot = (lax.broadcasted_iota(jnp.int32, (rows_of, experts), 1) == d).astype(f32)

    ones = jnp.ones((8, ffn), bf)
    gg_part[...] = jnp.zeros_like(gg_part)

    def slope_chunk(c):
        slot_logits = nt(flat(xrows, pair(c)), wr_ref[...])
        own_logit = jnp.sum(slot_logits * mine_hot, axis=-1, keepdims=True)
        other_logit = jnp.sum(slot_logits * flat(other, pair(c)), axis=-1, keepdims=True)
        gate = 1.0 / (1.0 + jnp.exp(other_logit - own_logit))
        dy_flat = flat(dyrows, pair(c))
        og[pair(c)] = (dy_flat.astype(f32) * gate).astype(bf).reshape(2, micro, cap, width)
        grad = nn(dy_flat, downt[...])
        pg[pair(c)] = (grad * gate * flat(dgelu, pair(c)).astype(f32)).astype(bf).reshape(2, micro, cap, ffn)
        product = (grad * flat(hidden, pair(c)).astype(f32)).astype(bf)
        for i in range(2):
            for m in range(micro):
                at = (i * micro + m) * cap
                gg_part[m, 2 * c + i, :, 0:cap] = nt(ones, product[at : at + cap])

    def back_chunk(c):
        remote(gg_part.at[u, pair(c)], gg_other.at[pair(c)], sem_gg_core, sib, c).start()
        split_sum(c, nn(flat(pg, pair(c)), upt[...]), cg_send, cg_recv, sem_cg)

    def both_chunk(c):
        front_chunk(c)
        slope_chunk(c)

    def back_finish(c):
        hand_back(c, cg_send, cg_recv, sem_cg, cgb, cgret, sem_rc)
        all_here(gg_other.at[pair(c)], sem_gg_core, c)
        gg_send[pair(c)] = gg_part[t, pair(c)] + gg_other[pair(c)]

        def give(k):
            remote(gg_send.at[k], gg_recv.at[k], sem_gg, (s, partner_at(k), t)).start()

        def keep():
            gg_recv[0] = gg_send[0]

        if isinstance(c, int):
            give(2 * c)
        else:
            pl.when(c == 0)(keep)
            pl.when(c > 0)(lambda: give(2 * c))
        give(2 * c + 1)

    def hidden_of(m):
        return jnp.concatenate([hidden[k, m] for k in range(experts)], axis=0)

    def expert_rows():
        eo_send[...] = nn(hidden_of(u), downv[...]).astype(bf).reshape(eo_send.shape)
        eo_copy = remote(eo_send, eo_recv, sem_eo, sib)
        eo_copy.start()
        total = nn(hidden_of(t), downv[...])
        eo_copy.wait_recv()
        eob[...] = (total + eo_recv[...].astype(f32).reshape(slots, width)).astype(bf).reshape(eob.shape)

    def send_back(source, landing, base):
        for k in steps:
            remote(source.at[k], landing.at[k], base, (s, peer[k], t)).start()
        landing[0] = source[0]

    def layer_output():
        result = mid[...] + tn(spread_gates(gate_t), eoret[...].reshape(slots, width))
        out_own[...] = result
        return result

    def own_half():
        return pl.ds(pl.multiple_of(t * half, half), half)

    def other_half():
        return pl.ds(pl.multiple_of(u * half, half), half)

    def hand_out(rows_ref, out_ref, index):
        copy = remote(rows_ref.at[:, other_half()], out_ref.at[t], index, sib)
        copy.start()
        out_ref[t] = rows_ref[:, own_half()]
        copy.wait()

    def gather_factors():
        no_all[t, d] = no1[t]
        mix_all[d] = mixed[...]
        ring_gather(
            [
                (lambda q: no_all.at[t, q, 0 : length // 2], sem_ring_no, 0),
                (lambda q: no_all.at[t, q, length // 2 : length], sem_ring_no, 0),
                (lambda q: mix_all.at[q, 0], sem_ring_mix, 2),
                (lambda q: mix_all.at[q, 1], sem_ring_mix, 2),
            ]
        )
        all_sent(no_all.at[t, 1:experts], sem_ring_no)
        all_sent(mix_all.at[1:experts], sem_ring_mix)
        copy = remote(no_all.at[t], no_all.at[t], sem_noall, sib)
        copy.start()
        copy.wait()

    @pl.when(s == 0)
    def _():
        load_up.wait()
        load_down.wait()
        stream(arrivals, front_chunk, rows_chunk, rows_finish, True, True)
        wait_back(eob, eoret, sem_re)
        x_send[...] = layer_output().astype(bf)
        x_copy.start()
        hand_out(out_own, secout_ref, sem_so)
        turn_weights()
        other_experts()
        gather_factors()
        x_copy.wait_send()
        dy_copy.wait_recv()
        arrivals_y = dispatch(dyb[...], disp_y, dyrows, sem_ddy, sem_ddyf, 1)
        stream(arrivals_y, slope_chunk, back_chunk, back_finish, True, True)

    @pl.when(s == 1)
    def _():
        stream(arrivals, both_chunk, back_chunk, back_finish, True, False)
        expert_rows()

    wait_back(gg_send, gg_recv, sem_gg)
    wait_back(cgb, cgret, sem_rc)

    @pl.when(s == 1)
    def _():
        send_back(eob, eoret, sem_re)


    gg_rows = []
    for e in range(experts):
        high, low = split_low(gg_recv[e][:, 0:cap])
        spot_rows = place[e * cap : (e + 1) * cap, :]
        gg_rows.append((nn(high, spot_rows) + nn(low, spot_rows))[0:1, :])
    gate_grad = jnp.concatenate(gg_rows, axis=0)
    gates = gate_t[...]
    logit_grad = (gates * (gate_grad - jnp.sum(gates * gate_grad, axis=0, keepdims=True))).astype(bf)
    router_grad = nn(tn(turn, logit_grad).astype(bf), ntb[...])
    two_grad = tn(logit_grad, wrp[...]) + tn(place[...], cgret[...].reshape(slots, width))
    dy = dyb[...].astype(f32)
    middle = mid[...]
    scale = inverse_rms(middle)
    normed = middle * scale
    gain_two_grad = jnp.sum(two_grad * normed, axis=0, keepdims=True)
    groups = width // 128
    small_send[...] = jnp.zeros_like(small_send)
    for g in range(groups):
        small_send[g, 0:experts, :] = router_grad[:, g * 128 : (g + 1) * 128]
        small_send[g, experts + 1 : experts + 2, :] = gain_two_grad[:, g * 128 : (g + 1) * 128]
    scaled = two_grad * gain_two
    middle_grad = dy + scale * (scaled - normed * jnp.mean(scaled * normed, axis=-1, keepdims=True))
    mgrad[...] = middle_grad
    ag[t] = middle_grad.astype(bf)
    ag_copy = remote(ag.at[t], ag.at[t], sem_ag, sib)
    ag_copy.start()

    agt_rows = width // experts
    agt_own = remote(agt.at[block(d, agt_rows)], agt_all.at[d, t], sem_agtf, sib)

    @pl.when(s == 0)
    def _():
        agt[...] = jnp.transpose(ag[t])
        for k in reversed(steps):
            remote(agt.at[block(peer[k], agt_rows)], agt_all.at[d, t], sem_agt, (s, peer[k], t)).start()
        agt_all[d, t] = agt[block(d, agt_rows), :]
        agt_own.start()

    qgt_rows = 3 * cols // experts

    def attend_back(m, i):
        mg[m] = nn(ag[m], outwt[...]).astype(bf)
        for p in range(pairs):
            at = slice(p * 128, (p + 1) * 128)
            mg_pair = mg[m, :, at]
            probs = probs_buf[m, p]
            keys2 = both_heads(qkvb[1, m, :, at])
            queries2 = both_heads(qkvb[0, m, :, at])
            mg2 = both_heads(mg_pair)
            prob_grad = nt(mg_pair, both_heads(qkvb[2, m, :, at]))
            raws = []
            key_grad = jnp.zeros((length, 128), f32)
            value_grad = jnp.zeros((length, 128), f32)
            for h in range(2):
                lane = slice(h * length, (h + 1) * length)
                part = probs[:, lane]
                step = prob_grad[:, lane]
                score_grad = part * (step - jnp.sum(part * step, axis=-1, keepdims=True))
                score_sum[2 * p + h] += score_grad
                raw = (0.125 * score_grad).astype(bf)
                raws.append(raw)
                key_grad = key_grad + tn(raw, queries2[h * length : (h + 1) * length])
                value_grad = value_grad + tn(part.astype(bf), mg2[h * length : (h + 1) * length])
            query_grad = nn(jnp.concatenate(raws, axis=1), keys2)
            for c, grad in enumerate((query_grad, key_grad, value_grad)):
                qkvg[c, m, :, at] = grad.astype(bf)

        @pl.when(s == 0)
        def _():
            for c in range(3):
                qgt[i, c * cols : (c + 1) * cols, :] = jnp.transpose(qkvg[c, m])
            for k in reversed([k for k in steps if k not in relayed]):
                rows = block(peer[k], qgt_rows)
                remote(qgt.at[i, rows], qt_all.at[d, i], sem_qgt, (s, peer[k], t), k).start()
            qt_all[d, i] = qgt[i, block(d, qgt_rows), :]

    score_sum[...] = jnp.zeros_like(score_sum)

    def back_one(i, carry):
        @pl.when(i == 1)
        def _():
            ag_copy.wait()

        attend_back(t + i * (u - t), i)
        return carry

    lax.fori_loop(0, micro, back_one, 0)

    def relay_q_copy(i, k):
        return remote(qgt.at[:, block(peer[k], qgt_rows)], relay_q.at[i], sem_relay_q, across, i)

    @pl.when(s == 0)
    def _():
        for i, k in enumerate(relayed):
            relay_q_copy(i, k).start()


    def project_back(m):
        total = nn(qkvg[0, m], qkvwt[0])
        for c in range(1, 3):
            total = total + nn(qkvg[c, m], qkvwt[c])
        return total

    no_send[...] = project_back(u).astype(bf)
    no_copy = remote(no_send, no_recv, sem_no, sib)
    no_copy.start()
    one_grad = project_back(t)
    no_copy.wait()
    one_grad = one_grad + no_recv[...].astype(f32)
    x_rows = xb[t].astype(f32)
    scale = inverse_rms(x_rows)
    normed = x_rows * scale
    gain_one_grad = jnp.sum(one_grad * normed, axis=0, keepdims=True)
    scaled = one_grad * gain_one
    input_grad = mgrad[...] + scale * (scaled - normed * jnp.mean(scaled * normed, axis=-1, keepdims=True))
    ig_own[...] = input_grad
    dy_send[...] = input_grad.astype(bf)

    @pl.when(s == 1)
    def _():
        dy_copy.start()

    hand_out(ig_own, ingrad_ref, sem_ig)

    sums = []
    for head in range(2 * pairs):
        high, low = split_low(score_sum[head])
        turned = pltpu.roll(nn(high, mirror) + nn(low, mirror), 0, 1, stride=1, stride_axis=0)
        sums.append(jnp.sum(turned, axis=0, keepdims=True))
    high, low = split_low(jnp.concatenate(sums, axis=0))
    small_send[groups, 0 : 2 * pairs, 0 : lay.buckets] = nt(high, dist_rows) + nt(low, dist_rows)
    for g in range(groups):
        small_send[g, experts : experts + 1, :] = gain_one_grad[:, g * 128 : (g + 1) * 128]
    for k in steps:
        remote(small_send.at[peer[k]], small_in.at[k], sem_small, (s, peer[k], t)).start()
    small_in[0] = small_send[d]

    wide = lay.wide
    every = micro * slots

    def expert_grads(n, carry):
        at = pl.ds(pl.multiple_of(n * wide, wide), wide)
        guv[:, at] = tn(xrows[...].reshape(every, width), pg[:, :, :, at].reshape(every, wide)).astype(bf)
        gdv[at, :] = tn(hidden[:, :, :, at].reshape(every, wide), og[...].reshape(every, width)).astype(bf)
        return carry

    lax.fori_loop(0, ffn // wide, expert_grads, 0)

    qkv_rows = 3 * cols // experts
    share = shared_ref.shape[1] // 4
    parts = [slice(c * share, (c + 1) * share) for c in range(4)]

    def pack_out(total):
        half_rows = agt_rows // 2
        return jnp.concatenate([total[..., 0:half_rows, :], total[..., half_rows:, :]], axis=-1).astype(bf)

    @pl.when(s == 0)
    def _():
        all_here(agt_all.at[1:experts, 0], sem_agt)
        for k in steps:
            held = agt_all.at[peer[k], t]
            remote(held, held, sem_agtf, sib).start()
        all_here(agt_all.at[:, 0], sem_agtf)
        all_sent(agt_all.at[1:experts, 0], sem_agt)
        all_sent(agt_all.at[:, 0], sem_agtf)
        total = jnp.zeros((agt_rows, cols), f32)
        for q in range(experts):
            for m in range(micro):
                total = total + nn(agt_all[q, m], mix_all[q, m])
        shared_ref[d, qkv_rows:, :] = pack_out(total)

        def qkv_slice(q):
            rows = jnp.concatenate([qt_all[q, 0], qt_all[q, 1]], axis=1)
            return nn(rows, jnp.concatenate([no_all[t, q], no_all[u, q]], axis=0))

        total = qkv_slice(d)
        for k in [k for k in reversed(steps) if k not in relayed] + list(relayed):
            all_here(qt_all.at[0], sem_qgt, k)
            total = total + qkv_slice(peer[k])
        all_sent(qt_all.at[0 : experts - 1 - len(relayed)], sem_qgt)
        all_sent(relay_q, sem_relay_q)
        shared_ref[d, 0:qkv_rows, :] = total.astype(bf)

    @pl.when(s == 1)
    def _():
        normed_rows = no1[...].reshape(micro * length, width)
        own = jnp.concatenate([tn(qkvg[c].reshape(micro * length, cols), normed_rows) for c in range(3)], axis=0)
        rs_buf[:, 0:qkv_rows, :] = own.astype(bf).reshape(experts, qkv_rows, width)
        own = tn(ag[...].reshape(micro * length, width), mixed[...].reshape(micro * length, cols))
        rs_buf[:, qkv_rows:, :] = pack_out(own.reshape(experts, agt_rows, cols))

        relay(dyrows, sem_ddy, 1)

        def owner_at(number, direction, k):
            return ring_device(ring_at + direction * (hops(number, direction) - k))

        def hop(number, direction, k):
            index = hop_index(number, direction, k)
            return remote(
                rs_buf.at[owner_at(number, direction, k), parts[number]],
                rs_in.at[index % ring_hops, parts[number]],
                sem_ring_sum,
                (s, ring_device(ring_at + direction), t),
                index,
            )

        lines = lines_of(len(parts))
        for k in range(experts // 2):
            for line in lines:
                if k < hops(*line):
                    if k > 0:
                        rows = parts[line[0]]
                        owner = owner_at(*line, k)
                        hop(*line, k - 1).wait_recv()
                        came = rs_in[hop_index(*line, k - 1) % ring_hops, rows, :].astype(f32)
                        rs_buf[owner, rows, :] = (rs_buf[owner, rows, :].astype(f32) + came).astype(bf)
                    hop(*line, k).start()
        for number, rows in enumerate(parts):
            total = rs_buf[d, rows, :].astype(f32)
            for direction in (1, -1):
                last = hops(number, direction) - 1
                hop(number, direction, last).wait_recv()
                total = total + rs_in[hop_index(number, direction, last) % ring_hops, rows, :].astype(f32)
            shared_ref[d, rows, :] = total.astype(bf)
        for i, k in enumerate(relayed):
            all_here(relay_q.at[i], sem_relay_q, i)
            remote(relay_q.at[i], qt_all.at[d], (sem_pass_q[0], sem_qgt[1] + k), (0, peer[k], t)).start()

    all_here(small_in.at[1:experts], sem_small)
    small_total = small_in[0]
    for k in steps:
        small_total = small_total + small_in[k]
    small_all[d] = small_total
    for k in steps:
        remote(small_all.at[d], small_all.at[d], sem_back, (s, peer[k], t)).start()

    sums_copy = remote(small_all, small_sib, sem_sums, sib)

    def pass_sums():
        all_here(small_all.at[1:experts], sem_back)
        sums_copy.start()


    streams = [
        (lambda q, rows=rows: shared_ref.at[q, rows], sem_ring_out, 0) for rows in parts
    ]

    ring_gather(streams, pass_sums)
    sums_copy.wait_recv()
    for g in range(groups):
        lanes = slice(g * 128, (g + 1) * 128)
        grouter_ref[:, lanes] = small_all[g, 0:experts, :] + small_sib[g, 0:experts, :]
        ggain_ref[:, lanes] = small_all[g, experts : experts + 2, :] + small_sib[g, experts : experts + 2, :]
    gbias_ref[...] = small_all[groups, 0 : 2 * pairs, :]
    @pl.when(s == 1)
    def _():
        dy_copy.wait_send()
        for sem in sem_pass:
            all_sent(relay_buf.at[0 : len(relayed)], sem)
        all_sent(rs_in, sem_ring_sum)
        all_sent(relay_q, sem_pass_q)
        wait_back(eob, eoret, sem_re)
        layer_output()
        hand_out(out_own, secout_ref, sem_so)

    all_sent(rr.at[1:experts], sem_routes)
    all_sent(eo_send, sem_eo)
    all_sent(cg_send, sem_cg)
    all_sent(gg_part.at[0], sem_gg_core)
    all_sent(small_in.at[1:experts], sem_small)
    all_sent(small_all.at[1:experts], sem_back)
    all_sent(small_all, sem_sums)
    all_sent(shared_ref.at[1:experts], sem_ring_out)


def widen_kernel(
    sec_ref, ing_ref, gain_ref, shared_ref, bias_ref, router_ref, up_ref, down_ref,
    sec_out, ing_out, gain_out, bias_out, router_out, qkv_out, out_out, up_out, down_out,
    up_wide, down_wide, qkv_wide, out_wide, bias_wide, out_sem,
):
    f32 = jnp.float32
    parts = 6
    experts, shared_rows, width = shared_ref.shape
    cols = out_wide.shape[0]
    qkv_rows = 3 * cols // experts
    wide = ((up_ref, up_wide, up_out), (down_ref, down_wide, down_out))
    stores = []

    def store(src, dst):
        copy = pltpu.make_async_copy(src, dst, out_sem.at[len(stores)])
        copy.start()
        stores.append(copy)

    def widen(i, n):
        src, dst, out = wide[i]
        size = src.shape[0] // parts
        rows = pl.ds(n * size, size)
        dst[rows, :] = src[rows, :].astype(f32)
        store(dst.at[rows], out.at[rows])

    def turn_qkv(c):
        block = shared_ref[:, 0:qkv_rows, :].reshape(3 * cols, width)[c * cols : (c + 1) * cols]
        qkv_wide[c] = jnp.transpose(block.astype(f32))
        store(qkv_wide.at[c], qkv_out.at[c])

    store(sec_ref, sec_out)
    store(ing_ref, ing_out)
    widen(0, 0)
    store(gain_ref, gain_out)
    store(router_ref, router_out)
    for h in range(bias_wide.shape[0]):
        bias_wide[h] = bias_ref[h : h + 1, 0 : bias_wide.shape[2]]
    store(bias_wide, bias_out)
    widen(0, 1)
    widen(0, 2)
    turn_qkv(0)
    widen(0, 3)
    widen(0, 4)
    turn_qkv(1)
    widen(0, 5)
    widen(1, 0)
    turn_qkv(2)
    widen(1, 1)
    widen(1, 2)
    out_block = jnp.concatenate(
        [
            shared_ref[e, qkv_rows:, h * cols : (h + 1) * cols].astype(f32)
            for e in range(experts)
            for h in range(2)
        ],
        axis=0,
    )
    out_wide[...] = jnp.transpose(out_block)
    store(out_wide, out_out)
    widen(1, 3)
    widen(1, 4)
    widen(1, 5)
    for copy in stores:
        copy.wait()


def fused_local(
    tokens,
    cotangent,
    segments,
    pad_mask,
    routes,
    dist_bucket,
    norm_gains,
    qkv_weight,
    out_weight,
    rel_bias,
    router_weight,
    expert_up,
    expert_down,
):
    micro, _, length, width = tokens.shape
    experts = router_weight.shape[2]
    cap = max(2, 3 * length // experts)
    cols = out_weight.shape[1]
    heads = rel_bias.shape[2]
    ffn = expert_up.shape[3]
    slots = experts * cap
    pairs = cols // 128
    shared_rows = 3 * cols // experts + width // experts // 2
    lay = Layout()
    lay.experts = experts
    lay.cap = cap
    lay.buckets = rel_bias.shape[1]
    lay.wide = min(ffn, 256)
    chunks = experts // 2
    lay.sems = (36, 7 * chunks + experts + 8 * (experts - 1) + 24)
    bf = jnp.bfloat16
    f32 = jnp.float32
    vm = pltpu.VMEM
    shape = jax.ShapeDtypeStruct
    dma = pltpu.SemaphoreType.DMA
    scratch = [
        vm((micro, length), jnp.int32),
        vm((micro, length), jnp.int32),
        vm((micro, 2, length), jnp.int32),
        vm((1, length), jnp.int32),
        vm((2, width), bf),
        vm((heads, lay.buckets), bf),
        vm((experts, width), bf),
        vm((width, ffn), bf),
        vm((ffn, width), bf),
        vm((ffn, width), bf),
        vm((width, ffn), bf),
        vm((3, cols, width), bf),
        vm((width, cols), bf),
        vm((3, width, cols), bf),
        vm((cols, width), bf),
        vm((micro, length, width), bf),
        vm((length, width), bf),
        vm((experts, micro, 2, length), jnp.int32),
        vm((slots, length), bf),
        vm((micro, pairs, length, 2 * length), f32),
        vm((micro, pairs, length, 2 * length), f32),
        vm((micro, length, width), bf),
        vm((3, micro, length, cols), bf),
        vm((micro, length, cols), bf),
        vm((length, width), f32),
        vm((length, width), f32),
        vm((length, width), f32),
        vm((length, width), bf),
        vm((experts, length), f32),
        vm((experts, length), f32),
        vm((experts, width), bf),
        vm((2 * pairs, length, length), f32),
        vm((experts, cap, width), bf),
        vm((experts, micro, cap, width), bf),
        vm((experts, cap, width), bf),
        vm((experts, micro, cap, width), bf),
        vm((experts, micro, cap, ffn), bf),
        vm((experts, micro, cap, ffn), bf),
        vm((micro, 2, cap, width), f32),
        vm((experts, cap, width), bf),
        vm((experts, cap, width), bf),
        vm((experts, cap, width), bf),
        vm((experts, cap, width), bf),
        vm((length, width), f32),
        vm((experts, micro, cap, experts), f32),
        vm((experts, micro, cap, width), bf),
        vm((micro, experts, 8, 128), f32),
        vm((experts, 8, 128), f32),
        vm((experts, 8, 128), f32),
        vm((experts, 8, 128), f32),
        vm((experts, micro, cap, ffn), bf),
        vm((experts, cap, width), bf),
        vm((experts, cap, width), bf),
        vm((experts, cap, width), bf),
        vm((experts, cap, width), bf),
        vm((length, width), f32),
        vm((micro, length, width), bf),
        vm((micro, length, cols), bf),
        vm((3, micro, length, cols), bf),
        vm((length, width), bf),
        vm((length, width), bf),
        vm((length, width), f32),
        vm((length, width), bf),
        vm((micro, experts, length, width), bf),
        vm((experts, micro, length, cols), bf),
        vm((micro, 3 * cols, length), bf),
        vm((experts, micro, 3 * cols // experts, length), bf),
        vm((width, length), bf),
        vm((experts, micro, width // experts, length), bf),
        vm((experts, 2 * experts, 128), f32),
        vm((experts, 2 * experts, 128), f32),
        vm((experts, 2 * experts, 128), f32),
        vm((experts, 2 * experts, 128), f32),
        vm((length, width), bf),
        vm((experts, shared_rows, width), bf),
        vm((experts - 1, shared_rows, width), bf),
        vm((4, cap, width), bf),
        vm((2, micro, 3 * cols // experts, length), bf),
        dma((12,)),
        dma((lay.sems[0],)),
        dma((lay.sems[1],)),
    ]
    whole = pl.BlockSpec(memory_space=pltpu.VMEM)
    anywhere = pl.BlockSpec(memory_space=pl.ANY)
    out_shape = (
        vm((micro, length, width // 2), f32),
        vm((micro, length, width // 2), f32),
        vm((2, width), f32),
        vm((experts, shared_rows, width), bf),
        vm((heads, 128), f32),
        vm((experts, width), f32),
        vm((width, ffn), bf),
        vm((ffn, width), bf),
    )
    results = pl.pallas_call(
        partial(layer_kernel, lay),
        out_shape=out_shape,
        in_specs=[anywhere] * 13,
        out_specs=[whole] * 8,
        scratch_shapes=scratch,
        name="two_sections",
        compiler_params=pltpu.CompilerParams(
            collective_id=0, has_side_effects=True, vmem_limit_bytes=55 * 1024 * 1024
        ),
    )(
        tokens[:, 0],
        cotangent[:, 0],
        segments[:, 0],
        pad_mask[:, 0],
        routes[:, 0].transpose(0, 2, 1),
        dist_bucket[None],
        norm_gains[0],
        qkv_weight[0].transpose(1, 0, 2),
        out_weight[0],
        rel_bias[0].T,
        router_weight[0].T,
        expert_up[0, 0],
        expert_down[0, 0],
    )
    section_out, input_grads, gains, bias, router, qkv, out, up, down = pl.pallas_call(
        widen_kernel,
        out_shape=(
            shape((micro, length, width // 2), f32),
            shape((micro, length, width // 2), f32),
            shape((2, width), f32),
            shape((heads, 1, lay.buckets), f32),
            shape((experts, width), f32),
            shape((3, width, cols), f32),
            shape((cols, width), f32),
            shape((width, ffn), f32),
            shape((ffn, width), f32),
        ),
        in_specs=[whole] * 8,
        out_specs=[anywhere] * 9,
        scratch_shapes=[
            vm((width, ffn), f32),
            vm((ffn, width), f32),
            vm((3, width, cols), f32),
            vm((cols, width), f32),
            vm((heads, 1, lay.buckets), f32),
            dma((21,)),
        ],
        name="widen",
        compiler_params=pltpu.CompilerParams(vmem_limit_bytes=40 * 1024 * 1024),
    )(*[pltpu.with_memory_space_constraint(result, pltpu.VMEM) for result in results])
    return (
        section_out[None, :, None],
        input_grads[None, :, None],
        gains[None],
        qkv.transpose(1, 0, 2)[None],
        out[None],
        bias.transpose(1, 2, 0),
        router.T[None],
        up[None, None],
        down[None, None],
    )


def fits_kernel(mesh):
    return mesh.shape["section"] == 2 and mesh.shape["tensor"] == 2 and mesh.shape["dp"] == 8


def solution(mesh):
    in_specs = (
        P(None, "dp", None, None),
        P(None, "dp", None, None),
        P(None, "dp", None),
        P(None, "dp", None),
        P(None, "dp", None, None),
        P(),
        P("section", None, None),
        P("section", None, None, "tensor"),
        P("section", "tensor", None),
        P("section", None, "tensor"),
        P("section", None, None),
        P("section", "dp", None, "tensor"),
        P("section", "dp", "tensor", None),
    )
    out_specs = (
        P("section", None, "dp", None, "tensor"),
        P("section", None, "dp", None, "tensor"),
        P("section", None, None),
        P("section", None, None, "tensor"),
        P("section", "tensor", None),
        P("section", None, "tensor"),
        P("section", None, None),
        P("section", "dp", None, "tensor"),
        P("section", "dp", "tensor", None),
    )
    body = fused_local if fits_kernel(mesh) else local
    return jax.shard_map(body, mesh=mesh, in_specs=in_specs, out_specs=out_specs, check_vma=False)
```

```python
from functools import partial

import jax
import jax.numpy as jnp
from jax import lax
from jax.experimental import pallas as pl
from jax.experimental.pallas import tpu as pltpu
from jax.sharding import PartitionSpec as P

norm_eps = 1e-06
masked_score = -1e30
highest = lax.Precision.HIGHEST


def shifted(block, axis, distance):
    devices = range(lax.axis_size(axis))
    route = [(i - distance, i) for i in devices if i - distance in devices]
    return lax.ppermute(block, axis, route)


def normalize(values, gain_row):
    scale_inv = lax.rsqrt(jnp.mean(values * values, axis=-1, keepdims=True) + norm_eps)
    return values * scale_inv * gain_row


def normalize_back(values, gain_row, upstream):
    scale_inv = lax.rsqrt(jnp.mean(values * values, axis=-1, keepdims=True) + norm_eps)
    normed = values * scale_inv
    gain_grad = jnp.sum(upstream * normed, axis=0)
    scaled = upstream * gain_row
    input_grad = scale_inv * (scaled - normed * jnp.mean(scaled * normed, axis=-1, keepdims=True))
    return (input_grad, gain_grad)


def send_rows(rows):
    return lax.all_to_all(rows, "dp", split_axis=0, concat_axis=0, tiled=True)


def sum_slots(partial_rows):
    return lax.psum(partial_rows, "tensor")


def score_context(segment_row, pad_row, dist_bucket, bucket_count):
    length = segment_row.shape[0]
    places = jnp.arange(length, dtype=jnp.int32)
    offsets = jnp.clip(places[:, None] - places[None, :], 0, length - 1)
    bucket_grid = jnp.take(dist_bucket, offsets)
    bucket_onehot = (
        bucket_grid[:, :, None] == jnp.arange(bucket_count, dtype=jnp.int32)[None, None, :]
    ).astype(jnp.float32)
    allowed = (places[None, :] <= places[:, None]) & (segment_row[:, None] == segment_row[None, :])
    allowed = allowed & ((pad_row[None, :] == 1) | (places[None, :] == places[:, None]))
    return (bucket_onehot, allowed)


def attention_front(inputs, context, weights):
    segment_row, pad_row, route_rows, dist_bucket = context
    gain_pair, qkv_weight, out_weight, bias_table, router_weight, upper_weight, lower_weight = (
        weights
    )
    length = inputs.shape[0]
    head_count = bias_table.shape[1]
    bucket_onehot, allowed = score_context(segment_row, pad_row, dist_bucket, bias_table.shape[0])
    normed_one = normalize(inputs, gain_pair[0]).astype(jnp.bfloat16)
    qkv_rows = jnp.einsum(
        "ld,dch->lch", normed_one, qkv_weight, preferred_element_type=jnp.float32
    ).astype(jnp.bfloat16)
    head_dim = qkv_rows.shape[2] // head_count
    queries = qkv_rows[:, 0].reshape(length, head_count, head_dim)
    keys_in = qkv_rows[:, 1].reshape(length, head_count, head_dim)
    values_in = qkv_rows[:, 2].reshape(length, head_count, head_dim)
    raw_scores = jnp.einsum("qhd,khd->hqk", queries, keys_in, preferred_element_type=jnp.float32)
    bias_grid = jnp.einsum(
        "qkb,bh->hqk", bucket_onehot, bias_table.astype(jnp.float32), precision=highest
    )
    logits = jnp.where(allowed[None], 0.125 * raw_scores + bias_grid, masked_score)
    exp_terms = jnp.exp(logits - jnp.max(logits, axis=-1, keepdims=True))
    attn_probs = exp_terms / jnp.sum(exp_terms, axis=-1, keepdims=True)
    mixed_rows = jnp.einsum(
        "hqk,khd->qhd",
        attn_probs.astype(jnp.bfloat16),
        values_in,
        preferred_element_type=jnp.float32,
    )
    mixed_rows = mixed_rows.reshape(length, -1).astype(jnp.bfloat16)
    return (normed_one, queries, keys_in, values_in, attn_probs, mixed_rows, bucket_onehot)


def slot_tables(route_rows, experts, capacity):
    flat_routes = route_rows.reshape(-1)
    route_hits = (flat_routes[:, None] == jnp.arange(experts, dtype=jnp.int32)[None, :]).astype(
        jnp.int32
    )
    earlier = jnp.cumsum(route_hits, axis=0) - route_hits
    position = jnp.sum(earlier * route_hits, axis=1)
    target = flat_routes * capacity + position
    slot_hits = (
        jnp.arange(experts * capacity, dtype=jnp.int32)[:, None] == target[None, :]
    ).astype(jnp.int32)
    source = jnp.sum(slot_hits * jnp.arange(target.shape[0], dtype=jnp.int32)[None, :], axis=1)
    filled = jnp.sum(slot_hits, axis=1) > 0
    return (target, source, filled, route_hits)


def route_gates(normed_two, router_weight, route_hits):
    length = normed_two.shape[0]
    logits = jnp.dot(normed_two, router_weight, preferred_element_type=jnp.float32)
    route_onehot = route_hits.reshape(length, 2, -1).astype(jnp.float32)
    chosen = jnp.einsum("le,lre->lr", logits, route_onehot, precision=highest)
    return (jax.nn.softmax(chosen, axis=-1), route_onehot)


def gather_back(back_slots, target, length):
    flat_slots = back_slots.reshape(-1, back_slots.shape[-1])
    return jnp.take(flat_slots, target, axis=0).reshape(length, 2, -1)


def forward_rest(inputs, front, context, weights):
    segment_row, pad_row, route_rows, dist_bucket = context
    gain_pair, qkv_weight, out_weight, bias_table, router_weight, upper_weight, lower_weight = (
        weights
    )
    mixed_rows = front[5]
    length, model_width = inputs.shape
    experts = router_weight.shape[1]
    capacity = max(2, 3 * length // experts)
    local_experts = upper_weight.shape[0]
    attn_out = lax.psum(
        jnp.dot(mixed_rows, out_weight, preferred_element_type=jnp.float32), "tensor"
    )
    middle = inputs + attn_out
    normed_two = normalize(middle, gain_pair[1]).astype(jnp.bfloat16)
    target, source, filled, route_hits = slot_tables(route_rows, experts, capacity)
    outgoing = jnp.where(
        filled[:, None], jnp.take(normed_two, source // 2, axis=0), jnp.zeros((), jnp.bfloat16)
    )
    outgoing = outgoing.reshape(experts, capacity, model_width)
    arrived = send_rows(outgoing)
    grouped = arrived.reshape(-1, local_experts, capacity, model_width)
    pre_act = jnp.einsum(
        "secd,edf->secf", grouped, upper_weight, preferred_element_type=jnp.float32
    )
    hidden = jax.nn.gelu(pre_act, approximate=False).astype(jnp.bfloat16)
    partial_out = jnp.einsum(
        "secf,efd->secd", hidden, lower_weight, preferred_element_type=jnp.float32
    )
    summed = sum_slots(partial_out)
    returned = summed.astype(jnp.bfloat16).reshape(arrived.shape[0], arrived.shape[1], -1)
    back_slots = send_rows(returned)
    gate_probs, route_onehot = route_gates(normed_two, router_weight, route_hits)
    back_rows = gather_back(back_slots, target, length)
    output = middle + jnp.sum(gate_probs[:, :, None] * back_rows.astype(jnp.float32), axis=1)
    return (output, (attn_out, arrived, back_slots, pre_act))


def backward_layer(inputs, upstream, context, weights, front, saved_state):
    segment_row, pad_row, route_rows, dist_bucket = context
    gain_pair, qkv_weight, out_weight, bias_table, router_weight, upper_weight, lower_weight = (
        weights
    )
    normed_one, queries, keys_in, values_in, attn_probs, mixed_rows, bucket_onehot = front
    attn_out, arrived_rows, back_slots, pre_rows = saved_state
    length, model_width = inputs.shape
    head_count = bias_table.shape[1]
    head_cols = qkv_weight.shape[2]
    experts = router_weight.shape[1]
    capacity = max(2, 3 * length // experts)
    local_experts = upper_weight.shape[0]
    middle = inputs + attn_out
    normed_two = normalize(middle, gain_pair[1]).astype(jnp.bfloat16)
    target, source, filled, route_hits = slot_tables(route_rows, experts, capacity)
    gate_probs, route_onehot = route_gates(normed_two, router_weight, route_hits)
    back_rows = gather_back(back_slots, target, length)
    gate_grad = jnp.sum(upstream[:, None, :] * back_rows.astype(jnp.float32), axis=-1)
    chosen_grad = gate_probs * (gate_grad - jnp.sum(gate_probs * gate_grad, axis=-1, keepdims=True))
    logit_grad = jnp.einsum("lr,lre->le", chosen_grad, route_onehot, precision=highest).astype(
        jnp.bfloat16
    )
    router_grad = jnp.dot(normed_two.T, logit_grad, preferred_element_type=jnp.float32)
    normed_two_grad = jnp.dot(logit_grad, router_weight.T, preferred_element_type=jnp.float32)
    route_grads = (
        (gate_probs[:, :, None] * upstream[:, None, :])
        .reshape(2 * length, model_width)
        .astype(jnp.bfloat16)
    )
    slot_grads = jnp.where(
        filled[:, None], jnp.take(route_grads, source, axis=0), jnp.zeros((), jnp.bfloat16)
    )
    arrived_grads = send_rows(slot_grads.reshape(experts, capacity, model_width))
    grouped = arrived_rows.reshape(-1, local_experts, capacity, model_width)
    grouped_grads = arrived_grads.reshape(-1, local_experts, capacity, model_width)
    hidden, gelu_pull = jax.vjp(partial(jax.nn.gelu, approximate=False), pre_rows)
    hidden_low = hidden.astype(jnp.bfloat16)
    down_grad = jnp.einsum(
        "secf,secd->efd", hidden_low, grouped_grads, preferred_element_type=jnp.float32
    )
    hidden_grad = jnp.einsum(
        "secd,efd->secf", grouped_grads, lower_weight, preferred_element_type=jnp.float32
    )
    pre_grad = gelu_pull(hidden_grad)[0].astype(jnp.bfloat16)
    up_grad = jnp.einsum("secd,secf->edf", grouped, pre_grad, preferred_element_type=jnp.float32)
    rows_grad = sum_slots(
        jnp.einsum("secf,edf->secd", pre_grad, upper_weight, preferred_element_type=jnp.float32)
    )
    sent_back = send_rows(
        rows_grad.astype(jnp.bfloat16).reshape(arrived_rows.shape[0], arrived_rows.shape[1], -1)
    )
    copy_grads = gather_back(sent_back, target, length).astype(jnp.float32)
    normed_two_grad = normed_two_grad + jnp.sum(copy_grads, axis=1)
    middle_part, gain_two = normalize_back(middle, gain_pair[1], normed_two_grad)
    middle_grad = upstream + middle_part
    attn_grad = middle_grad.astype(jnp.bfloat16)
    out_grad = jnp.dot(mixed_rows.T, attn_grad, preferred_element_type=jnp.float32)
    mixed_grad = jnp.dot(attn_grad, out_weight.T, preferred_element_type=jnp.float32).astype(
        jnp.bfloat16
    )
    mixed_grad = mixed_grad.reshape(length, head_count, -1)
    prob_grad = jnp.einsum(
        "qhd,khd->hqk", mixed_grad, values_in, preferred_element_type=jnp.float32
    )
    value_grad = jnp.einsum(
        "hqk,qhd->khd",
        attn_probs.astype(jnp.bfloat16),
        mixed_grad,
        preferred_element_type=jnp.float32,
    )
    score_grad = attn_probs * (prob_grad - jnp.sum(prob_grad * attn_probs, axis=-1, keepdims=True))
    table_grad = jnp.einsum("hqk,qkb->bh", score_grad, bucket_onehot, precision=highest)
    raw_grad = (0.125 * score_grad).astype(jnp.bfloat16)
    query_grad = jnp.einsum("hqk,khd->qhd", raw_grad, keys_in, preferred_element_type=jnp.float32)
    key_grad = jnp.einsum("hqk,qhd->khd", raw_grad, queries, preferred_element_type=jnp.float32)
    qkv_grad = (
        jnp.stack([query_grad, key_grad, value_grad], axis=1)
        .reshape(length, 3, head_cols)
        .astype(jnp.bfloat16)
    )
    qkv_weight_grad = jnp.einsum(
        "ld,lch->dch", normed_one, qkv_grad, preferred_element_type=jnp.float32
    )
    normed_one_grad = lax.psum(
        jnp.einsum("lch,dch->ld", qkv_grad, qkv_weight, preferred_element_type=jnp.float32),
        "tensor",
    )
    input_part, gain_one = normalize_back(inputs, gain_pair[0], normed_one_grad)
    input_grad = middle_grad + input_part
    gain_grads = jnp.stack([gain_one, gain_two])
    return (
        input_grad,
        (gain_grads, qkv_weight_grad, out_grad, table_grad, router_grad, up_grad, down_grad),
    )


def pick_context(segments, pad_mask, routes, dist_bucket, micro_slot):
    segment_row = lax.dynamic_index_in_dim(segments[:, 0], micro_slot, 0, False)
    pad_row = lax.dynamic_index_in_dim(pad_mask[:, 0], micro_slot, 0, False)
    route_rows = lax.dynamic_index_in_dim(routes[:, 0], micro_slot, 0, False)
    return (segment_row, pad_row, route_rows, dist_bucket)


def place_row(store_all, new_value, micro_slot, is_valid):
    current = lax.dynamic_index_in_dim(store_all, micro_slot, 0, False)
    return lax.dynamic_update_index_in_dim(
        store_all, jnp.where(is_valid, new_value, current), micro_slot, 0
    )


def pick_row(store_all, micro_slot):
    return lax.dynamic_index_in_dim(store_all, micro_slot, 0, False)


def mask_grad(grad_value, is_valid):
    return jnp.where(is_valid, grad_value, jnp.zeros((), grad_value.dtype))


def tensor_half(full_rows, tensor_id, half_width):
    return lax.dynamic_slice_in_dim(full_rows, tensor_id * half_width, half_width, 2)[None, :, None]


def local(
    tokens,
    cotangent,
    segments,
    pad_mask,
    routes,
    dist_bucket,
    norm_gains,
    qkv_weight,
    out_weight,
    rel_bias,
    router_weight,
    expert_up,
    expert_down,
):
    section_id = lax.axis_index("section")
    section_count = lax.axis_size("section")
    micro_count = tokens.shape[0]
    length = tokens.shape[2]
    model_width = tokens.shape[3]
    tick_count = micro_count + section_count - 1
    weights = (
        norm_gains[0].astype(jnp.float32),
        qkv_weight[0],
        out_weight[0],
        rel_bias[0],
        router_weight[0],
        expert_up[0],
        expert_down[0],
    )
    empty_rows = jnp.zeros((length, model_width), jnp.bfloat16)
    arriving = empty_rows
    kept_inputs = jnp.zeros((micro_count, length, model_width), jnp.bfloat16)
    section_out = jnp.zeros((micro_count, length, model_width), jnp.float32)
    for tick_index in range(tick_count):
        micro_index = tick_index - section_id
        is_valid = (micro_index >= 0) & (micro_index < micro_count)
        micro_slot = jnp.clip(micro_index, 0, micro_count - 1)
        own_rows = tokens[tick_index, 0] if tick_index < micro_count else empty_rows
        layer_in = jnp.where(section_id == 0, own_rows, arriving)
        context = pick_context(segments, pad_mask, routes, dist_bucket, micro_slot)
        inputs = layer_in.astype(jnp.float32)
        front = attention_front(inputs, context, weights)
        result, saved_state = forward_rest(inputs, front, context, weights)
        section_out = place_row(section_out, result, micro_slot, is_valid)
        kept_inputs = place_row(kept_inputs, layer_in, micro_slot, is_valid)
        arriving = shifted(result.astype(jnp.bfloat16), "section", 1)
    returning = empty_rows
    input_store = jnp.zeros((micro_count, length, model_width), jnp.float32)
    totals = None
    for tick_index in range(tick_count):
        micro_index = tick_index - (section_count - 1 - section_id)
        is_valid = (micro_index >= 0) & (micro_index < micro_count)
        micro_slot = jnp.clip(micro_index, 0, micro_count - 1)
        own_rows = cotangent[tick_index, 0] if tick_index < micro_count else empty_rows
        upstream = jnp.where(section_id == section_count - 1, own_rows, returning).astype(
            jnp.float32
        )
        inputs = pick_row(kept_inputs, micro_slot).astype(jnp.float32)
        context = pick_context(segments, pad_mask, routes, dist_bucket, micro_slot)
        front = attention_front(inputs, context, weights)
        saved_state = forward_rest(inputs, front, context, weights)[1]
        input_grad, grad_set = backward_layer(
            inputs, upstream, context, weights, front, saved_state
        )
        input_store = place_row(input_store, input_grad, micro_slot, is_valid)
        grad_set = jax.tree.map(partial(mask_grad, is_valid=is_valid), grad_set)
        totals = grad_set if totals is None else jax.tree.map(jnp.add, totals, grad_set)
        returning = shifted(input_grad.astype(jnp.bfloat16), "section", -1)
    shared = lax.psum((totals[0], totals[1], totals[2], totals[3], totals[4]), "dp")
    tensor_id = lax.axis_index("tensor")
    half_width = model_width // lax.axis_size("tensor")
    return (
        tensor_half(section_out, tensor_id, half_width),
        tensor_half(input_store, tensor_id, half_width),
        shared[0][None],
        shared[1][None],
        shared[2][None],
        shared[3][None],
        shared[4][None],
        totals[5][None],
        totals[6][None],
    )


def gelu_parts(values):
    share = 0.5 + 0.5 * lax.erf(values * 0.7071067811865476)
    return (values * share, share + values * (0.3989422804014327 * jnp.exp(-0.5 * values * values)))


def nn(left, right):
    return lax.dot_general(left, right, (((1,), (0,)), ((), ())), preferred_element_type=jnp.float32)


def nt(left, right):
    return lax.dot_general(left, right, (((1,), (1,)), ((), ())), preferred_element_type=jnp.float32)


def tn(left, right):
    return lax.dot_general(left, right, (((0,), (0,)), ((), ())), preferred_element_type=jnp.float32)


def split_low(values):
    high = values.astype(jnp.bfloat16)
    return (high, (values - high.astype(jnp.float32)).astype(jnp.bfloat16))


def inverse_rms(values):
    return lax.rsqrt(jnp.mean(values * values, axis=-1, keepdims=True) + norm_eps)


class Layout:
    pass


def layer_kernel(lay, *refs):
    (
        tok_ref, cot_ref, seg_hbm, pad_hbm, routes_hbm, dist_hbm, gains_hbm, qkvw_hbm, outw_hbm, relb_hbm, wr_hbm,
        up_ref, down_ref,
        secout_ref, ingrad_ref, ggain_ref, shared_ref, gbias_ref, grouter_ref, guv, gdv,
        seg_ref, pad_ref, routes_ref, dist_ref, gains_ref, relb_ref, wr_ref, upv, downv, upt, downt, qkvwt, outwt, qkvw_ref, outw_ref, xb, dyb, rr, place, bias_buf, probs_buf, no1, qkvb, mixed, att_send, att_recv, mid, ntb,
        gate_t, hit_t, wrp, score_sum, disp_x, xrows, disp_y, dyrows, hidden, dgelu, halves, eo_send, eo_recv, eob, eoret, out_own,
        other, gate_slots, og, gg_part, gg_other, gg_send, gg_recv, pg, cg_send, cg_recv, cgb, cgret, mgrad, ag, mg, qkvg,
        no_send, no_recv, ig_own, dy_send,
        no_all, mix_all, qgt, qt_all, agt, agt_all, small_send, small_in, small_all, small_sib,
        x_send, rs_buf, rs_in, relay_buf, relay_q,
        wsem, ss, rs,
    ) = refs
    bf = jnp.bfloat16
    f32 = jnp.float32
    micro, length, width = tok_ref.shape
    experts = lay.experts
    cap = lay.cap
    cols = outw_ref.shape[0]
    pairs = cols // 128
    ffn = up_ref.shape[1]
    slots = experts * cap
    half = width // 2
    s = lax.axis_index("section")
    d = lax.axis_index("dp")
    t = lax.axis_index("tensor")
    u = 1 - t
    sib = (s, d, u)
    across = (1 - s, d, t)
    bits = [lax.rem(d // bit, 2) for bit in (1, 2, 4)]

    def partner(flip):
        index = d
        for place, bit in enumerate((1, 2, 4)):
            index = index + (flip // bit) % 2 * (bit - 2 * bit * bits[place])
        return index

    peer = [partner(flip) for flip in (0, 4, 1, 6, 2, 5, 3, 7)]
    steps = range(1, experts)
    relayed = (5, 7)
    chunks = range(experts // 2)

    def pair(c):
        return pl.ds(2 * c, 2)

    def partner_at(k):
        c = k // 2
        return partner(c + (k % 2) * (4 + 2 * (c % 2) + c // 2 - c))


    def remote(src, dst, sem, device, k=0):
        return pltpu.make_async_remote_copy(
            src_ref=src,
            dst_ref=dst,
            send_sem=ss.at[sem[0]],
            recv_sem=rs.at[sem[1] + k],
            device_id=device,
            device_id_type=pl.DeviceIdType.MESH,
        )

    counter = [0, 0]

    def take(arrivals=1):
        pair_of = (counter[0], counter[1])
        counter[0] += 1
        counter[1] += arrivals
        return pair_of

    def all_sent(like, sem):
        remote(like, like, sem, sib).wait_send()

    def all_here(like, sem, k=0):
        remote(like, like, sem, sib, k).wait_recv()

    ring_hops = experts - 1
    sem_routes = take()
    sem_x = take()
    sem_relay = [take(len(relayed)) for _ in range(2)]
    sem_pass = [take(0) for _ in range(2)]
    sem_relay_q = take(len(relayed))
    sem_pass_q = take(0)
    sem_xf = take()
    sem_dy = take()
    sem_att = take()
    sem_eo = take(len(chunks))
    sem_cg = take(len(chunks))
    sem_ag = take()
    sem_no = take()
    sem_so = take()
    sem_ig = take()
    sem_dx = take(len(chunks))
    sem_dxf = take(len(chunks))
    sem_ddy = take(len(chunks))
    sem_ddyf = take(len(chunks))
    sem_re = take()
    sem_rc = take()
    sem_gg = take()
    sem_gg_core = take(len(chunks))
    sem_qgt = take(experts)
    sem_agt = take()
    sem_agtf = take()
    sem_small = take()
    sem_back = take()
    sem_sums = take()
    sem_noall = take()
    sem_ring_no = take(2 * ring_hops)
    sem_ring_mix = take(2 * ring_hops)
    sem_ring_sum = (take(0)[0], sem_ring_no[1])
    sem_ring_out = take(4 * ring_hops)
    assert tuple(counter) == lay.sems

    def block(index, rows):
        return pl.ds(pl.multiple_of(index * rows, rows), rows)

    place_y = lax.rem(d, 2)
    place_z = d // 2
    ring_at = place_z + place_y * (experts - 1 - 2 * place_z)

    def ring_device(position):
        p = lax.rem(position + 2 * experts, experts)
        return 2 * p + (p // (experts // 2)) * (2 * experts - 1 - 4 * p)

    def hops(number, direction):
        return experts // 2 - (number % 2 == (direction > 0))

    def hop_index(number, direction, k):
        return number * ring_hops + k + (0 if direction > 0 else hops(number, 1))

    def lines_of(amount):
        return [(number, direction) for number in range(amount) for direction in (1, -1)]

    def ring_gather(parts, at_half=None):
        def hop(number, direction, k):
            view, sem, first = parts[number]
            held = view(ring_device(ring_at - direction * k))
            index = hop_index(number, direction, k) - first * ring_hops
            return remote(held, held, sem, (s, ring_device(ring_at + direction), t), index)

        lines = lines_of(len(parts))
        for line in lines:
            hop(*line, 0).start()

        def one(k, carry):
            for line in lines:
                hop(*line, k - 1).wait_recv()
                hop(*line, k).start()
            return carry

        short = experts // 2 - 1
        lax.fori_loop(1, short, one, 0)
        if at_half is not None:
            at_half()
        for line in lines:
            hop(*line, short - 1).wait_recv()
            if hops(*line) > short:
                hop(*line, short).start()
        for line in lines:
            if hops(*line) > short:
                hop(*line, short).wait_recv()

    small_loads = [
        pltpu.make_async_copy(src, dst, wsem.at[5 + i])
        for i, (src, dst) in enumerate(
            (
                (routes_hbm, routes_ref),
                (wr_hbm, wr_ref),
                (seg_hbm, seg_ref),
                (pad_hbm, pad_ref),
                (dist_hbm, dist_ref),
                (gains_hbm, gains_ref),
                (relb_hbm, relb_ref),
            )
        )
    ]
    for copy in small_loads:
        copy.start()
    load_up = pltpu.make_async_copy(up_ref, upv, wsem.at[0])
    load_down = pltpu.make_async_copy(down_ref, downv, wsem.at[1])
    load_qkvw = pltpu.make_async_copy(qkvw_hbm, qkvw_ref, wsem.at[2])
    load_outw = pltpu.make_async_copy(outw_hbm, outw_ref, wsem.at[3])
    load_tok = pltpu.make_async_copy(tok_ref, xb, wsem.at[4])
    load_cot = pltpu.make_async_copy(cot_ref.at[t], dyb, wsem.at[4])

    @pl.when(s == 0)
    def _():
        load_tok.start()

    @pl.when(s == 1)
    def _():
        load_cot.start()

    load_qkvw.start()
    load_outw.start()
    load_up.start()
    load_down.start()

    barrier = pltpu.get_barrier_semaphore()
    for k in steps:
        pl.semaphore_signal(barrier, inc=1, device_id=(s, peer[k], t), device_id_type=pl.DeviceIdType.MESH)
    pl.semaphore_signal(barrier, inc=1, device_id=sib, device_id_type=pl.DeviceIdType.MESH)
    for k in (0,) + relayed:
        pl.semaphore_signal(barrier, inc=1, device_id=(1 - s, peer[k], t), device_id_type=pl.DeviceIdType.MESH)
    pl.semaphore_wait(barrier, experts + 1 + len(relayed))

    for copy in small_loads:
        copy.wait()

    for k in steps:
        remote(routes_ref, rr.at[k], sem_routes, (s, peer[k], t)).start()
    rr[0] = routes_ref[...]

    lanes8 = lax.broadcasted_iota(jnp.int32, (experts, length), 0)
    row_at = lax.broadcasted_iota(jnp.int32, (length, length), 0)
    col_at = lax.broadcasted_iota(jnp.int32, (length, length), 1)
    before = (row_at < col_at).astype(bf)
    slot_at = lax.broadcasted_iota(jnp.int32, (cap, length), 0).astype(f32)

    expert_of = jnp.zeros((experts, length), jnp.int32)
    for k in range(experts):
        expert_of = jnp.where(lanes8 == k, peer[k], expert_of)
    turn = (lax.broadcasted_iota(jnp.int32, (experts, experts), 1) == expert_of[:, 0:experts]).astype(f32).astype(bf)
    wrp[...] = nn(turn, wr_ref[...]).astype(bf)
    own_routes = routes_ref[t]
    hits = (expert_of == own_routes[0:1, :]) | (expert_of == own_routes[1:2, :])
    hit_f = hits.astype(f32)
    hit_t[...] = hit_f
    spot = jnp.where(hits, nn(hit_f.astype(bf), before), -1.0)
    for e in range(experts):
        place[e * cap : (e + 1) * cap, :] = (slot_at == spot[e : e + 1, :]).astype(f32).astype(bf)

    def to_relay(source, k, leg):
        i = relayed.index(k)
        return remote(source, relay_buf.at[leg * len(relayed) + i], sem_relay[leg], across, i)

    def relay(landing, sem, leg):
        for i, k in enumerate(relayed):
            held = relay_buf.at[leg * len(relayed) + i]
            all_here(held, sem_relay[leg], i)
            through = (sem_pass[leg][0], sem[1] + k // 2)
            remote(held, landing.at[k, t], through, (0, peer[k], t)).start()

    def dispatch(rows, send, landing, sem, sem_fwd, leg=None, both=False):
        send[...] = nn(place[...], rows).astype(bf).reshape(send.shape)

        def direct(k):
            remote(send.at[k], landing.at[k, t], sem, (s, peer[k], t), k // 2).start()

        def start_relayed():
            for k in relayed:
                to_relay(send.at[k], k, leg).start()

        def start_direct():
            for k in relayed:
                direct(k)

        direct(1)
        if both:
            pl.when(s == 0)(start_relayed)
        elif leg is not None:
            start_relayed()
        for k in steps[1:]:
            if k not in relayed:
                direct(k)
        if both:
            pl.when(s == 1)(start_direct)
        elif leg is None:
            start_direct()
        landing[0, t] = send[0]

        def arrive(c):
            held = landing.at[pair(c), t]
            all_here(landing.at[1, t] if isinstance(c, int) and c == 0 else held, sem, c)
            remote(held, held, sem_fwd, sib, c).start()

        def joined(c):
            all_here(landing.at[pair(c), t], sem_fwd, c)

        def drain(zero):
            all_sent(send, sem_fwd)
            if zero:
                all_sent(send.at[0 : experts - 1 - len(relayed)], sem)
                all_sent(send.at[0 : len(relayed)], sem_relay[leg])
            else:
                all_sent(send.at[1:experts], sem)

        return arrive, joined, drain

    def stream(dispatched, first, second, finish_chunk, eager, zero):
        arrive, joined, drain = dispatched
        last = len(chunks) - 1
        arrive(0)
        joined(0)

        def one(c, carry):
            first(c)
            if eager:
                pl.when(c > 0)(lambda: finish_chunk(c - 1))
                pl.when(c < last)(lambda: arrive(c + 1))
                second(c)
            else:
                second(c)

                @pl.when(c < last)
                def _():
                    arrive(c + 1)
                    finish_chunk(c)


            @pl.when(c < last)
            def _():
                joined(c + 1)

            return carry

        lax.fori_loop(0, len(chunks), one, 0)
        finish_chunk(last)
        drain(zero)

    def turn_weights():
        upt[...] = jnp.transpose(upv[...])
        downt[...] = jnp.transpose(downv[...])
        for c in range(3):
            qkvwt[c] = jnp.transpose(qkvw_ref[c])
        outwt[...] = jnp.transpose(outw_ref[...])

    def other_experts():
        all_here(rr.at[1:experts], sem_routes)

        def one(i, carry):
            q = i // micro
            m = i % micro
            pair = rr[q, m]
            first = pair[0:1, :] == d
            mine = first | (pair[1:2, :] == d)
            mine_f = jnp.broadcast_to(mine.astype(f32), (experts, length))
            spots = jnp.where(mine_f > 0.0, nn(mine_f.astype(bf), before), -1.0)
            where_slot = (slot_at == spots[0:1, :]).astype(f32).astype(bf)
            partner = jnp.where(first, pair[1:2, :], pair[0:1, :])
            partner_hot = (lanes8 == partner).astype(f32).astype(bf)
            other[q, m] = nt(where_slot, partner_hot)
            return carry

        lax.fori_loop(0, experts * micro, one, 0)

    @pl.when(s == 0)
    def _():
        load_tok.wait()
        load_qkvw.wait()
        load_outw.wait()

    @pl.when(s == 1)
    def _():
        load_cot.wait()
        relay(xrows, sem_dx, 0)
        load_up.wait()
        load_down.wait()
        load_qkvw.wait()
        load_outw.wait()
        turn_weights()
        other_experts()
        arrive, joined, drain = dispatch(dyb[...], disp_y, dyrows, sem_ddy, sem_ddyf)

        def pass_one(c, carry):
            arrive(c)
            return carry

        def join_one(c, carry):
            joined(c)
            return carry

        arrive(0)
        lax.fori_loop(1, len(chunks), pass_one, 0)
        lax.fori_loop(0, len(chunks), join_one, 0)
        drain(False)

    dist_rows = (
        lax.broadcasted_iota(jnp.int32, (lay.buckets, length), 0) == dist_ref[...]
    ).astype(f32).astype(bf)
    bias_rows = nn(relb_ref[...], dist_rows).astype(bf)
    mirror = ((row_at + col_at == length) | (row_at + col_at == 0)).astype(f32).astype(bf)
    bias_back = nn(bias_rows, mirror)
    for m in range(micro):
        seg_rows = jnp.broadcast_to(seg_ref[m : m + 1, :].astype(f32), (length, length))
        pads = jnp.broadcast_to(pad_ref[m : m + 1, :], (length, length))
        allowed = (col_at <= row_at) & (seg_rows == jnp.transpose(seg_rows))
        allowed = allowed & ((pads == 1) | (col_at == row_at))
        for p in range(pairs):
            for h in range(2):
                head = 2 * p + h
                grid = pltpu.roll(
                    jnp.broadcast_to(bias_back[head : head + 1, :], (length, length)), 0, 1, stride=1, stride_axis=0
                )
                bias_buf[m, p, :, h * length : (h + 1) * length] = jnp.where(allowed, grid, masked_score)

    x_copy = remote(x_send, xb.at[t], sem_x, across)
    dy_copy = remote(dy_send, dyb, sem_dy, across)
    x_forward = remote(xb.at[t], xb.at[t], sem_xf, sib)

    def spread_gates(gates_ref):
        return jnp.concatenate(
            [
                jnp.broadcast_to(gates_ref[e : e + 1, :], (cap, length)) * place[e * cap : (e + 1) * cap, :].astype(f32)
                for e in range(experts)
            ],
            axis=0,
        ).astype(bf)

    @pl.when(s == 1)
    def _():
        x_copy.wait_recv()
        x_forward.start()

    gain_one = gains_ref[0:1, :].astype(f32)
    gain_two = gains_ref[1:2, :].astype(f32)
    low_lanes = lax.broadcasted_iota(jnp.int32, (length, 128), 1) < 64

    def both_heads(pair_block):
        zero = jnp.zeros((), bf)
        return jnp.concatenate(
            [jnp.where(low_lanes, pair_block, zero), jnp.where(low_lanes, zero, pair_block)], axis=0
        )

    def attend(m):
        x_rows = xb[m].astype(f32)
        no1[m] = (x_rows * inverse_rms(x_rows) * gain_one).astype(bf)
        for c in range(3):
            qkvb[c, m] = nn(no1[m], qkvw_ref[c]).astype(bf)
        for p in range(pairs):
            at = slice(p * 128, (p + 1) * 128)
            scores = 0.125 * nt(qkvb[0, m, :, at], both_heads(qkvb[1, m, :, at])) + bias_buf[m, p]
            for h in range(2):
                part = scores[:, h * length : (h + 1) * length]
                terms = jnp.exp(part - jnp.max(part, axis=-1, keepdims=True))
                probs_buf[m, p, :, h * length : (h + 1) * length] = terms * (
                    1.0 / jnp.sum(terms, axis=-1, keepdims=True)
                )
            mixed[m, :, at] = nn(probs_buf[m, p].astype(bf), both_heads(qkvb[2, m, :, at])).astype(bf)

    att_copy = remote(att_send, att_recv, sem_att, sib)

    def project_other():
        att_send[...] = nn(mixed[u], outw_ref[...]).astype(bf)
        att_copy.start()

    begin = u + s * (t - u)

    def attend_one(i, carry):
        @pl.when((s == 1) & (i == 1))
        def _():
            x_forward.wait()

        attend(begin + i * (1 - 2 * begin))

        @pl.when((s == 0) & (i == 0))
        def _():
            project_other()

        return carry

    lax.fori_loop(0, micro, attend_one, 0)

    @pl.when(s == 1)
    def _():
        project_other()

    part_own = nn(mixed[t], outw_ref[...])
    att_copy.wait()
    middle = xb[t].astype(f32) + part_own + att_recv[...].astype(f32)
    mid[...] = middle
    ntb[...] = (middle * inverse_rms(middle) * gain_two).astype(bf)

    arrivals = dispatch(ntb[...], disp_x, xrows, sem_dx, sem_dxf, 0, True)
    logits_t = jnp.where(hit_t[...] > 0.0, nt(wrp[...], ntb[...]), masked_score)
    terms = jnp.exp(logits_t - jnp.max(logits_t, axis=0, keepdims=True))
    gate_t[...] = terms / jnp.sum(terms, axis=0, keepdims=True)
    rows_of = 2 * micro * cap

    def flat(ref, chunk):
        return ref[chunk].reshape(rows_of, ref.shape[-1])

    def front_chunk(c):
        value, slope = gelu_parts(nn(flat(xrows, pair(c)), upv[...]))
        hidden[pair(c)] = value.astype(bf).reshape(2, micro, cap, ffn)
        dgelu[pair(c)] = slope.astype(bf).reshape(2, micro, cap, ffn)

    def split_sum(c, total, send, recv, base):
        for m in range(micro):
            halves[m] = total.reshape(2, micro, cap, width)[:, m]
        send[pair(c)] = halves[u].astype(bf)
        remote(send.at[pair(c)], recv.at[pair(c)], base, sib, c).start()

    def hand_back(c, send, recv, base, total, landing, base_back):
        all_here(recv.at[pair(c)], base, c)
        total[pair(c)] = (halves[t] + recv[pair(c)].astype(f32)).astype(bf)

        def give(k):
            remote(total.at[k], landing.at[k], base_back, (s, partner_at(k), t)).start()

        def keep():
            landing[0] = total[0]

        if isinstance(c, int):
            give(2 * c)
        else:
            pl.when(c == 0)(keep)
            pl.when(c > 0)(lambda: give(2 * c))
        give(2 * c + 1)

    def wait_back(total, landing, sem):
        all_here(landing.at[1:experts], sem)
        all_sent(total.at[1:experts], sem)

    def rows_chunk(c):
        split_sum(c, nn(flat(hidden, pair(c)), downv[...]), eo_send, eo_recv, sem_eo)

    def rows_finish(c):
        hand_back(c, eo_send, eo_recv, sem_eo, eob, eoret, sem_re)

    mine_hot = (lax.broadcasted_iota(jnp.int32, (rows_of, experts), 1) == d).astype(f32)

    ones = jnp.ones((8, ffn), bf)
    gg_part[...] = jnp.zeros_like(gg_part)

    def gate_chunk(c):
        slot_logits = nt(flat(xrows, pair(c)), wr_ref[...])
        own_logit = jnp.sum(slot_logits * mine_hot, axis=-1, keepdims=True)
        other_logit = jnp.sum(slot_logits * flat(other, pair(c)), axis=-1, keepdims=True)
        gate = 1.0 / (1.0 + jnp.exp(other_logit - own_logit))
        gate_slots[pair(c)] = gate.reshape(2, micro, cap, 1)

    def slope_chunk(c):
        dy_flat = flat(dyrows, pair(c))
        gate = flat(gate_slots, pair(c))
        grad = nn(dy_flat, downt[...])
        pg[pair(c)] = (grad * gate * flat(dgelu, pair(c)).astype(f32)).astype(bf).reshape(2, micro, cap, ffn)
        product = (grad * flat(hidden, pair(c)).astype(f32)).astype(bf)
        for i in range(2):
            for m in range(micro):
                at = (i * micro + m) * cap
                gg_part[m, 2 * c + i, :, 0:cap] = nt(ones, product[at : at + cap])

    def back_chunk(c):
        remote(gg_part.at[u, pair(c)], gg_other.at[pair(c)], sem_gg_core, sib, c).start()
        split_sum(c, nn(flat(pg, pair(c)), upt[...]), cg_send, cg_recv, sem_cg)

    def both_chunk(c):
        front_chunk(c)
        gate_chunk(c)
        slope_chunk(c)

    def back_finish(c):
        hand_back(c, cg_send, cg_recv, sem_cg, cgb, cgret, sem_rc)
        all_here(gg_other.at[pair(c)], sem_gg_core, c)
        gg_send[pair(c)] = gg_part[t, pair(c)] + gg_other[pair(c)]

        def give(k):
            remote(gg_send.at[k], gg_recv.at[k], sem_gg, (s, partner_at(k), t)).start()

        def keep():
            gg_recv[0] = gg_send[0]

        if isinstance(c, int):
            give(2 * c)
        else:
            pl.when(c == 0)(keep)
            pl.when(c > 0)(lambda: give(2 * c))
        give(2 * c + 1)

    def hidden_of(m):
        return jnp.concatenate([hidden[k, m] for k in range(experts)], axis=0)

    def expert_rows():
        eo_send[...] = nn(hidden_of(u), downv[...]).astype(bf).reshape(eo_send.shape)
        eo_copy = remote(eo_send, eo_recv, sem_eo, sib)
        eo_copy.start()
        total = nn(hidden_of(t), downv[...])
        eo_copy.wait_recv()
        eob[...] = (total + eo_recv[...].astype(f32).reshape(slots, width)).astype(bf).reshape(eob.shape)

    def send_back(source, landing, base):
        for k in steps:
            remote(source.at[k], landing.at[k], base, (s, peer[k], t)).start()
        landing[0] = source[0]

    def layer_output():
        result = mid[...] + tn(spread_gates(gate_t), eoret[...].reshape(slots, width))
        out_own[...] = result
        return result

    def own_half():
        return pl.ds(pl.multiple_of(t * half, half), half)

    def other_half():
        return pl.ds(pl.multiple_of(u * half, half), half)

    def hand_out(rows_ref, out_ref, index):
        copy = remote(rows_ref.at[:, other_half()], out_ref.at[t], index, sib)
        copy.start()
        out_ref[t] = rows_ref[:, own_half()]
        copy.wait()

    def gather_factors():
        no_all[t, d] = no1[t]
        mix_all[d] = mixed[...]
        ring_gather(
            [
                (lambda q: no_all.at[t, q, 0 : length // 2], sem_ring_no, 0),
                (lambda q: no_all.at[t, q, length // 2 : length], sem_ring_no, 0),
                (lambda q: mix_all.at[q, 0], sem_ring_mix, 2),
                (lambda q: mix_all.at[q, 1], sem_ring_mix, 2),
            ]
        )
        all_sent(no_all.at[t, 1:experts], sem_ring_no)
        all_sent(mix_all.at[1:experts], sem_ring_mix)
        copy = remote(no_all.at[t], no_all.at[t], sem_noall, sib)
        copy.start()
        copy.wait()

    @pl.when(s == 0)
    def _():
        load_up.wait()
        load_down.wait()
        stream(arrivals, front_chunk, rows_chunk, rows_finish, True, True)
        wait_back(eob, eoret, sem_re)
        x_send[...] = layer_output().astype(bf)
        x_copy.start()
        hand_out(out_own, secout_ref, sem_so)
        turn_weights()
        other_experts()

        def gate_one(c, carry):
            gate_chunk(c)
            return carry

        lax.fori_loop(0, len(chunks), gate_one, 0)
        gather_factors()
        x_copy.wait_send()
        dy_copy.wait_recv()
        arrivals_y = dispatch(dyb[...], disp_y, dyrows, sem_ddy, sem_ddyf, 1)
        stream(arrivals_y, slope_chunk, back_chunk, back_finish, True, True)

    @pl.when(s == 1)
    def _():
        stream(arrivals, both_chunk, back_chunk, back_finish, True, False)
        expert_rows()

    wait_back(gg_send, gg_recv, sem_gg)
    wait_back(cgb, cgret, sem_rc)

    @pl.when(s == 1)
    def _():
        send_back(eob, eoret, sem_re)


    gg_rows = []
    for e in range(experts):
        high, low = split_low(gg_recv[e][:, 0:cap])
        spot_rows = place[e * cap : (e + 1) * cap, :]
        gg_rows.append((nn(high, spot_rows) + nn(low, spot_rows))[0:1, :])
    gate_grad = jnp.concatenate(gg_rows, axis=0)
    gates = gate_t[...]
    logit_grad = (gates * (gate_grad - jnp.sum(gates * gate_grad, axis=0, keepdims=True))).astype(bf)
    two_grad = tn(logit_grad, wrp[...]) + tn(place[...], cgret[...].reshape(slots, width))
    dy = dyb[...].astype(f32)
    middle = mid[...]
    scale = inverse_rms(middle)
    normed = middle * scale
    scaled = two_grad * gain_two
    middle_grad = dy + scale * (scaled - normed * jnp.mean(scaled * normed, axis=-1, keepdims=True))
    mgrad[...] = middle_grad
    ag[t] = middle_grad.astype(bf)
    ag_copy = remote(ag.at[t], ag.at[t], sem_ag, sib)
    ag_copy.start()

    agt_rows = width // experts
    agt_own = remote(agt.at[block(d, agt_rows)], agt_all.at[d, t], sem_agtf, sib)

    @pl.when(s == 0)
    def _():
        agt[...] = jnp.transpose(ag[t])
        for k in reversed(steps):
            remote(agt.at[block(peer[k], agt_rows)], agt_all.at[d, t], sem_agt, (s, peer[k], t)).start()
        agt_all[d, t] = agt[block(d, agt_rows), :]
        agt_own.start()

    two_normed = normed
    groups = width // 128
    qgt_rows = 3 * cols // experts

    def attend_back(m, i):
        mg[m] = nn(ag[m], outwt[...]).astype(bf)
        for p in range(pairs):
            at = slice(p * 128, (p + 1) * 128)
            mg_pair = mg[m, :, at]
            probs = probs_buf[m, p]
            keys2 = both_heads(qkvb[1, m, :, at])
            queries2 = both_heads(qkvb[0, m, :, at])
            mg2 = both_heads(mg_pair)
            prob_grad = nt(mg_pair, both_heads(qkvb[2, m, :, at]))
            raws = []
            key_grad = jnp.zeros((length, 128), f32)
            value_grad = jnp.zeros((length, 128), f32)
            for h in range(2):
                lane = slice(h * length, (h + 1) * length)
                part = probs[:, lane]
                step = prob_grad[:, lane]
                score_grad = part * (step - jnp.sum(part * step, axis=-1, keepdims=True))
                score_sum[2 * p + h] += score_grad
                raw = (0.125 * score_grad).astype(bf)
                raws.append(raw)
                key_grad = key_grad + tn(raw, queries2[h * length : (h + 1) * length])
                value_grad = value_grad + tn(part.astype(bf), mg2[h * length : (h + 1) * length])
            query_grad = nn(jnp.concatenate(raws, axis=1), keys2)
            for c, grad in enumerate((query_grad, key_grad, value_grad)):
                qkvg[c, m, :, at] = grad.astype(bf)

        @pl.when(s == 0)
        def _():
            for c in range(3):
                qgt[i, c * cols : (c + 1) * cols, :] = jnp.transpose(qkvg[c, m])
            for k in reversed([k for k in steps if k not in relayed]):
                rows = block(peer[k], qgt_rows)
                remote(qgt.at[i, rows], qt_all.at[d, i], sem_qgt, (s, peer[k], t), k).start()
            qt_all[d, i] = qgt[i, block(d, qgt_rows), :]

    score_sum[...] = jnp.zeros_like(score_sum)

    def back_one(i, carry):
        @pl.when(i == 1)
        def _():
            ag_copy.wait()

        attend_back(t + i * (u - t), i)
        return carry

    lax.fori_loop(0, micro, back_one, 0)

    def relay_q_copy(i, k):
        return remote(qgt.at[:, block(peer[k], qgt_rows)], relay_q.at[i], sem_relay_q, across, i)

    @pl.when(s == 0)
    def _():
        for i, k in enumerate(relayed):
            relay_q_copy(i, k).start()


    def project_back(m):
        total = nn(qkvg[0, m], qkvwt[0])
        for c in range(1, 3):
            total = total + nn(qkvg[c, m], qkvwt[c])
        return total

    no_send[...] = project_back(u).astype(bf)
    no_copy = remote(no_send, no_recv, sem_no, sib)
    no_copy.start()
    one_grad = project_back(t)
    no_copy.wait()
    one_grad = one_grad + no_recv[...].astype(f32)
    x_rows = xb[t].astype(f32)
    scale = inverse_rms(x_rows)
    normed = x_rows * scale
    scaled = one_grad * gain_one
    input_grad = mgrad[...] + scale * (scaled - normed * jnp.mean(scaled * normed, axis=-1, keepdims=True))
    dy_send[...] = input_grad.astype(bf)

    @pl.when(s == 1)
    def _():
        dy_copy.start()

    ig_own[...] = input_grad
    gain_one_grad = jnp.sum(one_grad * normed, axis=0, keepdims=True)
    hand_out(ig_own, ingrad_ref, sem_ig)

    router_grad = nn(tn(turn, logit_grad).astype(bf), ntb[...])
    gain_two_grad = jnp.sum(two_grad * two_normed, axis=0, keepdims=True)
    small_send[...] = jnp.zeros_like(small_send)
    for g in range(groups):
        small_send[g, 0:experts, :] = router_grad[:, g * 128 : (g + 1) * 128]
        small_send[g, experts + 1 : experts + 2, :] = gain_two_grad[:, g * 128 : (g + 1) * 128]
    sums = []
    for head in range(2 * pairs):
        high, low = split_low(score_sum[head])
        turned = pltpu.roll(nn(high, mirror) + nn(low, mirror), 0, 1, stride=1, stride_axis=0)
        sums.append(jnp.sum(turned, axis=0, keepdims=True))
    high, low = split_low(jnp.concatenate(sums, axis=0))
    small_send[groups, 0 : 2 * pairs, 0 : lay.buckets] = nt(high, dist_rows) + nt(low, dist_rows)
    for g in range(groups):
        small_send[g, experts : experts + 1, :] = gain_one_grad[:, g * 128 : (g + 1) * 128]
    for k in steps:
        remote(small_send.at[peer[k]], small_in.at[k], sem_small, (s, peer[k], t)).start()
    small_in[0] = small_send[d]

    wide = lay.wide
    every = micro * slots

    for k in range(experts):
        og[k] = (dyrows[k].astype(f32) * gate_slots[k]).astype(bf)

    def expert_grads(n, carry):
        at = pl.ds(pl.multiple_of(n * wide, wide), wide)
        guv[:, at] = tn(xrows[...].reshape(every, width), pg[:, :, :, at].reshape(every, wide)).astype(bf)
        gdv[at, :] = tn(hidden[:, :, :, at].reshape(every, wide), og[...].reshape(every, width)).astype(bf)
        return carry

    lax.fori_loop(0, ffn // wide, expert_grads, 0)

    qkv_rows = 3 * cols // experts
    share = shared_ref.shape[1] // 4
    parts = [slice(c * share, (c + 1) * share) for c in range(4)]

    def pack_out(total):
        half_rows = agt_rows // 2
        return jnp.concatenate([total[..., 0:half_rows, :], total[..., half_rows:, :]], axis=-1).astype(bf)

    @pl.when(s == 0)
    def _():
        all_here(agt_all.at[1:experts, 0], sem_agt)
        for k in steps:
            held = agt_all.at[peer[k], t]
            remote(held, held, sem_agtf, sib).start()
        all_here(agt_all.at[:, 0], sem_agtf)
        all_sent(agt_all.at[1:experts, 0], sem_agt)
        all_sent(agt_all.at[:, 0], sem_agtf)
        total = jnp.zeros((agt_rows, cols), f32)
        for q in range(experts):
            for m in range(micro):
                total = total + nn(agt_all[q, m], mix_all[q, m])
        shared_ref[d, qkv_rows:, :] = pack_out(total)

        def qkv_slice(q):
            rows = jnp.concatenate([qt_all[q, 0], qt_all[q, 1]], axis=1)
            return nn(rows, jnp.concatenate([no_all[t, q], no_all[u, q]], axis=0))

        total = qkv_slice(d)
        for k in [k for k in reversed(steps) if k not in relayed] + list(relayed):
            all_here(qt_all.at[0], sem_qgt, k)
            total = total + qkv_slice(peer[k])
        all_sent(qt_all.at[0 : experts - 1 - len(relayed)], sem_qgt)
        all_sent(relay_q, sem_relay_q)
        shared_ref[d, 0:qkv_rows, :] = total.astype(bf)

    @pl.when(s == 1)
    def _():
        normed_rows = no1[...].reshape(micro * length, width)
        own = jnp.concatenate([tn(qkvg[c].reshape(micro * length, cols), normed_rows) for c in range(3)], axis=0)
        rs_buf[:, 0:qkv_rows, :] = own.astype(bf).reshape(experts, qkv_rows, width)
        own = tn(ag[...].reshape(micro * length, width), mixed[...].reshape(micro * length, cols))
        rs_buf[:, qkv_rows:, :] = pack_out(own.reshape(experts, agt_rows, cols))

        relay(dyrows, sem_ddy, 1)

        def owner_at(number, direction, k):
            return ring_device(ring_at + direction * (hops(number, direction) - k))

        def hop(number, direction, k):
            index = hop_index(number, direction, k)
            return remote(
                rs_buf.at[owner_at(number, direction, k), parts[number]],
                rs_in.at[index % ring_hops, parts[number]],
                sem_ring_sum,
                (s, ring_device(ring_at + direction), t),
                index,
            )

        lines = lines_of(len(parts))
        for k in range(experts // 2):
            for line in lines:
                if k < hops(*line):
                    if k > 0:
                        rows = parts[line[0]]
                        owner = owner_at(*line, k)
                        hop(*line, k - 1).wait_recv()
                        came = rs_in[hop_index(*line, k - 1) % ring_hops, rows, :].astype(f32)
                        rs_buf[owner, rows, :] = (rs_buf[owner, rows, :].astype(f32) + came).astype(bf)
                    hop(*line, k).start()
        for number, rows in enumerate(parts):
            total = rs_buf[d, rows, :].astype(f32)
            for direction in (1, -1):
                last = hops(number, direction) - 1
                hop(number, direction, last).wait_recv()
                total = total + rs_in[hop_index(number, direction, last) % ring_hops, rows, :].astype(f32)
            shared_ref[d, rows, :] = total.astype(bf)
        for i, k in enumerate(relayed):
            all_here(relay_q.at[i], sem_relay_q, i)
            remote(relay_q.at[i], qt_all.at[d], (sem_pass_q[0], sem_qgt[1] + k), (0, peer[k], t)).start()

    all_here(small_in.at[1:experts], sem_small)
    small_total = small_in[0]
    for k in steps:
        small_total = small_total + small_in[k]
    small_all[d] = small_total
    for k in steps:
        remote(small_all.at[d], small_all.at[d], sem_back, (s, peer[k], t)).start()

    sums_copy = remote(small_all, small_sib, sem_sums, sib)

    def pass_sums():
        all_here(small_all.at[1:experts], sem_back)
        sums_copy.start()


    streams = [
        (lambda q, rows=rows: shared_ref.at[q, rows], sem_ring_out, 0) for rows in parts
    ]

    ring_gather(streams, pass_sums)
    sums_copy.wait_recv()
    for g in range(groups):
        lanes = slice(g * 128, (g + 1) * 128)
        grouter_ref[:, lanes] = small_all[g, 0:experts, :] + small_sib[g, 0:experts, :]
        ggain_ref[:, lanes] = small_all[g, experts : experts + 2, :] + small_sib[g, experts : experts + 2, :]
    gbias_ref[...] = small_all[groups, 0 : 2 * pairs, :]
    @pl.when(s == 1)
    def _():
        dy_copy.wait_send()
        for sem in sem_pass:
            all_sent(relay_buf.at[0 : len(relayed)], sem)
        all_sent(rs_in, sem_ring_sum)
        all_sent(relay_q, sem_pass_q)
        wait_back(eob, eoret, sem_re)
        layer_output()
        hand_out(out_own, secout_ref, sem_so)

    all_sent(rr.at[1:experts], sem_routes)
    all_sent(eo_send, sem_eo)
    all_sent(cg_send, sem_cg)
    all_sent(gg_part.at[0], sem_gg_core)
    all_sent(small_in.at[1:experts], sem_small)
    all_sent(small_all.at[1:experts], sem_back)
    all_sent(small_all, sem_sums)
    all_sent(shared_ref.at[1:experts], sem_ring_out)


def widen_kernel(
    sec_ref, ing_ref, gain_ref, shared_ref, bias_ref, router_ref, up_ref, down_ref,
    sec_out, ing_out, gain_out, bias_out, router_out, qkv_out, out_out, up_out, down_out,
    up_wide, down_wide, qkv_wide, out_wide, bias_wide, out_sem,
):
    f32 = jnp.float32
    parts = 6
    experts, shared_rows, width = shared_ref.shape
    cols = out_wide.shape[0]
    qkv_rows = 3 * cols // experts
    wide = ((up_ref, up_wide, up_out), (down_ref, down_wide, down_out))
    stores = []

    def store(src, dst):
        copy = pltpu.make_async_copy(src, dst, out_sem.at[len(stores)])
        copy.start()
        stores.append(copy)

    def widen(i, n):
        src, dst, out = wide[i]
        size = src.shape[0] // parts
        rows = pl.ds(n * size, size)
        dst[rows, :] = src[rows, :].astype(f32)
        store(dst.at[rows], out.at[rows])

    def turn_qkv(c):
        block = shared_ref[:, 0:qkv_rows, :].reshape(3 * cols, width)[c * cols : (c + 1) * cols]
        qkv_wide[c] = jnp.transpose(block.astype(f32))
        store(qkv_wide.at[c], qkv_out.at[c])

    store(sec_ref, sec_out)
    store(ing_ref, ing_out)
    widen(0, 0)
    store(gain_ref, gain_out)
    store(router_ref, router_out)
    for h in range(bias_wide.shape[0]):
        bias_wide[h] = bias_ref[h : h + 1, 0 : bias_wide.shape[2]]
    store(bias_wide, bias_out)
    widen(0, 1)
    widen(0, 2)
    turn_qkv(0)
    widen(0, 3)
    widen(0, 4)
    turn_qkv(1)
    widen(0, 5)
    widen(1, 0)
    turn_qkv(2)
    widen(1, 1)
    widen(1, 2)
    out_block = jnp.concatenate(
        [
            shared_ref[e, qkv_rows:, h * cols : (h + 1) * cols].astype(f32)
            for e in range(experts)
            for h in range(2)
        ],
        axis=0,
    )
    out_wide[...] = jnp.transpose(out_block)
    store(out_wide, out_out)
    widen(1, 3)
    widen(1, 4)
    widen(1, 5)
    for copy in stores:
        copy.wait()


def fused_local(
    tokens,
    cotangent,
    segments,
    pad_mask,
    routes,
    dist_bucket,
    norm_gains,
    qkv_weight,
    out_weight,
    rel_bias,
    router_weight,
    expert_up,
    expert_down,
):
    micro, _, length, width = tokens.shape
    experts = router_weight.shape[2]
    cap = max(2, 3 * length // experts)
    cols = out_weight.shape[1]
    heads = rel_bias.shape[2]
    ffn = expert_up.shape[3]
    slots = experts * cap
    pairs = cols // 128
    shared_rows = 3 * cols // experts + width // experts // 2
    lay = Layout()
    lay.experts = experts
    lay.cap = cap
    lay.buckets = rel_bias.shape[1]
    lay.wide = min(ffn, 256)
    chunks = experts // 2
    lay.sems = (36, 7 * chunks + experts + 8 * (experts - 1) + 24)
    bf = jnp.bfloat16
    f32 = jnp.float32
    vm = pltpu.VMEM
    shape = jax.ShapeDtypeStruct
    dma = pltpu.SemaphoreType.DMA
    scratch = [
        vm((micro, length), jnp.int32),
        vm((micro, length), jnp.int32),
        vm((micro, 2, length), jnp.int32),
        vm((1, length), jnp.int32),
        vm((2, width), bf),
        vm((heads, lay.buckets), bf),
        vm((experts, width), bf),
        vm((width, ffn), bf),
        vm((ffn, width), bf),
        vm((ffn, width), bf),
        vm((width, ffn), bf),
        vm((3, cols, width), bf),
        vm((width, cols), bf),
        vm((3, width, cols), bf),
        vm((cols, width), bf),
        vm((micro, length, width), bf),
        vm((length, width), bf),
        vm((experts, micro, 2, length), jnp.int32),
        vm((slots, length), bf),
        vm((micro, pairs, length, 2 * length), f32),
        vm((micro, pairs, length, 2 * length), f32),
        vm((micro, length, width), bf),
        vm((3, micro, length, cols), bf),
        vm((micro, length, cols), bf),
        vm((length, width), bf),
        vm((length, width), bf),
        vm((length, width), f32),
        vm((length, width), bf),
        vm((experts, length), f32),
        vm((experts, length), f32),
        vm((experts, width), bf),
        vm((2 * pairs, length, length), f32),
        vm((experts, cap, width), bf),
        vm((experts, micro, cap, width), bf),
        vm((experts, cap, width), bf),
        vm((experts, micro, cap, width), bf),
        vm((experts, micro, cap, ffn), bf),
        vm((experts, micro, cap, ffn), bf),
        vm((micro, 2, cap, width), f32),
        vm((experts, cap, width), bf),
        vm((experts, cap, width), bf),
        vm((experts, cap, width), bf),
        vm((experts, cap, width), bf),
        vm((length, width), f32),
        vm((experts, micro, cap, experts), f32),
        vm((experts, micro, cap, 1), f32),
        vm((experts, micro, cap, width), bf),
        vm((micro, experts, 8, 128), f32),
        vm((experts, 8, 128), f32),
        vm((experts, 8, 128), f32),
        vm((experts, 8, 128), f32),
        vm((experts, micro, cap, ffn), bf),
        vm((experts, cap, width), bf),
        vm((experts, cap, width), bf),
        vm((experts, cap, width), bf),
        vm((experts, cap, width), bf),
        vm((length, width), f32),
        vm((micro, length, width), bf),
        vm((micro, length, cols), bf),
        vm((3, micro, length, cols), bf),
        vm((length, width), bf),
        vm((length, width), bf),
        vm((length, width), f32),
        vm((length, width), bf),
        vm((micro, experts, length, width), bf),
        vm((experts, micro, length, cols), bf),
        vm((micro, 3 * cols, length), bf),
        vm((experts, micro, 3 * cols // experts, length), bf),
        vm((width, length), bf),
        vm((experts, micro, width // experts, length), bf),
        vm((experts, 2 * experts, 128), f32),
        vm((experts, 2 * experts, 128), f32),
        vm((experts, 2 * experts, 128), f32),
        vm((experts, 2 * experts, 128), f32),
        vm((length, width), bf),
        vm((experts, shared_rows, width), bf),
        vm((experts - 1, shared_rows, width), bf),
        vm((4, cap, width), bf),
        vm((2, micro, 3 * cols // experts, length), bf),
        dma((12,)),
        dma((lay.sems[0],)),
        dma((lay.sems[1],)),
    ]
    whole = pl.BlockSpec(memory_space=pltpu.VMEM)
    anywhere = pl.BlockSpec(memory_space=pl.ANY)
    out_shape = (
        vm((micro, length, width // 2), f32),
        vm((micro, length, width // 2), f32),
        vm((2, width), f32),
        vm((experts, shared_rows, width), bf),
        vm((heads, 128), f32),
        vm((experts, width), f32),
        vm((width, ffn), bf),
        vm((ffn, width), bf),
    )
    results = pl.pallas_call(
        partial(layer_kernel, lay),
        out_shape=out_shape,
        in_specs=[anywhere] * 13,
        out_specs=[whole] * 8,
        scratch_shapes=scratch,
        name="two_sections",
        compiler_params=pltpu.CompilerParams(
            collective_id=0, has_side_effects=True, vmem_limit_bytes=56 * 1024 * 1024
        ),
    )(
        tokens[:, 0],
        cotangent[:, 0],
        segments[:, 0],
        pad_mask[:, 0],
        routes[:, 0].transpose(0, 2, 1),
        dist_bucket[None],
        norm_gains[0],
        qkv_weight[0].transpose(1, 0, 2),
        out_weight[0],
        rel_bias[0].T,
        router_weight[0].T,
        expert_up[0, 0],
        expert_down[0, 0],
    )
    section_out, input_grads, gains, bias, router, qkv, out, up, down = pl.pallas_call(
        widen_kernel,
        out_shape=(
            shape((micro, length, width // 2), f32),
            shape((micro, length, width // 2), f32),
            shape((2, width), f32),
            shape((heads, 1, lay.buckets), f32),
            shape((experts, width), f32),
            shape((3, width, cols), f32),
            shape((cols, width), f32),
            shape((width, ffn), f32),
            shape((ffn, width), f32),
        ),
        in_specs=[whole] * 8,
        out_specs=[anywhere] * 9,
        scratch_shapes=[
            vm((width, ffn), f32),
            vm((ffn, width), f32),
            vm((3, width, cols), f32),
            vm((cols, width), f32),
            vm((heads, 1, lay.buckets), f32),
            dma((21,)),
        ],
        name="widen",
        compiler_params=pltpu.CompilerParams(vmem_limit_bytes=40 * 1024 * 1024),
    )(*[pltpu.with_memory_space_constraint(result, pltpu.VMEM) for result in results])
    return (
        section_out[None, :, None],
        input_grads[None, :, None],
        gains[None],
        qkv.transpose(1, 0, 2)[None],
        out[None],
        bias.transpose(1, 2, 0),
        router.T[None],
        up[None, None],
        down[None, None],
    )


def fits_kernel(mesh):
    return mesh.shape["section"] == 2 and mesh.shape["tensor"] == 2 and mesh.shape["dp"] == 8


def solution(mesh):
    in_specs = (
        P(None, "dp", None, None),
        P(None, "dp", None, None),
        P(None, "dp", None),
        P(None, "dp", None),
        P(None, "dp", None, None),
        P(),
        P("section", None, None),
        P("section", None, None, "tensor"),
        P("section", "tensor", None),
        P("section", None, "tensor"),
        P("section", None, None),
        P("section", "dp", None, "tensor"),
        P("section", "dp", "tensor", None),
    )
    out_specs = (
        P("section", None, "dp", None, "tensor"),
        P("section", None, "dp", None, "tensor"),
        P("section", None, None),
        P("section", None, None, "tensor"),
        P("section", "tensor", None),
        P("section", None, "tensor"),
        P("section", None, None),
        P("section", "dp", None, "tensor"),
        P("section", "dp", "tensor", None),
    )
    body = fused_local if fits_kernel(mesh) else local
    return jax.shard_map(body, mesh=mesh, in_specs=in_specs, out_specs=out_specs, check_vma=False)
```

```python
from functools import partial

import jax
import jax.numpy as jnp
from jax import lax
from jax.experimental import pallas as pl
from jax.experimental.pallas import tpu as pltpu
from jax.sharding import PartitionSpec as P

norm_eps = 1e-06
masked_score = -1e30
highest = lax.Precision.HIGHEST


def shifted(block, axis, distance):
    devices = range(lax.axis_size(axis))
    route = [(i - distance, i) for i in devices if i - distance in devices]
    return lax.ppermute(block, axis, route)


def normalize(values, gain_row):
    scale_inv = lax.rsqrt(jnp.mean(values * values, axis=-1, keepdims=True) + norm_eps)
    return values * scale_inv * gain_row


def normalize_back(values, gain_row, upstream):
    scale_inv = lax.rsqrt(jnp.mean(values * values, axis=-1, keepdims=True) + norm_eps)
    normed = values * scale_inv
    gain_grad = jnp.sum(upstream * normed, axis=0)
    scaled = upstream * gain_row
    input_grad = scale_inv * (scaled - normed * jnp.mean(scaled * normed, axis=-1, keepdims=True))
    return (input_grad, gain_grad)


def send_rows(rows):
    return lax.all_to_all(rows, "dp", split_axis=0, concat_axis=0, tiled=True)


def sum_slots(partial_rows):
    return lax.psum(partial_rows, "tensor")


def score_context(segment_row, pad_row, dist_bucket, bucket_count):
    length = segment_row.shape[0]
    places = jnp.arange(length, dtype=jnp.int32)
    offsets = jnp.clip(places[:, None] - places[None, :], 0, length - 1)
    bucket_grid = jnp.take(dist_bucket, offsets)
    bucket_onehot = (
        bucket_grid[:, :, None] == jnp.arange(bucket_count, dtype=jnp.int32)[None, None, :]
    ).astype(jnp.float32)
    allowed = (places[None, :] <= places[:, None]) & (segment_row[:, None] == segment_row[None, :])
    allowed = allowed & ((pad_row[None, :] == 1) | (places[None, :] == places[:, None]))
    return (bucket_onehot, allowed)


def attention_front(inputs, context, weights):
    segment_row, pad_row, route_rows, dist_bucket = context
    gain_pair, qkv_weight, out_weight, bias_table, router_weight, upper_weight, lower_weight = (
        weights
    )
    length = inputs.shape[0]
    head_count = bias_table.shape[1]
    bucket_onehot, allowed = score_context(segment_row, pad_row, dist_bucket, bias_table.shape[0])
    normed_one = normalize(inputs, gain_pair[0]).astype(jnp.bfloat16)
    qkv_rows = jnp.einsum(
        "ld,dch->lch", normed_one, qkv_weight, preferred_element_type=jnp.float32
    ).astype(jnp.bfloat16)
    head_dim = qkv_rows.shape[2] // head_count
    queries = qkv_rows[:, 0].reshape(length, head_count, head_dim)
    keys_in = qkv_rows[:, 1].reshape(length, head_count, head_dim)
    values_in = qkv_rows[:, 2].reshape(length, head_count, head_dim)
    raw_scores = jnp.einsum("qhd,khd->hqk", queries, keys_in, preferred_element_type=jnp.float32)
    bias_grid = jnp.einsum(
        "qkb,bh->hqk", bucket_onehot, bias_table.astype(jnp.float32), precision=highest
    )
    logits = jnp.where(allowed[None], 0.125 * raw_scores + bias_grid, masked_score)
    exp_terms = jnp.exp(logits - jnp.max(logits, axis=-1, keepdims=True))
    attn_probs = exp_terms / jnp.sum(exp_terms, axis=-1, keepdims=True)
    mixed_rows = jnp.einsum(
        "hqk,khd->qhd",
        attn_probs.astype(jnp.bfloat16),
        values_in,
        preferred_element_type=jnp.float32,
    )
    mixed_rows = mixed_rows.reshape(length, -1).astype(jnp.bfloat16)
    return (normed_one, queries, keys_in, values_in, attn_probs, mixed_rows, bucket_onehot)


def slot_tables(route_rows, experts, capacity):
    flat_routes = route_rows.reshape(-1)
    route_hits = (flat_routes[:, None] == jnp.arange(experts, dtype=jnp.int32)[None, :]).astype(
        jnp.int32
    )
    earlier = jnp.cumsum(route_hits, axis=0) - route_hits
    position = jnp.sum(earlier * route_hits, axis=1)
    target = flat_routes * capacity + position
    slot_hits = (
        jnp.arange(experts * capacity, dtype=jnp.int32)[:, None] == target[None, :]
    ).astype(jnp.int32)
    source = jnp.sum(slot_hits * jnp.arange(target.shape[0], dtype=jnp.int32)[None, :], axis=1)
    filled = jnp.sum(slot_hits, axis=1) > 0
    return (target, source, filled, route_hits)


def route_gates(normed_two, router_weight, route_hits):
    length = normed_two.shape[0]
    logits = jnp.dot(normed_two, router_weight, preferred_element_type=jnp.float32)
    route_onehot = route_hits.reshape(length, 2, -1).astype(jnp.float32)
    chosen = jnp.einsum("le,lre->lr", logits, route_onehot, precision=highest)
    return (jax.nn.softmax(chosen, axis=-1), route_onehot)


def gather_back(back_slots, target, length):
    flat_slots = back_slots.reshape(-1, back_slots.shape[-1])
    return jnp.take(flat_slots, target, axis=0).reshape(length, 2, -1)


def forward_rest(inputs, front, context, weights):
    segment_row, pad_row, route_rows, dist_bucket = context
    gain_pair, qkv_weight, out_weight, bias_table, router_weight, upper_weight, lower_weight = (
        weights
    )
    mixed_rows = front[5]
    length, model_width = inputs.shape
    experts = router_weight.shape[1]
    capacity = max(2, 3 * length // experts)
    local_experts = upper_weight.shape[0]
    attn_out = lax.psum(
        jnp.dot(mixed_rows, out_weight, preferred_element_type=jnp.float32), "tensor"
    )
    middle = inputs + attn_out
    normed_two = normalize(middle, gain_pair[1]).astype(jnp.bfloat16)
    target, source, filled, route_hits = slot_tables(route_rows, experts, capacity)
    outgoing = jnp.where(
        filled[:, None], jnp.take(normed_two, source // 2, axis=0), jnp.zeros((), jnp.bfloat16)
    )
    outgoing = outgoing.reshape(experts, capacity, model_width)
    arrived = send_rows(outgoing)
    grouped = arrived.reshape(-1, local_experts, capacity, model_width)
    pre_act = jnp.einsum(
        "secd,edf->secf", grouped, upper_weight, preferred_element_type=jnp.float32
    )
    hidden = jax.nn.gelu(pre_act, approximate=False).astype(jnp.bfloat16)
    partial_out = jnp.einsum(
        "secf,efd->secd", hidden, lower_weight, preferred_element_type=jnp.float32
    )
    summed = sum_slots(partial_out)
    returned = summed.astype(jnp.bfloat16).reshape(arrived.shape[0], arrived.shape[1], -1)
    back_slots = send_rows(returned)
    gate_probs, route_onehot = route_gates(normed_two, router_weight, route_hits)
    back_rows = gather_back(back_slots, target, length)
    output = middle + jnp.sum(gate_probs[:, :, None] * back_rows.astype(jnp.float32), axis=1)
    return (output, (attn_out, arrived, back_slots, pre_act))


def backward_layer(inputs, upstream, context, weights, front, saved_state):
    segment_row, pad_row, route_rows, dist_bucket = context
    gain_pair, qkv_weight, out_weight, bias_table, router_weight, upper_weight, lower_weight = (
        weights
    )
    normed_one, queries, keys_in, values_in, attn_probs, mixed_rows, bucket_onehot = front
    attn_out, arrived_rows, back_slots, pre_rows = saved_state
    length, model_width = inputs.shape
    head_count = bias_table.shape[1]
    head_cols = qkv_weight.shape[2]
    experts = router_weight.shape[1]
    capacity = max(2, 3 * length // experts)
    local_experts = upper_weight.shape[0]
    middle = inputs + attn_out
    normed_two = normalize(middle, gain_pair[1]).astype(jnp.bfloat16)
    target, source, filled, route_hits = slot_tables(route_rows, experts, capacity)
    gate_probs, route_onehot = route_gates(normed_two, router_weight, route_hits)
    back_rows = gather_back(back_slots, target, length)
    gate_grad = jnp.sum(upstream[:, None, :] * back_rows.astype(jnp.float32), axis=-1)
    chosen_grad = gate_probs * (gate_grad - jnp.sum(gate_probs * gate_grad, axis=-1, keepdims=True))
    logit_grad = jnp.einsum("lr,lre->le", chosen_grad, route_onehot, precision=highest).astype(
        jnp.bfloat16
    )
    router_grad = jnp.dot(normed_two.T, logit_grad, preferred_element_type=jnp.float32)
    normed_two_grad = jnp.dot(logit_grad, router_weight.T, preferred_element_type=jnp.float32)
    route_grads = (
        (gate_probs[:, :, None] * upstream[:, None, :])
        .reshape(2 * length, model_width)
        .astype(jnp.bfloat16)
    )
    slot_grads = jnp.where(
        filled[:, None], jnp.take(route_grads, source, axis=0), jnp.zeros((), jnp.bfloat16)
    )
    arrived_grads = send_rows(slot_grads.reshape(experts, capacity, model_width))
    grouped = arrived_rows.reshape(-1, local_experts, capacity, model_width)
    grouped_grads = arrived_grads.reshape(-1, local_experts, capacity, model_width)
    hidden, gelu_pull = jax.vjp(partial(jax.nn.gelu, approximate=False), pre_rows)
    hidden_low = hidden.astype(jnp.bfloat16)
    down_grad = jnp.einsum(
        "secf,secd->efd", hidden_low, grouped_grads, preferred_element_type=jnp.float32
    )
    hidden_grad = jnp.einsum(
        "secd,efd->secf", grouped_grads, lower_weight, preferred_element_type=jnp.float32
    )
    pre_grad = gelu_pull(hidden_grad)[0].astype(jnp.bfloat16)
    up_grad = jnp.einsum("secd,secf->edf", grouped, pre_grad, preferred_element_type=jnp.float32)
    rows_grad = sum_slots(
        jnp.einsum("secf,edf->secd", pre_grad, upper_weight, preferred_element_type=jnp.float32)
    )
    sent_back = send_rows(
        rows_grad.astype(jnp.bfloat16).reshape(arrived_rows.shape[0], arrived_rows.shape[1], -1)
    )
    copy_grads = gather_back(sent_back, target, length).astype(jnp.float32)
    normed_two_grad = normed_two_grad + jnp.sum(copy_grads, axis=1)
    middle_part, gain_two = normalize_back(middle, gain_pair[1], normed_two_grad)
    middle_grad = upstream + middle_part
    attn_grad = middle_grad.astype(jnp.bfloat16)
    out_grad = jnp.dot(mixed_rows.T, attn_grad, preferred_element_type=jnp.float32)
    mixed_grad = jnp.dot(attn_grad, out_weight.T, preferred_element_type=jnp.float32).astype(
        jnp.bfloat16
    )
    mixed_grad = mixed_grad.reshape(length, head_count, -1)
    prob_grad = jnp.einsum(
        "qhd,khd->hqk", mixed_grad, values_in, preferred_element_type=jnp.float32
    )
    value_grad = jnp.einsum(
        "hqk,qhd->khd",
        attn_probs.astype(jnp.bfloat16),
        mixed_grad,
        preferred_element_type=jnp.float32,
    )
    score_grad = attn_probs * (prob_grad - jnp.sum(prob_grad * attn_probs, axis=-1, keepdims=True))
    table_grad = jnp.einsum("hqk,qkb->bh", score_grad, bucket_onehot, precision=highest)
    raw_grad = (0.125 * score_grad).astype(jnp.bfloat16)
    query_grad = jnp.einsum("hqk,khd->qhd", raw_grad, keys_in, preferred_element_type=jnp.float32)
    key_grad = jnp.einsum("hqk,qhd->khd", raw_grad, queries, preferred_element_type=jnp.float32)
    qkv_grad = (
        jnp.stack([query_grad, key_grad, value_grad], axis=1)
        .reshape(length, 3, head_cols)
        .astype(jnp.bfloat16)
    )
    qkv_weight_grad = jnp.einsum(
        "ld,lch->dch", normed_one, qkv_grad, preferred_element_type=jnp.float32
    )
    normed_one_grad = lax.psum(
        jnp.einsum("lch,dch->ld", qkv_grad, qkv_weight, preferred_element_type=jnp.float32),
        "tensor",
    )
    input_part, gain_one = normalize_back(inputs, gain_pair[0], normed_one_grad)
    input_grad = middle_grad + input_part
    gain_grads = jnp.stack([gain_one, gain_two])
    return (
        input_grad,
        (gain_grads, qkv_weight_grad, out_grad, table_grad, router_grad, up_grad, down_grad),
    )


def pick_context(segments, pad_mask, routes, dist_bucket, micro_slot):
    segment_row = lax.dynamic_index_in_dim(segments[:, 0], micro_slot, 0, False)
    pad_row = lax.dynamic_index_in_dim(pad_mask[:, 0], micro_slot, 0, False)
    route_rows = lax.dynamic_index_in_dim(routes[:, 0], micro_slot, 0, False)
    return (segment_row, pad_row, route_rows, dist_bucket)


def place_row(store_all, new_value, micro_slot, is_valid):
    current = lax.dynamic_index_in_dim(store_all, micro_slot, 0, False)
    return lax.dynamic_update_index_in_dim(
        store_all, jnp.where(is_valid, new_value, current), micro_slot, 0
    )


def pick_row(store_all, micro_slot):
    return lax.dynamic_index_in_dim(store_all, micro_slot, 0, False)


def mask_grad(grad_value, is_valid):
    return jnp.where(is_valid, grad_value, jnp.zeros((), grad_value.dtype))


def tensor_half(full_rows, tensor_id, half_width):
    return lax.dynamic_slice_in_dim(full_rows, tensor_id * half_width, half_width, 2)[None, :, None]


def local(
    tokens,
    cotangent,
    segments,
    pad_mask,
    routes,
    dist_bucket,
    norm_gains,
    qkv_weight,
    out_weight,
    rel_bias,
    router_weight,
    expert_up,
    expert_down,
):
    section_id = lax.axis_index("section")
    section_count = lax.axis_size("section")
    micro_count = tokens.shape[0]
    length = tokens.shape[2]
    model_width = tokens.shape[3]
    tick_count = micro_count + section_count - 1
    weights = (
        norm_gains[0].astype(jnp.float32),
        qkv_weight[0],
        out_weight[0],
        rel_bias[0],
        router_weight[0],
        expert_up[0],
        expert_down[0],
    )
    empty_rows = jnp.zeros((length, model_width), jnp.bfloat16)
    arriving = empty_rows
    kept_inputs = jnp.zeros((micro_count, length, model_width), jnp.bfloat16)
    section_out = jnp.zeros((micro_count, length, model_width), jnp.float32)
    for tick_index in range(tick_count):
        micro_index = tick_index - section_id
        is_valid = (micro_index >= 0) & (micro_index < micro_count)
        micro_slot = jnp.clip(micro_index, 0, micro_count - 1)
        own_rows = tokens[tick_index, 0] if tick_index < micro_count else empty_rows
        layer_in = jnp.where(section_id == 0, own_rows, arriving)
        context = pick_context(segments, pad_mask, routes, dist_bucket, micro_slot)
        inputs = layer_in.astype(jnp.float32)
        front = attention_front(inputs, context, weights)
        result, saved_state = forward_rest(inputs, front, context, weights)
        section_out = place_row(section_out, result, micro_slot, is_valid)
        kept_inputs = place_row(kept_inputs, layer_in, micro_slot, is_valid)
        arriving = shifted(result.astype(jnp.bfloat16), "section", 1)
    returning = empty_rows
    input_store = jnp.zeros((micro_count, length, model_width), jnp.float32)
    totals = None
    for tick_index in range(tick_count):
        micro_index = tick_index - (section_count - 1 - section_id)
        is_valid = (micro_index >= 0) & (micro_index < micro_count)
        micro_slot = jnp.clip(micro_index, 0, micro_count - 1)
        own_rows = cotangent[tick_index, 0] if tick_index < micro_count else empty_rows
        upstream = jnp.where(section_id == section_count - 1, own_rows, returning).astype(
            jnp.float32
        )
        inputs = pick_row(kept_inputs, micro_slot).astype(jnp.float32)
        context = pick_context(segments, pad_mask, routes, dist_bucket, micro_slot)
        front = attention_front(inputs, context, weights)
        saved_state = forward_rest(inputs, front, context, weights)[1]
        input_grad, grad_set = backward_layer(
            inputs, upstream, context, weights, front, saved_state
        )
        input_store = place_row(input_store, input_grad, micro_slot, is_valid)
        grad_set = jax.tree.map(partial(mask_grad, is_valid=is_valid), grad_set)
        totals = grad_set if totals is None else jax.tree.map(jnp.add, totals, grad_set)
        returning = shifted(input_grad.astype(jnp.bfloat16), "section", -1)
    shared = lax.psum((totals[0], totals[1], totals[2], totals[3], totals[4]), "dp")
    tensor_id = lax.axis_index("tensor")
    half_width = model_width // lax.axis_size("tensor")
    return (
        tensor_half(section_out, tensor_id, half_width),
        tensor_half(input_store, tensor_id, half_width),
        shared[0][None],
        shared[1][None],
        shared[2][None],
        shared[3][None],
        shared[4][None],
        totals[5][None],
        totals[6][None],
    )


def gelu_parts(values):
    share = 0.5 + 0.5 * lax.erf(values * 0.7071067811865476)
    return (values * share, share + values * (0.3989422804014327 * jnp.exp(-0.5 * values * values)))


def nn(left, right):
    return lax.dot_general(left, right, (((1,), (0,)), ((), ())), preferred_element_type=jnp.float32)


def nt(left, right):
    return lax.dot_general(left, right, (((1,), (1,)), ((), ())), preferred_element_type=jnp.float32)


def tn(left, right):
    return lax.dot_general(left, right, (((0,), (0,)), ((), ())), preferred_element_type=jnp.float32)


def split_low(values):
    high = values.astype(jnp.bfloat16)
    return (high, (values - high.astype(jnp.float32)).astype(jnp.bfloat16))


def inverse_rms(values):
    return lax.rsqrt(jnp.mean(values * values, axis=-1, keepdims=True) + norm_eps)


class Layout:
    pass


def layer_kernel(lay, *refs):
    (
        tok_ref, cot_ref, seg_hbm, pad_hbm, routes_hbm, dist_hbm, gains_hbm, qkvw_hbm, outw_hbm, relb_hbm, wr_hbm,
        up_ref, down_ref,
        secout_ref, ingrad_ref, ggain_ref, shared_ref, gbias_ref, grouter_ref, guv, gdv,
        seg_ref, pad_ref, routes_ref, dist_ref, gains_ref, relb_ref, wr_ref, upv, downv, upt, downt, qkvwt, outwt, qkvw_ref, outw_ref, xb, dyb, rr, place, bias_buf, probs_buf, no1, qkvb, mixed, att_send, att_recv, mid, ntb,
        gate_t, hit_t, wrp, score_sum, disp_x, xrows, disp_y, dyrows, hidden, dgelu, halves, eo_send, eo_recv, eob, eoret, out_own,
        other, gate_slots, og, gg_part, gg_other, gg_send, gg_recv, pg, cg_send, cg_recv, cgb, cgret, mgrad, ag, mg, qkvg,
        no_send, no_recv, ig_own, dy_send,
        no_all, mix_all, qgt, qt_all, agt, agt_all, small_send, small_in, small_all, small_sib,
        x_send, rs_buf, rs_in, relay_buf, relay_q,
        wsem, ss, rs,
    ) = refs
    bf = jnp.bfloat16
    f32 = jnp.float32
    micro, length, width = tok_ref.shape
    experts = lay.experts
    cap = lay.cap
    cols = outw_ref.shape[0]
    pairs = cols // 128
    ffn = up_ref.shape[1]
    slots = experts * cap
    half = width // 2
    s = lax.axis_index("section")
    d = lax.axis_index("dp")
    t = lax.axis_index("tensor")
    u = 1 - t
    sib = (s, d, u)
    across = (1 - s, d, t)
    bits = [lax.rem(d // bit, 2) for bit in (1, 2, 4)]

    def partner(flip):
        index = d
        for place, bit in enumerate((1, 2, 4)):
            index = index + (flip // bit) % 2 * (bit - 2 * bit * bits[place])
        return index

    peer = [partner(flip) for flip in (0, 4, 1, 6, 2, 5, 3, 7)]
    steps = range(1, experts)
    relayed = (5, 7)
    chunks = range(experts // 2)

    def pair(c):
        return pl.ds(2 * c, 2)

    def partner_at(k):
        c = k // 2
        return partner(c + (k % 2) * (4 + 2 * (c % 2) + c // 2 - c))


    def remote(src, dst, sem, device, k=0):
        return pltpu.make_async_remote_copy(
            src_ref=src,
            dst_ref=dst,
            send_sem=ss.at[sem[0]],
            recv_sem=rs.at[sem[1] + k],
            device_id=device,
            device_id_type=pl.DeviceIdType.MESH,
        )

    counter = [0, 0]

    def take(arrivals=1):
        pair_of = (counter[0], counter[1])
        counter[0] += 1
        counter[1] += arrivals
        return pair_of

    def all_sent(like, sem):
        remote(like, like, sem, sib).wait_send()

    def all_here(like, sem, k=0):
        remote(like, like, sem, sib, k).wait_recv()

    ring_hops = experts - 1
    sem_routes = take()
    sem_x = take()
    sem_relay = [take(len(relayed)) for _ in range(2)]
    sem_pass = [take(0) for _ in range(2)]
    sem_relay_q = take(len(relayed))
    sem_pass_q = take(0)
    sem_xf = take()
    sem_dy = take()
    sem_att = take()
    sem_eo = take(len(chunks))
    sem_cg = take(len(chunks))
    sem_ag = take()
    sem_no = take()
    sem_so = take()
    sem_ig = take()
    sem_dx = take(len(chunks))
    sem_dxf = take(len(chunks))
    sem_ddy = take(len(chunks))
    sem_ddyf = take(len(chunks))
    sem_re = take()
    sem_rc = take()
    sem_gg = take()
    sem_gg_core = take(len(chunks))
    sem_qgt = take(experts)
    sem_agt = take()
    sem_agtf = take()
    sem_small = take()
    sem_back = take()
    sem_sums = take()
    sem_noall = take()
    sem_ring_no = take(2 * ring_hops)
    sem_ring_mix = take(2 * ring_hops)
    sem_ring_sum = (take(0)[0], sem_ring_no[1])
    sem_ring_out = take(4 * ring_hops)
    assert tuple(counter) == lay.sems

    def block(index, rows):
        return pl.ds(pl.multiple_of(index * rows, rows), rows)

    place_y = lax.rem(d, 2)
    place_z = d // 2
    ring_at = place_z + place_y * (experts - 1 - 2 * place_z)

    def ring_device(position):
        p = lax.rem(position + 2 * experts, experts)
        return 2 * p + (p // (experts // 2)) * (2 * experts - 1 - 4 * p)

    def hops(number, direction):
        return experts // 2 - (number % 2 == (direction > 0))

    def hop_index(number, direction, k):
        return number * ring_hops + k + (0 if direction > 0 else hops(number, 1))

    def lines_of(amount):
        return [(number, direction) for number in range(amount) for direction in (1, -1)]

    def ring_gather(parts, at_half=None):
        def hop(number, direction, k):
            view, sem, first = parts[number]
            held = view(ring_device(ring_at - direction * k))
            index = hop_index(number, direction, k) - first * ring_hops
            return remote(held, held, sem, (s, ring_device(ring_at + direction), t), index)

        lines = lines_of(len(parts))
        for line in lines:
            hop(*line, 0).start()

        def one(k, carry):
            for line in lines:
                hop(*line, k - 1).wait_recv()
                hop(*line, k).start()
            return carry

        short = experts // 2 - 1
        lax.fori_loop(1, short, one, 0)
        if at_half is not None:
            at_half()
        for line in lines:
            hop(*line, short - 1).wait_recv()
            if hops(*line) > short:
                hop(*line, short).start()
        for line in lines:
            if hops(*line) > short:
                hop(*line, short).wait_recv()

    small_loads = [
        pltpu.make_async_copy(src, dst, wsem.at[5 + i])
        for i, (src, dst) in enumerate(
            (
                (routes_hbm, routes_ref),
                (wr_hbm, wr_ref),
                (seg_hbm, seg_ref),
                (pad_hbm, pad_ref),
                (dist_hbm, dist_ref),
                (gains_hbm, gains_ref),
                (relb_hbm, relb_ref),
            )
        )
    ]
    for copy in small_loads:
        copy.start()
    load_up = pltpu.make_async_copy(up_ref, upv, wsem.at[0])
    load_down = pltpu.make_async_copy(down_ref, downv, wsem.at[1])
    load_qkvw = pltpu.make_async_copy(qkvw_hbm, qkvw_ref, wsem.at[2])
    load_outw = pltpu.make_async_copy(outw_hbm, outw_ref, wsem.at[3])
    load_tok = pltpu.make_async_copy(tok_ref, xb, wsem.at[4])
    load_cot = pltpu.make_async_copy(cot_ref.at[t], dyb, wsem.at[4])

    @pl.when(s == 0)
    def _():
        load_tok.start()

    @pl.when(s == 1)
    def _():
        load_cot.start()

    load_qkvw.start()
    load_outw.start()
    load_up.start()
    load_down.start()

    barrier = pltpu.get_barrier_semaphore()
    for k in steps:
        pl.semaphore_signal(barrier, inc=1, device_id=(s, peer[k], t), device_id_type=pl.DeviceIdType.MESH)
    pl.semaphore_signal(barrier, inc=1, device_id=sib, device_id_type=pl.DeviceIdType.MESH)
    for k in (0,) + relayed:
        pl.semaphore_signal(barrier, inc=1, device_id=(1 - s, peer[k], t), device_id_type=pl.DeviceIdType.MESH)
    pl.semaphore_wait(barrier, experts + 1 + len(relayed))

    for copy in small_loads:
        copy.wait()

    for k in steps:
        remote(routes_ref, rr.at[k], sem_routes, (s, peer[k], t)).start()
    rr[0] = routes_ref[...]

    lanes8 = lax.broadcasted_iota(jnp.int32, (experts, length), 0)
    row_at = lax.broadcasted_iota(jnp.int32, (length, length), 0)
    col_at = lax.broadcasted_iota(jnp.int32, (length, length), 1)
    before = (row_at < col_at).astype(bf)
    slot_at = lax.broadcasted_iota(jnp.int32, (cap, length), 0).astype(f32)

    expert_of = jnp.zeros((experts, length), jnp.int32)
    for k in range(experts):
        expert_of = jnp.where(lanes8 == k, peer[k], expert_of)
    turn = (lax.broadcasted_iota(jnp.int32, (experts, experts), 1) == expert_of[:, 0:experts]).astype(f32).astype(bf)
    wrp[...] = nn(turn, wr_ref[...]).astype(bf)
    own_routes = routes_ref[t]
    hits = (expert_of == own_routes[0:1, :]) | (expert_of == own_routes[1:2, :])
    hit_f = hits.astype(f32)
    hit_t[...] = hit_f
    spot = jnp.where(hits, nn(hit_f.astype(bf), before), -1.0)
    for e in range(experts):
        place[e * cap : (e + 1) * cap, :] = (slot_at == spot[e : e + 1, :]).astype(f32).astype(bf)

    def to_relay(source, k, leg):
        i = relayed.index(k)
        return remote(source, relay_buf.at[leg * len(relayed) + i], sem_relay[leg], across, i)

    def relay(landing, sem, leg):
        for i, k in enumerate(relayed):
            held = relay_buf.at[leg * len(relayed) + i]
            all_here(held, sem_relay[leg], i)
            through = (sem_pass[leg][0], sem[1] + k // 2)
            remote(held, landing.at[k, t], through, (0, peer[k], t)).start()

    def dispatch(rows, send, landing, sem, sem_fwd, leg=None, both=False):
        send[...] = nn(place[...], rows).astype(bf).reshape(send.shape)

        def direct(k):
            remote(send.at[k], landing.at[k, t], sem, (s, peer[k], t), k // 2).start()

        def start_relayed():
            for k in relayed:
                to_relay(send.at[k], k, leg).start()

        def start_direct():
            for k in relayed:
                direct(k)

        direct(1)
        if both:
            pl.when(s == 0)(start_relayed)
        elif leg is not None:
            start_relayed()
        for k in steps[1:]:
            if k not in relayed:
                direct(k)
        if both:
            pl.when(s == 1)(start_direct)
        elif leg is None:
            start_direct()
        landing[0, t] = send[0]

        def arrive(c):
            held = landing.at[pair(c), t]
            all_here(landing.at[1, t] if isinstance(c, int) and c == 0 else held, sem, c)
            remote(held, held, sem_fwd, sib, c).start()

        def joined(c):
            all_here(landing.at[pair(c), t], sem_fwd, c)

        def drain(zero):
            all_sent(send, sem_fwd)
            if zero:
                all_sent(send.at[0 : experts - 1 - len(relayed)], sem)
                all_sent(send.at[0 : len(relayed)], sem_relay[leg])
            else:
                all_sent(send.at[1:experts], sem)

        return arrive, joined, drain

    def stream(dispatched, first, second, finish_chunk, eager, zero):
        arrive, joined, drain = dispatched
        last = len(chunks) - 1
        arrive(0)
        joined(0)

        def one(c, carry):
            first(c)
            if eager:
                pl.when(c > 0)(lambda: finish_chunk(c - 1))
                pl.when(c < last)(lambda: arrive(c + 1))
                second(c)
            else:
                second(c)

                @pl.when(c < last)
                def _():
                    arrive(c + 1)
                    finish_chunk(c)


            @pl.when(c < last)
            def _():
                joined(c + 1)

            return carry

        lax.fori_loop(0, len(chunks), one, 0)
        finish_chunk(last)
        drain(zero)

    def turn_weights():
        upt[...] = jnp.transpose(upv[...])
        downt[...] = jnp.transpose(downv[...])
        for c in range(3):
            qkvwt[c] = jnp.transpose(qkvw_ref[c])
        outwt[...] = jnp.transpose(outw_ref[...])

    def other_experts():
        all_here(rr.at[1:experts], sem_routes)

        def one(i, carry):
            q = i // micro
            m = i % micro
            pair = rr[q, m]
            first = pair[0:1, :] == d
            mine = first | (pair[1:2, :] == d)
            mine_f = jnp.broadcast_to(mine.astype(f32), (experts, length))
            spots = jnp.where(mine_f > 0.0, nn(mine_f.astype(bf), before), -1.0)
            where_slot = (slot_at == spots[0:1, :]).astype(f32).astype(bf)
            partner = jnp.where(first, pair[1:2, :], pair[0:1, :])
            partner_hot = (lanes8 == partner).astype(f32).astype(bf)
            other[q, m] = nt(where_slot, partner_hot)
            return carry

        lax.fori_loop(0, experts * micro, one, 0)

    @pl.when(s == 0)
    def _():
        load_tok.wait()
        load_qkvw.wait()
        load_outw.wait()

    @pl.when(s == 1)
    def _():
        load_cot.wait()
        relay(xrows, sem_dx, 0)
        load_up.wait()
        load_down.wait()
        load_qkvw.wait()
        load_outw.wait()
        turn_weights()
        other_experts()
        arrive, joined, drain = dispatch(dyb[...], disp_y, dyrows, sem_ddy, sem_ddyf)

        def pass_one(c, carry):
            arrive(c)
            return carry

        def join_one(c, carry):
            joined(c)
            return carry

        arrive(0)
        lax.fori_loop(1, len(chunks), pass_one, 0)
        lax.fori_loop(0, len(chunks), join_one, 0)
        drain(False)

    dist_rows = (
        lax.broadcasted_iota(jnp.int32, (lay.buckets, length), 0) == dist_ref[...]
    ).astype(f32).astype(bf)
    bias_rows = nn(relb_ref[...], dist_rows).astype(bf)
    mirror = ((row_at + col_at == length) | (row_at + col_at == 0)).astype(f32).astype(bf)
    bias_back = nn(bias_rows, mirror)
    for m in range(micro):
        seg_rows = jnp.broadcast_to(seg_ref[m : m + 1, :].astype(f32), (length, length))
        pads = jnp.broadcast_to(pad_ref[m : m + 1, :], (length, length))
        allowed = (col_at <= row_at) & (seg_rows == jnp.transpose(seg_rows))
        allowed = allowed & ((pads == 1) | (col_at == row_at))
        for p in range(pairs):
            for h in range(2):
                head = 2 * p + h
                grid = pltpu.roll(
                    jnp.broadcast_to(bias_back[head : head + 1, :], (length, length)), 0, 1, stride=1, stride_axis=0
                )
                bias_buf[m, p, :, h * length : (h + 1) * length] = jnp.where(allowed, grid, masked_score)

    x_copy = remote(x_send, xb.at[t], sem_x, across)
    dy_copy = remote(dy_send, dyb, sem_dy, across)
    x_forward = remote(xb.at[t], xb.at[t], sem_xf, sib)

    def spread_gates(gates_ref):
        return jnp.concatenate(
            [
                jnp.broadcast_to(gates_ref[e : e + 1, :], (cap, length)) * place[e * cap : (e + 1) * cap, :].astype(f32)
                for e in range(experts)
            ],
            axis=0,
        ).astype(bf)

    @pl.when(s == 1)
    def _():
        x_copy.wait_recv()
        x_forward.start()

    gain_one = gains_ref[0:1, :].astype(f32)
    gain_two = gains_ref[1:2, :].astype(f32)
    low_lanes = lax.broadcasted_iota(jnp.int32, (length, 128), 1) < 64

    def both_heads(pair_block):
        zero = jnp.zeros((), bf)
        return jnp.concatenate(
            [jnp.where(low_lanes, pair_block, zero), jnp.where(low_lanes, zero, pair_block)], axis=0
        )

    def attend(m):
        x_rows = xb[m].astype(f32)
        no1[m] = (x_rows * inverse_rms(x_rows) * gain_one).astype(bf)
        for c in range(3):
            qkvb[c, m] = nn(no1[m], qkvw_ref[c]).astype(bf)
        for p in range(pairs):
            at = slice(p * 128, (p + 1) * 128)
            scores = 0.125 * nt(qkvb[0, m, :, at], both_heads(qkvb[1, m, :, at])) + bias_buf[m, p]
            for h in range(2):
                part = scores[:, h * length : (h + 1) * length]
                terms = jnp.exp(part - jnp.max(part, axis=-1, keepdims=True))
                probs_buf[m, p, :, h * length : (h + 1) * length] = terms * (
                    1.0 / jnp.sum(terms, axis=-1, keepdims=True)
                )
            mixed[m, :, at] = nn(probs_buf[m, p].astype(bf), both_heads(qkvb[2, m, :, at])).astype(bf)

    att_copy = remote(att_send, att_recv, sem_att, sib)

    def project_other():
        att_send[...] = nn(mixed[u], outw_ref[...]).astype(bf)
        att_copy.start()

    begin = u + s * (t - u)

    def attend_one(i, carry):
        @pl.when((s == 1) & (i == 1))
        def _():
            x_forward.wait()

        attend(begin + i * (1 - 2 * begin))

        @pl.when((s == 0) & (i == 0))
        def _():
            project_other()

        return carry

    lax.fori_loop(0, micro, attend_one, 0)

    @pl.when(s == 1)
    def _():
        project_other()

    part_own = nn(mixed[t], outw_ref[...])
    att_copy.wait()
    middle = xb[t].astype(f32) + part_own + att_recv[...].astype(f32)
    mid[...] = middle
    ntb[...] = (middle * inverse_rms(middle) * gain_two).astype(bf)

    arrivals = dispatch(ntb[...], disp_x, xrows, sem_dx, sem_dxf, 0, True)
    logits_t = jnp.where(hit_t[...] > 0.0, nt(wrp[...], ntb[...]), masked_score)
    terms = jnp.exp(logits_t - jnp.max(logits_t, axis=0, keepdims=True))
    gate_t[...] = terms / jnp.sum(terms, axis=0, keepdims=True)
    rows_of = 2 * micro * cap

    def flat(ref, chunk):
        return ref[chunk].reshape(rows_of, ref.shape[-1])

    def front_chunk(c):
        value, slope = gelu_parts(nn(flat(xrows, pair(c)), upv[...]))
        hidden[pair(c)] = value.astype(bf).reshape(2, micro, cap, ffn)
        dgelu[pair(c)] = slope.astype(bf).reshape(2, micro, cap, ffn)

    def split_sum(c, total, send, recv, base):
        for m in range(micro):
            halves[m] = total.reshape(2, micro, cap, width)[:, m]
        send[pair(c)] = halves[u].astype(bf)
        remote(send.at[pair(c)], recv.at[pair(c)], base, sib, c).start()

    def hand_back(c, send, recv, base, total, landing, base_back):
        all_here(recv.at[pair(c)], base, c)
        total[pair(c)] = (halves[t] + recv[pair(c)].astype(f32)).astype(bf)

        def give(k):
            remote(total.at[k], landing.at[k], base_back, (s, partner_at(k), t)).start()

        def keep():
            landing[0] = total[0]

        if isinstance(c, int):
            give(2 * c)
        else:
            pl.when(c == 0)(keep)
            pl.when(c > 0)(lambda: give(2 * c))
        give(2 * c + 1)

    def wait_back(total, landing, sem):
        all_here(landing.at[1:experts], sem)
        all_sent(total.at[1:experts], sem)

    def rows_chunk(c):
        split_sum(c, nn(flat(hidden, pair(c)), downv[...]), eo_send, eo_recv, sem_eo)

    def rows_finish(c):
        hand_back(c, eo_send, eo_recv, sem_eo, eob, eoret, sem_re)

    mine_hot = (lax.broadcasted_iota(jnp.int32, (rows_of, experts), 1) == d).astype(f32)

    ones = jnp.ones((8, ffn), bf)
    gg_part[...] = jnp.zeros_like(gg_part)

    def gate_chunk(c):
        slot_logits = nt(flat(xrows, pair(c)), wr_ref[...])
        own_logit = jnp.sum(slot_logits * mine_hot, axis=-1, keepdims=True)
        other_logit = jnp.sum(slot_logits * flat(other, pair(c)), axis=-1, keepdims=True)
        gate = 1.0 / (1.0 + jnp.exp(other_logit - own_logit))
        gate_slots[pair(c)] = gate.reshape(2, micro, cap, 1)

    def slope_chunk(c):
        dy_flat = flat(dyrows, pair(c))
        gate = flat(gate_slots, pair(c))
        grad = nn(dy_flat, downt[...])
        pg[pair(c)] = (grad * gate * flat(dgelu, pair(c)).astype(f32)).astype(bf).reshape(2, micro, cap, ffn)
        product = (grad * flat(hidden, pair(c)).astype(f32)).astype(bf)
        for i in range(2):
            for m in range(micro):
                at = (i * micro + m) * cap
                gg_part[m, 2 * c + i, :, 0:cap] = nt(ones, product[at : at + cap])

    def back_chunk(c):
        remote(gg_part.at[u, pair(c)], gg_other.at[pair(c)], sem_gg_core, sib, c).start()
        split_sum(c, nn(flat(pg, pair(c)), upt[...]), cg_send, cg_recv, sem_cg)

    def both_chunk(c):
        front_chunk(c)
        gate_chunk(c)
        slope_chunk(c)

    def back_finish(c):
        hand_back(c, cg_send, cg_recv, sem_cg, cgb, cgret, sem_rc)
        all_here(gg_other.at[pair(c)], sem_gg_core, c)
        gg_send[pair(c)] = gg_part[t, pair(c)] + gg_other[pair(c)]

        def give(k):
            remote(gg_send.at[k], gg_recv.at[k], sem_gg, (s, partner_at(k), t)).start()

        def keep():
            gg_recv[0] = gg_send[0]

        if isinstance(c, int):
            give(2 * c)
        else:
            pl.when(c == 0)(keep)
            pl.when(c > 0)(lambda: give(2 * c))
        give(2 * c + 1)

    def hidden_of(m):
        return jnp.concatenate([hidden[k, m] for k in range(experts)], axis=0)

    def expert_rows():
        eo_send[...] = nn(hidden_of(u), downv[...]).astype(bf).reshape(eo_send.shape)
        eo_copy = remote(eo_send, eo_recv, sem_eo, sib)
        eo_copy.start()
        total = nn(hidden_of(t), downv[...])
        eo_copy.wait_recv()
        eob[...] = (total + eo_recv[...].astype(f32).reshape(slots, width)).astype(bf).reshape(eob.shape)

    def send_back(source, landing, base):
        for k in steps:
            remote(source.at[k], landing.at[k], base, (s, peer[k], t)).start()
        landing[0] = source[0]

    def layer_output():
        result = mid[...] + tn(spread_gates(gate_t), eoret[...].reshape(slots, width))
        out_own[...] = result
        return result

    def own_half():
        return pl.ds(pl.multiple_of(t * half, half), half)

    def other_half():
        return pl.ds(pl.multiple_of(u * half, half), half)

    def hand_out(rows_ref, out_ref, index):
        copy = remote(rows_ref.at[:, other_half()], out_ref.at[t], index, sib)
        copy.start()
        out_ref[t] = rows_ref[:, own_half()]
        copy.wait()

    def gather_factors():
        no_all[t, d] = no1[t]
        mix_all[d] = mixed[...]
        ring_gather(
            [
                (lambda q: no_all.at[t, q, 0 : length // 2], sem_ring_no, 0),
                (lambda q: no_all.at[t, q, length // 2 : length], sem_ring_no, 0),
                (lambda q: mix_all.at[q, 0], sem_ring_mix, 2),
                (lambda q: mix_all.at[q, 1], sem_ring_mix, 2),
            ]
        )
        all_sent(no_all.at[t, 1:experts], sem_ring_no)
        all_sent(mix_all.at[1:experts], sem_ring_mix)
        copy = remote(no_all.at[t], no_all.at[t], sem_noall, sib)
        copy.start()
        copy.wait()

    @pl.when(s == 0)
    def _():
        load_up.wait()
        load_down.wait()
        stream(arrivals, front_chunk, rows_chunk, rows_finish, True, True)
        wait_back(eob, eoret, sem_re)
        x_send[...] = layer_output().astype(bf)
        x_copy.start()
        hand_out(out_own, secout_ref, sem_so)
        turn_weights()
        other_experts()

        def gate_one(c, carry):
            gate_chunk(c)
            return carry

        lax.fori_loop(0, len(chunks), gate_one, 0)
        gather_factors()
        x_copy.wait_send()
        dy_copy.wait_recv()
        arrivals_y = dispatch(dyb[...], disp_y, dyrows, sem_ddy, sem_ddyf, 1)
        stream(arrivals_y, slope_chunk, back_chunk, back_finish, True, True)

    @pl.when(s == 1)
    def _():
        stream(arrivals, both_chunk, back_chunk, back_finish, True, False)
        expert_rows()

    wait_back(gg_send, gg_recv, sem_gg)
    wait_back(cgb, cgret, sem_rc)

    @pl.when(s == 1)
    def _():
        send_back(eob, eoret, sem_re)


    gg_rows = []
    for e in range(experts):
        high, low = split_low(gg_recv[e][:, 0:cap])
        spot_rows = place[e * cap : (e + 1) * cap, :]
        gg_rows.append((nn(high, spot_rows) + nn(low, spot_rows))[0:1, :])
    gate_grad = jnp.concatenate(gg_rows, axis=0)
    gates = gate_t[...]
    logit_grad = (gates * (gate_grad - jnp.sum(gates * gate_grad, axis=0, keepdims=True))).astype(bf)
    two_grad = tn(logit_grad, wrp[...]) + tn(place[...], cgret[...].reshape(slots, width))
    dy = dyb[...].astype(f32)
    middle = mid[...]
    scale = inverse_rms(middle)
    normed = middle * scale
    scaled = two_grad * gain_two
    middle_grad = dy + scale * (scaled - normed * jnp.mean(scaled * normed, axis=-1, keepdims=True))
    mgrad[...] = middle_grad
    ag[t] = middle_grad.astype(bf)
    ag_copy = remote(ag.at[t], ag.at[t], sem_ag, sib)
    ag_copy.start()

    agt_rows = width // experts
    agt_own = remote(agt.at[block(d, agt_rows)], agt_all.at[d, t], sem_agtf, sib)

    @pl.when(s == 0)
    def _():
        agt[...] = jnp.transpose(ag[t])
        for k in reversed(steps):
            remote(agt.at[block(peer[k], agt_rows)], agt_all.at[d, t], sem_agt, (s, peer[k], t)).start()
        agt_all[d, t] = agt[block(d, agt_rows), :]
        agt_own.start()

    two_normed = normed
    groups = width // 128
    qgt_rows = 3 * cols // experts

    def attend_back(m, i):
        mg[m] = nn(ag[m], outwt[...]).astype(bf)
        for p in range(pairs):
            at = slice(p * 128, (p + 1) * 128)
            mg_pair = mg[m, :, at]
            probs = probs_buf[m, p]
            keys2 = both_heads(qkvb[1, m, :, at])
            queries2 = both_heads(qkvb[0, m, :, at])
            mg2 = both_heads(mg_pair)
            prob_grad = nt(mg_pair, both_heads(qkvb[2, m, :, at]))
            raws = []
            key_grad = jnp.zeros((length, 128), f32)
            value_grad = jnp.zeros((length, 128), f32)
            for h in range(2):
                lane = slice(h * length, (h + 1) * length)
                part = probs[:, lane]
                step = prob_grad[:, lane]
                score_grad = part * (step - jnp.sum(part * step, axis=-1, keepdims=True))
                score_sum[2 * p + h] += score_grad
                raw = (0.125 * score_grad).astype(bf)
                raws.append(raw)
                key_grad = key_grad + tn(raw, queries2[h * length : (h + 1) * length])
                value_grad = value_grad + tn(part.astype(bf), mg2[h * length : (h + 1) * length])
            query_grad = nn(jnp.concatenate(raws, axis=1), keys2)
            for c, grad in enumerate((query_grad, key_grad, value_grad)):
                qkvg[c, m, :, at] = grad.astype(bf)

        @pl.when(s == 0)
        def _():
            for c in range(3):
                qgt[i, c * cols : (c + 1) * cols, :] = jnp.transpose(qkvg[c, m])
            for k in reversed([k for k in steps if k not in relayed]):
                rows = block(peer[k], qgt_rows)
                remote(qgt.at[i, rows], qt_all.at[d, i], sem_qgt, (s, peer[k], t), k).start()
            qt_all[d, i] = qgt[i, block(d, qgt_rows), :]

    score_sum[...] = jnp.zeros_like(score_sum)

    attend_back(t, 0)
    ag_copy.wait()
    attend_back(u, 1)

    def relay_q_copy(i, k):
        return remote(qgt.at[:, block(peer[k], qgt_rows)], relay_q.at[i], sem_relay_q, across, i)

    @pl.when(s == 0)
    def _():
        for i, k in enumerate(relayed):
            relay_q_copy(i, k).start()


    def project_back(m):
        total = nn(qkvg[0, m], qkvwt[0])
        for c in range(1, 3):
            total = total + nn(qkvg[c, m], qkvwt[c])
        return total

    no_send[...] = project_back(u).astype(bf)
    no_copy = remote(no_send, no_recv, sem_no, sib)
    no_copy.start()
    one_grad = project_back(t)
    no_copy.wait()
    one_grad = one_grad + no_recv[...].astype(f32)
    x_rows = xb[t].astype(f32)
    scale = inverse_rms(x_rows)
    normed = x_rows * scale
    scaled = one_grad * gain_one
    input_grad = mgrad[...] + scale * (scaled - normed * jnp.mean(scaled * normed, axis=-1, keepdims=True))
    dy_send[...] = input_grad.astype(bf)

    @pl.when(s == 1)
    def _():
        dy_copy.start()

    ig_own[...] = input_grad
    gain_one_grad = jnp.sum(one_grad * normed, axis=0, keepdims=True)
    hand_out(ig_own, ingrad_ref, sem_ig)

    router_grad = nn(tn(turn, logit_grad).astype(bf), ntb[...])
    gain_two_grad = jnp.sum(two_grad * two_normed, axis=0, keepdims=True)
    small_send[...] = jnp.zeros_like(small_send)
    for g in range(groups):
        small_send[g, 0:experts, :] = router_grad[:, g * 128 : (g + 1) * 128]
        small_send[g, experts + 1 : experts + 2, :] = gain_two_grad[:, g * 128 : (g + 1) * 128]
    sums = []
    for head in range(2 * pairs):
        high, low = split_low(score_sum[head])
        turned = pltpu.roll(nn(high, mirror) + nn(low, mirror), 0, 1, stride=1, stride_axis=0)
        sums.append(jnp.sum(turned, axis=0, keepdims=True))
    high, low = split_low(jnp.concatenate(sums, axis=0))
    small_send[groups, 0 : 2 * pairs, 0 : lay.buckets] = nt(high, dist_rows) + nt(low, dist_rows)
    for g in range(groups):
        small_send[g, experts : experts + 1, :] = gain_one_grad[:, g * 128 : (g + 1) * 128]
    for k in steps:
        remote(small_send.at[peer[k]], small_in.at[k], sem_small, (s, peer[k], t)).start()
    small_in[0] = small_send[d]

    wide = lay.wide
    every = micro * slots

    for k in range(experts):
        og[k] = (dyrows[k].astype(f32) * gate_slots[k]).astype(bf)

    def expert_grads(n, carry):
        at = pl.ds(pl.multiple_of(n * wide, wide), wide)
        guv[:, at] = tn(xrows[...].reshape(every, width), pg[:, :, :, at].reshape(every, wide)).astype(bf)
        gdv[at, :] = tn(hidden[:, :, :, at].reshape(every, wide), og[...].reshape(every, width)).astype(bf)
        return carry

    lax.fori_loop(0, ffn // wide, expert_grads, 0)

    qkv_rows = 3 * cols // experts
    share = shared_ref.shape[1] // 4
    parts = [slice(c * share, (c + 1) * share) for c in range(4)]

    def pack_out(total):
        half_rows = agt_rows // 2
        return jnp.concatenate([total[..., 0:half_rows, :], total[..., half_rows:, :]], axis=-1).astype(bf)

    @pl.when(s == 0)
    def _():
        all_here(agt_all.at[1:experts, 0], sem_agt)
        for k in steps:
            held = agt_all.at[peer[k], t]
            remote(held, held, sem_agtf, sib).start()
        all_here(agt_all.at[:, 0], sem_agtf)
        all_sent(agt_all.at[1:experts, 0], sem_agt)
        all_sent(agt_all.at[:, 0], sem_agtf)
        total = jnp.zeros((agt_rows, cols), f32)
        for q in range(experts):
            for m in range(micro):
                total = total + nn(agt_all[q, m], mix_all[q, m])
        shared_ref[d, qkv_rows:, :] = pack_out(total)

        def qkv_slice(q):
            rows = jnp.concatenate([qt_all[q, 0], qt_all[q, 1]], axis=1)
            return nn(rows, jnp.concatenate([no_all[t, q], no_all[u, q]], axis=0))

        total = qkv_slice(d)
        for k in [k for k in reversed(steps) if k not in relayed] + list(relayed):
            all_here(qt_all.at[0], sem_qgt, k)
            total = total + qkv_slice(peer[k])
        all_sent(qt_all.at[0 : experts - 1 - len(relayed)], sem_qgt)
        all_sent(relay_q, sem_relay_q)
        shared_ref[d, 0:qkv_rows, :] = total.astype(bf)

    @pl.when(s == 1)
    def _():
        normed_rows = no1[...].reshape(micro * length, width)
        own = jnp.concatenate([tn(qkvg[c].reshape(micro * length, cols), normed_rows) for c in range(3)], axis=0)
        rs_buf[:, 0:qkv_rows, :] = own.astype(bf).reshape(experts, qkv_rows, width)
        own = tn(ag[...].reshape(micro * length, width), mixed[...].reshape(micro * length, cols))
        rs_buf[:, qkv_rows:, :] = pack_out(own.reshape(experts, agt_rows, cols))

        relay(dyrows, sem_ddy, 1)

        def owner_at(number, direction, k):
            return ring_device(ring_at + direction * (hops(number, direction) - k))

        def hop(number, direction, k):
            index = hop_index(number, direction, k)
            return remote(
                rs_buf.at[owner_at(number, direction, k), parts[number]],
                rs_in.at[index % ring_hops, parts[number]],
                sem_ring_sum,
                (s, ring_device(ring_at + direction), t),
                index,
            )

        lines = lines_of(len(parts))
        for k in range(experts // 2):
            for line in lines:
                if k < hops(*line):
                    if k > 0:
                        rows = parts[line[0]]
                        owner = owner_at(*line, k)
                        hop(*line, k - 1).wait_recv()
                        came = rs_in[hop_index(*line, k - 1) % ring_hops, rows, :].astype(f32)
                        rs_buf[owner, rows, :] = (rs_buf[owner, rows, :].astype(f32) + came).astype(bf)
                    hop(*line, k).start()
        for number, rows in enumerate(parts):
            total = rs_buf[d, rows, :].astype(f32)
            for direction in (1, -1):
                last = hops(number, direction) - 1
                hop(number, direction, last).wait_recv()
                total = total + rs_in[hop_index(number, direction, last) % ring_hops, rows, :].astype(f32)
            shared_ref[d, rows, :] = total.astype(bf)
        for i, k in enumerate(relayed):
            all_here(relay_q.at[i], sem_relay_q, i)
            remote(relay_q.at[i], qt_all.at[d], (sem_pass_q[0], sem_qgt[1] + k), (0, peer[k], t)).start()

    all_here(small_in.at[1:experts], sem_small)
    small_total = small_in[0]
    for k in steps:
        small_total = small_total + small_in[k]
    small_all[d] = small_total
    for k in steps:
        remote(small_all.at[d], small_all.at[d], sem_back, (s, peer[k], t)).start()

    sums_copy = remote(small_all, small_sib, sem_sums, sib)

    def pass_sums():
        all_here(small_all.at[1:experts], sem_back)
        sums_copy.start()


    streams = [
        (lambda q, rows=rows: shared_ref.at[q, rows], sem_ring_out, 0) for rows in parts
    ]

    ring_gather(streams, pass_sums)
    sums_copy.wait_recv()
    for g in range(groups):
        lanes = slice(g * 128, (g + 1) * 128)
        grouter_ref[:, lanes] = small_all[g, 0:experts, :] + small_sib[g, 0:experts, :]
        ggain_ref[:, lanes] = small_all[g, experts : experts + 2, :] + small_sib[g, experts : experts + 2, :]
    gbias_ref[...] = small_all[groups, 0 : 2 * pairs, :]
    @pl.when(s == 1)
    def _():
        dy_copy.wait_send()
        for sem in sem_pass:
            all_sent(relay_buf.at[0 : len(relayed)], sem)
        all_sent(rs_in, sem_ring_sum)
        all_sent(relay_q, sem_pass_q)
        wait_back(eob, eoret, sem_re)
        layer_output()
        hand_out(out_own, secout_ref, sem_so)

    all_sent(rr.at[1:experts], sem_routes)
    all_sent(eo_send, sem_eo)
    all_sent(cg_send, sem_cg)
    all_sent(gg_part.at[0], sem_gg_core)
    all_sent(small_in.at[1:experts], sem_small)
    all_sent(small_all.at[1:experts], sem_back)
    all_sent(small_all, sem_sums)
    all_sent(shared_ref.at[1:experts], sem_ring_out)


def widen_kernel(
    sec_ref, ing_ref, gain_ref, shared_ref, bias_ref, router_ref, up_ref, down_ref,
    sec_out, ing_out, gain_out, bias_out, router_out, qkv_out, out_out, up_out, down_out,
    up_wide, down_wide, qkv_wide, out_wide, bias_wide, out_sem,
):
    f32 = jnp.float32
    parts = 6
    experts, shared_rows, width = shared_ref.shape
    cols = out_wide.shape[0]
    qkv_rows = 3 * cols // experts
    wide = ((up_ref, up_wide, up_out), (down_ref, down_wide, down_out))
    stores = []

    def store(src, dst):
        copy = pltpu.make_async_copy(src, dst, out_sem.at[len(stores)])
        copy.start()
        stores.append(copy)

    def widen(i, n):
        src, dst, out = wide[i]
        size = src.shape[0] // parts
        rows = pl.ds(n * size, size)
        dst[rows, :] = src[rows, :].astype(f32)
        store(dst.at[rows], out.at[rows])

    def turn_qkv(c):
        block = shared_ref[:, 0:qkv_rows, :].reshape(3 * cols, width)[c * cols : (c + 1) * cols]
        qkv_wide[c] = jnp.transpose(block.astype(f32))
        store(qkv_wide.at[c], qkv_out.at[c])

    store(sec_ref, sec_out)
    store(ing_ref, ing_out)
    widen(0, 0)
    store(gain_ref, gain_out)
    store(router_ref, router_out)
    for h in range(bias_wide.shape[0]):
        bias_wide[h] = bias_ref[h : h + 1, 0 : bias_wide.shape[2]]
    store(bias_wide, bias_out)
    widen(0, 1)
    widen(0, 2)
    turn_qkv(0)
    widen(0, 3)
    widen(0, 4)
    turn_qkv(1)
    widen(0, 5)
    widen(1, 0)
    turn_qkv(2)
    widen(1, 1)
    widen(1, 2)
    out_block = jnp.concatenate(
        [
            shared_ref[e, qkv_rows:, h * cols : (h + 1) * cols].astype(f32)
            for e in range(experts)
            for h in range(2)
        ],
        axis=0,
    )
    out_wide[...] = jnp.transpose(out_block)
    store(out_wide, out_out)
    widen(1, 3)
    widen(1, 4)
    widen(1, 5)
    for copy in stores:
        copy.wait()


def fused_local(
    tokens,
    cotangent,
    segments,
    pad_mask,
    routes,
    dist_bucket,
    norm_gains,
    qkv_weight,
    out_weight,
    rel_bias,
    router_weight,
    expert_up,
    expert_down,
):
    micro, _, length, width = tokens.shape
    experts = router_weight.shape[2]
    cap = max(2, 3 * length // experts)
    cols = out_weight.shape[1]
    heads = rel_bias.shape[2]
    ffn = expert_up.shape[3]
    slots = experts * cap
    pairs = cols // 128
    shared_rows = 3 * cols // experts + width // experts // 2
    lay = Layout()
    lay.experts = experts
    lay.cap = cap
    lay.buckets = rel_bias.shape[1]
    lay.wide = min(ffn, 256)
    chunks = experts // 2
    lay.sems = (36, 7 * chunks + experts + 8 * (experts - 1) + 24)
    bf = jnp.bfloat16
    f32 = jnp.float32
    vm = pltpu.VMEM
    shape = jax.ShapeDtypeStruct
    dma = pltpu.SemaphoreType.DMA
    scratch = [
        vm((micro, length), jnp.int32),
        vm((micro, length), jnp.int32),
        vm((micro, 2, length), jnp.int32),
        vm((1, length), jnp.int32),
        vm((2, width), bf),
        vm((heads, lay.buckets), bf),
        vm((experts, width), bf),
        vm((width, ffn), bf),
        vm((ffn, width), bf),
        vm((ffn, width), bf),
        vm((width, ffn), bf),
        vm((3, cols, width), bf),
        vm((width, cols), bf),
        vm((3, width, cols), bf),
        vm((cols, width), bf),
        vm((micro, length, width), bf),
        vm((length, width), bf),
        vm((experts, micro, 2, length), jnp.int32),
        vm((slots, length), bf),
        vm((micro, pairs, length, 2 * length), f32),
        vm((micro, pairs, length, 2 * length), f32),
        vm((micro, length, width), bf),
        vm((3, micro, length, cols), bf),
        vm((micro, length, cols), bf),
        vm((length, width), bf),
        vm((length, width), bf),
        vm((length, width), f32),
        vm((length, width), bf),
        vm((experts, length), f32),
        vm((experts, length), f32),
        vm((experts, width), bf),
        vm((2 * pairs, length, length), f32),
        vm((experts, cap, width), bf),
        vm((experts, micro, cap, width), bf),
        vm((experts, cap, width), bf),
        vm((experts, micro, cap, width), bf),
        vm((experts, micro, cap, ffn), bf),
        vm((experts, micro, cap, ffn), bf),
        vm((micro, 2, cap, width), f32),
        vm((experts, cap, width), bf),
        vm((experts, cap, width), bf),
        vm((experts, cap, width), bf),
        vm((experts, cap, width), bf),
        vm((length, width), f32),
        vm((experts, micro, cap, experts), f32),
        vm((experts, micro, cap, 1), f32),
        vm((experts, micro, cap, width), bf),
        vm((micro, experts, 8, 128), f32),
        vm((experts, 8, 128), f32),
        vm((experts, 8, 128), f32),
        vm((experts, 8, 128), f32),
        vm((experts, micro, cap, ffn), bf),
        vm((experts, cap, width), bf),
        vm((experts, cap, width), bf),
        vm((experts, cap, width), bf),
        vm((experts, cap, width), bf),
        vm((length, width), f32),
        vm((micro, length, width), bf),
        vm((micro, length, cols), bf),
        vm((3, micro, length, cols), bf),
        vm((length, width), bf),
        vm((length, width), bf),
        vm((length, width), f32),
        vm((length, width), bf),
        vm((micro, experts, length, width), bf),
        vm((experts, micro, length, cols), bf),
        vm((micro, 3 * cols, length), bf),
        vm((experts, micro, 3 * cols // experts, length), bf),
        vm((width, length), bf),
        vm((experts, micro, width // experts, length), bf),
        vm((experts, 2 * experts, 128), f32),
        vm((experts, 2 * experts, 128), f32),
        vm((experts, 2 * experts, 128), f32),
        vm((experts, 2 * experts, 128), f32),
        vm((length, width), bf),
        vm((experts, shared_rows, width), bf),
        vm((experts - 1, shared_rows, width), bf),
        vm((4, cap, width), bf),
        vm((2, micro, 3 * cols // experts, length), bf),
        dma((12,)),
        dma((lay.sems[0],)),
        dma((lay.sems[1],)),
    ]
    whole = pl.BlockSpec(memory_space=pltpu.VMEM)
    anywhere = pl.BlockSpec(memory_space=pl.ANY)
    out_shape = (
        vm((micro, length, width // 2), f32),
        vm((micro, length, width // 2), f32),
        vm((2, width), f32),
        vm((experts, shared_rows, width), bf),
        vm((heads, 128), f32),
        vm((experts, width), f32),
        vm((width, ffn), bf),
        vm((ffn, width), bf),
    )
    results = pl.pallas_call(
        partial(layer_kernel, lay),
        out_shape=out_shape,
        in_specs=[anywhere] * 13,
        out_specs=[whole] * 8,
        scratch_shapes=scratch,
        name="two_sections",
        compiler_params=pltpu.CompilerParams(
            collective_id=0, has_side_effects=True, vmem_limit_bytes=56 * 1024 * 1024
        ),
    )(
        tokens[:, 0],
        cotangent[:, 0],
        segments[:, 0],
        pad_mask[:, 0],
        routes[:, 0].transpose(0, 2, 1),
        dist_bucket[None],
        norm_gains[0],
        qkv_weight[0].transpose(1, 0, 2),
        out_weight[0],
        rel_bias[0].T,
        router_weight[0].T,
        expert_up[0, 0],
        expert_down[0, 0],
    )
    section_out, input_grads, gains, bias, router, qkv, out, up, down = pl.pallas_call(
        widen_kernel,
        out_shape=(
            shape((micro, length, width // 2), f32),
            shape((micro, length, width // 2), f32),
            shape((2, width), f32),
            shape((heads, 1, lay.buckets), f32),
            shape((experts, width), f32),
            shape((3, width, cols), f32),
            shape((cols, width), f32),
            shape((width, ffn), f32),
            shape((ffn, width), f32),
        ),
        in_specs=[whole] * 8,
        out_specs=[anywhere] * 9,
        scratch_shapes=[
            vm((width, ffn), f32),
            vm((ffn, width), f32),
            vm((3, width, cols), f32),
            vm((cols, width), f32),
            vm((heads, 1, lay.buckets), f32),
            dma((21,)),
        ],
        name="widen",
        compiler_params=pltpu.CompilerParams(vmem_limit_bytes=40 * 1024 * 1024),
    )(*[pltpu.with_memory_space_constraint(result, pltpu.VMEM) for result in results])
    return (
        section_out[None, :, None],
        input_grads[None, :, None],
        gains[None],
        qkv.transpose(1, 0, 2)[None],
        out[None],
        bias.transpose(1, 2, 0),
        router.T[None],
        up[None, None],
        down[None, None],
    )


def fits_kernel(mesh):
    return mesh.shape["section"] == 2 and mesh.shape["tensor"] == 2 and mesh.shape["dp"] == 8


def solution(mesh):
    in_specs = (
        P(None, "dp", None, None),
        P(None, "dp", None, None),
        P(None, "dp", None),
        P(None, "dp", None),
        P(None, "dp", None, None),
        P(),
        P("section", None, None),
        P("section", None, None, "tensor"),
        P("section", "tensor", None),
        P("section", None, "tensor"),
        P("section", None, None),
        P("section", "dp", None, "tensor"),
        P("section", "dp", "tensor", None),
    )
    out_specs = (
        P("section", None, "dp", None, "tensor"),
        P("section", None, "dp", None, "tensor"),
        P("section", None, None),
        P("section", None, None, "tensor"),
        P("section", "tensor", None),
        P("section", None, "tensor"),
        P("section", None, None),
        P("section", "dp", None, "tensor"),
        P("section", "dp", "tensor", None),
    )
    body = fused_local if fits_kernel(mesh) else local
    return jax.shard_map(body, mesh=mesh, in_specs=in_specs, out_specs=out_specs, check_vma=False)
```

```python
from functools import partial

import jax
import jax.numpy as jnp
from jax import lax
from jax.experimental import pallas as pl
from jax.experimental.pallas import tpu as pltpu
from jax.sharding import PartitionSpec as P

norm_eps = 1e-06
masked_score = -1e30
highest = lax.Precision.HIGHEST


def shifted(block, axis, distance):
    devices = range(lax.axis_size(axis))
    route = [(i - distance, i) for i in devices if i - distance in devices]
    return lax.ppermute(block, axis, route)


def normalize(values, gain_row):
    scale_inv = lax.rsqrt(jnp.mean(values * values, axis=-1, keepdims=True) + norm_eps)
    return values * scale_inv * gain_row


def normalize_back(values, gain_row, upstream):
    scale_inv = lax.rsqrt(jnp.mean(values * values, axis=-1, keepdims=True) + norm_eps)
    normed = values * scale_inv
    gain_grad = jnp.sum(upstream * normed, axis=0)
    scaled = upstream * gain_row
    input_grad = scale_inv * (scaled - normed * jnp.mean(scaled * normed, axis=-1, keepdims=True))
    return (input_grad, gain_grad)


def send_rows(rows):
    return lax.all_to_all(rows, "dp", split_axis=0, concat_axis=0, tiled=True)


def sum_slots(partial_rows):
    return lax.psum(partial_rows, "tensor")


def score_context(segment_row, pad_row, dist_bucket, bucket_count):
    length = segment_row.shape[0]
    places = jnp.arange(length, dtype=jnp.int32)
    offsets = jnp.clip(places[:, None] - places[None, :], 0, length - 1)
    bucket_grid = jnp.take(dist_bucket, offsets)
    bucket_onehot = (
        bucket_grid[:, :, None] == jnp.arange(bucket_count, dtype=jnp.int32)[None, None, :]
    ).astype(jnp.float32)
    allowed = (places[None, :] <= places[:, None]) & (segment_row[:, None] == segment_row[None, :])
    allowed = allowed & ((pad_row[None, :] == 1) | (places[None, :] == places[:, None]))
    return (bucket_onehot, allowed)


def attention_front(inputs, context, weights):
    segment_row, pad_row, route_rows, dist_bucket = context
    gain_pair, qkv_weight, out_weight, bias_table, router_weight, upper_weight, lower_weight = (
        weights
    )
    length = inputs.shape[0]
    head_count = bias_table.shape[1]
    bucket_onehot, allowed = score_context(segment_row, pad_row, dist_bucket, bias_table.shape[0])
    normed_one = normalize(inputs, gain_pair[0]).astype(jnp.bfloat16)
    qkv_rows = jnp.einsum(
        "ld,dch->lch", normed_one, qkv_weight, preferred_element_type=jnp.float32
    ).astype(jnp.bfloat16)
    head_dim = qkv_rows.shape[2] // head_count
    queries = qkv_rows[:, 0].reshape(length, head_count, head_dim)
    keys_in = qkv_rows[:, 1].reshape(length, head_count, head_dim)
    values_in = qkv_rows[:, 2].reshape(length, head_count, head_dim)
    raw_scores = jnp.einsum("qhd,khd->hqk", queries, keys_in, preferred_element_type=jnp.float32)
    bias_grid = jnp.einsum(
        "qkb,bh->hqk", bucket_onehot, bias_table.astype(jnp.float32), precision=highest
    )
    logits = jnp.where(allowed[None], 0.125 * raw_scores + bias_grid, masked_score)
    exp_terms = jnp.exp(logits - jnp.max(logits, axis=-1, keepdims=True))
    attn_probs = exp_terms / jnp.sum(exp_terms, axis=-1, keepdims=True)
    mixed_rows = jnp.einsum(
        "hqk,khd->qhd",
        attn_probs.astype(jnp.bfloat16),
        values_in,
        preferred_element_type=jnp.float32,
    )
    mixed_rows = mixed_rows.reshape(length, -1).astype(jnp.bfloat16)
    return (normed_one, queries, keys_in, values_in, attn_probs, mixed_rows, bucket_onehot)


def slot_tables(route_rows, experts, capacity):
    flat_routes = route_rows.reshape(-1)
    route_hits = (flat_routes[:, None] == jnp.arange(experts, dtype=jnp.int32)[None, :]).astype(
        jnp.int32
    )
    earlier = jnp.cumsum(route_hits, axis=0) - route_hits
    position = jnp.sum(earlier * route_hits, axis=1)
    target = flat_routes * capacity + position
    slot_hits = (
        jnp.arange(experts * capacity, dtype=jnp.int32)[:, None] == target[None, :]
    ).astype(jnp.int32)
    source = jnp.sum(slot_hits * jnp.arange(target.shape[0], dtype=jnp.int32)[None, :], axis=1)
    filled = jnp.sum(slot_hits, axis=1) > 0
    return (target, source, filled, route_hits)


def route_gates(normed_two, router_weight, route_hits):
    length = normed_two.shape[0]
    logits = jnp.dot(normed_two, router_weight, preferred_element_type=jnp.float32)
    route_onehot = route_hits.reshape(length, 2, -1).astype(jnp.float32)
    chosen = jnp.einsum("le,lre->lr", logits, route_onehot, precision=highest)
    return (jax.nn.softmax(chosen, axis=-1), route_onehot)


def gather_back(back_slots, target, length):
    flat_slots = back_slots.reshape(-1, back_slots.shape[-1])
    return jnp.take(flat_slots, target, axis=0).reshape(length, 2, -1)


def forward_rest(inputs, front, context, weights):
    segment_row, pad_row, route_rows, dist_bucket = context
    gain_pair, qkv_weight, out_weight, bias_table, router_weight, upper_weight, lower_weight = (
        weights
    )
    mixed_rows = front[5]
    length, model_width = inputs.shape
    experts = router_weight.shape[1]
    capacity = max(2, 3 * length // experts)
    local_experts = upper_weight.shape[0]
    attn_out = lax.psum(
        jnp.dot(mixed_rows, out_weight, preferred_element_type=jnp.float32), "tensor"
    )
    middle = inputs + attn_out
    normed_two = normalize(middle, gain_pair[1]).astype(jnp.bfloat16)
    target, source, filled, route_hits = slot_tables(route_rows, experts, capacity)
    outgoing = jnp.where(
        filled[:, None], jnp.take(normed_two, source // 2, axis=0), jnp.zeros((), jnp.bfloat16)
    )
    outgoing = outgoing.reshape(experts, capacity, model_width)
    arrived = send_rows(outgoing)
    grouped = arrived.reshape(-1, local_experts, capacity, model_width)
    pre_act = jnp.einsum(
        "secd,edf->secf", grouped, upper_weight, preferred_element_type=jnp.float32
    )
    hidden = jax.nn.gelu(pre_act, approximate=False).astype(jnp.bfloat16)
    partial_out = jnp.einsum(
        "secf,efd->secd", hidden, lower_weight, preferred_element_type=jnp.float32
    )
    summed = sum_slots(partial_out)
    returned = summed.astype(jnp.bfloat16).reshape(arrived.shape[0], arrived.shape[1], -1)
    back_slots = send_rows(returned)
    gate_probs, route_onehot = route_gates(normed_two, router_weight, route_hits)
    back_rows = gather_back(back_slots, target, length)
    output = middle + jnp.sum(gate_probs[:, :, None] * back_rows.astype(jnp.float32), axis=1)
    return (output, (attn_out, arrived, back_slots, pre_act))


def backward_layer(inputs, upstream, context, weights, front, saved_state):
    segment_row, pad_row, route_rows, dist_bucket = context
    gain_pair, qkv_weight, out_weight, bias_table, router_weight, upper_weight, lower_weight = (
        weights
    )
    normed_one, queries, keys_in, values_in, attn_probs, mixed_rows, bucket_onehot = front
    attn_out, arrived_rows, back_slots, pre_rows = saved_state
    length, model_width = inputs.shape
    head_count = bias_table.shape[1]
    head_cols = qkv_weight.shape[2]
    experts = router_weight.shape[1]
    capacity = max(2, 3 * length // experts)
    local_experts = upper_weight.shape[0]
    middle = inputs + attn_out
    normed_two = normalize(middle, gain_pair[1]).astype(jnp.bfloat16)
    target, source, filled, route_hits = slot_tables(route_rows, experts, capacity)
    gate_probs, route_onehot = route_gates(normed_two, router_weight, route_hits)
    back_rows = gather_back(back_slots, target, length)
    gate_grad = jnp.sum(upstream[:, None, :] * back_rows.astype(jnp.float32), axis=-1)
    chosen_grad = gate_probs * (gate_grad - jnp.sum(gate_probs * gate_grad, axis=-1, keepdims=True))
    logit_grad = jnp.einsum("lr,lre->le", chosen_grad, route_onehot, precision=highest).astype(
        jnp.bfloat16
    )
    router_grad = jnp.dot(normed_two.T, logit_grad, preferred_element_type=jnp.float32)
    normed_two_grad = jnp.dot(logit_grad, router_weight.T, preferred_element_type=jnp.float32)
    route_grads = (
        (gate_probs[:, :, None] * upstream[:, None, :])
        .reshape(2 * length, model_width)
        .astype(jnp.bfloat16)
    )
    slot_grads = jnp.where(
        filled[:, None], jnp.take(route_grads, source, axis=0), jnp.zeros((), jnp.bfloat16)
    )
    arrived_grads = send_rows(slot_grads.reshape(experts, capacity, model_width))
    grouped = arrived_rows.reshape(-1, local_experts, capacity, model_width)
    grouped_grads = arrived_grads.reshape(-1, local_experts, capacity, model_width)
    hidden, gelu_pull = jax.vjp(partial(jax.nn.gelu, approximate=False), pre_rows)
    hidden_low = hidden.astype(jnp.bfloat16)
    down_grad = jnp.einsum(
        "secf,secd->efd", hidden_low, grouped_grads, preferred_element_type=jnp.float32
    )
    hidden_grad = jnp.einsum(
        "secd,efd->secf", grouped_grads, lower_weight, preferred_element_type=jnp.float32
    )
    pre_grad = gelu_pull(hidden_grad)[0].astype(jnp.bfloat16)
    up_grad = jnp.einsum("secd,secf->edf", grouped, pre_grad, preferred_element_type=jnp.float32)
    rows_grad = sum_slots(
        jnp.einsum("secf,edf->secd", pre_grad, upper_weight, preferred_element_type=jnp.float32)
    )
    sent_back = send_rows(
        rows_grad.astype(jnp.bfloat16).reshape(arrived_rows.shape[0], arrived_rows.shape[1], -1)
    )
    copy_grads = gather_back(sent_back, target, length).astype(jnp.float32)
    normed_two_grad = normed_two_grad + jnp.sum(copy_grads, axis=1)
    middle_part, gain_two = normalize_back(middle, gain_pair[1], normed_two_grad)
    middle_grad = upstream + middle_part
    attn_grad = middle_grad.astype(jnp.bfloat16)
    out_grad = jnp.dot(mixed_rows.T, attn_grad, preferred_element_type=jnp.float32)
    mixed_grad = jnp.dot(attn_grad, out_weight.T, preferred_element_type=jnp.float32).astype(
        jnp.bfloat16
    )
    mixed_grad = mixed_grad.reshape(length, head_count, -1)
    prob_grad = jnp.einsum(
        "qhd,khd->hqk", mixed_grad, values_in, preferred_element_type=jnp.float32
    )
    value_grad = jnp.einsum(
        "hqk,qhd->khd",
        attn_probs.astype(jnp.bfloat16),
        mixed_grad,
        preferred_element_type=jnp.float32,
    )
    score_grad = attn_probs * (prob_grad - jnp.sum(prob_grad * attn_probs, axis=-1, keepdims=True))
    table_grad = jnp.einsum("hqk,qkb->bh", score_grad, bucket_onehot, precision=highest)
    raw_grad = (0.125 * score_grad).astype(jnp.bfloat16)
    query_grad = jnp.einsum("hqk,khd->qhd", raw_grad, keys_in, preferred_element_type=jnp.float32)
    key_grad = jnp.einsum("hqk,qhd->khd", raw_grad, queries, preferred_element_type=jnp.float32)
    qkv_grad = (
        jnp.stack([query_grad, key_grad, value_grad], axis=1)
        .reshape(length, 3, head_cols)
        .astype(jnp.bfloat16)
    )
    qkv_weight_grad = jnp.einsum(
        "ld,lch->dch", normed_one, qkv_grad, preferred_element_type=jnp.float32
    )
    normed_one_grad = lax.psum(
        jnp.einsum("lch,dch->ld", qkv_grad, qkv_weight, preferred_element_type=jnp.float32),
        "tensor",
    )
    input_part, gain_one = normalize_back(inputs, gain_pair[0], normed_one_grad)
    input_grad = middle_grad + input_part
    gain_grads = jnp.stack([gain_one, gain_two])
    return (
        input_grad,
        (gain_grads, qkv_weight_grad, out_grad, table_grad, router_grad, up_grad, down_grad),
    )


def pick_context(segments, pad_mask, routes, dist_bucket, micro_slot):
    segment_row = lax.dynamic_index_in_dim(segments[:, 0], micro_slot, 0, False)
    pad_row = lax.dynamic_index_in_dim(pad_mask[:, 0], micro_slot, 0, False)
    route_rows = lax.dynamic_index_in_dim(routes[:, 0], micro_slot, 0, False)
    return (segment_row, pad_row, route_rows, dist_bucket)


def place_row(store_all, new_value, micro_slot, is_valid):
    current = lax.dynamic_index_in_dim(store_all, micro_slot, 0, False)
    return lax.dynamic_update_index_in_dim(
        store_all, jnp.where(is_valid, new_value, current), micro_slot, 0
    )


def pick_row(store_all, micro_slot):
    return lax.dynamic_index_in_dim(store_all, micro_slot, 0, False)


def mask_grad(grad_value, is_valid):
    return jnp.where(is_valid, grad_value, jnp.zeros((), grad_value.dtype))


def tensor_half(full_rows, tensor_id, half_width):
    return lax.dynamic_slice_in_dim(full_rows, tensor_id * half_width, half_width, 2)[None, :, None]


def local(
    tokens,
    cotangent,
    segments,
    pad_mask,
    routes,
    dist_bucket,
    norm_gains,
    qkv_weight,
    out_weight,
    rel_bias,
    router_weight,
    expert_up,
    expert_down,
):
    section_id = lax.axis_index("section")
    section_count = lax.axis_size("section")
    micro_count = tokens.shape[0]
    length = tokens.shape[2]
    model_width = tokens.shape[3]
    tick_count = micro_count + section_count - 1
    weights = (
        norm_gains[0].astype(jnp.float32),
        qkv_weight[0],
        out_weight[0],
        rel_bias[0],
        router_weight[0],
        expert_up[0],
        expert_down[0],
    )
    empty_rows = jnp.zeros((length, model_width), jnp.bfloat16)
    arriving = empty_rows
    kept_inputs = jnp.zeros((micro_count, length, model_width), jnp.bfloat16)
    section_out = jnp.zeros((micro_count, length, model_width), jnp.float32)
    for tick_index in range(tick_count):
        micro_index = tick_index - section_id
        is_valid = (micro_index >= 0) & (micro_index < micro_count)
        micro_slot = jnp.clip(micro_index, 0, micro_count - 1)
        own_rows = tokens[tick_index, 0] if tick_index < micro_count else empty_rows
        layer_in = jnp.where(section_id == 0, own_rows, arriving)
        context = pick_context(segments, pad_mask, routes, dist_bucket, micro_slot)
        inputs = layer_in.astype(jnp.float32)
        front = attention_front(inputs, context, weights)
        result, saved_state = forward_rest(inputs, front, context, weights)
        section_out = place_row(section_out, result, micro_slot, is_valid)
        kept_inputs = place_row(kept_inputs, layer_in, micro_slot, is_valid)
        arriving = shifted(result.astype(jnp.bfloat16), "section", 1)
    returning = empty_rows
    input_store = jnp.zeros((micro_count, length, model_width), jnp.float32)
    totals = None
    for tick_index in range(tick_count):
        micro_index = tick_index - (section_count - 1 - section_id)
        is_valid = (micro_index >= 0) & (micro_index < micro_count)
        micro_slot = jnp.clip(micro_index, 0, micro_count - 1)
        own_rows = cotangent[tick_index, 0] if tick_index < micro_count else empty_rows
        upstream = jnp.where(section_id == section_count - 1, own_rows, returning).astype(
            jnp.float32
        )
        inputs = pick_row(kept_inputs, micro_slot).astype(jnp.float32)
        context = pick_context(segments, pad_mask, routes, dist_bucket, micro_slot)
        front = attention_front(inputs, context, weights)
        saved_state = forward_rest(inputs, front, context, weights)[1]
        input_grad, grad_set = backward_layer(
            inputs, upstream, context, weights, front, saved_state
        )
        input_store = place_row(input_store, input_grad, micro_slot, is_valid)
        grad_set = jax.tree.map(partial(mask_grad, is_valid=is_valid), grad_set)
        totals = grad_set if totals is None else jax.tree.map(jnp.add, totals, grad_set)
        returning = shifted(input_grad.astype(jnp.bfloat16), "section", -1)
    shared = lax.psum((totals[0], totals[1], totals[2], totals[3], totals[4]), "dp")
    tensor_id = lax.axis_index("tensor")
    half_width = model_width // lax.axis_size("tensor")
    return (
        tensor_half(section_out, tensor_id, half_width),
        tensor_half(input_store, tensor_id, half_width),
        shared[0][None],
        shared[1][None],
        shared[2][None],
        shared[3][None],
        shared[4][None],
        totals[5][None],
        totals[6][None],
    )


def gelu_parts(values):
    share = 0.5 + 0.5 * lax.erf(values * 0.7071067811865476)
    return (values * share, share + values * (0.3989422804014327 * jnp.exp(-0.5 * values * values)))


def nn(left, right):
    return lax.dot_general(left, right, (((1,), (0,)), ((), ())), preferred_element_type=jnp.float32)


def nt(left, right):
    return lax.dot_general(left, right, (((1,), (1,)), ((), ())), preferred_element_type=jnp.float32)


def tn(left, right):
    return lax.dot_general(left, right, (((0,), (0,)), ((), ())), preferred_element_type=jnp.float32)


def split_low(values):
    high = values.astype(jnp.bfloat16)
    return (high, (values - high.astype(jnp.float32)).astype(jnp.bfloat16))


def inverse_rms(values):
    return lax.rsqrt(jnp.mean(values * values, axis=-1, keepdims=True) + norm_eps)


class Layout:
    pass


def layer_kernel(lay, *refs):
    (
        tok_ref, cot_ref, seg_hbm, pad_hbm, routes_hbm, dist_hbm, gains_hbm, qkvw_hbm, outw_hbm, relb_hbm, wr_hbm,
        up_ref, down_ref,
        secout_ref, ingrad_ref, ggain_ref, shared_ref, gbias_ref, grouter_ref, guv, gdv,
        seg_ref, pad_ref, routes_ref, dist_ref, gains_ref, relb_ref, wr_ref, upv, downv, upt, downt, qkvwt, outwt, qkvw_ref, outw_ref, xb, dyb, rr, place, bias_buf, probs_buf, no1, qkvb, mixed, att_send, att_recv, mid, ntb,
        gate_t, hit_t, wrp, score_sum, disp_x, xrows, disp_y, dyrows, hidden, dgelu, halves, eo_send, eo_recv, eob, eoret, out_own,
        other, gate_slots, og, gg_part, gg_other, gg_send, gg_recv, pg, cg_send, cg_recv, cgb, cgret, mgrad, ag, mg, qkvg,
        no_send, no_recv, ig_own, dy_send,
        no_all, mix_all, qgt, qt_all, agt, agt_all, small_send, small_in, small_all, small_sib,
        x_send, rs_buf, rs_in, relay_buf, relay_q,
        wsem, ss, rs,
    ) = refs
    bf = jnp.bfloat16
    f32 = jnp.float32
    micro, length, width = tok_ref.shape
    experts = lay.experts
    cap = lay.cap
    cols = outw_ref.shape[0]
    pairs = cols // 128
    ffn = up_ref.shape[1]
    slots = experts * cap
    half = width // 2
    s = lax.axis_index("section")
    d = lax.axis_index("dp")
    t = lax.axis_index("tensor")
    u = 1 - t
    sib = (s, d, u)
    across = (1 - s, d, t)
    bits = [lax.rem(d // bit, 2) for bit in (1, 2, 4)]

    def partner(flip):
        index = d
        for place, bit in enumerate((1, 2, 4)):
            index = index + (flip // bit) % 2 * (bit - 2 * bit * bits[place])
        return index

    peer = [partner(flip) for flip in (0, 4, 1, 6, 2, 5, 3, 7)]
    steps = range(1, experts)
    relayed = (5, 7)
    chunks = range(experts // 2)

    def pair(c):
        return pl.ds(2 * c, 2)

    def partner_at(k):
        c = k // 2
        return partner(c + (k % 2) * (4 + 2 * (c % 2) + c // 2 - c))


    def remote(src, dst, sem, device, k=0):
        return pltpu.make_async_remote_copy(
            src_ref=src,
            dst_ref=dst,
            send_sem=ss.at[sem[0]],
            recv_sem=rs.at[sem[1] + k],
            device_id=device,
            device_id_type=pl.DeviceIdType.MESH,
        )

    counter = [0, 0]

    def take(arrivals=1):
        pair_of = (counter[0], counter[1])
        counter[0] += 1
        counter[1] += arrivals
        return pair_of

    def all_sent(like, sem):
        remote(like, like, sem, sib).wait_send()

    def all_here(like, sem, k=0):
        remote(like, like, sem, sib, k).wait_recv()

    ring_hops = experts - 1
    sem_routes = take()
    sem_x = take()
    sem_relay = [take(len(relayed)) for _ in range(2)]
    sem_pass = [take(0) for _ in range(2)]
    sem_relay_q = take(len(relayed))
    sem_pass_q = take(0)
    sem_xf = take()
    sem_dy = take()
    sem_att = take()
    sem_eo = take(len(chunks))
    sem_cg = take(len(chunks))
    sem_ag = take()
    sem_no = take()
    sem_so = take()
    sem_ig = take()
    sem_dx = take(len(chunks))
    sem_dxf = take(len(chunks))
    sem_ddy = take(len(chunks))
    sem_ddyf = take(len(chunks))
    sem_re = take()
    sem_rc = take()
    sem_gg = take()
    sem_gg_core = take(len(chunks))
    sem_qgt = take(experts)
    sem_agt = take()
    sem_agtf = take()
    sem_small = take()
    sem_back = take()
    sem_sums = take()
    sem_noall = take()
    sem_ring_no = take(2 * ring_hops)
    sem_ring_mix = take(2 * ring_hops)
    sem_ring_sum = (take(0)[0], sem_ring_no[1])
    sem_ring_out = take(4 * ring_hops)
    assert tuple(counter) == lay.sems

    def block(index, rows):
        return pl.ds(pl.multiple_of(index * rows, rows), rows)

    place_y = lax.rem(d, 2)
    place_z = d // 2
    ring_at = place_z + place_y * (experts - 1 - 2 * place_z)

    def ring_device(position):
        p = lax.rem(position + 2 * experts, experts)
        return 2 * p + (p // (experts // 2)) * (2 * experts - 1 - 4 * p)

    def hops(number, direction):
        return experts // 2 - (number % 2 == (direction > 0))

    def hop_index(number, direction, k):
        return number * ring_hops + k + (0 if direction > 0 else hops(number, 1))

    def lines_of(amount):
        return [(number, direction) for number in range(amount) for direction in (1, -1)]

    def ring_gather(parts, at_half=None):
        def hop(number, direction, k):
            view, sem, first = parts[number]
            held = view(ring_device(ring_at - direction * k))
            index = hop_index(number, direction, k) - first * ring_hops
            return remote(held, held, sem, (s, ring_device(ring_at + direction), t), index)

        lines = lines_of(len(parts))
        for line in lines:
            hop(*line, 0).start()

        def one(k, carry):
            for line in lines:
                hop(*line, k - 1).wait_recv()
                hop(*line, k).start()
            return carry

        short = experts // 2 - 1
        lax.fori_loop(1, short, one, 0)
        if at_half is not None:
            at_half()
        for line in lines:
            hop(*line, short - 1).wait_recv()
            if hops(*line) > short:
                hop(*line, short).start()
        for line in lines:
            if hops(*line) > short:
                hop(*line, short).wait_recv()

    small_loads = [
        pltpu.make_async_copy(src, dst, wsem.at[5 + i])
        for i, (src, dst) in enumerate(
            (
                (routes_hbm, routes_ref),
                (wr_hbm, wr_ref),
                (seg_hbm, seg_ref),
                (pad_hbm, pad_ref),
                (dist_hbm, dist_ref),
                (gains_hbm, gains_ref),
                (relb_hbm, relb_ref),
            )
        )
    ]
    for copy in small_loads:
        copy.start()
    load_up = pltpu.make_async_copy(up_ref, upv, wsem.at[0])
    load_down = pltpu.make_async_copy(down_ref, downv, wsem.at[1])
    load_qkvw = pltpu.make_async_copy(qkvw_hbm, qkvw_ref, wsem.at[2])
    load_outw = pltpu.make_async_copy(outw_hbm, outw_ref, wsem.at[3])
    load_tok = pltpu.make_async_copy(tok_ref, xb, wsem.at[4])
    load_cot = pltpu.make_async_copy(cot_ref.at[t], dyb, wsem.at[4])

    @pl.when(s == 0)
    def _():
        load_tok.start()

    @pl.when(s == 1)
    def _():
        load_cot.start()

    load_qkvw.start()
    load_outw.start()
    load_up.start()
    load_down.start()

    barrier = pltpu.get_barrier_semaphore()
    for k in steps:
        pl.semaphore_signal(barrier, inc=1, device_id=(s, peer[k], t), device_id_type=pl.DeviceIdType.MESH)
    pl.semaphore_signal(barrier, inc=1, device_id=sib, device_id_type=pl.DeviceIdType.MESH)
    for k in (0,) + relayed:
        pl.semaphore_signal(barrier, inc=1, device_id=(1 - s, peer[k], t), device_id_type=pl.DeviceIdType.MESH)
    pl.semaphore_wait(barrier, experts + 1 + len(relayed))

    for copy in small_loads:
        copy.wait()

    for k in steps:
        remote(routes_ref, rr.at[k], sem_routes, (s, peer[k], t)).start()
    rr[0] = routes_ref[...]

    lanes8 = lax.broadcasted_iota(jnp.int32, (experts, length), 0)
    row_at = lax.broadcasted_iota(jnp.int32, (length, length), 0)
    col_at = lax.broadcasted_iota(jnp.int32, (length, length), 1)
    before = (row_at < col_at).astype(bf)
    slot_at = lax.broadcasted_iota(jnp.int32, (cap, length), 0).astype(f32)

    expert_of = jnp.zeros((experts, length), jnp.int32)
    for k in range(experts):
        expert_of = jnp.where(lanes8 == k, peer[k], expert_of)
    turn = (lax.broadcasted_iota(jnp.int32, (experts, experts), 1) == expert_of[:, 0:experts]).astype(f32).astype(bf)
    wrp[...] = nn(turn, wr_ref[...]).astype(bf)
    own_routes = routes_ref[t]
    hits = (expert_of == own_routes[0:1, :]) | (expert_of == own_routes[1:2, :])
    hit_f = hits.astype(f32)
    hit_t[...] = hit_f
    spot = jnp.where(hits, nn(hit_f.astype(bf), before), -1.0)
    for e in range(experts):
        place[e * cap : (e + 1) * cap, :] = (slot_at == spot[e : e + 1, :]).astype(f32).astype(bf)

    def to_relay(source, k, leg):
        i = relayed.index(k)
        return remote(source, relay_buf.at[leg * len(relayed) + i], sem_relay[leg], across, i)

    def relay(landing, sem, leg):
        for i, k in enumerate(relayed):
            held = relay_buf.at[leg * len(relayed) + i]
            all_here(held, sem_relay[leg], i)
            through = (sem_pass[leg][0], sem[1] + k // 2)
            remote(held, landing.at[k, t], through, (0, peer[k], t)).start()

    def dispatch(rows, send, landing, sem, sem_fwd, leg=None, both=False):
        send[...] = nn(place[...], rows).astype(bf).reshape(send.shape)

        def direct(k):
            remote(send.at[k], landing.at[k, t], sem, (s, peer[k], t), k // 2).start()

        def start_relayed():
            for k in relayed:
                to_relay(send.at[k], k, leg).start()

        def start_direct():
            for k in relayed:
                direct(k)

        direct(1)
        if both:
            pl.when(s == 0)(start_relayed)
        elif leg is not None:
            start_relayed()
        for k in steps[1:]:
            if k not in relayed:
                direct(k)
        if both:
            pl.when(s == 1)(start_direct)
        elif leg is None:
            start_direct()
        landing[0, t] = send[0]

        def arrive(c):
            held = landing.at[pair(c), t]
            all_here(landing.at[1, t] if isinstance(c, int) and c == 0 else held, sem, c)
            remote(held, held, sem_fwd, sib, c).start()

        def joined(c):
            all_here(landing.at[pair(c), t], sem_fwd, c)

        def drain(zero):
            all_sent(send, sem_fwd)
            if zero:
                all_sent(send.at[0 : experts - 1 - len(relayed)], sem)
                all_sent(send.at[0 : len(relayed)], sem_relay[leg])
            else:
                all_sent(send.at[1:experts], sem)

        return arrive, joined, drain

    def stream(dispatched, first, second, finish_chunk, eager, zero):
        arrive, joined, drain = dispatched
        last = len(chunks) - 1
        arrive(0)
        joined(0)

        def one(c, carry):
            first(c)
            if eager:
                pl.when(c > 0)(lambda: finish_chunk(c - 1))
                pl.when(c < last)(lambda: arrive(c + 1))
                second(c)
            else:
                second(c)

                @pl.when(c < last)
                def _():
                    arrive(c + 1)
                    finish_chunk(c)


            @pl.when(c < last)
            def _():
                joined(c + 1)

            return carry

        lax.fori_loop(0, len(chunks), one, 0)
        finish_chunk(last)
        drain(zero)

    def turn_weights():
        upt[...] = jnp.transpose(upv[...])
        downt[...] = jnp.transpose(downv[...])
        for c in range(3):
            qkvwt[c] = jnp.transpose(qkvw_ref[c])
        outwt[...] = jnp.transpose(outw_ref[...])

    def other_experts():
        all_here(rr.at[1:experts], sem_routes)

        def one(i, carry):
            q = i // micro
            m = i % micro
            pair = rr[q, m]
            first = pair[0:1, :] == d
            mine = first | (pair[1:2, :] == d)
            mine_f = jnp.broadcast_to(mine.astype(f32), (experts, length))
            spots = jnp.where(mine_f > 0.0, nn(mine_f.astype(bf), before), -1.0)
            where_slot = (slot_at == spots[0:1, :]).astype(f32).astype(bf)
            partner = jnp.where(first, pair[1:2, :], pair[0:1, :])
            partner_hot = (lanes8 == partner).astype(f32).astype(bf)
            other[q, m] = nt(where_slot, partner_hot)
            return carry

        lax.fori_loop(0, experts * micro, one, 0)

    @pl.when(s == 0)
    def _():
        load_tok.wait()
        load_qkvw.wait()
        load_outw.wait()

    @pl.when(s == 1)
    def _():
        load_cot.wait()
        relay(xrows, sem_dx, 0)
        load_up.wait()
        load_down.wait()
        load_qkvw.wait()
        load_outw.wait()
        turn_weights()
        other_experts()
        arrive, joined, drain = dispatch(dyb[...], disp_y, dyrows, sem_ddy, sem_ddyf)

        def pass_one(c, carry):
            arrive(c)
            return carry

        def join_one(c, carry):
            joined(c)
            return carry

        arrive(0)
        lax.fori_loop(1, len(chunks), pass_one, 0)
        lax.fori_loop(0, len(chunks), join_one, 0)
        drain(False)

    dist_rows = (
        lax.broadcasted_iota(jnp.int32, (lay.buckets, length), 0) == dist_ref[...]
    ).astype(f32).astype(bf)
    bias_rows = nn(relb_ref[...], dist_rows).astype(bf)
    mirror = ((row_at + col_at == length) | (row_at + col_at == 0)).astype(f32).astype(bf)
    bias_back = nn(bias_rows, mirror)
    for m in range(micro):
        seg_rows = jnp.broadcast_to(seg_ref[m : m + 1, :].astype(f32), (length, length))
        pads = jnp.broadcast_to(pad_ref[m : m + 1, :], (length, length))
        allowed = (col_at <= row_at) & (seg_rows == jnp.transpose(seg_rows))
        allowed = allowed & ((pads == 1) | (col_at == row_at))
        for p in range(pairs):
            for h in range(2):
                head = 2 * p + h
                grid = pltpu.roll(
                    jnp.broadcast_to(bias_back[head : head + 1, :], (length, length)), 0, 1, stride=1, stride_axis=0
                )
                bias_buf[m, p, :, h * length : (h + 1) * length] = jnp.where(allowed, grid, masked_score)

    x_copy = remote(x_send, xb.at[t], sem_x, across)
    dy_copy = remote(dy_send, dyb, sem_dy, across)
    x_forward = remote(xb.at[t], xb.at[t], sem_xf, sib)

    def spread_gates(gates_ref):
        return jnp.concatenate(
            [
                jnp.broadcast_to(gates_ref[e : e + 1, :], (cap, length)) * place[e * cap : (e + 1) * cap, :].astype(f32)
                for e in range(experts)
            ],
            axis=0,
        ).astype(bf)

    @pl.when(s == 1)
    def _():
        x_copy.wait_recv()
        x_forward.start()

    gain_one = gains_ref[0:1, :].astype(f32)
    gain_two = gains_ref[1:2, :].astype(f32)
    low_lanes = lax.broadcasted_iota(jnp.int32, (length, 128), 1) < 64

    def both_heads(pair_block):
        zero = jnp.zeros((), bf)
        return jnp.concatenate(
            [jnp.where(low_lanes, pair_block, zero), jnp.where(low_lanes, zero, pair_block)], axis=0
        )

    def attend(m):
        x_rows = xb[m].astype(f32)
        no1[m] = (x_rows * inverse_rms(x_rows) * gain_one).astype(bf)
        for c in range(3):
            qkvb[c, m] = nn(no1[m], qkvw_ref[c]).astype(bf)
        for p in range(pairs):
            at = slice(p * 128, (p + 1) * 128)
            scores = 0.125 * nt(qkvb[0, m, :, at], both_heads(qkvb[1, m, :, at])) + bias_buf[m, p]
            for h in range(2):
                part = scores[:, h * length : (h + 1) * length]
                terms = jnp.exp(part - jnp.max(part, axis=-1, keepdims=True))
                probs_buf[m, p, :, h * length : (h + 1) * length] = terms * (
                    1.0 / jnp.sum(terms, axis=-1, keepdims=True)
                )
            mixed[m, :, at] = nn(probs_buf[m, p].astype(bf), both_heads(qkvb[2, m, :, at])).astype(bf)

    att_copy = remote(att_send, att_recv, sem_att, sib)

    def project_other():
        att_send[...] = nn(mixed[u], outw_ref[...]).astype(bf)
        att_copy.start()

    begin = u + s * (t - u)

    attend(begin)
    pl.when(s == 0)(project_other)

    @pl.when(s == 1)
    def _():
        x_forward.wait()

    attend(1 - begin)

    @pl.when(s == 1)
    def _():
        project_other()

    part_own = nn(mixed[t], outw_ref[...])
    att_copy.wait()
    middle = xb[t].astype(f32) + part_own + att_recv[...].astype(f32)
    mid[...] = middle
    ntb[...] = (middle * inverse_rms(middle) * gain_two).astype(bf)

    arrivals = dispatch(ntb[...], disp_x, xrows, sem_dx, sem_dxf, 0, True)
    logits_t = jnp.where(hit_t[...] > 0.0, nt(wrp[...], ntb[...]), masked_score)
    terms = jnp.exp(logits_t - jnp.max(logits_t, axis=0, keepdims=True))
    gate_t[...] = terms / jnp.sum(terms, axis=0, keepdims=True)
    rows_of = 2 * micro * cap

    def flat(ref, chunk):
        return ref[chunk].reshape(rows_of, ref.shape[-1])

    def front_chunk(c):
        value, slope = gelu_parts(nn(flat(xrows, pair(c)), upv[...]))
        hidden[pair(c)] = value.astype(bf).reshape(2, micro, cap, ffn)
        dgelu[pair(c)] = slope.astype(bf).reshape(2, micro, cap, ffn)

    def split_sum(c, total, send, recv, base):
        for m in range(micro):
            halves[m] = total.reshape(2, micro, cap, width)[:, m]
        send[pair(c)] = halves[u].astype(bf)
        remote(send.at[pair(c)], recv.at[pair(c)], base, sib, c).start()

    def hand_back(c, send, recv, base, total, landing, base_back):
        all_here(recv.at[pair(c)], base, c)
        total[pair(c)] = (halves[t] + recv[pair(c)].astype(f32)).astype(bf)

        def give(k):
            remote(total.at[k], landing.at[k], base_back, (s, partner_at(k), t)).start()

        def keep():
            landing[0] = total[0]

        if isinstance(c, int):
            give(2 * c)
        else:
            pl.when(c == 0)(keep)
            pl.when(c > 0)(lambda: give(2 * c))
        give(2 * c + 1)

    def wait_back(total, landing, sem):
        all_here(landing.at[1:experts], sem)
        all_sent(total.at[1:experts], sem)

    def rows_chunk(c):
        split_sum(c, nn(flat(hidden, pair(c)), downv[...]), eo_send, eo_recv, sem_eo)

    def rows_finish(c):
        hand_back(c, eo_send, eo_recv, sem_eo, eob, eoret, sem_re)

    mine_hot = (lax.broadcasted_iota(jnp.int32, (rows_of, experts), 1) == d).astype(f32)

    ones = jnp.ones((8, ffn), bf)
    gg_part[...] = jnp.zeros_like(gg_part)

    def gate_chunk(c):
        slot_logits = nt(flat(xrows, pair(c)), wr_ref[...])
        own_logit = jnp.sum(slot_logits * mine_hot, axis=-1, keepdims=True)
        other_logit = jnp.sum(slot_logits * flat(other, pair(c)), axis=-1, keepdims=True)
        gate = 1.0 / (1.0 + jnp.exp(other_logit - own_logit))
        gate_slots[pair(c)] = gate.reshape(2, micro, cap, 1)

    def slope_chunk(c):
        dy_flat = flat(dyrows, pair(c))
        gate = flat(gate_slots, pair(c))
        grad = nn(dy_flat, downt[...])
        pg[pair(c)] = (grad * gate * flat(dgelu, pair(c)).astype(f32)).astype(bf).reshape(2, micro, cap, ffn)
        product = (grad * flat(hidden, pair(c)).astype(f32)).astype(bf)
        for i in range(2):
            for m in range(micro):
                at = (i * micro + m) * cap
                gg_part[m, 2 * c + i, :, 0:cap] = nt(ones, product[at : at + cap])

    def back_chunk(c):
        remote(gg_part.at[u, pair(c)], gg_other.at[pair(c)], sem_gg_core, sib, c).start()
        split_sum(c, nn(flat(pg, pair(c)), upt[...]), cg_send, cg_recv, sem_cg)

    def both_chunk(c):
        front_chunk(c)
        gate_chunk(c)
        slope_chunk(c)

    def back_finish(c):
        hand_back(c, cg_send, cg_recv, sem_cg, cgb, cgret, sem_rc)
        all_here(gg_other.at[pair(c)], sem_gg_core, c)
        gg_send[pair(c)] = gg_part[t, pair(c)] + gg_other[pair(c)]

        def give(k):
            remote(gg_send.at[k], gg_recv.at[k], sem_gg, (s, partner_at(k), t)).start()

        def keep():
            gg_recv[0] = gg_send[0]

        if isinstance(c, int):
            give(2 * c)
        else:
            pl.when(c == 0)(keep)
            pl.when(c > 0)(lambda: give(2 * c))
        give(2 * c + 1)

    def hidden_of(m):
        return jnp.concatenate([hidden[k, m] for k in range(experts)], axis=0)

    def expert_rows():
        eo_send[...] = nn(hidden_of(u), downv[...]).astype(bf).reshape(eo_send.shape)
        eo_copy = remote(eo_send, eo_recv, sem_eo, sib)
        eo_copy.start()
        total = nn(hidden_of(t), downv[...])
        eo_copy.wait_recv()
        eob[...] = (total + eo_recv[...].astype(f32).reshape(slots, width)).astype(bf).reshape(eob.shape)

    def send_back(source, landing, base):
        for k in steps:
            remote(source.at[k], landing.at[k], base, (s, peer[k], t)).start()
        landing[0] = source[0]

    def layer_output():
        result = mid[...] + tn(spread_gates(gate_t), eoret[...].reshape(slots, width))
        out_own[...] = result
        return result

    def own_half():
        return pl.ds(pl.multiple_of(t * half, half), half)

    def other_half():
        return pl.ds(pl.multiple_of(u * half, half), half)

    def hand_out(rows_ref, out_ref, index):
        copy = remote(rows_ref.at[:, other_half()], out_ref.at[t], index, sib)
        copy.start()
        out_ref[t] = rows_ref[:, own_half()]
        copy.wait()

    def gather_factors():
        no_all[t, d] = no1[t]
        mix_all[d] = mixed[...]
        ring_gather(
            [
                (lambda q: no_all.at[t, q, 0 : length // 2], sem_ring_no, 0),
                (lambda q: no_all.at[t, q, length // 2 : length], sem_ring_no, 0),
                (lambda q: mix_all.at[q, 0], sem_ring_mix, 2),
                (lambda q: mix_all.at[q, 1], sem_ring_mix, 2),
            ]
        )
        all_sent(no_all.at[t, 1:experts], sem_ring_no)
        all_sent(mix_all.at[1:experts], sem_ring_mix)
        copy = remote(no_all.at[t], no_all.at[t], sem_noall, sib)
        copy.start()
        copy.wait()

    @pl.when(s == 0)
    def _():
        load_up.wait()
        load_down.wait()
        stream(arrivals, front_chunk, rows_chunk, rows_finish, True, True)
        wait_back(eob, eoret, sem_re)
        x_send[...] = layer_output().astype(bf)
        x_copy.start()
        hand_out(out_own, secout_ref, sem_so)
        turn_weights()
        other_experts()

        def gate_one(c, carry):
            gate_chunk(c)
            return carry

        lax.fori_loop(0, len(chunks), gate_one, 0)
        gather_factors()
        x_copy.wait_send()
        dy_copy.wait_recv()
        arrivals_y = dispatch(dyb[...], disp_y, dyrows, sem_ddy, sem_ddyf, 1)
        stream(arrivals_y, slope_chunk, back_chunk, back_finish, True, True)

    @pl.when(s == 1)
    def _():
        stream(arrivals, both_chunk, back_chunk, back_finish, True, False)
        expert_rows()

    wait_back(gg_send, gg_recv, sem_gg)
    wait_back(cgb, cgret, sem_rc)

    @pl.when(s == 1)
    def _():
        send_back(eob, eoret, sem_re)


    gg_rows = []
    for e in range(experts):
        high, low = split_low(gg_recv[e][:, 0:cap])
        spot_rows = place[e * cap : (e + 1) * cap, :]
        gg_rows.append((nn(high, spot_rows) + nn(low, spot_rows))[0:1, :])
    gate_grad = jnp.concatenate(gg_rows, axis=0)
    gates = gate_t[...]
    logit_grad = (gates * (gate_grad - jnp.sum(gates * gate_grad, axis=0, keepdims=True))).astype(bf)
    two_grad = tn(logit_grad, wrp[...]) + tn(place[...], cgret[...].reshape(slots, width))
    dy = dyb[...].astype(f32)
    middle = mid[...]
    scale = inverse_rms(middle)
    normed = middle * scale
    scaled = two_grad * gain_two
    middle_grad = dy + scale * (scaled - normed * jnp.mean(scaled * normed, axis=-1, keepdims=True))
    mgrad[...] = middle_grad
    ag[t] = middle_grad.astype(bf)
    ag_copy = remote(ag.at[t], ag.at[t], sem_ag, sib)
    ag_copy.start()

    agt_rows = width // experts
    agt_own = remote(agt.at[block(d, agt_rows)], agt_all.at[d, t], sem_agtf, sib)

    @pl.when(s == 0)
    def _():
        agt[...] = jnp.transpose(ag[t])
        for k in reversed(steps):
            remote(agt.at[block(peer[k], agt_rows)], agt_all.at[d, t], sem_agt, (s, peer[k], t)).start()
        agt_all[d, t] = agt[block(d, agt_rows), :]
        agt_own.start()

    two_normed = normed
    groups = width // 128
    qgt_rows = 3 * cols // experts

    def attend_back(m, i):
        mg[m] = nn(ag[m], outwt[...]).astype(bf)
        for p in range(pairs):
            at = slice(p * 128, (p + 1) * 128)
            mg_pair = mg[m, :, at]
            probs = probs_buf[m, p]
            keys2 = both_heads(qkvb[1, m, :, at])
            queries2 = both_heads(qkvb[0, m, :, at])
            mg2 = both_heads(mg_pair)
            prob_grad = nt(mg_pair, both_heads(qkvb[2, m, :, at]))
            raws = []
            key_grad = jnp.zeros((length, 128), f32)
            value_grad = jnp.zeros((length, 128), f32)
            for h in range(2):
                lane = slice(h * length, (h + 1) * length)
                part = probs[:, lane]
                step = prob_grad[:, lane]
                score_grad = part * (step - jnp.sum(part * step, axis=-1, keepdims=True))
                score_sum[2 * p + h] += score_grad
                raw = (0.125 * score_grad).astype(bf)
                raws.append(raw)
                key_grad = key_grad + tn(raw, queries2[h * length : (h + 1) * length])
                value_grad = value_grad + tn(part.astype(bf), mg2[h * length : (h + 1) * length])
            query_grad = nn(jnp.concatenate(raws, axis=1), keys2)
            for c, grad in enumerate((query_grad, key_grad, value_grad)):
                qkvg[c, m, :, at] = grad.astype(bf)

        @pl.when(s == 0)
        def _():
            for c in range(3):
                qgt[i, c * cols : (c + 1) * cols, :] = jnp.transpose(qkvg[c, m])
            for k in reversed([k for k in steps if k not in relayed]):
                rows = block(peer[k], qgt_rows)
                remote(qgt.at[i, rows], qt_all.at[d, i], sem_qgt, (s, peer[k], t), k).start()
            qt_all[d, i] = qgt[i, block(d, qgt_rows), :]

    score_sum[...] = jnp.zeros_like(score_sum)

    attend_back(t, 0)
    ag_copy.wait()
    attend_back(u, 1)

    def relay_q_copy(i, k):
        return remote(qgt.at[:, block(peer[k], qgt_rows)], relay_q.at[i], sem_relay_q, across, i)

    @pl.when(s == 0)
    def _():
        for i, k in enumerate(relayed):
            relay_q_copy(i, k).start()


    def project_back(m):
        total = nn(qkvg[0, m], qkvwt[0])
        for c in range(1, 3):
            total = total + nn(qkvg[c, m], qkvwt[c])
        return total

    no_send[...] = project_back(u).astype(bf)
    no_copy = remote(no_send, no_recv, sem_no, sib)
    no_copy.start()
    one_grad = project_back(t)
    no_copy.wait()
    one_grad = one_grad + no_recv[...].astype(f32)
    x_rows = xb[t].astype(f32)
    scale = inverse_rms(x_rows)
    normed = x_rows * scale
    scaled = one_grad * gain_one
    input_grad = mgrad[...] + scale * (scaled - normed * jnp.mean(scaled * normed, axis=-1, keepdims=True))
    dy_send[...] = input_grad.astype(bf)

    @pl.when(s == 1)
    def _():
        dy_copy.start()

    ig_own[...] = input_grad
    gain_one_grad = jnp.sum(one_grad * normed, axis=0, keepdims=True)
    hand_out(ig_own, ingrad_ref, sem_ig)

    router_grad = nn(tn(turn, logit_grad).astype(bf), ntb[...])
    gain_two_grad = jnp.sum(two_grad * two_normed, axis=0, keepdims=True)
    small_send[...] = jnp.zeros_like(small_send)
    for g in range(groups):
        small_send[g, 0:experts, :] = router_grad[:, g * 128 : (g + 1) * 128]
        small_send[g, experts + 1 : experts + 2, :] = gain_two_grad[:, g * 128 : (g + 1) * 128]
    sums = []
    for head in range(2 * pairs):
        high, low = split_low(score_sum[head])
        turned = pltpu.roll(nn(high, mirror) + nn(low, mirror), 0, 1, stride=1, stride_axis=0)
        sums.append(jnp.sum(turned, axis=0, keepdims=True))
    high, low = split_low(jnp.concatenate(sums, axis=0))
    small_send[groups, 0 : 2 * pairs, 0 : lay.buckets] = nt(high, dist_rows) + nt(low, dist_rows)
    for g in range(groups):
        small_send[g, experts : experts + 1, :] = gain_one_grad[:, g * 128 : (g + 1) * 128]
    for k in steps:
        remote(small_send.at[peer[k]], small_in.at[k], sem_small, (s, peer[k], t)).start()
    small_in[0] = small_send[d]

    wide = lay.wide
    every = micro * slots

    for k in range(experts):
        og[k] = (dyrows[k].astype(f32) * gate_slots[k]).astype(bf)

    def expert_grads(n, carry):
        at = pl.ds(pl.multiple_of(n * wide, wide), wide)
        guv[:, at] = tn(xrows[...].reshape(every, width), pg[:, :, :, at].reshape(every, wide)).astype(bf)
        gdv[at, :] = tn(hidden[:, :, :, at].reshape(every, wide), og[...].reshape(every, width)).astype(bf)
        return carry

    lax.fori_loop(0, ffn // wide, expert_grads, 0)

    qkv_rows = 3 * cols // experts
    share = shared_ref.shape[1] // 4
    parts = [slice(c * share, (c + 1) * share) for c in range(4)]

    def pack_out(total):
        half_rows = agt_rows // 2
        return jnp.concatenate([total[..., 0:half_rows, :], total[..., half_rows:, :]], axis=-1).astype(bf)

    @pl.when(s == 0)
    def _():
        all_here(agt_all.at[1:experts, 0], sem_agt)
        for k in steps:
            held = agt_all.at[peer[k], t]
            remote(held, held, sem_agtf, sib).start()
        all_here(agt_all.at[:, 0], sem_agtf)
        all_sent(agt_all.at[1:experts, 0], sem_agt)
        all_sent(agt_all.at[:, 0], sem_agtf)
        total = jnp.zeros((agt_rows, cols), f32)
        for q in range(experts):
            for m in range(micro):
                total = total + nn(agt_all[q, m], mix_all[q, m])
        shared_ref[d, qkv_rows:, :] = pack_out(total)

        def qkv_slice(q):
            rows = jnp.concatenate([qt_all[q, 0], qt_all[q, 1]], axis=1)
            return nn(rows, jnp.concatenate([no_all[t, q], no_all[u, q]], axis=0))

        total = qkv_slice(d)
        for k in [k for k in reversed(steps) if k not in relayed] + list(relayed):
            all_here(qt_all.at[0], sem_qgt, k)
            total = total + qkv_slice(peer[k])
        all_sent(qt_all.at[0 : experts - 1 - len(relayed)], sem_qgt)
        all_sent(relay_q, sem_relay_q)
        shared_ref[d, 0:qkv_rows, :] = total.astype(bf)

    @pl.when(s == 1)
    def _():
        normed_rows = no1[...].reshape(micro * length, width)
        own = jnp.concatenate([tn(qkvg[c].reshape(micro * length, cols), normed_rows) for c in range(3)], axis=0)
        rs_buf[:, 0:qkv_rows, :] = own.astype(bf).reshape(experts, qkv_rows, width)
        own = tn(ag[...].reshape(micro * length, width), mixed[...].reshape(micro * length, cols))
        rs_buf[:, qkv_rows:, :] = pack_out(own.reshape(experts, agt_rows, cols))

        relay(dyrows, sem_ddy, 1)

        def owner_at(number, direction, k):
            return ring_device(ring_at + direction * (hops(number, direction) - k))

        def hop(number, direction, k):
            index = hop_index(number, direction, k)
            return remote(
                rs_buf.at[owner_at(number, direction, k), parts[number]],
                rs_in.at[index % ring_hops, parts[number]],
                sem_ring_sum,
                (s, ring_device(ring_at + direction), t),
                index,
            )

        lines = lines_of(len(parts))
        for k in range(experts // 2):
            for line in lines:
                if k < hops(*line):
                    if k > 0:
                        rows = parts[line[0]]
                        owner = owner_at(*line, k)
                        hop(*line, k - 1).wait_recv()
                        came = rs_in[hop_index(*line, k - 1) % ring_hops, rows, :].astype(f32)
                        rs_buf[owner, rows, :] = (rs_buf[owner, rows, :].astype(f32) + came).astype(bf)
                    hop(*line, k).start()
        for number, rows in enumerate(parts):
            total = rs_buf[d, rows, :].astype(f32)
            for direction in (1, -1):
                last = hops(number, direction) - 1
                hop(number, direction, last).wait_recv()
                total = total + rs_in[hop_index(number, direction, last) % ring_hops, rows, :].astype(f32)
            shared_ref[d, rows, :] = total.astype(bf)
        for i, k in enumerate(relayed):
            all_here(relay_q.at[i], sem_relay_q, i)
            remote(relay_q.at[i], qt_all.at[d], (sem_pass_q[0], sem_qgt[1] + k), (0, peer[k], t)).start()

    all_here(small_in.at[1:experts], sem_small)
    small_total = small_in[0]
    for k in steps:
        small_total = small_total + small_in[k]
    small_all[d] = small_total
    for k in steps:
        remote(small_all.at[d], small_all.at[d], sem_back, (s, peer[k], t)).start()

    sums_copy = remote(small_all, small_sib, sem_sums, sib)

    def pass_sums():
        all_here(small_all.at[1:experts], sem_back)
        sums_copy.start()


    streams = [
        (lambda q, rows=rows: shared_ref.at[q, rows], sem_ring_out, 0) for rows in parts
    ]

    ring_gather(streams, pass_sums)
    sums_copy.wait_recv()
    for g in range(groups):
        lanes = slice(g * 128, (g + 1) * 128)
        grouter_ref[:, lanes] = small_all[g, 0:experts, :] + small_sib[g, 0:experts, :]
        ggain_ref[:, lanes] = small_all[g, experts : experts + 2, :] + small_sib[g, experts : experts + 2, :]
    gbias_ref[...] = small_all[groups, 0 : 2 * pairs, :]
    @pl.when(s == 1)
    def _():
        dy_copy.wait_send()
        for sem in sem_pass:
            all_sent(relay_buf.at[0 : len(relayed)], sem)
        all_sent(rs_in, sem_ring_sum)
        all_sent(relay_q, sem_pass_q)
        wait_back(eob, eoret, sem_re)
        layer_output()
        hand_out(out_own, secout_ref, sem_so)

    all_sent(rr.at[1:experts], sem_routes)
    all_sent(eo_send, sem_eo)
    all_sent(cg_send, sem_cg)
    all_sent(gg_part.at[0], sem_gg_core)
    all_sent(small_in.at[1:experts], sem_small)
    all_sent(small_all.at[1:experts], sem_back)
    all_sent(small_all, sem_sums)
    all_sent(shared_ref.at[1:experts], sem_ring_out)


def widen_kernel(
    sec_ref, ing_ref, gain_ref, shared_ref, bias_ref, router_ref, up_ref, down_ref,
    sec_out, ing_out, gain_out, bias_out, router_out, qkv_out, out_out, up_out, down_out,
    up_wide, down_wide, qkv_wide, out_wide, bias_wide, out_sem,
):
    f32 = jnp.float32
    parts = 6
    experts, shared_rows, width = shared_ref.shape
    cols = out_wide.shape[0]
    qkv_rows = 3 * cols // experts
    wide = ((up_ref, up_wide, up_out), (down_ref, down_wide, down_out))
    stores = []

    def store(src, dst):
        copy = pltpu.make_async_copy(src, dst, out_sem.at[len(stores)])
        copy.start()
        stores.append(copy)

    def widen(i, n):
        src, dst, out = wide[i]
        size = src.shape[0] // parts
        rows = pl.ds(n * size, size)
        dst[rows, :] = src[rows, :].astype(f32)
        store(dst.at[rows], out.at[rows])

    def turn_qkv(c):
        block = shared_ref[:, 0:qkv_rows, :].reshape(3 * cols, width)[c * cols : (c + 1) * cols]
        qkv_wide[c] = jnp.transpose(block.astype(f32))
        store(qkv_wide.at[c], qkv_out.at[c])

    store(sec_ref, sec_out)
    store(ing_ref, ing_out)
    widen(0, 0)
    store(gain_ref, gain_out)
    store(router_ref, router_out)
    for h in range(bias_wide.shape[0]):
        bias_wide[h] = bias_ref[h : h + 1, 0 : bias_wide.shape[2]]
    store(bias_wide, bias_out)
    widen(0, 1)
    widen(0, 2)
    turn_qkv(0)
    widen(0, 3)
    widen(0, 4)
    turn_qkv(1)
    widen(0, 5)
    widen(1, 0)
    turn_qkv(2)
    widen(1, 1)
    widen(1, 2)
    out_block = jnp.concatenate(
        [
            shared_ref[e, qkv_rows:, h * cols : (h + 1) * cols].astype(f32)
            for e in range(experts)
            for h in range(2)
        ],
        axis=0,
    )
    out_wide[...] = jnp.transpose(out_block)
    store(out_wide, out_out)
    widen(1, 3)
    widen(1, 4)
    widen(1, 5)
    for copy in stores:
        copy.wait()


def fused_local(
    tokens,
    cotangent,
    segments,
    pad_mask,
    routes,
    dist_bucket,
    norm_gains,
    qkv_weight,
    out_weight,
    rel_bias,
    router_weight,
    expert_up,
    expert_down,
):
    micro, _, length, width = tokens.shape
    experts = router_weight.shape[2]
    cap = max(2, 3 * length // experts)
    cols = out_weight.shape[1]
    heads = rel_bias.shape[2]
    ffn = expert_up.shape[3]
    slots = experts * cap
    pairs = cols // 128
    shared_rows = 3 * cols // experts + width // experts // 2
    lay = Layout()
    lay.experts = experts
    lay.cap = cap
    lay.buckets = rel_bias.shape[1]
    lay.wide = min(ffn, 256)
    chunks = experts // 2
    lay.sems = (36, 7 * chunks + experts + 8 * (experts - 1) + 24)
    bf = jnp.bfloat16
    f32 = jnp.float32
    vm = pltpu.VMEM
    shape = jax.ShapeDtypeStruct
    dma = pltpu.SemaphoreType.DMA
    scratch = [
        vm((micro, length), jnp.int32),
        vm((micro, length), jnp.int32),
        vm((micro, 2, length), jnp.int32),
        vm((1, length), jnp.int32),
        vm((2, width), bf),
        vm((heads, lay.buckets), bf),
        vm((experts, width), bf),
        vm((width, ffn), bf),
        vm((ffn, width), bf),
        vm((ffn, width), bf),
        vm((width, ffn), bf),
        vm((3, cols, width), bf),
        vm((width, cols), bf),
        vm((3, width, cols), bf),
        vm((cols, width), bf),
        vm((micro, length, width), bf),
        vm((length, width), bf),
        vm((experts, micro, 2, length), jnp.int32),
        vm((slots, length), bf),
        vm((micro, pairs, length, 2 * length), f32),
        vm((micro, pairs, length, 2 * length), f32),
        vm((micro, length, width), bf),
        vm((3, micro, length, cols), bf),
        vm((micro, length, cols), bf),
        vm((length, width), bf),
        vm((length, width), bf),
        vm((length, width), f32),
        vm((length, width), bf),
        vm((experts, length), f32),
        vm((experts, length), f32),
        vm((experts, width), bf),
        vm((2 * pairs, length, length), f32),
        vm((experts, cap, width), bf),
        vm((experts, micro, cap, width), bf),
        vm((experts, cap, width), bf),
        vm((experts, micro, cap, width), bf),
        vm((experts, micro, cap, ffn), bf),
        vm((experts, micro, cap, ffn), bf),
        vm((micro, 2, cap, width), f32),
        vm((experts, cap, width), bf),
        vm((experts, cap, width), bf),
        vm((experts, cap, width), bf),
        vm((experts, cap, width), bf),
        vm((length, width), f32),
        vm((experts, micro, cap, experts), f32),
        vm((experts, micro, cap, 1), f32),
        vm((experts, micro, cap, width), bf),
        vm((micro, experts, 8, 128), f32),
        vm((experts, 8, 128), f32),
        vm((experts, 8, 128), f32),
        vm((experts, 8, 128), f32),
        vm((experts, micro, cap, ffn), bf),
        vm((experts, cap, width), bf),
        vm((experts, cap, width), bf),
        vm((experts, cap, width), bf),
        vm((experts, cap, width), bf),
        vm((length, width), f32),
        vm((micro, length, width), bf),
        vm((micro, length, cols), bf),
        vm((3, micro, length, cols), bf),
        vm((length, width), bf),
        vm((length, width), bf),
        vm((length, width), f32),
        vm((length, width), bf),
        vm((micro, experts, length, width), bf),
        vm((experts, micro, length, cols), bf),
        vm((micro, 3 * cols, length), bf),
        vm((experts, micro, 3 * cols // experts, length), bf),
        vm((width, length), bf),
        vm((experts, micro, width // experts, length), bf),
        vm((experts, 2 * experts, 128), f32),
        vm((experts, 2 * experts, 128), f32),
        vm((experts, 2 * experts, 128), f32),
        vm((experts, 2 * experts, 128), f32),
        vm((length, width), bf),
        vm((experts, shared_rows, width), bf),
        vm((experts - 1, shared_rows, width), bf),
        vm((4, cap, width), bf),
        vm((2, micro, 3 * cols // experts, length), bf),
        dma((12,)),
        dma((lay.sems[0],)),
        dma((lay.sems[1],)),
    ]
    whole = pl.BlockSpec(memory_space=pltpu.VMEM)
    anywhere = pl.BlockSpec(memory_space=pl.ANY)
    out_shape = (
        vm((micro, length, width // 2), f32),
        vm((micro, length, width // 2), f32),
        vm((2, width), f32),
        vm((experts, shared_rows, width), bf),
        vm((heads, 128), f32),
        vm((experts, width), f32),
        vm((width, ffn), bf),
        vm((ffn, width), bf),
    )
    results = pl.pallas_call(
        partial(layer_kernel, lay),
        out_shape=out_shape,
        in_specs=[anywhere] * 13,
        out_specs=[whole] * 8,
        scratch_shapes=scratch,
        name="two_sections",
        compiler_params=pltpu.CompilerParams(
            collective_id=0, has_side_effects=True, vmem_limit_bytes=56 * 1024 * 1024
        ),
    )(
        tokens[:, 0],
        cotangent[:, 0],
        segments[:, 0],
        pad_mask[:, 0],
        routes[:, 0].transpose(0, 2, 1),
        dist_bucket[None],
        norm_gains[0],
        qkv_weight[0].transpose(1, 0, 2),
        out_weight[0],
        rel_bias[0].T,
        router_weight[0].T,
        expert_up[0, 0],
        expert_down[0, 0],
    )
    section_out, input_grads, gains, bias, router, qkv, out, up, down = pl.pallas_call(
        widen_kernel,
        out_shape=(
            shape((micro, length, width // 2), f32),
            shape((micro, length, width // 2), f32),
            shape((2, width), f32),
            shape((heads, 1, lay.buckets), f32),
            shape((experts, width), f32),
            shape((3, width, cols), f32),
            shape((cols, width), f32),
            shape((width, ffn), f32),
            shape((ffn, width), f32),
        ),
        in_specs=[whole] * 8,
        out_specs=[anywhere] * 9,
        scratch_shapes=[
            vm((width, ffn), f32),
            vm((ffn, width), f32),
            vm((3, width, cols), f32),
            vm((cols, width), f32),
            vm((heads, 1, lay.buckets), f32),
            dma((21,)),
        ],
        name="widen",
        compiler_params=pltpu.CompilerParams(vmem_limit_bytes=40 * 1024 * 1024),
    )(*[pltpu.with_memory_space_constraint(result, pltpu.VMEM) for result in results])
    return (
        section_out[None, :, None],
        input_grads[None, :, None],
        gains[None],
        qkv.transpose(1, 0, 2)[None],
        out[None],
        bias.transpose(1, 2, 0),
        router.T[None],
        up[None, None],
        down[None, None],
    )


def fits_kernel(mesh):
    return mesh.shape["section"] == 2 and mesh.shape["tensor"] == 2 and mesh.shape["dp"] == 8


def solution(mesh):
    in_specs = (
        P(None, "dp", None, None),
        P(None, "dp", None, None),
        P(None, "dp", None),
        P(None, "dp", None),
        P(None, "dp", None, None),
        P(),
        P("section", None, None),
        P("section", None, None, "tensor"),
        P("section", "tensor", None),
        P("section", None, "tensor"),
        P("section", None, None),
        P("section", "dp", None, "tensor"),
        P("section", "dp", "tensor", None),
    )
    out_specs = (
        P("section", None, "dp", None, "tensor"),
        P("section", None, "dp", None, "tensor"),
        P("section", None, None),
        P("section", None, None, "tensor"),
        P("section", "tensor", None),
        P("section", None, "tensor"),
        P("section", None, None),
        P("section", "dp", None, "tensor"),
        P("section", "dp", "tensor", None),
    )
    body = fused_local if fits_kernel(mesh) else local
    return jax.shard_map(body, mesh=mesh, in_specs=in_specs, out_specs=out_specs, check_vma=False)
```
